32 devices in a mesh: groups: 2 (over x), ctx: 16 (over z, y, core).
Axes of the slice: x: 2, y: 2, z: 4, core: 2. Of those that a mesh axis runs over, the one named last changes fastest.
Arguments:
- queries: bfloat16 [4096, 8192], P(('groups', 'ctx')), parts along dimension 0, may hold values from -112 to 112
- keys: bfloat16 [4096, 1024], P(('groups', 'ctx')), parts along dimension 0, may hold values from -4.04 to 4.04
- values: bfloat16 [4096, 1024], P(('groups', 'ctx')), parts along dimension 0, may hold values from -4 to 4
- norm_gain: float32 [8192], replicated, may hold values from 0.1 to 1.9
- expert_ids: int32 [4096, 2], P(('groups', 'ctx')), parts along dimension 0, may hold values from 0 to 15, as said below
- gates: float32 [4096, 2], P(('groups', 'ctx')), parts along dimension 0, may hold values from 0.2 to 1
- w_gate: bfloat16 [8192, 12288], P(None, 'ctx'), may hold values from -0.0625 to 0.0625
- w_up: bfloat16 [8192, 12288], P(None, 'ctx'), may hold values from -0.0625 to 0.0625
- w_down: bfloat16 [12288, 8192], P('ctx'), may hold values from -0.0546875 to 0.0546875
Outputs:
- attention: bfloat16 [4096, 8192], P(('groups', 'ctx')), parts along dimension 0
- mixed: bfloat16 [4096, 8192], P(('groups', 'ctx')), parts along dimension 0
The draws below stay inside these ranges and needn't reach their ends.
There are 2 independent parts, one for each index of `groups`. The reference program is written for one: setup_inputs(seed, part) draws one part's arguments, and reference() takes and returns one part's arrays. A program takes and returns all parts, laid end to end along the dimension named above; an argument that names none is the same for every part. Nothing has to cross between parts.
Inputs may be any that keep to these rules, and one draw needn't show every extreme that they name: `expert_ids`: each token names two different experts. In each aligned block of 128 rows (the rows of one device) between 8 and 16 rows name expert 0, and in some block exactly 16 do.
All inputs are finite; a program needn't handle non-finite values.
Results may differ from the reference program's by a relative error of at most 0.02.
Values may be sent and summed in bfloat16 or wider, within the bound.
No kernel may reach another device: no remote copies, remote signals or barrier semaphores. Data moves between devices by JAX's collectives and lax.ppermute only.
A program may use at most 128 MiB of HBM per device.

```python
import jax
import jax.numpy as jnp
from jax import lax

D = 8192
HQ = 64
HK = 8
DH = 128
EXPERTS = 16
TOP = 2
FF = 12288
TOK_DEV = 128
CAP = 16
FF_DEV = 768
KVW = 1024
SEQ = 2048


def shared_keys(key):
    base = jax.random.normal(key, (SEQ, HK * DH), jnp.float32)
    return jnp.clip(base, -4.0, 4.0)


def draw_keys(key, part):
    base = shared_keys(key)
    result = base
    return result.astype(jnp.bfloat16)


def draw_queries(key, part):
    key = jax.random.fold_in(key, 7)
    result = jnp.clip(jax.random.normal(key, (SEQ, HQ * DH), jnp.float32), -4.0, 4.0)
    return result.astype(jnp.bfloat16)


def draw_expert_ids(key, part):
    key = jax.random.fold_in(key, 11)
    blocks = SEQ // TOK_DEV
    keys_all = jax.random.split(key, 6)
    counts = jax.random.randint(keys_all[0], (blocks,), CAP // 2, CAP + 1)
    full_block = jax.random.randint(keys_all[1], (), 0, blocks)
    counts = counts.at[full_block].set(CAP)
    scores = jax.random.randint(keys_all[2], (blocks, TOK_DEV), 0, 1 << 20)
    scores = scores * TOK_DEV + jnp.arange(TOK_DEV, dtype=jnp.int32)[None, :]
    order = jnp.argsort(jnp.argsort(scores, axis=1), axis=1).astype(jnp.int32)
    chosen = order < counts[:, None]
    position = jax.random.randint(keys_all[3], (blocks, TOK_DEV), 0, 2)
    first = jax.random.randint(keys_all[4], (blocks, TOK_DEV), 1, EXPERTS)
    step = jax.random.randint(keys_all[5], (blocks, TOK_DEV), 1, EXPERTS - 1)
    second = 1 + (first - 1 + step) % (EXPERTS - 1)
    column_a = jnp.where(chosen, jnp.where(position == 0, 0, first), first)
    column_b = jnp.where(chosen, jnp.where(position == 0, first, 0), second)
    result = jnp.stack([column_a.reshape(-1), column_b.reshape(-1)], axis=1)
    return result.astype(jnp.int32)


def block_scale(rng, dims, shards, least, top_value):
    def one(dim, parts):
        steps = jax.random.uniform(jax.random.fold_in(jax.random.fold_in(rng, 6), dim), (parts,), jnp.float32, least / len(shards), top_value / len(shards))
        return jnp.repeat(jnp.exp(steps), dims[dim] // parts).reshape((-1,) + (1,) * (len(dims) - dim - 1))

    gain = one(*shards[0])
    for cut in shards[1:]:
        gain = gain * one(*cut)
    return gain


def scatter_about(stream_key, extent, scale, bound, cuts=(), kind=jnp.bfloat16):
    level = block_scale(stream_key, extent, cuts, -0.22, 0.18) if cuts else 1.0
    entries = jax.random.normal(stream_key, extent, jnp.float32) * scale * level
    return jnp.minimum(jnp.maximum(entries, -bound), bound).astype(kind)


def setup_inputs(seed: int = 0, part: int = 0) -> dict:
    streams_of = jax.random.split(jax.random.key(seed), 10)
    part_splits = jax.random.split(jax.random.fold_in(streams_of[9], part), 10)
    return {
        "queries": draw_queries(jax.random.fold_in(jax.random.fold_in(streams_of[9], part), 71), part),
        "keys": draw_keys(jax.random.fold_in(jax.random.fold_in(streams_of[9], part), 71), part),
        "values": scatter_about(part_splits[2], (SEQ, KVW), 1.0, 4.0, ((0, 16),)),
        "norm_gain": jnp.clip(1.0 + 0.18 * jax.random.normal(streams_of[3], (D,), jnp.float32), 0.1, 1.9),
        "expert_ids": draw_expert_ids(jax.random.fold_in(jax.random.fold_in(streams_of[9], part), 71), part),
        "gates": jnp.clip(0.2 + 0.8 * jax.random.uniform(part_splits[5], (SEQ, TOP), jnp.float32) ** block_scale(part_splits[5], (SEQ, TOP), ((0, 16),), -0.2, 0.2), 0.2, 1.0),
        "w_gate": scatter_about(streams_of[6], (D, FF), D ** -0.5, 0.0625, ((1, 16),)),
        "w_up": scatter_about(streams_of[7], (D, FF), D ** -0.5, 0.0625, ((1, 16),)),
        "w_down": scatter_about(streams_of[8], (FF, D), FF ** -0.5, 0.0546875, ((0, 16),)),
    }


def attend(queries, keys, values):
    seq = queries.shape[0]
    group = HQ // HK
    scale = 1.0 / DH ** 0.5
    qf = queries.astype(jnp.float32).reshape(seq, HK, group, DH)
    kf = keys.astype(jnp.float32).reshape(seq, HK, DH)
    vf = values.astype(jnp.float32).reshape(seq, HK, DH)
    block = min(seq, 256)
    count = seq // block
    key_pos = jnp.arange(seq, dtype=jnp.int32)

    def one_block(index):
        start = index * block
        query_rows = lax.dynamic_slice_in_dim(qf, start, block, 0)
        scores = jnp.einsum('qhgd,khd->qhgk', query_rows, kf) * scale
        query_pos = start + jnp.arange(block, dtype=jnp.int32)
        allowed = (key_pos[None, :] <= query_pos[:, None])[:, None, None, :]
        scores = jnp.where(allowed, scores, -jnp.inf)
        top = lax.optimization_barrier(jnp.max(scores, axis=-1, keepdims=True))
        weights = jnp.where(allowed, jnp.exp(scores - top), 0.0)
        total = lax.optimization_barrier(jnp.sum(weights, axis=-1))
        rounded = lax.optimization_barrier(weights.astype(jnp.bfloat16)).astype(jnp.float32)
        summed = jnp.einsum('qhgk,khd->qhgd', rounded, vf)
        result = summed / total[..., None]
        return result.reshape(block, HQ * DH).astype(jnp.bfloat16)
    blocks = lax.map(one_block, jnp.arange(count, dtype=jnp.int32))
    return blocks.reshape(seq, HQ * DH)

def reference(queries, keys, values, norm_gain, expert_ids, gates, w_gate, w_up, w_down):
    attention = attend(queries, keys, values)
    wide = attention.astype(jnp.float32)
    factor = lax.rsqrt(lax.optimization_barrier(jnp.mean(wide * wide, axis=-1, keepdims=True)) + 1e-05)
    normed = (wide * factor * norm_gain[None, :]).astype(jnp.bfloat16)
    seq = queries.shape[0]
    blocks = seq // TOK_DEV
    hits = (expert_ids == 0).astype(jnp.int32)
    chosen = lax.optimization_barrier(jnp.sum(hits, axis=1)).reshape(blocks, TOK_DEV)
    slot = (jnp.cumsum(chosen, axis=1) - chosen).astype(jnp.int32)
    block_id = jnp.arange(blocks, dtype=jnp.int32)[:, None]
    place = (block_id * CAP + slot).astype(jnp.int32).reshape(-1)
    total_rows = blocks * CAP
    target = jnp.where(chosen.reshape(-1) > 0, place, total_rows).astype(jnp.int32)
    rows = jnp.zeros((total_rows + 1, D), jnp.bfloat16).at[target].set(normed)[:total_rows]
    pieces = FF // FF_DEV

    def add_piece(total, index):
        start = (index * FF_DEV).astype(jnp.int32)
        gate_cols = lax.dynamic_slice_in_dim(w_gate, start, FF_DEV, 1)
        up_cols = lax.dynamic_slice_in_dim(w_up, start, FF_DEV, 1)
        down_rows = lax.dynamic_slice_in_dim(w_down, start, FF_DEV, 0)
        gate = jnp.dot(rows, gate_cols, preferred_element_type=jnp.float32)
        upper = jnp.dot(rows, up_cols, preferred_element_type=jnp.float32)
        hidden = (jax.nn.silu(gate) * upper).astype(jnp.bfloat16)
        part = jnp.dot(hidden, down_rows, preferred_element_type=jnp.float32).astype(jnp.bfloat16)
        return (total + lax.optimization_barrier(part).astype(jnp.float32), None)
    start_total = jnp.zeros((total_rows, D), jnp.float32)
    summed, _ = lax.scan(add_piece, start_total, jnp.arange(pieces, dtype=jnp.int32))
    expert_out = summed.astype(jnp.bfloat16)
    picked = jnp.take(expert_out, jnp.minimum(target, total_rows - 1), axis=0).astype(jnp.float32)
    weight = lax.optimization_barrier(jnp.sum(gates * hits.astype(jnp.float32), axis=1))
    mixed = (picked * weight[:, None]).astype(jnp.bfloat16)
    return (attention, mixed)
```

```python
import functools
import math

import jax
import jax.numpy as jnp
from jax import lax
from jax.experimental import pallas as pl
from jax.experimental.pallas import tpu as pltpu
from jax.sharding import PartitionSpec as P

HQ = 64
HK = 8
DH = 128
CAP = 16
GROUP = HQ // HK
WIDE = GROUP * DH
LOG_SCALE = math.log2(math.e) / math.sqrt(DH)
MASKED = -1e30
STACK = 2
MIB = 1 << 20


def ring_order(chips):
    return list(range(0, chips, 2)) + list(range(1, chips, 2))[::-1]


def permutations(chips):
    order = ring_order(chips)
    right, left = [], []
    for place in range(chips):
        here, there = order[place], order[(place + 1) % chips]
        for core in range(2):
            right.append((2 * here + core, 2 * there + core))
            left.append((2 * there + core, 2 * here + core))
    sibling = [(i, i ^ 1) for i in range(2 * chips)]
    return right, left, sibling


def chip_at(me, step, chips):
    chip = me // 2
    place = jnp.where(chip % 2 == 0, chip // 2, chips - 1 - chip // 2)
    source = (place - step + 2 * chips) % chips
    return jnp.where(source < chips // 2, 2 * source, 2 * (chips - 1 - source) + 1)


def head_rows(q_ref, first):
    return jnp.concatenate(
        [q_ref[:, h * DH : (h + 1) * DH] for h in range(first, first + STACK)], axis=0
    )


def with_ones(values):
    return jnp.concatenate([values, jnp.ones_like(values)], axis=1)


def scores_of(queries, keys):
    return LOG_SCALE * lax.dot_general(
        queries, keys, (((1,), (1,)), ((), ())), preferred_element_type=jnp.float32
    )


def pack_stats(tops, totals, tokens):
    lane = lax.broadcasted_iota(jnp.int32, (tokens, DH), 1)
    tile = jnp.zeros((tokens, DH), jnp.float32)
    for h in range(GROUP):
        tile = jnp.where(lane == h, tops[h], tile)
        tile = jnp.where(lane == GROUP + h, totals[h], tile)
    return tile


def split_heads(stacked, tokens):
    return [stacked[i * tokens : (i + 1) * tokens] for i in range(STACK)]


def own_kernel(me_ref, q_ref, key_ref, value_ref, sib_key_ref, sib_value_ref, acc_ref, stat_ref):
    tokens = q_ref.shape[0]
    keys = jnp.concatenate([key_ref[...], sib_key_ref[...]], axis=0)
    values = with_ones(jnp.concatenate([value_ref[...], sib_value_ref[...]], axis=0))
    shape = (STACK * tokens, 2 * tokens)
    token = lax.broadcasted_iota(jnp.int32, shape, 0) % tokens
    column = lax.broadcasted_iota(jnp.int32, shape, 1)
    limit = jnp.where(me_ref[0] % 2 == 1, 2 * tokens, tokens)
    allowed = column <= jnp.where(column < tokens, token, limit - 1)
    tops, totals = [], []
    for first in range(0, GROUP, STACK):
        scores = jnp.where(allowed, scores_of(head_rows(q_ref, first), keys), MASKED)
        top = jnp.max(scores, axis=1, keepdims=True)
        weights = jnp.exp2(scores - top).astype(jnp.bfloat16)
        update = jnp.dot(weights, values, preferred_element_type=jnp.float32)
        acc_ref[0, first * tokens : (first + STACK) * tokens, :] = update[:, :DH]
        tops += split_heads(top, tokens)
        totals += split_heads(update[:, DH:], tokens)
    stat_ref[0] = pack_stats(tops, totals, tokens)


def fold_chip(q_ref, keys, values, acc_ref, stat_ref):
    tokens = q_ref.shape[0]
    values = with_ones(values)
    tops, totals = [], []
    stats = stat_ref[0]
    for first in range(0, GROUP, STACK):
        scores = scores_of(head_rows(q_ref, first), keys)
        old = jnp.concatenate([stats[:, h : h + 1] for h in range(first, first + STACK)], axis=0)
        total = jnp.concatenate(
            [stats[:, GROUP + h : GROUP + h + 1] for h in range(first, first + STACK)], axis=0
        )
        top = jnp.maximum(old, jnp.max(scores, axis=1, keepdims=True))
        factor = jnp.exp2(old - top)
        weights = jnp.exp2(scores - top).astype(jnp.bfloat16)
        update = jnp.dot(weights, values, preferred_element_type=jnp.float32)
        rows = slice(first * tokens, (first + STACK) * tokens)
        acc_ref[0, rows, :] = acc_ref[0, rows, :] * factor + update[:, :DH]
        tops += split_heads(top, tokens)
        totals += split_heads(total * factor + update[:, DH:], tokens)
    stat_ref[0] = pack_stats(tops, totals, tokens)


def step_kernel(chips, step, me_ref, q_ref, *refs):
    (rk, rv, rsk, rsv, lk, lv, lsk, lsv, acc_in, stat_in, acc_ref, stat_ref) = refs
    me = me_ref[0]
    acc_ref[...] = acc_in[...]
    stat_ref[...] = stat_in[...]
    for place, key, value, sib_key, sib_value in (
        (step, rk, rv, rsk, rsv),
        (-step, lk, lv, lsk, lsv),
    ):

        @pl.when(chip_at(me, place, chips) < me // 2)
        def _():
            keys = jnp.concatenate([key[...], sib_key[...]], axis=0)
            values = jnp.concatenate([value[...], sib_value[...]], axis=0)
            fold_chip(q_ref, keys, values, acc_ref, stat_ref)


def last_kernel(chips, me_ref, q_ref, *refs):
    (key, value, sib_key, sib_value, acc_in, stat_in, gain_ref, table_ref) = refs[:8]
    (out_ref, low_ref, high_ref, acc_ref, stat_ref) = refs[8:]
    tokens = q_ref.shape[0]
    head = pl.program_id(0)
    me = me_ref[0]
    acc_ref[...] = acc_in[...]
    stat_ref[...] = stat_in[...]

    @pl.when(chip_at(me, chips // 2, chips) < me // 2)
    def _():
        keys = jnp.concatenate([key[...], sib_key[...]], axis=0)
        values = jnp.concatenate([value[...], sib_value[...]], axis=0)
        fold_chip(q_ref, keys, values, acc_ref, stat_ref)

    stats = stat_ref[0]
    pieces = []
    for h in range(GROUP):
        total = stats[:, GROUP + h : GROUP + h + 1]
        pieces.append((acc_ref[0, h * tokens : (h + 1) * tokens, :] / total).astype(jnp.bfloat16))
    columns = pl.ds(pl.multiple_of(head * WIDE, WIDE), WIDE)
    out_ref[:, columns] = jnp.concatenate(pieces, axis=1)

    @pl.when(head == HK - 1)
    def _():
        width = out_ref.shape[1]
        picked = jnp.dot(table_ref[...], out_ref[...], preferred_element_type=jnp.float32)
        mean = jnp.sum(picked * picked, axis=1, keepdims=True) / width
        normed = (picked * lax.rsqrt(mean + 1e-05) * gain_ref[...]).astype(jnp.bfloat16)
        low_ref[...] = normed[:, : width // 2]
        high_ref[...] = normed[:, width // 2 :]


def attention_calls(me, queries, gain, table, chips, own, steps, opposite):
    tokens, width = queries.shape
    half = chips // 2
    head_block = pl.BlockSpec((tokens, WIDE), lambda g, me: (0, g))
    kv_block = pl.BlockSpec((tokens, DH), lambda g, me: (0, g))
    acc_block = pl.BlockSpec((1, GROUP * tokens, DH), lambda g, me: (g, 0, 0))
    stat_block = pl.BlockSpec((1, tokens, DH), lambda g, me: (g, 0, 0))
    state_shapes = [
        jax.ShapeDtypeStruct((HK, GROUP * tokens, DH), jnp.float32),
        jax.ShapeDtypeStruct((HK, tokens, DH), jnp.float32),
    ]
    params = pltpu.CompilerParams(
        dimension_semantics=("arbitrary",), vmem_limit_bytes=24 * MIB
    )

    def cost(keys):
        return pl.CostEstimate(
            flops=4 * tokens * width * keys, bytes_accessed=12 * MIB, transcendentals=tokens * HQ * keys
        )

    state = pl.pallas_call(
        own_kernel,
        grid_spec=pltpu.PrefetchScalarGridSpec(
            num_scalar_prefetch=1,
            grid=(HK,),
            in_specs=[head_block] + [kv_block] * 4,
            out_specs=[acc_block, stat_block],
        ),
        out_shape=state_shapes,
        compiler_params=params,
        cost_estimate=cost(2 * tokens),
        name="attend_own",
    )(me, queries, *own)
    for step, pieces in enumerate(steps, start=1):
        state = pl.pallas_call(
            functools.partial(step_kernel, chips, step),
            grid_spec=pltpu.PrefetchScalarGridSpec(
                num_scalar_prefetch=1,
                grid=(HK,),
                in_specs=[head_block] + [kv_block] * 8 + [acc_block, stat_block],
                out_specs=[acc_block, stat_block],
            ),
            out_shape=state_shapes,
            compiler_params=params,
            cost_estimate=cost(4 * tokens),
            name="attend_step",
        )(me, queries, *pieces, *state)
    whole = lambda shape: pl.BlockSpec(shape, lambda g, me: (0, 0))
    return pl.pallas_call(
        functools.partial(last_kernel, chips),
        grid_spec=pltpu.PrefetchScalarGridSpec(
            num_scalar_prefetch=1,
            grid=(HK,),
            in_specs=[head_block]
            + [kv_block] * 4
            + [acc_block, stat_block, whole((1, width)), whole((CAP, tokens))],
            out_specs=[whole((tokens, width)), whole((CAP, width // 2)), whole((CAP, width // 2))],
            scratch_shapes=[
                pltpu.VMEM((1, GROUP * tokens, DH), jnp.float32),
                pltpu.VMEM((1, tokens, DH), jnp.float32),
            ],
        ),
        out_shape=[
            jax.ShapeDtypeStruct((tokens, width), jnp.bfloat16),
            jax.ShapeDtypeStruct((CAP, width // 2), jnp.bfloat16),
            jax.ShapeDtypeStruct((CAP, width // 2), jnp.bfloat16),
        ],
        compiler_params=params,
        cost_estimate=cost(2 * tokens),
        name="attend_last",
    )(me, queries, *opposite, *state, gain, table)


def expert_kernel(count, depth_steps, *refs):
    lows, highs = refs[:count], refs[count : 2 * count]
    gate_ref, up_ref, down_ref, own_ref, sib_ref = refs[2 * count : 2 * count + 5]
    rows_ref, gate_sum, up_sum, hidden_ref, sems = refs[2 * count + 5 :]
    step = pl.program_id(0)
    half = rows_ref.shape[1] // 2
    depth = gate_ref.shape[0]

    @pl.when(step == 0)
    def _():
        copies = []
        for side, blocks in enumerate((lows, highs)):
            for j, block in enumerate(blocks):
                target = rows_ref.at[pl.ds(j * CAP, CAP), pl.ds(side * half, half)]
                copies.append(pltpu.make_async_copy(block, target, sems.at[side * count + j]))
        for copy in copies:
            copy.start()
        for copy in copies:
            copy.wait()
        gate_sum[...] = jnp.zeros_like(gate_sum)
        up_sum[...] = jnp.zeros_like(up_sum)

    @pl.when(step < depth_steps)
    def _():
        columns = pl.ds(pl.multiple_of(step * depth, depth), depth)
        part = rows_ref[:, columns]
        gate_sum[...] += jnp.dot(part, gate_ref[...], preferred_element_type=jnp.float32)
        up_sum[...] += jnp.dot(part, up_ref[...], preferred_element_type=jnp.float32)

    @pl.when(step == depth_steps - 1)
    def _():
        gate = gate_sum[...]
        hidden_ref[...] = (gate / (1.0 + jnp.exp(-gate)) * up_sum[...]).astype(jnp.bfloat16)

    @pl.when(step >= depth_steps)
    def _():
        part = jnp.dot(hidden_ref[...], down_ref[...], preferred_element_type=jnp.float32)
        part = part.astype(jnp.bfloat16)
        middle = part.shape[0] // 2
        own_ref[...] = part[:middle]
        sib_ref[...] = part[middle:]


def expert_call(lows, highs, w_gate, w_up, w_down):
    count = len(lows)
    rows = count * CAP
    width, units = w_gate.shape
    depth = min(1024, width)
    depth_steps = width // depth
    cols = min(1024, width)
    out_steps = width // cols
    weight_block = pl.BlockSpec((depth, units), lambda i: (jnp.minimum(i, depth_steps - 1), 0))
    down_block = pl.BlockSpec((units, cols), lambda i: (0, jnp.maximum(i - depth_steps, 0)))
    out_block = pl.BlockSpec((rows // 2, cols), lambda i: (0, jnp.maximum(i - depth_steps, 0)))
    anywhere = pl.BlockSpec(memory_space=pl.ANY)
    return pl.pallas_call(
        functools.partial(expert_kernel, count, depth_steps),
        grid=(depth_steps + out_steps,),
        in_specs=[anywhere] * (2 * count) + [weight_block, weight_block, down_block],
        out_specs=[out_block, out_block],
        out_shape=[jax.ShapeDtypeStruct((rows // 2, width), jnp.bfloat16)] * 2,
        scratch_shapes=[
            pltpu.VMEM((rows, width), jnp.bfloat16),
            pltpu.VMEM((rows, units), jnp.float32),
            pltpu.VMEM((rows, units), jnp.float32),
            pltpu.VMEM((rows, units), jnp.bfloat16),
            pltpu.SemaphoreType.DMA((2 * count,)),
        ],
        compiler_params=pltpu.CompilerParams(
            dimension_semantics=("arbitrary",), vmem_limit_bytes=40 * MIB
        ),
        cost_estimate=pl.CostEstimate(
            flops=6 * rows * width * units,
            bytes_accessed=6 * width * units + 4 * rows * width,
            transcendentals=rows * units,
        ),
        name="expert",
    )(*lows, *highs, w_gate, w_up, w_down)


def spread_kernel(own_ref, sib_ref, right_ref, left_ref, table_ref, weight_ref, out_ref):
    total = own_ref[...].astype(jnp.float32) + sib_ref[...].astype(jnp.float32)
    total += right_ref[...].astype(jnp.float32) + left_ref[...].astype(jnp.float32)
    spread = lax.dot_general(
        table_ref[...],
        total.astype(jnp.bfloat16),
        (((0,), (0,)), ((), ())),
        preferred_element_type=jnp.float32,
    )
    out_ref[...] = (spread * weight_ref[...]).astype(jnp.bfloat16)


def spread_call(own, sib, right, left, table, weight):
    tokens = table.shape[1]
    width = own.shape[1]
    cols = min(2048, width)
    block = pl.BlockSpec((CAP, cols), lambda i: (0, i))
    return pl.pallas_call(
        spread_kernel,
        grid=(width // cols,),
        in_specs=[block] * 4
        + [pl.BlockSpec((CAP, tokens), lambda i: (0, 0)), pl.BlockSpec((tokens, 1), lambda i: (0, 0))],
        out_specs=pl.BlockSpec((tokens, cols), lambda i: (0, i)),
        out_shape=jax.ShapeDtypeStruct((tokens, width), jnp.bfloat16),
        compiler_params=pltpu.CompilerParams(dimension_semantics=("arbitrary",)),
        name="spread",
    )(own, sib, right, left, table, weight)


def add(a, b):
    return (a.astype(jnp.float32) + b.astype(jnp.float32)).astype(jnp.bfloat16)


def per_device(chips, queries, keys, values, norm_gain, expert_ids, gates, w_gate, w_up, w_down):
    right, left, sibling = permutations(chips)
    half = chips // 2
    go_right = lambda x: lax.ppermute(x, "ctx", right)
    go_left = lambda x: lax.ppermute(x, "ctx", left)
    swap = lambda x: lax.ppermute(x, "ctx", sibling)

    me = lax.axis_index("ctx").astype(jnp.int32).reshape(1)
    tokens = queries.shape[0]
    hits = (expert_ids == 0).astype(jnp.float32)
    chosen = jnp.sum(hits, axis=1)
    position = jnp.arange(tokens, dtype=jnp.int32)
    before = (position[None, :] < position[:, None]).astype(jnp.float32)
    slot = jnp.sum(before * chosen[None, :], axis=1).astype(jnp.int32)
    table = jnp.logical_and(
        slot[None, :] == jnp.arange(CAP, dtype=jnp.int32)[:, None], chosen[None, :] > 0
    ).astype(jnp.bfloat16)
    weight = jnp.sum(gates * hits, axis=1, keepdims=True)

    own = (keys, values, swap(keys), swap(values))
    from_left, from_right = (keys, values), (keys, values)
    steps = []
    for _ in range(1, half):
        from_left = tuple(go_right(x) for x in from_left)
        from_right = tuple(go_left(x) for x in from_right)
        steps.append(
            (*from_left, *(swap(x) for x in from_left), *from_right, *(swap(x) for x in from_right))
        )
    far_keys, far_values = go_right(from_left[0]), go_left(from_right[1])
    opposite = (far_keys, far_values, swap(far_keys), swap(far_values))
    attention, low, high = attention_calls(
        me, queries, norm_gain[None, :], table, chips, own, steps, opposite
    )

    lows_right, highs_right, lows_left, highs_left = [low], [high], [low], [high]
    for _ in range(1, half):
        lows_right.append(go_right(lows_right[-1]))
        highs_right.append(go_right(highs_right[-1]))
        lows_left.append(go_left(lows_left[-1]))
        highs_left.append(go_left(highs_left[-1]))
    lows = lows_right + lows_left[1:] + [go_right(lows_right[-1])]
    highs = highs_right + highs_left[1:] + [go_left(highs_left[-1])]
    lows += [swap(x) for x in lows]
    highs += [swap(x) for x in highs]
    mine, theirs = expert_call(lows, highs, w_gate, w_up, w_down)

    other = swap(theirs)
    width = mine.shape[1]

    def block(index):
        rows = slice(index * CAP, (index + 1) * CAP)
        return mine[rows].astype(jnp.float32) + other[rows].astype(jnp.float32)

    far = block(chips - 1).astype(jnp.bfloat16)
    to_right = go_right(far[:, : width // 2])
    to_left = go_left(far[:, width // 2 :])
    for distance in range(half - 1, 0, -1):
        ahead, back = block(half - 1 + distance), block(distance)
        if distance == half - 1:
            ahead = jnp.concatenate(
                [ahead[:, : width // 2] + to_right.astype(jnp.float32), ahead[:, width // 2 :]], axis=1
            )
            back = jnp.concatenate(
                [back[:, : width // 2], back[:, width // 2 :] + to_left.astype(jnp.float32)], axis=1
            )
        else:
            ahead = ahead + to_right.astype(jnp.float32)
            back = back + to_left.astype(jnp.float32)
        to_right = go_right(ahead.astype(jnp.bfloat16))
        to_left = go_left(back.astype(jnp.bfloat16))
    mixed = spread_call(mine[:CAP], other[:CAP], to_right, to_left, table, weight)
    return (attention, mixed)


def solution(mesh):
    placed = (
        P(("groups", "ctx"), None),
        P(("groups", "ctx"), None),
        P(("groups", "ctx"), None),
        P(),
        P(("groups", "ctx"), None),
        P(("groups", "ctx"), None),
        P(None, "ctx"),
        P(None, "ctx"),
        P("ctx", None),
    )
    return jax.shard_map(
        functools.partial(per_device, mesh.shape["ctx"] // 2),
        mesh=mesh,
        in_specs=placed,
        out_specs=(P(("groups", "ctx"), None), P(("groups", "ctx"), None)),
        check_vma=False,
    )
```

```python
import functools
import math

import jax
import jax.numpy as jnp
from jax import lax
from jax.experimental import pallas as pl
from jax.experimental.pallas import tpu as pltpu
from jax.sharding import PartitionSpec as P

HQ = 64
HK = 8
DH = 128
CAP = 16
GROUP = HQ // HK
WIDE = GROUP * DH
LOG_SCALE = math.log2(math.e) / math.sqrt(DH)
MASKED = -1e30
PIECES = 2
STACK = 4
MIB = 1 << 20


def ring_order(chips):
    return list(range(0, chips, 2)) + list(range(1, chips, 2))[::-1]


def permutations(chips):
    order = ring_order(chips)
    right, left = [], []
    for place in range(chips):
        here, there = order[place], order[(place + 1) % chips]
        for core in range(2):
            right.append((2 * here + core, 2 * there + core))
            left.append((2 * there + core, 2 * here + core))
    sibling = [(i, i ^ 1) for i in range(2 * chips)]
    return right, left, sibling


def chip_at(me, step, chips):
    chip = me // 2
    place = jnp.where(chip % 2 == 0, chip // 2, chips - 1 - chip // 2)
    source = (place - step + 2 * chips) % chips
    return jnp.where(source < chips // 2, 2 * source, 2 * (chips - 1 - source) + 1)


def head_rows(q_ref, first):
    return jnp.concatenate(
        [q_ref[:, h * DH : (h + 1) * DH] for h in range(first, first + STACK)], axis=0
    )


def with_ones(values):
    return jnp.concatenate([values, jnp.ones_like(values)], axis=1)


def scores_of(queries, keys):
    return LOG_SCALE * lax.dot_general(
        queries, keys, (((1,), (1,)), ((), ())), preferred_element_type=jnp.float32
    )


def weights_of(scores, top):
    return jnp.exp2(scores - jnp.concatenate([top] * (scores.shape[1] // DH), axis=1))


def row_top(scores):
    return jnp.broadcast_to(jnp.max(scores, axis=1, keepdims=True), (scores.shape[0], DH))


def chip_block(own_ref, sib_ref):
    tokens = own_ref.shape[0] // 2
    keys = jnp.concatenate([own_ref[:tokens], sib_ref[:tokens]], axis=0)
    values = jnp.concatenate([own_ref[tokens:], sib_ref[tokens:]], axis=0)
    return keys, with_ones(values)


def own_kernel(me_ref, q_ref, own_ref, sib_ref, acc_ref, total_ref, top_ref):
    tokens = q_ref.shape[0]
    keys, values = chip_block(own_ref, sib_ref)
    shape = (STACK * tokens, 2 * tokens)
    token = lax.broadcasted_iota(jnp.int32, shape, 0) % tokens
    column = lax.broadcasted_iota(jnp.int32, shape, 1)
    limit = jnp.where(me_ref[0] % 2 == 1, 2 * tokens, tokens)
    allowed = column <= jnp.where(column < tokens, token, limit - 1)
    for first in range(0, GROUP, STACK):
        rows = slice(first * tokens, (first + STACK) * tokens)
        scores = jnp.where(allowed, scores_of(head_rows(q_ref, first), keys), MASKED)
        top = row_top(scores)
        weights = weights_of(scores, top).astype(jnp.bfloat16)
        update = jnp.dot(weights, values, preferred_element_type=jnp.float32)
        acc_ref[0, rows, :] = update[:, :DH]
        total_ref[0, rows, :] = update[:, DH:]
        top_ref[0, rows, :] = top


def fold_chip(q_ref, own_ref, sib_ref, acc_ref, total_ref, top_ref):
    tokens = q_ref.shape[0]
    keys, values = chip_block(own_ref, sib_ref)
    for first in range(0, GROUP, STACK):
        rows = slice(first * tokens, (first + STACK) * tokens)
        scores = scores_of(head_rows(q_ref, first), keys)
        old = top_ref[0, rows, :]
        top = jnp.maximum(old, row_top(scores))
        factor = jnp.exp2(old - top)
        weights = weights_of(scores, top).astype(jnp.bfloat16)
        update = jnp.dot(weights, values, preferred_element_type=jnp.float32)
        acc_ref[0, rows, :] = acc_ref[0, rows, :] * factor + update[:, :DH]
        total_ref[0, rows, :] = total_ref[0, rows, :] * factor + update[:, DH:]
        top_ref[0, rows, :] = top


def copy_state(sources, targets):
    for source, target in zip(sources, targets):
        target[...] = source[...]


def step_kernel(chips, step, me_ref, q_ref, *refs):
    pieces, state_in, state = refs[:4], refs[4:7], refs[7:]
    me = me_ref[0]
    copy_state(state_in, state)
    for place, own_ref, sib_ref in ((step, *pieces[:2]), (-step, *pieces[2:])):

        @pl.when(chip_at(me, place, chips) < me // 2)
        def _():
            fold_chip(q_ref, own_ref, sib_ref, *state)


def last_kernel(chips, me_ref, q_ref, *refs):
    (key, value, sib_key, sib_value), state_in = refs[:4], refs[4:7]
    (gain_ref, table_ref, out_ref, picked_ref, own_ref, sib_ref), state = refs[7:13], refs[13:]
    tokens = q_ref.shape[0]
    head = pl.program_id(0)
    me = me_ref[0]
    copy_state(state_in, state)

    @pl.when(chip_at(me, chips // 2, chips) < me // 2)
    def _():
        own_ref[:tokens], own_ref[tokens:] = key[...], value[...]
        sib_ref[:tokens], sib_ref[tokens:] = sib_key[...], sib_value[...]
        fold_chip(q_ref, own_ref, sib_ref, *state)

    acc_ref, total_ref, _ = state
    result = (acc_ref[0] / total_ref[0]).astype(jnp.bfloat16)
    columns = pl.ds(pl.multiple_of(head * WIDE, WIDE), WIDE)
    out_ref[:, columns] = jnp.concatenate(
        [result[h * tokens : (h + 1) * tokens] for h in range(GROUP)], axis=1
    )

    @pl.when(head == HK - 1)
    def _():
        width = out_ref.shape[1]
        picked = jnp.dot(table_ref[...], out_ref[...], preferred_element_type=jnp.float32)
        mean = jnp.sum(picked * picked, axis=1, keepdims=True) / width
        picked_ref[...] = (picked * lax.rsqrt(mean + 1e-05) * gain_ref[...]).astype(jnp.bfloat16)


class Attention:
    def __init__(self, me, queries, chips):
        self.me, self.queries, self.chips = me, queries, chips
        tokens = queries.shape[0]
        self.head_block = pl.BlockSpec((tokens, WIDE), lambda g, me: (0, g))
        self.pair_block = pl.BlockSpec((2 * tokens, DH), lambda g, me: (0, g))
        self.kv_block = pl.BlockSpec((tokens, DH), lambda g, me: (0, g))
        self.state_blocks = [pl.BlockSpec((1, GROUP * tokens, DH), lambda g, me: (g, 0, 0))] * 3
        self.state_shapes = [jax.ShapeDtypeStruct((HK, GROUP * tokens, DH), jnp.float32)] * 3

    def call(self, kernel, name, keys, in_specs, out_specs, out_shape, args, scratch=()):
        tokens, width = self.queries.shape
        return pl.pallas_call(
            kernel,
            grid_spec=pltpu.PrefetchScalarGridSpec(
                num_scalar_prefetch=1,
                grid=(HK,),
                in_specs=[self.head_block] + in_specs,
                out_specs=out_specs,
                scratch_shapes=scratch,
            ),
            out_shape=out_shape,
            compiler_params=pltpu.CompilerParams(
                dimension_semantics=("arbitrary",), vmem_limit_bytes=24 * MIB
            ),
            cost_estimate=pl.CostEstimate(
                flops=8 * tokens * width * keys,
                bytes_accessed=24 * MIB,
                transcendentals=tokens * HQ * keys,
            ),
            name=name,
        )(self.me, self.queries, *args)

    def own(self, own, sib):
        keys = 2 * self.queries.shape[0]
        return self.call(
            own_kernel, "attend_own", keys, [self.pair_block] * 2, self.state_blocks, self.state_shapes, (own, sib)
        )

    def step(self, step, pieces, state):
        keys = 4 * self.queries.shape[0]
        return self.call(
            functools.partial(step_kernel, self.chips, step),
            "attend_step",
            keys,
            [self.pair_block] * 4 + self.state_blocks,
            self.state_blocks,
            self.state_shapes,
            (*pieces, *state),
        )

    def last(self, pieces, state, gain, table):
        tokens, width = self.queries.shape
        whole = lambda shape: pl.BlockSpec(shape, lambda g, me: (0, 0))
        return self.call(
            functools.partial(last_kernel, self.chips),
            "attend_last",
            2 * tokens,
            [self.kv_block] * 4 + self.state_blocks + [whole((1, width)), whole((CAP, tokens))],
            [whole((tokens, width)), whole((CAP, width))],
            [
                jax.ShapeDtypeStruct((tokens, width), jnp.bfloat16),
                jax.ShapeDtypeStruct((CAP, width), jnp.bfloat16),
            ],
            (*pieces, *state, gain, table),
            [pltpu.VMEM((2 * tokens, DH), jnp.bfloat16)] * 2
            + [pltpu.VMEM((1, GROUP * tokens, DH), jnp.float32)] * 3,
        )


def hidden_kernel(chips, *refs):
    blocks, (gate_ref, up_ref, out_ref) = refs[: 2 * chips + 2], refs[2 * chips + 2 : 2 * chips + 5]
    rows_ref, gate_sum, up_sum, sems = refs[2 * chips + 5 :]
    step = pl.program_id(0)
    half = rows_ref.shape[1] // 2
    depth = gate_ref.shape[0]

    @pl.when(step == 0)
    def _():
        copies = []
        for core in range(2):
            mine = blocks[core * (chips + 1) : (core + 1) * (chips + 1)]
            for j in range(chips):
                rows = pl.ds((core * chips + j) * CAP, CAP)
                if j < chips - 1:
                    copies.append((mine[j], rows_ref.at[rows, :]))
                else:
                    copies.append((mine[j], rows_ref.at[rows, pl.ds(0, half)]))
                    copies.append((mine[j + 1], rows_ref.at[rows, pl.ds(half, half)]))
        copies = [
            pltpu.make_async_copy(source, target, sems.at[i])
            for i, (source, target) in enumerate(copies)
        ]
        for copy in copies:
            copy.start()
        gate_sum[...] = jnp.zeros_like(gate_sum)
        up_sum[...] = jnp.zeros_like(up_sum)
        for copy in copies:
            copy.wait()

    columns = pl.ds(pl.multiple_of(step * depth, depth), depth)
    part = rows_ref[:, columns]
    gate_sum[...] += jnp.dot(part, gate_ref[...], preferred_element_type=jnp.float32)
    up_sum[...] += jnp.dot(part, up_ref[...], preferred_element_type=jnp.float32)

    @pl.when(step == pl.num_programs(0) - 1)
    def _():
        gate = gate_sum[...]
        out_ref[...] = (gate / (1.0 + jnp.exp(-gate)) * up_sum[...]).astype(jnp.bfloat16)


def hidden_call(chips, blocks, w_gate, w_up):
    rows = 2 * chips * CAP
    width, units = w_gate.shape
    depth = min(1024, width)
    weight_block = pl.BlockSpec((depth, units), lambda i: (i, 0))
    return pl.pallas_call(
        functools.partial(hidden_kernel, chips),
        grid=(width // depth,),
        in_specs=[pl.BlockSpec(memory_space=pl.ANY)] * len(blocks) + [weight_block] * 2,
        out_specs=pl.BlockSpec((rows, units), lambda i: (0, 0)),
        out_shape=jax.ShapeDtypeStruct((rows, units), jnp.bfloat16),
        scratch_shapes=[
            pltpu.VMEM((rows, width), jnp.bfloat16),
            pltpu.VMEM((rows, units), jnp.float32),
            pltpu.VMEM((rows, units), jnp.float32),
            pltpu.SemaphoreType.DMA((len(blocks),)),
        ],
        compiler_params=pltpu.CompilerParams(
            dimension_semantics=("arbitrary",), vmem_limit_bytes=32 * MIB
        ),
        cost_estimate=pl.CostEstimate(
            flops=4 * rows * width * units,
            bytes_accessed=4 * width * units + 2 * rows * width,
            transcendentals=rows * units,
        ),
        name="hidden",
    )(*blocks, w_gate, w_up)


def down_kernel(hidden_ref, down_ref, own_ref, sib_ref):
    part = jnp.dot(hidden_ref[...], down_ref[...], preferred_element_type=jnp.float32)
    part = part.astype(jnp.bfloat16)
    middle = part.shape[0] // 2
    own_ref[...] = part[:middle]
    sib_ref[...] = part[middle:]


def down_call(hidden, w_down, piece, pieces):
    rows, units = hidden.shape
    width = w_down.shape[1] // pieces
    cols = min(1024, width)
    steps = width // cols
    out_block = pl.BlockSpec((rows // 2, cols), lambda i: (0, i))
    return pl.pallas_call(
        down_kernel,
        grid=(steps,),
        in_specs=[
            pl.BlockSpec((rows, units), lambda i: (0, 0)),
            pl.BlockSpec((units, cols), lambda i: (0, piece * steps + i)),
        ],
        out_specs=[out_block, out_block],
        out_shape=[jax.ShapeDtypeStruct((rows // 2, width), jnp.bfloat16)] * 2,
        compiler_params=pltpu.CompilerParams(
            dimension_semantics=("arbitrary",), vmem_limit_bytes=32 * MIB
        ),
        cost_estimate=pl.CostEstimate(
            flops=2 * rows * width * units,
            bytes_accessed=2 * width * units + 2 * rows * width,
            transcendentals=0,
        ),
        name="down",
    )(hidden, w_down)


def spread_kernel(per_piece, *refs):
    table_ref, weight_ref, out_ref = refs[-3:]
    for piece in range(len(refs[:-3]) // 4):

        @pl.when(pl.program_id(0) // per_piece == piece)
        def _():
            parts = [ref[...].astype(jnp.float32) for ref in refs[4 * piece : 4 * piece + 4]]
            total = parts[0] + parts[1] + parts[2] + parts[3]
            spread = lax.dot_general(
                table_ref[...],
                total.astype(jnp.bfloat16),
                (((0,), (0,)), ((), ())),
                preferred_element_type=jnp.float32,
            )
            out_ref[...] = (spread * weight_ref[...]).astype(jnp.bfloat16)


def spread_call(groups, table, weight):
    tokens = table.shape[1]
    piece_width = groups[0][0].shape[1]
    width = piece_width * len(groups)
    cols = min(2048, piece_width)
    per_piece = piece_width // cols

    def block(piece):
        return pl.BlockSpec(
            (CAP, cols), lambda i: (0, jnp.clip(i - piece * per_piece, 0, per_piece - 1))
        )

    return pl.pallas_call(
        functools.partial(spread_kernel, per_piece),
        grid=(width // cols,),
        in_specs=[block(piece) for piece in range(len(groups)) for _ in range(4)]
        + [pl.BlockSpec((CAP, tokens), lambda i: (0, 0)), pl.BlockSpec((tokens, 1), lambda i: (0, 0))],
        out_specs=pl.BlockSpec((tokens, cols), lambda i: (0, i)),
        out_shape=jax.ShapeDtypeStruct((tokens, width), jnp.bfloat16),
        compiler_params=pltpu.CompilerParams(dimension_semantics=("arbitrary",)),
        name="spread",
    )(*[x for group in groups for x in group], table, weight)


def reduce_chip_rows(mine, other, half, chips, go_right, go_left):
    middle = mine.shape[1] // 2

    def block(index):
        rows = slice(index * CAP, (index + 1) * CAP)
        return mine[rows].astype(jnp.float32) + other[rows].astype(jnp.float32)

    far = block(chips - 1).astype(jnp.bfloat16)
    ahead, back = far[:, :middle], far[:, middle:]
    for distance in range(half - 1, -1, -1):
        ahead, back = lax.optimization_barrier((ahead, back))
        to_right, to_left = go_right(ahead), go_left(back)
        yield
        if distance == 0:
            break
        ahead, back = block(half - 1 + distance), block(distance)
        if distance == half - 1:
            ahead = jnp.concatenate(
                [ahead[:, :middle] + to_right.astype(jnp.float32), ahead[:, middle:]], axis=1
            )
            back = jnp.concatenate(
                [back[:, :middle], back[:, middle:] + to_left.astype(jnp.float32)], axis=1
            )
        else:
            ahead = ahead + to_right.astype(jnp.float32)
            back = back + to_left.astype(jnp.float32)
        ahead, back = ahead.astype(jnp.bfloat16), back.astype(jnp.bfloat16)
    return (mine, other, to_right, to_left)


def run_together(generators):
    results = [None] * len(generators)
    active = list(range(len(generators)))
    while active:
        for i in list(active):
            try:
                next(generators[i])
            except StopIteration as stop:
                results[i] = stop.value
                active.remove(i)
    return results


def per_device(chips, queries, keys, values, norm_gain, expert_ids, gates, w_gate, w_up, w_down):
    right, left, sibling = permutations(chips)
    half = chips // 2
    go_right = lambda x: lax.ppermute(x, "ctx", right)
    go_left = lambda x: lax.ppermute(x, "ctx", left)
    swap = lambda x: lax.ppermute(x, "ctx", sibling)

    me = lax.axis_index("ctx").astype(jnp.int32).reshape(1)
    tokens = queries.shape[0]
    hits = (expert_ids == 0).astype(jnp.float32)
    chosen = jnp.sum(hits, axis=1)
    position = jnp.arange(tokens, dtype=jnp.int32)
    before = (position[None, :] < position[:, None]).astype(jnp.float32)
    slot = jnp.sum(before * chosen[None, :], axis=1).astype(jnp.int32)
    table = jnp.logical_and(
        slot[None, :] == jnp.arange(CAP, dtype=jnp.int32)[:, None], chosen[None, :] > 0
    ).astype(jnp.bfloat16)
    weight = jnp.sum(gates * hits, axis=1, keepdims=True)

    attention = Attention(me, queries, chips)
    own = jnp.concatenate([keys, values], axis=0)
    from_left, from_right, own_sib = go_right(own), go_left(own), swap(own)
    state = attention.own(own, own_sib)
    for step in range(1, half):
        from_left, from_right, state = lax.optimization_barrier((from_left, from_right, state))
        pieces = (from_left, swap(from_left), from_right, swap(from_right))
        if step < half - 1:
            from_left, from_right = go_right(from_left), go_left(from_right)
        else:
            far_keys, far_values = go_right(from_left[:tokens]), go_left(from_right[tokens:])
        state = attention.step(step, pieces, state)
    far_keys, far_values, state = lax.optimization_barrier((far_keys, far_values, state))
    opposite = (far_keys, far_values, swap(far_keys), swap(far_values))
    result, picked = attention.last(opposite, state, norm_gain[None, :], table)

    middle = picked.shape[1] // 2
    blocks_right, blocks_left = [picked], [picked]
    for _ in range(1, half):
        blocks_right.append(go_right(blocks_right[-1]))
        blocks_left.append(go_left(blocks_left[-1]))
    blocks = blocks_right + blocks_left[1:]
    blocks += [go_right(blocks_right[-1][:, :middle]), go_left(blocks_left[-1][:, middle:])]
    blocks += [swap(x) for x in blocks]
    hidden = hidden_call(chips, blocks, w_gate, w_up)

    sums = []
    for piece in range(PIECES):
        mine, theirs = down_call(hidden, w_down, piece, PIECES)
        sums.append(reduce_chip_rows(mine, swap(theirs), half, chips, go_right, go_left))
    mixed = spread_call(run_together(sums), table, weight)
    return (result, mixed)


def solution(mesh):
    placed = (
        P(("groups", "ctx"), None),
        P(("groups", "ctx"), None),
        P(("groups", "ctx"), None),
        P(),
        P(("groups", "ctx"), None),
        P(("groups", "ctx"), None),
        P(None, "ctx"),
        P(None, "ctx"),
        P("ctx", None),
    )
    return jax.shard_map(
        functools.partial(per_device, mesh.shape["ctx"] // 2),
        mesh=mesh,
        in_specs=placed,
        out_specs=(P(("groups", "ctx"), None), P(("groups", "ctx"), None)),
        check_vma=False,
    )
```

```python
import functools
import math

import jax
import jax.numpy as jnp
from jax import lax
from jax.experimental import pallas as pl
from jax.experimental.pallas import tpu as pltpu
from jax.sharding import PartitionSpec as P

HQ = 64
HK = 8
DH = 128
CAP = 16
GROUP = HQ // HK
WIDE = GROUP * DH
LOG_SCALE = math.log2(math.e) / math.sqrt(DH)
MASKED = -1e30
PIECES = 2
SUM_LIMIT = 2.0**100
PARTS = 3
STACK = 4
MIB = 1 << 20


def in_hbm(x):
    return pltpu.with_memory_space_constraint(x, pltpu.HBM)


def ring_order(chips):
    return list(range(0, chips, 2)) + list(range(1, chips, 2))[::-1]


def permutations(chips):
    order = ring_order(chips)
    right, left = [], []
    for place in range(chips):
        here, there = order[place], order[(place + 1) % chips]
        for core in range(2):
            right.append((2 * here + core, 2 * there + core))
            left.append((2 * there + core, 2 * here + core))
    sibling = [(i, i ^ 1) for i in range(2 * chips)]
    return right, left, sibling


def chip_at(me, step, chips):
    chip = me // 2
    place = jnp.where(chip % 2 == 0, chip // 2, chips - 1 - chip // 2)
    source = (place - step + 2 * chips) % chips
    return jnp.where(source < chips // 2, 2 * source, 2 * (chips - 1 - source) + 1)


def head_rows(q_ref, first):
    return jnp.concatenate(
        [q_ref[:, h * DH : (h + 1) * DH] for h in range(first, first + STACK)], axis=0
    )


def with_ones(values):
    return jnp.concatenate([values, jnp.ones_like(values)], axis=1)


def scores_of(queries, keys):
    return LOG_SCALE * lax.dot_general(
        queries, keys, (((1,), (1,)), ((), ())), preferred_element_type=jnp.float32
    )


def weights_of(scores, shift):
    return jnp.exp2(scores - jnp.concatenate([shift] * (scores.shape[1] // DH), axis=1))


def row_top(scores):
    return jnp.broadcast_to(jnp.max(scores, axis=1, keepdims=True), (scores.shape[0], DH))


def chip_block(own_ref, sib_ref):
    tokens = own_ref.shape[0] // 2
    keys = jnp.concatenate([own_ref[:tokens], sib_ref[:tokens]], axis=0)
    values = jnp.concatenate([own_ref[tokens:], sib_ref[tokens:]], axis=0)
    return keys, with_ones(values)


def allowed_own(me, tokens):
    shape = (STACK * tokens, 2 * tokens)
    token = lax.broadcasted_iota(jnp.int32, shape, 0) % tokens
    column = lax.broadcasted_iota(jnp.int32, shape, 1)
    limit = jnp.where(me % 2 == 1, 2 * tokens, tokens)
    return column <= jnp.where(column < tokens, token, limit - 1)


def own_kernel(me_ref, q_ref, own_ref, sib_ref, acc_ref, total_ref, shift_ref):
    tokens = q_ref.shape[0]
    keys, values = chip_block(own_ref, sib_ref)
    allowed = allowed_own(me_ref[0], tokens)
    for first in range(0, GROUP, STACK):
        rows = slice(first * tokens, (first + STACK) * tokens)
        scores = jnp.where(allowed, scores_of(head_rows(q_ref, first), keys), MASKED)
        shift = row_top(scores)
        weights = weights_of(scores, shift).astype(jnp.bfloat16)
        update = jnp.dot(weights, values, preferred_element_type=jnp.float32)
        acc_ref[0, rows, :] = update[:, :DH]
        total_ref[0, rows, :] = update[:, DH:]
        shift_ref[0, rows, :] = shift


def fold_chip(q_ref, keys, values, shift_ref, acc_ref, total_ref):
    tokens = q_ref.shape[0]
    for first in range(0, GROUP, STACK):
        rows = slice(first * tokens, (first + STACK) * tokens)
        scores = scores_of(head_rows(q_ref, first), keys)
        weights = weights_of(scores, shift_ref[0, rows, :]).astype(jnp.bfloat16)
        update = jnp.dot(weights, values, preferred_element_type=jnp.float32)
        acc_ref[0, rows, :] += update[:, :DH]
        total_ref[0, rows, :] += update[:, DH:]


def step_kernel(chips, step, me_ref, q_ref, *refs):
    pieces, shift_ref, state_in, state = refs[:4], refs[4], refs[5:7], refs[7:9]
    me = me_ref[0]
    for source, target in zip(state_in, state):
        target[...] = source[...]
    for place, own_ref, sib_ref in ((step, *pieces[:2]), (-step, *pieces[2:])):

        @pl.when(chip_at(me, place, chips) < me // 2)
        def _():
            keys, values = chip_block(own_ref, sib_ref)
            fold_chip(q_ref, keys, values, shift_ref, *state)


def running_attention(chips, me, sources, queries, out_ref, scratch, sem):
    q_ref, keys_ref, values_ref, acc_ref, total_ref, top_ref = scratch
    tokens = q_ref.shape[0]
    half = chips // 2
    places = [0] + [p for step in range(1, half) for p in (step, -step)] + [half]

    def fetch(source, target):
        copy = pltpu.make_async_copy(source, target, sem)
        copy.start()
        copy.wait()

    def one_head(head, carry):
        columns = pl.ds(pl.multiple_of(head * DH, DH), DH)
        wide = pl.ds(pl.multiple_of(head * WIDE, WIDE), WIDE)
        fetch(queries.at[:, wide], q_ref)
        for i, place in enumerate(places):
            if place != half:
                for core in range(2):
                    rows = pl.ds(core * tokens, tokens)
                    block = sources[2 * i + core]
                    fetch(block.at[pl.ds(0, tokens), columns], keys_ref.at[i, rows])
                    fetch(block.at[pl.ds(tokens, tokens), columns], values_ref.at[i, rows])
            else:
                key, value, sib_key, sib_value = sources[2 * i :]
                for core, (k, v) in enumerate(((key, value), (sib_key, sib_value))):
                    rows = pl.ds(core * tokens, tokens)
                    fetch(k.at[:, columns], keys_ref.at[i, rows])
                    fetch(v.at[:, columns], values_ref.at[i, rows])
        acc_ref[...] = jnp.zeros_like(acc_ref)
        total_ref[...] = jnp.zeros_like(total_ref)
        top_ref[...] = jnp.full_like(top_ref, 2 * MASKED)

        def one_chip(i, inner):
            forward = (i + 1) // 2
            place = jnp.where(i % 2 == 1, forward, -forward)
            chip = chip_at(me, place, chips)

            @pl.when(chip <= me // 2)
            def _():
                allowed = jnp.logical_or(allowed_own(me, tokens), chip < me // 2)
                keys, values = keys_ref[i], with_ones(values_ref[i])
                for first in range(0, GROUP, STACK):
                    rows = slice(first * tokens, (first + STACK) * tokens)
                    scores = jnp.where(allowed, scores_of(head_rows(q_ref, first), keys), MASKED)
                    old = top_ref[rows, :]
                    top = jnp.maximum(old, row_top(scores))
                    factor = jnp.exp2(old - top)
                    weights = weights_of(scores, top).astype(jnp.bfloat16)
                    update = jnp.dot(weights, values, preferred_element_type=jnp.float32)
                    acc_ref[rows, :] = acc_ref[rows, :] * factor + update[:, :DH]
                    total_ref[rows, :] = total_ref[rows, :] * factor + update[:, DH:]
                    top_ref[rows, :] = top

            return inner

        lax.fori_loop(0, chips, one_chip, 0)
        write_heads(out_ref, head, acc_ref[...], total_ref[...], tokens)
        return carry

    lax.fori_loop(0, HK, one_head, 0)


def write_heads(out_ref, head, acc, total, tokens):
    result = (acc / total).astype(jnp.bfloat16)
    columns = pl.ds(pl.multiple_of(head * WIDE, WIDE), WIDE)
    out_ref[:, columns] = jnp.concatenate(
        [result[h * tokens : (h + 1) * tokens] for h in range(GROUP)], axis=1
    )


def last_kernel(chips, me_ref, q_ref, *refs):
    (key, value, sib_key, sib_value, shift_ref), state_in = refs[:5], refs[5:7]
    gain_ref, table_ref, queries, sources = refs[7], refs[8], refs[9], refs[10 : 12 + 2 * chips]
    out_ref, picked_ref, acc_ref, total_ref, worst_ref, sem = refs[12 + 2 * chips : 18 + 2 * chips]
    scratch = refs[18 + 2 * chips :]
    tokens = q_ref.shape[0]
    head = pl.program_id(0)
    me = me_ref[0]
    acc_ref[...] = state_in[0][...]
    total_ref[...] = state_in[1][...]

    @pl.when(chip_at(me, chips // 2, chips) < me // 2)
    def _():
        keys = jnp.concatenate([key[...], sib_key[...]], axis=0)
        values = with_ones(jnp.concatenate([value[...], sib_value[...]], axis=0))
        fold_chip(q_ref, keys, values, shift_ref, acc_ref, total_ref)

    write_heads(out_ref, head, acc_ref[0], total_ref[0], tokens)

    @pl.when(head == 0)
    def _():
        worst_ref[...] = jnp.zeros_like(worst_ref)

    worst_ref[...] = jnp.maximum(worst_ref[...], total_ref[0])

    @pl.when(head == HK - 1)
    def _():
        fits = jnp.max(worst_ref[...]) <= SUM_LIMIT

        @pl.when(jnp.logical_not(fits))
        def _():
            running_attention(chips, me, sources, queries, out_ref, scratch, sem)

        width = out_ref.shape[1]
        picked = jnp.dot(table_ref[...], out_ref[...], preferred_element_type=jnp.float32)
        mean = jnp.sum(picked * picked, axis=1, keepdims=True) / width
        picked_ref[...] = (picked * lax.rsqrt(mean + 1e-05) * gain_ref[...]).astype(jnp.bfloat16)


class Attention:
    def __init__(self, me, queries, chips):
        self.me, self.queries, self.chips = me, in_hbm(queries), chips
        tokens = queries.shape[0]
        self.head_block = pl.BlockSpec((tokens, WIDE), lambda g, me: (0, g))
        self.pair_block = pl.BlockSpec((2 * tokens, DH), lambda g, me: (0, g))
        self.kv_block = pl.BlockSpec((tokens, DH), lambda g, me: (0, g))
        self.state_block = pl.BlockSpec((1, GROUP * tokens, DH), lambda g, me: (g, 0, 0))
        self.state_shape = jax.ShapeDtypeStruct((HK, GROUP * tokens, DH), jnp.float32)

    def call(self, kernel, name, in_specs, out_specs, out_shape, args, scratch=(), aliases=None):
        tokens, width = self.queries.shape
        return pl.pallas_call(
            kernel,
            grid_spec=pltpu.PrefetchScalarGridSpec(
                num_scalar_prefetch=1,
                grid=(HK,),
                in_specs=[self.head_block] + in_specs,
                out_specs=out_specs,
                scratch_shapes=scratch,
            ),
            out_shape=out_shape,
            input_output_aliases=aliases or {},
            compiler_params=pltpu.CompilerParams(
                dimension_semantics=("arbitrary",), vmem_limit_bytes=16 * MIB
            ),
            cost_estimate=pl.CostEstimate(
                flops=4 * tokens * width * tokens, bytes_accessed=4 * MIB, transcendentals=0
            ),
            name=name,
        )(self.me, self.queries, *args)

    def own(self, own, sib):
        return self.call(
            own_kernel,
            "attend_own",
            [self.pair_block] * 2,
            [self.state_block] * 3,
            [self.state_shape] * 3,
            (own, sib),
        )

    def step(self, step, pieces, shift, state):
        return self.call(
            functools.partial(step_kernel, self.chips, step),
            "attend_step",
            [self.pair_block] * 4 + [self.state_block] * 3,
            [self.state_block] * 2,
            [self.state_shape] * 2,
            (*pieces, shift, *state),
            aliases={7: 0, 8: 1},
        )

    def last(self, pieces, shift, state, gain, table, sources):
        tokens, width = self.queries.shape
        whole = lambda shape: pl.BlockSpec(shape, lambda g, me: (0, 0))
        anywhere = pl.BlockSpec(memory_space=pl.ANY)
        rows = GROUP * tokens
        return self.call(
            functools.partial(last_kernel, self.chips),
            "attend_last",
            [self.kv_block] * 4
            + [self.state_block] * 3
            + [whole((1, width)), whole((CAP, tokens))]
            + [anywhere] * (1 + len(sources)),
            [whole((tokens, width)), whole((CAP, width))],
            [
                jax.ShapeDtypeStruct((tokens, width), jnp.bfloat16),
                jax.ShapeDtypeStruct((CAP, width), jnp.bfloat16),
            ],
            (*pieces, shift, *state, gain, table, self.queries, *sources),
            [
                pltpu.VMEM((1, rows, DH), jnp.float32),
                pltpu.VMEM((1, rows, DH), jnp.float32),
                pltpu.VMEM((rows, DH), jnp.float32),
                pltpu.SemaphoreType.DMA,
                pltpu.VMEM((tokens, WIDE), jnp.bfloat16),
                pltpu.VMEM((self.chips, 2 * tokens, DH), jnp.bfloat16),
                pltpu.VMEM((self.chips, 2 * tokens, DH), jnp.bfloat16),
            ]
            + [pltpu.VMEM((rows, DH), jnp.float32)] * 3,
        )


def stack_kernel(upper_ref, lower_ref, out_ref, sems):
    rows = upper_ref.shape[0]
    copies = [
        pltpu.make_async_copy(ref, out_ref.at[pl.ds(i * rows, rows)], sems.at[i])
        for i, ref in enumerate((upper_ref, lower_ref))
    ]
    for copy in copies:
        copy.start()
    for copy in copies:
        copy.wait()


def stack(upper, lower):
    anywhere = pl.BlockSpec(memory_space=pl.ANY)
    return pl.pallas_call(
        stack_kernel,
        in_specs=[anywhere] * 2,
        out_specs=anywhere,
        out_shape=jax.ShapeDtypeStruct((2 * upper.shape[0], upper.shape[1]), upper.dtype),
        scratch_shapes=[pltpu.SemaphoreType.DMA((2,))],
        name="stack",
    )(in_hbm(upper), in_hbm(lower))


def load_kernel(source_ref, target_ref, sem):
    copy = pltpu.make_async_copy(source_ref, target_ref, sem)
    copy.start()
    copy.wait()


def load(x):
    return pl.pallas_call(
        load_kernel,
        in_specs=[pl.BlockSpec(memory_space=pltpu.HBM)],
        out_specs=pl.BlockSpec(memory_space=pl.ANY),
        out_shape=pltpu.VMEM(x.shape, x.dtype),
        scratch_shapes=[pltpu.SemaphoreType.DMA],
        compiler_params=pltpu.CompilerParams(vmem_limit_bytes=MIB),
        cost_estimate=pl.CostEstimate(flops=0, bytes_accessed=x.size, transcendentals=0),
        name="load",
    )(in_hbm(x))


def hidden_kernel(chips, *refs):
    blocks, (gate_ref, up_ref, out_ref) = refs[: 2 * chips + 2], refs[2 * chips + 2 : 2 * chips + 5]
    rows_ref, gate_sum, up_sum, sems = refs[2 * chips + 5 :]
    width = rows_ref.shape[1]
    half = width // 2
    depth = min(1024, width)
    copies = []
    for core in range(2):
        mine = blocks[core * (chips + 1) : (core + 1) * (chips + 1)]
        for j in range(chips):
            rows = pl.ds((core * chips + j) * CAP, CAP)
            if j < chips - 1:
                copies.append((mine[j], rows_ref.at[rows, :]))
            else:
                copies.append((mine[j], rows_ref.at[rows, pl.ds(0, half)]))
                copies.append((mine[j + 1], rows_ref.at[rows, pl.ds(half, half)]))
    copies = [
        pltpu.make_async_copy(source, target, sems.at[i]) for i, (source, target) in enumerate(copies)
    ]
    for copy in copies:
        copy.start()
    gate_sum[...] = jnp.zeros_like(gate_sum)
    up_sum[...] = jnp.zeros_like(up_sum)
    for copy in copies:
        copy.wait()

    def one_part(step, carry):
        place = pl.ds(pl.multiple_of(step * depth, depth), depth)
        part = rows_ref[:, place]
        gate_sum[...] += jnp.dot(part, gate_ref[place, :], preferred_element_type=jnp.float32)
        up_sum[...] += jnp.dot(part, up_ref[place, :], preferred_element_type=jnp.float32)
        return carry

    lax.fori_loop(0, width // depth, one_part, 0)
    gate = gate_sum[...]
    out_ref[...] = (gate / (1.0 + jnp.exp(-gate)) * up_sum[...]).astype(jnp.bfloat16)


def hidden_call(chips, blocks, w_gate, w_up):
    rows = 2 * chips * CAP
    width, units = w_gate.shape
    vmem = pl.BlockSpec(memory_space=pltpu.VMEM)
    return pl.pallas_call(
        functools.partial(hidden_kernel, chips),
        in_specs=[pl.BlockSpec(memory_space=pl.ANY)] * len(blocks) + [vmem] * 2,
        out_specs=vmem,
        out_shape=jax.ShapeDtypeStruct((rows, units), jnp.bfloat16),
        scratch_shapes=[
            pltpu.VMEM((rows, width), jnp.bfloat16),
            pltpu.VMEM((rows, units), jnp.float32),
            pltpu.VMEM((rows, units), jnp.float32),
            pltpu.SemaphoreType.DMA((len(blocks),)),
        ],
        compiler_params=pltpu.CompilerParams(vmem_limit_bytes=16 * MIB),
        cost_estimate=pl.CostEstimate(
            flops=4 * rows * width * units,
            bytes_accessed=4 * width * units + 2 * rows * width,
            transcendentals=rows * units,
        ),
        name="hidden",
    )(*blocks, w_gate, w_up)


def down_kernel(hidden_ref, down_ref, own_ref, sib_ref):
    part = jnp.dot(hidden_ref[...], down_ref[...], preferred_element_type=jnp.float32)
    part = part.astype(jnp.bfloat16)
    middle = part.shape[0] // 2
    own_ref[...] = part[:middle]
    sib_ref[...] = part[middle:]


def down_call(hidden, w_down, piece, pieces):
    rows, units = hidden.shape
    width = w_down.shape[1] // pieces
    cols = min(1024, width)
    steps = width // cols
    out_block = pl.BlockSpec((rows // 2, cols), lambda i: (0, i))
    return pl.pallas_call(
        down_kernel,
        grid=(steps,),
        in_specs=[
            pl.BlockSpec((rows, units), lambda i: (0, 0)),
            pl.BlockSpec((units, cols), lambda i: (0, piece * steps + i)),
        ],
        out_specs=[out_block, out_block],
        out_shape=[jax.ShapeDtypeStruct((rows // 2, width), jnp.bfloat16)] * 2,
        compiler_params=pltpu.CompilerParams(
            dimension_semantics=("arbitrary",), vmem_limit_bytes=16 * MIB
        ),
        cost_estimate=pl.CostEstimate(
            flops=2 * rows * width * units,
            bytes_accessed=2 * width * units + 2 * rows * width,
            transcendentals=0,
        ),
        name="down",
    )(hidden, w_down)


def spread_kernel(a_ref, b_ref, c_ref, d_ref, table_ref, *rest):
    out_ref = rest[-1]
    total = a_ref[...].astype(jnp.float32) + b_ref[...].astype(jnp.float32)
    total += c_ref[...].astype(jnp.float32) + d_ref[...].astype(jnp.float32)
    total = total.astype(jnp.bfloat16)
    out_ref[...] = lax.dot_general(
        table_ref[...],
        jnp.concatenate([total] * PARTS, axis=0),
        (((0,), (0,)), ((), ())),
        preferred_element_type=jnp.float32,
    ).astype(jnp.bfloat16)


def spread_call(parts, table, piece, pieces, previous):
    tokens = table.shape[1]
    piece_width = parts[0].shape[1]
    cols = min(2048, piece_width)
    steps = piece_width // cols
    earlier = [] if previous is None else [previous]
    return pl.pallas_call(
        spread_kernel,
        grid=(steps,),
        in_specs=[pl.BlockSpec((CAP, cols), lambda i: (0, i))] * 4
        + [pl.BlockSpec((PARTS * CAP, tokens), lambda i: (0, 0))]
        + [pl.BlockSpec(memory_space=pl.ANY)] * len(earlier),
        out_specs=pl.BlockSpec((tokens, cols), lambda i: (0, piece * steps + i)),
        out_shape=jax.ShapeDtypeStruct((tokens, piece_width * pieces), jnp.bfloat16),
        input_output_aliases={5: 0} if earlier else {},
        compiler_params=pltpu.CompilerParams(
            dimension_semantics=("arbitrary",), vmem_limit_bytes=16 * MIB
        ),
        name="spread",
    )(*parts, table, *earlier)


def reduce_chip_rows(mine, other, half, chips, go_right, go_left):
    middle = mine.shape[1] // 2

    def block(index):
        rows = slice(index * CAP, (index + 1) * CAP)
        return mine[rows].astype(jnp.float32) + other[rows].astype(jnp.float32)

    far = block(chips - 1).astype(jnp.bfloat16)
    ahead, back = far[:, :middle], far[:, middle:]
    for distance in range(half - 1, -1, -1):
        ahead, back = lax.optimization_barrier((ahead, back))
        to_right, to_left = go_right(ahead), go_left(back)
        yield
        if distance == 0:
            break
        ahead, back = block(half - 1 + distance), block(distance)
        if distance == half - 1:
            ahead = jnp.concatenate(
                [ahead[:, :middle] + to_right.astype(jnp.float32), ahead[:, middle:]], axis=1
            )
            back = jnp.concatenate(
                [back[:, :middle], back[:, middle:] + to_left.astype(jnp.float32)], axis=1
            )
        else:
            ahead = ahead + to_right.astype(jnp.float32)
            back = back + to_left.astype(jnp.float32)
        ahead, back = ahead.astype(jnp.bfloat16), back.astype(jnp.bfloat16)
    return (mine, other, to_right, to_left)


def run_together(generators):
    results = [None] * len(generators)
    active = list(range(len(generators)))
    while active:
        for i in list(active):
            try:
                next(generators[i])
            except StopIteration as stop:
                results[i] = stop.value
                active.remove(i)
    return results


def per_device(chips, queries, keys, values, norm_gain, expert_ids, gates, w_gate, w_up, w_down):
    right, left, sibling = permutations(chips)
    half = chips // 2
    go_right = lambda x: lax.ppermute(x, "ctx", right)
    go_left = lambda x: lax.ppermute(x, "ctx", left)
    swap = lambda x: lax.ppermute(x, "ctx", sibling)

    me = lax.axis_index("ctx").astype(jnp.int32).reshape(1)
    tokens = queries.shape[0]
    hits = (expert_ids == 0).astype(jnp.float32)
    chosen = jnp.sum(hits, axis=1)
    position = jnp.arange(tokens, dtype=jnp.int32)
    before = (position[None, :] < position[:, None]).astype(jnp.float32)
    slot = jnp.sum(before * chosen[None, :], axis=1).astype(jnp.int32)
    table = jnp.logical_and(
        slot[None, :] == jnp.arange(CAP, dtype=jnp.int32)[:, None], chosen[None, :] > 0
    ).astype(jnp.float32)
    rest = jnp.sum(gates * hits, axis=1)
    weights = []
    for _ in range(PARTS):
        part = lax.reduce_precision(rest, 8, 7)
        weights.append(table * part[None, :])
        rest = rest - part
    weighted = jnp.concatenate(weights, axis=0).astype(jnp.bfloat16)
    table = table.astype(jnp.bfloat16)

    attention = Attention(me, queries, chips)
    own = stack(keys, values)
    from_left, from_right, own_sib = go_right(own), go_left(own), swap(own)
    acc, total, shift = attention.own(own, own_sib)
    state = (acc, total)
    sources = [own, own_sib]
    for step in range(1, half):
        from_left, from_right, state = lax.optimization_barrier((from_left, from_right, state))
        pieces = (from_left, swap(from_left), from_right, swap(from_right))
        sources += pieces
        if step < half - 1:
            from_left, from_right = go_right(from_left), go_left(from_right)
        else:
            far_keys, far_values = go_right(from_left[:tokens]), go_left(from_right[tokens:])
        state = attention.step(step, pieces, shift, state)
    far_keys, far_values, state = lax.optimization_barrier((far_keys, far_values, state))
    opposite = (far_keys, far_values, swap(far_keys), swap(far_values))
    sources += opposite
    result, picked = attention.last(opposite, shift, state, norm_gain[None, :], table, sources)

    picked, loads = lax.optimization_barrier((picked, [w_gate, w_up, w_down]))
    middle = picked.shape[1] // 2
    from_left, from_right, waiting = picked, picked, [picked]
    blocks_right, blocks_left, swapped = [picked], [], []
    for step in range(1, half):
        from_left, from_right = go_right(from_left), go_left(from_right)
        if step <= len(loads):
            loads[step - 1] = load(loads[step - 1])
        from_left, from_right, waiting, loads = lax.optimization_barrier(
            (from_left, from_right, waiting, loads)
        )
        blocks_right.append(from_left)
        blocks_left.append(from_right)
        swapped += [swap(x) for x in waiting]
        waiting = [from_left, from_right]
    far = [go_right(from_left[:, :middle]), go_left(from_right[:, middle:])]
    swapped += [swap(x) for x in waiting + far]
    blocks = blocks_right + blocks_left + far
    others = swapped[:1] + swapped[1:-2:2] + swapped[2:-2:2] + swapped[-2:]
    hidden = hidden_call(chips, blocks + others, *loads[:2])
    w_down = pltpu.with_memory_space_constraint(loads[2], pltpu.VMEM)

    sums = []
    for piece in range(PIECES):
        mine, theirs = down_call(hidden, w_down, piece, PIECES)
        sums.append(reduce_chip_rows(mine, swap(theirs), half, chips, go_right, go_left))
    mixed = None
    for piece, parts in enumerate(run_together(sums)):
        mixed = spread_call(parts, weighted, piece, PIECES, mixed)
    return (result, mixed)


def solution(mesh):
    placed = (
        P(("groups", "ctx"), None),
        P(("groups", "ctx"), None),
        P(("groups", "ctx"), None),
        P(),
        P(("groups", "ctx"), None),
        P(("groups", "ctx"), None),
        P(None, "ctx"),
        P(None, "ctx"),
        P("ctx", None),
    )
    return jax.shard_map(
        functools.partial(per_device, mesh.shape["ctx"] // 2),
        mesh=mesh,
        in_specs=placed,
        out_specs=(P(("groups", "ctx"), None), P(("groups", "ctx"), None)),
        check_vma=False,
    )
```

```python
import functools
import math

import jax
import jax.numpy as jnp
from jax import lax
from jax.experimental import pallas as pl
from jax.experimental.pallas import tpu as pltpu
from jax.sharding import PartitionSpec as P

HQ = 64
HK = 8
DH = 128
CAP = 16
GROUP = HQ // HK
WIDE = GROUP * DH
LOG_SCALE = math.log2(math.e) / math.sqrt(DH)
MASKED = -1e30
PIECES = 2
SUM_LIMIT = 2.0**100
PARTS = 3
STACK = 4
MIB = 1 << 20


def in_hbm(x):
    return pltpu.with_memory_space_constraint(x, pltpu.HBM)


def ring_order(chips):
    return list(range(0, chips, 2)) + list(range(1, chips, 2))[::-1]


def permutations(chips):
    order = ring_order(chips)
    right, left = [], []
    for place in range(chips):
        here, there = order[place], order[(place + 1) % chips]
        for core in range(2):
            right.append((2 * here + core, 2 * there + core))
            left.append((2 * there + core, 2 * here + core))
    sibling = [(i, i ^ 1) for i in range(2 * chips)]
    return right, left, sibling


def chip_at(me, step, chips):
    chip = me // 2
    place = jnp.where(chip % 2 == 0, chip // 2, chips - 1 - chip // 2)
    source = (place - step + 2 * chips) % chips
    return jnp.where(source < chips // 2, 2 * source, 2 * (chips - 1 - source) + 1)


def head_rows(queries, first):
    return jnp.concatenate(
        [queries[:, h * DH : (h + 1) * DH] for h in range(first, first + STACK)], axis=0
    )


def with_ones(values):
    return jnp.concatenate([values, jnp.ones_like(values)], axis=1)


def scores_of(queries, keys):
    return LOG_SCALE * lax.dot_general(
        queries, keys, (((1,), (1,)), ((), ())), preferred_element_type=jnp.float32
    )


def weights_of(scores, shift):
    return jnp.exp2(scores - jnp.concatenate([shift] * (scores.shape[1] // DH), axis=1))


def row_top(scores):
    return jnp.broadcast_to(jnp.max(scores, axis=1, keepdims=True), (scores.shape[0], DH))


def chip_block(own, sib):
    tokens = own.shape[0] // 2
    keys = jnp.concatenate([own[:tokens], sib[:tokens]], axis=0)
    values = jnp.concatenate([own[tokens:], sib[tokens:]], axis=0)
    return keys, with_ones(values)


def allowed_own(me, tokens):
    shape = (STACK * tokens, 2 * tokens)
    token = lax.broadcasted_iota(jnp.int32, shape, 0) % tokens
    column = lax.broadcasted_iota(jnp.int32, shape, 1)
    limit = jnp.where(me % 2 == 1, 2 * tokens, tokens)
    return column <= jnp.where(column < tokens, token, limit - 1)


def head_group(q_ref, group):
    return q_ref[:, pl.ds(pl.multiple_of(group * WIDE, WIDE), WIDE)]


def for_groups(body):
    def step(group, carry):
        body(group, pl.ds(pl.multiple_of(group * DH, DH), DH))
        return carry

    lax.fori_loop(0, HK, step, 0)


def own_kernel(me_ref, q_ref, own_ref, sib_ref, acc_ref, total_ref, shift_ref):
    tokens = q_ref.shape[0]
    allowed = allowed_own(me_ref[0], tokens)

    def one_group(group, columns):
        keys, values = chip_block(own_ref[:, columns], sib_ref[:, columns])
        queries = head_group(q_ref, group)
        for first in range(0, GROUP, STACK):
            rows = slice(first * tokens, (first + STACK) * tokens)
            scores = jnp.where(allowed, scores_of(head_rows(queries, first), keys), MASKED)
            shift = row_top(scores)
            weights = weights_of(scores, shift).astype(jnp.bfloat16)
            update = jnp.dot(weights, values, preferred_element_type=jnp.float32)
            acc_ref[group, rows, :] = update[:, :DH]
            total_ref[group, rows, :] = update[:, DH:]
            shift_ref[group, rows, :] = shift

    for_groups(one_group)


def fold_chip(queries, keys, values, group, shift_ref, acc_ref, total_ref):
    tokens = queries.shape[0]
    for first in range(0, GROUP, STACK):
        rows = slice(first * tokens, (first + STACK) * tokens)
        scores = scores_of(head_rows(queries, first), keys)
        weights = weights_of(scores, shift_ref[group, rows, :]).astype(jnp.bfloat16)
        update = jnp.dot(weights, values, preferred_element_type=jnp.float32)
        acc_ref[group, rows, :] += update[:, :DH]
        total_ref[group, rows, :] += update[:, DH:]


def step_kernel(chips, step, me_ref, q_ref, *refs):
    pieces, shift_ref, state = refs[:4], refs[4], refs[7:9]
    me = me_ref[0]
    for place, own_ref, sib_ref in ((step, *pieces[:2]), (-step, *pieces[2:])):

        @pl.when(chip_at(me, place, chips) < me // 2)
        def _():
            def one_group(group, columns):
                keys, values = chip_block(own_ref[:, columns], sib_ref[:, columns])
                fold_chip(head_group(q_ref, group), keys, values, group, shift_ref, *state)

            for_groups(one_group)


def running_attention(chips, me, sources, q_ref, out_ref, scratch, sem):
    keys_ref, values_ref, acc_ref, total_ref, top_ref = scratch
    tokens = q_ref.shape[0]
    half = chips // 2
    places = [0] + [p for step in range(1, half) for p in (step, -step)] + [half]

    def fetch(source, target):
        copy = pltpu.make_async_copy(source, target, sem)
        copy.start()
        copy.wait()

    def one_head(head, carry):
        columns = pl.ds(pl.multiple_of(head * DH, DH), DH)
        queries = head_group(q_ref, head)
        for i, place in enumerate(places):
            if place != half:
                for core in range(2):
                    rows = pl.ds(core * tokens, tokens)
                    block = sources[2 * i + core]
                    fetch(block.at[pl.ds(0, tokens), columns], keys_ref.at[i, rows])
                    fetch(block.at[pl.ds(tokens, tokens), columns], values_ref.at[i, rows])
            else:
                key, value, sib_key, sib_value = sources[2 * i :]
                for core, (k, v) in enumerate(((key, value), (sib_key, sib_value))):
                    rows = pl.ds(core * tokens, tokens)
                    fetch(k.at[:, columns], keys_ref.at[i, rows])
                    fetch(v.at[:, columns], values_ref.at[i, rows])
        acc_ref[...] = jnp.zeros_like(acc_ref)
        total_ref[...] = jnp.zeros_like(total_ref)
        top_ref[...] = jnp.full_like(top_ref, 2 * MASKED)

        def one_chip(i, inner):
            forward = (i + 1) // 2
            place = jnp.where(i % 2 == 1, forward, -forward)
            chip = chip_at(me, place, chips)

            @pl.when(chip <= me // 2)
            def _():
                allowed = jnp.logical_or(allowed_own(me, tokens), chip < me // 2)
                keys, values = keys_ref[i], with_ones(values_ref[i])
                for first in range(0, GROUP, STACK):
                    rows = slice(first * tokens, (first + STACK) * tokens)
                    scores = jnp.where(allowed, scores_of(head_rows(queries, first), keys), MASKED)
                    old = top_ref[rows, :]
                    top = jnp.maximum(old, row_top(scores))
                    factor = jnp.exp2(old - top)
                    weights = weights_of(scores, top).astype(jnp.bfloat16)
                    update = jnp.dot(weights, values, preferred_element_type=jnp.float32)
                    acc_ref[rows, :] = acc_ref[rows, :] * factor + update[:, :DH]
                    total_ref[rows, :] = total_ref[rows, :] * factor + update[:, DH:]
                    top_ref[rows, :] = top

            return inner

        lax.fori_loop(0, chips, one_chip, 0)
        write_heads(out_ref, head, acc_ref[...], total_ref[...], tokens)
        return carry

    lax.fori_loop(0, HK, one_head, 0)


def write_heads(out_ref, head, acc, total, tokens):
    inverse = pl.reciprocal(total, approx=True)
    inverse = inverse * (2.0 - total * inverse)
    result = (acc * inverse).astype(jnp.bfloat16)
    columns = pl.ds(pl.multiple_of(head * WIDE, WIDE), WIDE)
    out_ref[:, columns] = jnp.concatenate(
        [result[h * tokens : (h + 1) * tokens] for h in range(GROUP)], axis=1
    )


def last_kernel(chips, me_ref, q_ref, *refs):
    key, value, sib_key, sib_value, shift_ref = refs[:5]
    gain_ref, table_ref, sources = refs[7], refs[8], refs[9 : 11 + 2 * chips]
    out_ref, picked_ref, *state = refs[11 + 2 * chips : 15 + 2 * chips]
    worst_ref, sem, *scratch = refs[15 + 2 * chips :]
    tokens = q_ref.shape[0]
    me = me_ref[0]

    @pl.when(chip_at(me, chips // 2, chips) < me // 2)
    def _():
        def one_group(group, columns):
            keys = jnp.concatenate([key[:, columns], sib_key[:, columns]], axis=0)
            values = jnp.concatenate([value[:, columns], sib_value[:, columns]], axis=0)
            queries = head_group(q_ref, group)
            fold_chip(queries, keys, with_ones(values), group, shift_ref, *state)

        for_groups(one_group)

    worst_ref[...] = jnp.zeros_like(worst_ref)

    def finish(group, columns):
        total = state[1][group]
        write_heads(out_ref, group, state[0][group], total, tokens)
        worst_ref[...] = jnp.maximum(worst_ref[...], total)

    for_groups(finish)
    fits = jnp.max(worst_ref[...]) <= SUM_LIMIT

    @pl.when(jnp.logical_not(fits))
    def _():
        running_attention(chips, me, sources, q_ref, out_ref, scratch, sem)

    width = out_ref.shape[1]
    picked = jnp.dot(table_ref[...], out_ref[...], preferred_element_type=jnp.float32)
    mean = jnp.sum(picked * picked, axis=1, keepdims=True) / width
    picked_ref[...] = (picked * lax.rsqrt(mean + 1e-05) * gain_ref[...]).astype(jnp.bfloat16)


class Attention:
    def __init__(self, me, queries, chips):
        self.me, self.queries, self.chips = me, queries, chips
        tokens = queries.shape[0]
        self.state_shape = pltpu.VMEM((HK, GROUP * tokens, DH), jnp.float32)

    def call(self, kernel, name, out_shape, args, others=(), scratch=(), aliases=None):
        tokens, width = self.queries.shape
        vmem = pl.BlockSpec(memory_space=pltpu.VMEM)
        return pl.pallas_call(
            kernel,
            in_specs=[pl.BlockSpec(memory_space=pltpu.SMEM)]
            + [vmem] * (1 + len(args))
            + [pl.BlockSpec(memory_space=pl.ANY)] * len(others),
            out_specs=[vmem] * len(out_shape),
            out_shape=out_shape,
            scratch_shapes=scratch,
            input_output_aliases=aliases or {},
            compiler_params=pltpu.CompilerParams(vmem_limit_bytes=16 * MIB),
            cost_estimate=pl.CostEstimate(
                flops=4 * tokens * width * tokens, bytes_accessed=4 * MIB, transcendentals=0
            ),
            name=name,
        )(self.me, self.queries, *args, *others)

    def own(self, own, sib):
        return self.call(own_kernel, "attend_own", [self.state_shape] * 3, (own, sib))

    def step(self, step, pieces, shift, state):
        return self.call(
            functools.partial(step_kernel, self.chips, step),
            "attend_step",
            [self.state_shape] * 2,
            (*pieces, shift, *state),
            aliases={7: 0, 8: 1},
        )

    def last(self, pieces, shift, state, gain, table, sources):
        tokens, width = self.queries.shape
        rows = GROUP * tokens
        return self.call(
            functools.partial(last_kernel, self.chips),
            "attend_last",
            [
                pltpu.VMEM((tokens, width), jnp.bfloat16),
                pltpu.VMEM((CAP, width), jnp.bfloat16),
                self.state_shape,
                self.state_shape,
            ],
            (*pieces, shift, *state, gain, table),
            sources,
            [
                pltpu.VMEM((rows, DH), jnp.float32),
                pltpu.SemaphoreType.DMA,
                pltpu.VMEM((self.chips, 2 * tokens, DH), jnp.bfloat16),
                pltpu.VMEM((self.chips, 2 * tokens, DH), jnp.bfloat16),
            ]
            + [pltpu.VMEM((rows, DH), jnp.float32)] * 3,
            aliases={7: 2, 8: 3},
        )[:2]


def load_kernel(source_ref, target_ref, sem):
    copy = pltpu.make_async_copy(source_ref, target_ref, sem)
    copy.start()
    copy.wait()


def load(x):
    return pl.pallas_call(
        load_kernel,
        in_specs=[pl.BlockSpec(memory_space=pltpu.HBM)],
        out_specs=pl.BlockSpec(memory_space=pl.ANY),
        out_shape=pltpu.VMEM(x.shape, x.dtype),
        scratch_shapes=[pltpu.SemaphoreType.DMA],
        compiler_params=pltpu.CompilerParams(vmem_limit_bytes=MIB),
        cost_estimate=pl.CostEstimate(flops=0, bytes_accessed=x.size, transcendentals=0),
        name="load",
    )(in_hbm(x))


def hidden_kernel(chips, *refs):
    blocks, (gate_ref, up_ref, out_ref) = refs[: 2 * chips + 2], refs[2 * chips + 2 : 2 * chips + 5]
    gate_sum, up_sum = refs[2 * chips + 5 :]
    width = gate_ref.shape[0]
    half = width // 2
    depth = min(1024, half)
    gate_sum[...] = jnp.zeros_like(gate_sum)
    up_sum[...] = jnp.zeros_like(up_sum)
    for side in range(2):
        sides = []
        for core in range(2):
            mine = blocks[core * (chips + 1) : (core + 1) * (chips + 1)]
            sides += [(ref, side * half) for ref in mine[: chips - 1]] + [(mine[chips - 1 + side], 0)]

        def one_part(step, carry):
            part = jnp.concatenate(
                [ref[:, pl.ds(pl.multiple_of(start + step * depth, depth), depth)] for ref, start in sides],
                axis=0,
            )
            place = pl.ds(pl.multiple_of(side * half + step * depth, depth), depth)
            gate_sum[...] += jnp.dot(part, gate_ref[place, :], preferred_element_type=jnp.float32)
            up_sum[...] += jnp.dot(part, up_ref[place, :], preferred_element_type=jnp.float32)
            return carry

        lax.fori_loop(0, half // depth, one_part, 0)
    gate = gate_sum[...]
    out_ref[...] = (gate / (1.0 + jnp.exp(-gate)) * up_sum[...]).astype(jnp.bfloat16)


def hidden_call(chips, blocks, w_gate, w_up):
    rows = 2 * chips * CAP
    width, units = w_gate.shape
    vmem = pl.BlockSpec(memory_space=pltpu.VMEM)
    return pl.pallas_call(
        functools.partial(hidden_kernel, chips),
        in_specs=[vmem] * (len(blocks) + 2),
        out_specs=vmem,
        out_shape=pltpu.VMEM((rows, units), jnp.bfloat16),
        scratch_shapes=[pltpu.VMEM((rows, units), jnp.float32)] * 2,
        compiler_params=pltpu.CompilerParams(vmem_limit_bytes=16 * MIB),
        cost_estimate=pl.CostEstimate(
            flops=4 * rows * width * units,
            bytes_accessed=4 * width * units + 2 * rows * width,
            transcendentals=rows * units,
        ),
        name="hidden",
    )(*blocks, w_gate, w_up)


def down_kernel(start, hidden_ref, down_ref, own_ref, sib_ref):
    middle, width = own_ref.shape
    cols = min(1024, width)

    def one_part(step, carry):
        source = pl.ds(pl.multiple_of(start + step * cols, cols), cols)
        target = pl.ds(pl.multiple_of(step * cols, cols), cols)
        part = jnp.dot(hidden_ref[...], down_ref[:, source], preferred_element_type=jnp.float32)
        part = part.astype(jnp.bfloat16)
        own_ref[:, target] = part[:middle]
        sib_ref[:, target] = part[middle:]
        return carry

    lax.fori_loop(0, width // cols, one_part, 0)


def down_call(hidden, w_down, piece, pieces):
    rows, units = hidden.shape
    width = w_down.shape[1] // pieces
    vmem = pl.BlockSpec(memory_space=pltpu.VMEM)
    return pl.pallas_call(
        functools.partial(down_kernel, piece * width),
        in_specs=[vmem] * 2,
        out_specs=[vmem] * 2,
        out_shape=[pltpu.VMEM((rows // 2, width), jnp.bfloat16)] * 2,
        compiler_params=pltpu.CompilerParams(vmem_limit_bytes=16 * MIB),
        cost_estimate=pl.CostEstimate(
            flops=2 * rows * width * units,
            bytes_accessed=2 * width * units + 2 * rows * width,
            transcendentals=0,
        ),
        name="down",
    )(hidden, w_down)


def spread_kernel(a_ref, b_ref, c_ref, d_ref, table_ref, *rest):
    out_ref = rest[-1]
    total = a_ref[...].astype(jnp.float32) + b_ref[...].astype(jnp.float32)
    total += c_ref[...].astype(jnp.float32) + d_ref[...].astype(jnp.float32)
    total = total.astype(jnp.bfloat16)
    out_ref[...] = lax.dot_general(
        table_ref[...],
        jnp.concatenate([total] * PARTS, axis=0),
        (((0,), (0,)), ((), ())),
        preferred_element_type=jnp.float32,
    ).astype(jnp.bfloat16)


def spread_call(parts, table, piece, pieces, previous):
    tokens = table.shape[1]
    piece_width = parts[0].shape[1]
    cols = min(2048, piece_width)
    steps = piece_width // cols
    earlier = [] if previous is None else [previous]
    return pl.pallas_call(
        spread_kernel,
        grid=(steps,),
        in_specs=[pl.BlockSpec((CAP, cols), lambda i: (0, i))] * 4
        + [pl.BlockSpec((PARTS * CAP, tokens), lambda i: (0, 0))]
        + [pl.BlockSpec(memory_space=pl.ANY)] * len(earlier),
        out_specs=pl.BlockSpec((tokens, cols), lambda i: (0, piece * steps + i)),
        out_shape=jax.ShapeDtypeStruct((tokens, piece_width * pieces), jnp.bfloat16),
        input_output_aliases={5: 0} if earlier else {},
        compiler_params=pltpu.CompilerParams(
            dimension_semantics=("arbitrary",), vmem_limit_bytes=16 * MIB
        ),
        name="spread",
    )(*parts, table, *earlier)


def reduce_chip_rows(mine, other, half, chips, go_right, go_left):
    middle = mine.shape[1] // 2

    def block(index):
        rows = slice(index * CAP, (index + 1) * CAP)
        return mine[rows].astype(jnp.float32) + other[rows].astype(jnp.float32)

    far = block(chips - 1).astype(jnp.bfloat16)
    ahead, back = far[:, :middle], far[:, middle:]
    for distance in range(half - 1, -1, -1):
        ahead, back = lax.optimization_barrier((ahead, back))
        to_right, to_left = go_right(ahead), go_left(back)
        yield
        if distance == 0:
            break
        ahead, back = block(half - 1 + distance), block(distance)
        if distance == half - 1:
            ahead = jnp.concatenate(
                [ahead[:, :middle] + to_right.astype(jnp.float32), ahead[:, middle:]], axis=1
            )
            back = jnp.concatenate(
                [back[:, :middle], back[:, middle:] + to_left.astype(jnp.float32)], axis=1
            )
        else:
            ahead = ahead + to_right.astype(jnp.float32)
            back = back + to_left.astype(jnp.float32)
        ahead, back = ahead.astype(jnp.bfloat16), back.astype(jnp.bfloat16)
    return (mine, other, to_right, to_left)


def run_together(generators):
    results = [None] * len(generators)
    active = list(range(len(generators)))
    while active:
        for i in list(active):
            try:
                next(generators[i])
            except StopIteration as stop:
                results[i] = stop.value
                active.remove(i)
    return results


def per_device(chips, queries, keys, values, norm_gain, expert_ids, gates, w_gate, w_up, w_down):
    right, left, sibling = permutations(chips)
    half = chips // 2
    go_right = lambda x: lax.ppermute(x, "ctx", right)
    go_left = lambda x: lax.ppermute(x, "ctx", left)
    swap = lambda x: lax.ppermute(x, "ctx", sibling)

    me = lax.axis_index("ctx").astype(jnp.int32).reshape(1)
    tokens = queries.shape[0]
    hits = (expert_ids == 0).astype(jnp.float32)
    chosen = jnp.sum(hits, axis=1)
    position = jnp.arange(tokens, dtype=jnp.int32)
    before = (position[None, :] < position[:, None]).astype(jnp.float32)
    slot = jnp.sum(before * chosen[None, :], axis=1).astype(jnp.int32)
    table = jnp.logical_and(
        slot[None, :] == jnp.arange(CAP, dtype=jnp.int32)[:, None], chosen[None, :] > 0
    ).astype(jnp.float32)
    rest = jnp.sum(gates * hits, axis=1)
    weights = []
    for _ in range(PARTS):
        part = lax.reduce_precision(rest, 8, 7)
        weights.append(table * part[None, :])
        rest = rest - part
    weighted = jnp.concatenate(weights, axis=0).astype(jnp.bfloat16)
    table = table.astype(jnp.bfloat16)

    attention = Attention(me, queries, chips)
    own = jnp.concatenate([keys, values], axis=0)
    from_left, from_right, own_sib = go_right(own), go_left(own), swap(own)
    acc, total, shift = attention.own(own, own_sib)
    state = (acc, total)
    sources = [own, own_sib]
    for step in range(1, half):
        from_left, from_right, state = lax.optimization_barrier((from_left, from_right, state))
        pieces = (from_left, swap(from_left), from_right, swap(from_right))
        sources += pieces
        if step < half - 1:
            from_left, from_right = go_right(from_left), go_left(from_right)
        else:
            far_keys, far_values = go_right(from_left[:tokens]), go_left(from_right[tokens:])
        state = attention.step(step, pieces, shift, state)
    far_keys, far_values, state = lax.optimization_barrier((far_keys, far_values, state))
    opposite = (far_keys, far_values, swap(far_keys), swap(far_values))
    sources += opposite
    result, picked = attention.last(opposite, shift, state, norm_gain[None, :], table, sources)

    picked, loads = lax.optimization_barrier((picked, [w_gate, w_up, w_down]))
    middle = picked.shape[1] // 2
    from_left, from_right, waiting = picked, picked, [picked]
    blocks_right, blocks_left, swapped = [picked], [], []
    for step in range(1, half):
        from_left, from_right = go_right(from_left), go_left(from_right)
        if step <= len(loads):
            loads[step - 1] = load(loads[step - 1])
        from_left, from_right, waiting, loads = lax.optimization_barrier(
            (from_left, from_right, waiting, loads)
        )
        blocks_right.append(from_left)
        blocks_left.append(from_right)
        swapped += [swap(x) for x in waiting]
        waiting = [from_left, from_right]
    far = [go_right(from_left[:, :middle]), go_left(from_right[:, middle:])]
    swapped += [swap(x) for x in waiting + far]
    blocks = blocks_right + blocks_left + far
    others = swapped[:1] + swapped[1:-2:2] + swapped[2:-2:2] + swapped[-2:]
    hidden = hidden_call(chips, blocks + others, *loads[:2])
    w_down = loads[2]

    sums = []
    for piece in range(PIECES):
        mine, theirs = down_call(hidden, w_down, piece, PIECES)
        sums.append(reduce_chip_rows(mine, swap(theirs), half, chips, go_right, go_left))
    mixed = None
    for piece, parts in enumerate(run_together(sums)):
        mixed = spread_call(parts, weighted, piece, PIECES, mixed)
    return (result, mixed)


def solution(mesh):
    placed = (
        P(("groups", "ctx"), None),
        P(("groups", "ctx"), None),
        P(("groups", "ctx"), None),
        P(),
        P(("groups", "ctx"), None),
        P(("groups", "ctx"), None),
        P(None, "ctx"),
        P(None, "ctx"),
        P("ctx", None),
    )
    return jax.shard_map(
        functools.partial(per_device, mesh.shape["ctx"] // 2),
        mesh=mesh,
        in_specs=placed,
        out_specs=(P(("groups", "ctx"), None), P(("groups", "ctx"), None)),
        check_vma=False,
    )
```

```python
import functools
import math

import jax
import jax.numpy as jnp
from jax import lax
from jax.experimental import pallas as pl
from jax.experimental.pallas import tpu as pltpu
from jax.sharding import PartitionSpec as P

HQ = 64
HK = 8
DH = 128
CAP = 16
GROUP = HQ // HK
WIDE = GROUP * DH
LOG_SCALE = math.log2(math.e) / math.sqrt(DH)
MASKED = -1e30
PIECES = 2
SUM_LIMIT = 2.0**100
PARTS = 3
STACK = 4
MIB = 1 << 20


def in_hbm(x):
    return pltpu.with_memory_space_constraint(x, pltpu.HBM)


def ring_order(chips):
    return list(range(0, chips, 2)) + list(range(1, chips, 2))[::-1]


def permutations(chips):
    order = ring_order(chips)
    right, left = [], []
    for place in range(chips):
        here, there = order[place], order[(place + 1) % chips]
        for core in range(2):
            right.append((2 * here + core, 2 * there + core))
            left.append((2 * there + core, 2 * here + core))
    sibling = [(i, i ^ 1) for i in range(2 * chips)]
    return right, left, sibling


def chip_at(me, step, chips):
    chip = me // 2
    place = jnp.where(chip % 2 == 0, chip // 2, chips - 1 - chip // 2)
    source = (place - step + 2 * chips) % chips
    return jnp.where(source < chips // 2, 2 * source, 2 * (chips - 1 - source) + 1)


def head_rows(queries, first):
    return jnp.concatenate(
        [queries[:, h * DH : (h + 1) * DH] for h in range(first, first + STACK)], axis=0
    )


def with_ones(values):
    return jnp.concatenate([values, jnp.ones_like(values)], axis=1)


def scores_of(queries, keys):
    return LOG_SCALE * lax.dot_general(
        queries, keys, (((1,), (1,)), ((), ())), preferred_element_type=jnp.float32
    )


def weights_of(scores, shift):
    return jnp.exp2(scores - jnp.concatenate([shift] * (scores.shape[1] // DH), axis=1))


def row_top(scores):
    return jnp.broadcast_to(jnp.max(scores, axis=1, keepdims=True), (scores.shape[0], DH))


def diagonal(tokens):
    shape = (STACK * tokens, tokens)
    token = lax.broadcasted_iota(jnp.int32, shape, 0) % tokens
    return lax.broadcasted_iota(jnp.int32, shape, 1) <= token


def head_group(q_ref, group):
    return q_ref[:, pl.ds(pl.multiple_of(group * WIDE, WIDE), WIDE)]


def for_groups(body):
    def step(group, carry):
        body(group, pl.ds(pl.multiple_of(group * DH, DH), DH))
        return carry

    lax.fori_loop(0, HK, step, 0)


def own_kernel(q_ref, own_ref, acc_ref, total_ref, shift_ref):
    tokens = q_ref.shape[0]
    allowed = diagonal(tokens)

    def one_group(group, columns):
        keys, values = own_ref[:tokens, columns], with_ones(own_ref[tokens:, columns])
        queries = head_group(q_ref, group)
        for first in range(0, GROUP, STACK):
            rows = slice(first * tokens, (first + STACK) * tokens)
            scores = jnp.where(allowed, scores_of(head_rows(queries, first), keys), MASKED)
            shift = row_top(scores)
            weights = weights_of(scores, shift).astype(jnp.bfloat16)
            update = jnp.dot(weights, values, preferred_element_type=jnp.float32)
            acc_ref[group, rows, :] = update[:, :DH]
            total_ref[group, rows, :] = update[:, DH:]
            shift_ref[group, rows, :] = shift

    for_groups(one_group)


def fold_blocks(q_ref, blocks, earlier, shift_ref, acc_ref, total_ref):
    tokens = q_ref.shape[0]
    anything = functools.reduce(jnp.logical_or, earlier)

    @pl.when(anything)
    def _():
        factors = [jnp.where(flag, 1.0, 0.0).astype(jnp.bfloat16) for flag in earlier]

        def one_group(group, columns):
            pairs = [block(columns) for block in blocks]
            keys = jnp.concatenate([key for key, _ in pairs], axis=0)
            values = jnp.concatenate(
                [with_ones(value) * factor for (_, value), factor in zip(pairs, factors)], axis=0
            )
            queries = head_group(q_ref, group)
            for first in range(0, GROUP, STACK):
                rows = slice(first * tokens, (first + STACK) * tokens)
                scores = scores_of(head_rows(queries, first), keys)
                weights = weights_of(scores, shift_ref[group, rows, :]).astype(jnp.bfloat16)
                update = jnp.dot(weights, values, preferred_element_type=jnp.float32)
                acc_ref[group, rows, :] += update[:, :DH]
                total_ref[group, rows, :] += update[:, DH:]

        for_groups(one_group)


def in_one(ref):
    tokens = ref.shape[0] // 2
    return lambda columns: (ref[:tokens, columns], ref[tokens:, columns])


def in_two(key_ref, value_ref):
    return lambda columns: (key_ref[:, columns], value_ref[:, columns])


def is_earlier(me, place, sibling, chips):
    core = 1 - me % 2 if sibling else me % 2
    return 2 * chip_at(me, place, chips) + core < me


def step_kernel(chips, places, me_ref, q_ref, *refs):
    count = len(places)
    blocks, shift_ref, state = refs[:count], refs[count], refs[count + 3 :]
    me = me_ref[0]
    earlier = [is_earlier(me, place, sibling, chips) for place, sibling in places]
    fold_blocks(q_ref, [in_one(ref) for ref in blocks], earlier, shift_ref, *state)


def allowed_in(chip, me, tokens):
    shape = (STACK * tokens, 2 * tokens)
    token = lax.broadcasted_iota(jnp.int32, shape, 0) % tokens
    column = lax.broadcasted_iota(jnp.int32, shape, 1)
    sibling = jnp.where(jnp.logical_or(me % 2 == 1, chip < me // 2), 2 * tokens, 0)
    own = jnp.where(chip < me // 2, 2 * tokens, token)
    return column <= jnp.where(column < tokens, own, sibling)


def running_attention(chips, me, sources, q_ref, out_ref, scratch, sem):
    keys_ref, values_ref, acc_ref, total_ref, top_ref = scratch
    tokens = q_ref.shape[0]
    half = chips // 2
    places = [0] + [p for step in range(1, half) for p in (step, -step)] + [half]

    def fetch(source, target):
        copy = pltpu.make_async_copy(source, target, sem)
        copy.start()
        copy.wait()

    def one_head(head, carry):
        columns = pl.ds(pl.multiple_of(head * DH, DH), DH)
        queries = head_group(q_ref, head)
        for i, place in enumerate(places):
            if place != half:
                for core in range(2):
                    rows = pl.ds(core * tokens, tokens)
                    block = sources[2 * i + core]
                    fetch(block.at[pl.ds(0, tokens), columns], keys_ref.at[i, rows])
                    fetch(block.at[pl.ds(tokens, tokens), columns], values_ref.at[i, rows])
            else:
                key, value, sib_key, sib_value = sources[2 * i :]
                for core, (k, v) in enumerate(((key, value), (sib_key, sib_value))):
                    rows = pl.ds(core * tokens, tokens)
                    fetch(k.at[:, columns], keys_ref.at[i, rows])
                    fetch(v.at[:, columns], values_ref.at[i, rows])
        acc_ref[...] = jnp.zeros_like(acc_ref)
        total_ref[...] = jnp.zeros_like(total_ref)
        top_ref[...] = jnp.full_like(top_ref, 2 * MASKED)

        def one_chip(i, inner):
            forward = (i + 1) // 2
            place = jnp.where(i % 2 == 1, forward, -forward)
            chip = chip_at(me, place, chips)

            @pl.when(chip <= me // 2)
            def _():
                allowed = allowed_in(chip, me, tokens)
                keys, values = keys_ref[i], with_ones(values_ref[i])
                for first in range(0, GROUP, STACK):
                    rows = slice(first * tokens, (first + STACK) * tokens)
                    scores = jnp.where(allowed, scores_of(head_rows(queries, first), keys), MASKED)
                    old = top_ref[rows, :]
                    top = jnp.maximum(old, row_top(scores))
                    factor = jnp.exp2(old - top)
                    weights = weights_of(scores, top).astype(jnp.bfloat16)
                    update = jnp.dot(weights, values, preferred_element_type=jnp.float32)
                    acc_ref[rows, :] = acc_ref[rows, :] * factor + update[:, :DH]
                    total_ref[rows, :] = total_ref[rows, :] * factor + update[:, DH:]
                    top_ref[rows, :] = top

            return inner

        lax.fori_loop(0, chips, one_chip, 0)
        write_heads(out_ref, head, acc_ref[...], total_ref[...], tokens)
        return carry

    lax.fori_loop(0, HK, one_head, 0)


def write_heads(out_ref, head, acc, total, tokens):
    inverse = pl.reciprocal(total, approx=True)
    inverse = inverse * (2.0 - total * inverse)
    result = (acc * inverse).astype(jnp.bfloat16)
    columns = pl.ds(pl.multiple_of(head * WIDE, WIDE), WIDE)
    out_ref[:, columns] = jnp.concatenate(
        [result[h * tokens : (h + 1) * tokens] for h in range(GROUP)], axis=1
    )


def last_kernel(chips, me_ref, q_ref, *refs):
    key, value, sib_key, sib_value, shift_ref = refs[:5]
    gain_ref, table_ref, sources = refs[7], refs[8], refs[9 : 11 + 2 * chips]
    picked_ref, *state, result_ref = refs[11 + 2 * chips : 15 + 2 * chips]
    out_ref, worst_ref, sem, out_sems, *scratch = refs[15 + 2 * chips :]
    tokens = q_ref.shape[0]
    me = me_ref[0]
    earlier = [is_earlier(me, chips // 2, sibling, chips) for sibling in (False, True)]
    blocks = [in_two(key, value), in_two(sib_key, sib_value)]
    fold_blocks(q_ref, blocks, earlier, shift_ref, *state)
    worst_ref[...] = jnp.zeros_like(worst_ref)

    def write_out(group):
        columns = pl.ds(pl.multiple_of(group * WIDE, WIDE), WIDE)
        return pltpu.make_async_copy(
            out_ref.at[:, columns], result_ref.at[:, columns], out_sems.at[group]
        )

    def finish(group, columns):
        total = state[1][group]
        write_heads(out_ref, group, state[0][group], total, tokens)
        worst_ref[...] = jnp.maximum(worst_ref[...], total)

    for_groups(finish)
    fits = jnp.max(worst_ref[...]) <= SUM_LIMIT

    @pl.when(jnp.logical_not(fits))
    def _():
        running_attention(chips, me, sources, q_ref, out_ref, scratch, sem)

    for group in range(HK):
        write_out(group).start()
    width = out_ref.shape[1]
    picked = jnp.dot(table_ref[...], out_ref[...], preferred_element_type=jnp.float32)
    mean = jnp.sum(picked * picked, axis=1, keepdims=True) / width
    picked_ref[...] = (picked * lax.rsqrt(mean + 1e-05) * gain_ref[...]).astype(jnp.bfloat16)
    for group in range(HK):
        write_out(group).wait()


class Attention:
    def __init__(self, me, queries, chips):
        self.me, self.queries, self.chips = me, queries, chips
        tokens = queries.shape[0]
        self.state_shape = pltpu.VMEM((HK, GROUP * tokens, DH), jnp.float32)

    def call(self, kernel, name, args, others, out_shape, out_others, scratch, aliases=None):
        tokens, width = self.queries.shape
        vmem, anywhere = pl.BlockSpec(memory_space=pltpu.VMEM), pl.BlockSpec(memory_space=pl.ANY)
        smem = pl.BlockSpec(memory_space=pltpu.SMEM)
        return pl.pallas_call(
            kernel,
            in_specs=[smem if x is self.me else vmem for x in args] + [anywhere] * len(others),
            out_specs=[vmem] * len(out_shape) + [anywhere] * len(out_others),
            out_shape=[*out_shape, *out_others],
            scratch_shapes=scratch,
            input_output_aliases=aliases or {},
            compiler_params=pltpu.CompilerParams(vmem_limit_bytes=12 * MIB),
            cost_estimate=pl.CostEstimate(
                flops=4 * tokens * width * tokens, bytes_accessed=4 * MIB, transcendentals=0
            ),
            name=name,
        )(*args, *others)

    def own(self, own):
        *state, shift = self.call(
            own_kernel, "attend_own", (self.queries, own), (), [self.state_shape] * 3, (), ()
        )
        return state, shift

    def step(self, blocks, places, shift, state):
        count = len(blocks)
        return self.call(
            functools.partial(step_kernel, self.chips, places),
            "attend_step",
            (self.me, self.queries, *blocks, shift, *state),
            (),
            [self.state_shape] * 2,
            (),
            (),
            {count + 3: 0, count + 4: 1},
        )

    def last(self, pieces, shift, state, gain, table, sources):
        tokens, width = self.queries.shape
        rows = GROUP * tokens
        out = jax.ShapeDtypeStruct((tokens, width), jnp.bfloat16)
        picked, _, _, result = self.call(
            functools.partial(last_kernel, self.chips),
            "attend_last",
            (self.me, self.queries, *pieces, shift, *state, gain, table),
            sources,
            [pltpu.VMEM((CAP, width), jnp.bfloat16), self.state_shape, self.state_shape],
            [out],
            [
                pltpu.VMEM((tokens, width), jnp.bfloat16),
                pltpu.VMEM((rows, DH), jnp.float32),
                pltpu.SemaphoreType.DMA,
                pltpu.SemaphoreType.DMA((HK,)),
                pltpu.VMEM((self.chips, 2 * tokens, DH), jnp.bfloat16),
                pltpu.VMEM((self.chips, 2 * tokens, DH), jnp.bfloat16),
            ]
            + [pltpu.VMEM((rows, DH), jnp.float32)] * 3,
            {7: 1, 8: 2},
        )
        return result, picked


def stack_kernel(upper_ref, lower_ref, out_ref, sems):
    rows = upper_ref.shape[0]
    copies = [
        pltpu.make_async_copy(ref, out_ref.at[pl.ds(i * rows, rows)], sems.at[i])
        for i, ref in enumerate((upper_ref, lower_ref))
    ]
    for copy in copies:
        copy.start()
    for copy in copies:
        copy.wait()


def stack(upper, lower):
    anywhere = pl.BlockSpec(memory_space=pl.ANY)
    return pl.pallas_call(
        stack_kernel,
        in_specs=[anywhere] * 2,
        out_specs=anywhere,
        out_shape=pltpu.VMEM((2 * upper.shape[0], upper.shape[1]), upper.dtype),
        scratch_shapes=[pltpu.SemaphoreType.DMA((2,))],
        compiler_params=pltpu.CompilerParams(vmem_limit_bytes=MIB),
        name="stack",
    )(in_hbm(upper), in_hbm(lower))


def load_kernel(start, source_ref, target_ref, sem):
    columns = pl.ds(start, target_ref.shape[1])
    copy = pltpu.make_async_copy(source_ref.at[:, columns], target_ref, sem)
    copy.start()
    copy.wait()


def load(x, piece=0, pieces=1):
    rows, width = x.shape[0], x.shape[1] // pieces
    return pl.pallas_call(
        functools.partial(load_kernel, piece * width),
        in_specs=[pl.BlockSpec(memory_space=pl.ANY)],
        out_specs=pl.BlockSpec(memory_space=pl.ANY),
        out_shape=pltpu.VMEM((rows, width), x.dtype),
        scratch_shapes=[pltpu.SemaphoreType.DMA],
        compiler_params=pltpu.CompilerParams(vmem_limit_bytes=MIB),
        cost_estimate=pl.CostEstimate(flops=0, bytes_accessed=rows * width, transcendentals=0),
        name="load",
    )(in_hbm(x))


def hidden_kernel(chips, *refs):
    blocks, (gate_ref, up_ref, out_ref) = refs[: 2 * chips + 2], refs[2 * chips + 2 : 2 * chips + 5]
    gate_sum, up_sum = refs[2 * chips + 5 :]
    width = gate_ref.shape[0]
    half = width // 2
    depth = min(1024, half)
    gate_sum[...] = jnp.zeros_like(gate_sum)
    up_sum[...] = jnp.zeros_like(up_sum)
    for side in range(2):
        sides = []
        for core in range(2):
            mine = blocks[core * (chips + 1) : (core + 1) * (chips + 1)]
            sides += [(ref, side * half) for ref in mine[: chips - 1]] + [(mine[chips - 1 + side], 0)]

        def one_part(step, carry):
            part = jnp.concatenate(
                [ref[:, pl.ds(pl.multiple_of(start + step * depth, depth), depth)] for ref, start in sides],
                axis=0,
            )
            place = pl.ds(pl.multiple_of(side * half + step * depth, depth), depth)
            gate_sum[...] += jnp.dot(part, gate_ref[place, :], preferred_element_type=jnp.float32)
            up_sum[...] += jnp.dot(part, up_ref[place, :], preferred_element_type=jnp.float32)
            return carry

        lax.fori_loop(0, half // depth, one_part, 0)
    gate = gate_sum[...]
    out_ref[...] = (gate / (1.0 + jnp.exp(-gate)) * up_sum[...]).astype(jnp.bfloat16)


def hidden_call(chips, blocks, w_gate, w_up):
    rows = 2 * chips * CAP
    width, units = w_gate.shape
    vmem = pl.BlockSpec(memory_space=pltpu.VMEM)
    return pl.pallas_call(
        functools.partial(hidden_kernel, chips),
        in_specs=[vmem] * (len(blocks) + 2),
        out_specs=vmem,
        out_shape=pltpu.VMEM((rows, units), jnp.bfloat16),
        scratch_shapes=[pltpu.VMEM((rows, units), jnp.float32)] * 2,
        compiler_params=pltpu.CompilerParams(vmem_limit_bytes=16 * MIB),
        cost_estimate=pl.CostEstimate(
            flops=4 * rows * width * units,
            bytes_accessed=4 * width * units + 2 * rows * width,
            transcendentals=rows * units,
        ),
        name="hidden",
    )(*blocks, w_gate, w_up)


def down_kernel(hidden_ref, down_ref, own_ref, sib_ref):
    middle, width = own_ref.shape
    cols = min(1024, width)

    def one_part(step, carry):
        columns = pl.ds(pl.multiple_of(step * cols, cols), cols)
        part = jnp.dot(hidden_ref[...], down_ref[:, columns], preferred_element_type=jnp.float32)
        part = part.astype(jnp.bfloat16)
        own_ref[:, columns] = part[:middle]
        sib_ref[:, columns] = part[middle:]
        return carry

    lax.fori_loop(0, width // cols, one_part, 0)


def down_call(hidden, w_down):
    rows, units = hidden.shape
    width = w_down.shape[1]
    vmem = pl.BlockSpec(memory_space=pltpu.VMEM)
    return pl.pallas_call(
        down_kernel,
        in_specs=[vmem] * 2,
        out_specs=[vmem] * 2,
        out_shape=[pltpu.VMEM((rows // 2, width), jnp.bfloat16)] * 2,
        compiler_params=pltpu.CompilerParams(vmem_limit_bytes=16 * MIB),
        cost_estimate=pl.CostEstimate(
            flops=2 * rows * width * units,
            bytes_accessed=2 * width * units + 2 * rows * width,
            transcendentals=0,
        ),
        name="down",
    )(hidden, w_down)


def spread_kernel(a_ref, b_ref, c_ref, d_ref, table_ref, *rest):
    out_ref = rest[-1]
    total = a_ref[...].astype(jnp.float32) + b_ref[...].astype(jnp.float32)
    total += c_ref[...].astype(jnp.float32) + d_ref[...].astype(jnp.float32)
    total = total.astype(jnp.bfloat16)
    out_ref[...] = lax.dot_general(
        table_ref[...],
        jnp.concatenate([total] * PARTS, axis=0),
        (((0,), (0,)), ((), ())),
        preferred_element_type=jnp.float32,
    ).astype(jnp.bfloat16)


def spread_call(parts, table, piece, pieces, previous):
    tokens = table.shape[1]
    piece_width = parts[0].shape[1]
    cols = min(2048, piece_width)
    steps = piece_width // cols
    earlier = [] if previous is None else [previous]
    return pl.pallas_call(
        spread_kernel,
        grid=(steps,),
        in_specs=[pl.BlockSpec((CAP, cols), lambda i: (0, i))] * 4
        + [pl.BlockSpec((PARTS * CAP, tokens), lambda i: (0, 0))]
        + [pl.BlockSpec(memory_space=pl.ANY)] * len(earlier),
        out_specs=pl.BlockSpec((tokens, cols), lambda i: (0, piece * steps + i)),
        out_shape=jax.ShapeDtypeStruct((tokens, piece_width * pieces), jnp.bfloat16),
        input_output_aliases={5: 0} if earlier else {},
        compiler_params=pltpu.CompilerParams(
            dimension_semantics=("arbitrary",), vmem_limit_bytes=16 * MIB
        ),
        name="spread",
    )(*parts, table, *earlier)


def reduce_chip_rows(mine, other, half, chips, go_right, go_left):
    middle = mine.shape[1] // 2

    def block(index):
        rows = slice(index * CAP, (index + 1) * CAP)
        return mine[rows].astype(jnp.float32) + other[rows].astype(jnp.float32)

    far = block(chips - 1).astype(jnp.bfloat16)
    ahead, back = far[:, :middle], far[:, middle:]
    for distance in range(half - 1, -1, -1):
        ahead, back = lax.optimization_barrier((ahead, back))
        to_right, to_left = go_right(ahead), go_left(back)
        yield
        if distance == 0:
            break
        ahead, back = block(half - 1 + distance), block(distance)
        if distance == half - 1:
            ahead = jnp.concatenate(
                [ahead[:, :middle] + to_right.astype(jnp.float32), ahead[:, middle:]], axis=1
            )
            back = jnp.concatenate(
                [back[:, :middle], back[:, middle:] + to_left.astype(jnp.float32)], axis=1
            )
        else:
            ahead = ahead + to_right.astype(jnp.float32)
            back = back + to_left.astype(jnp.float32)
        ahead, back = ahead.astype(jnp.bfloat16), back.astype(jnp.bfloat16)
    return (mine, other, to_right, to_left)


def run_together(generators):
    results = [None] * len(generators)
    active = list(range(len(generators)))
    while active:
        for i in list(active):
            try:
                next(generators[i])
            except StopIteration as stop:
                results[i] = stop.value
                active.remove(i)
    return results


def per_device(chips, queries, keys, values, norm_gain, expert_ids, gates, w_gate, w_up, w_down):
    right, left, sibling = permutations(chips)
    half = chips // 2
    go_right = lambda x: lax.ppermute(x, "ctx", right)
    go_left = lambda x: lax.ppermute(x, "ctx", left)
    swap = lambda x: lax.ppermute(x, "ctx", sibling)

    me = lax.axis_index("ctx").astype(jnp.int32).reshape(1)
    tokens = queries.shape[0]
    hits = (expert_ids == 0).astype(jnp.float32)
    chosen = jnp.sum(hits, axis=1)
    position = jnp.arange(tokens, dtype=jnp.int32)
    before = (position[None, :] < position[:, None]).astype(jnp.float32)
    slot = jnp.sum(before * chosen[None, :], axis=1).astype(jnp.int32)
    table = jnp.logical_and(
        slot[None, :] == jnp.arange(CAP, dtype=jnp.int32)[:, None], chosen[None, :] > 0
    ).astype(jnp.float32)
    rest = jnp.sum(gates * hits, axis=1)
    weights = []
    for _ in range(PARTS):
        part = lax.reduce_precision(rest, 8, 7)
        weights.append(table * part[None, :])
        rest = rest - part
    weighted = jnp.concatenate(weights, axis=0).astype(jnp.bfloat16)
    table = table.astype(jnp.bfloat16)

    attention = Attention(me, load(queries), chips)
    own = stack(keys, values)
    from_left, from_right = go_right(own), go_left(own)
    late, late_places = [swap(own)], [(0, True)]
    state, shift = attention.own(own)
    mine, others = [own], []
    for step in range(1, half):
        from_left, from_right, state, late = lax.optimization_barrier(
            (from_left, from_right, state, late)
        )
        blocks = [from_left, from_right, *late]
        places = [(step, False), (-step, False), *late_places]
        mine += [from_left, from_right]
        others += late
        late = [swap(from_left), swap(from_right)]
        late_places = [(step, True), (-step, True)]
        if step < half - 1:
            from_left, from_right = go_right(from_left), go_left(from_right)
        else:
            far_keys, far_values = go_right(from_left[:tokens]), go_left(from_right[tokens:])
        state = attention.step(blocks, places, shift, state)
    far_keys, far_values, state, late = lax.optimization_barrier(
        (far_keys, far_values, state, late)
    )
    state = attention.step(late, late_places, shift, state)
    others += late
    opposite = (far_keys, far_values, swap(far_keys), swap(far_values))
    sources = [x for pair in zip(mine, others) for x in pair] + list(opposite)
    result, picked = attention.last(opposite, shift, state, norm_gain[None, :], table, sources)

    picked, w_gate, w_up, w_down = lax.optimization_barrier((picked, w_gate, w_up, w_down))
    downs = []
    middle = picked.shape[1] // 2
    from_left, from_right, waiting = picked, picked, [picked]
    blocks_right, blocks_left, swapped = [picked], [], []
    for step in range(1, half):
        from_left, from_right = go_right(from_left), go_left(from_right)
        if step == 1:
            w_gate = load(w_gate)
        elif step == 2:
            w_up = load(w_up)
        elif step == 3:
            downs.append(load(w_down, 0, PIECES))
        from_left, from_right, waiting, w_gate, w_up, w_down, downs = lax.optimization_barrier(
            (from_left, from_right, waiting, w_gate, w_up, w_down, downs)
        )
        blocks_right.append(from_left)
        blocks_left.append(from_right)
        swapped += [swap(x) for x in waiting]
        waiting = [from_left, from_right]
    far = [go_right(from_left[:, :middle]), go_left(from_right[:, middle:])]
    downs += [load(w_down, piece, PIECES) for piece in range(len(downs), PIECES)]
    far, downs = lax.optimization_barrier((far, downs))
    swapped += [swap(x) for x in waiting + far]
    blocks = blocks_right + blocks_left + far
    others = swapped[:1] + swapped[1:-2:2] + swapped[2:-2:2] + swapped[-2:]
    hidden = hidden_call(chips, blocks + others, w_gate, w_up)

    sums = []
    for piece in range(PIECES):
        mine, theirs = down_call(hidden, downs[piece])
        sums.append(reduce_chip_rows(mine, swap(theirs), half, chips, go_right, go_left))
    mixed = None
    for piece, parts in enumerate(run_together(sums)):
        mixed = spread_call(parts, weighted, piece, PIECES, mixed)
    return (result, mixed)


def solution(mesh):
    placed = (
        P(("groups", "ctx"), None),
        P(("groups", "ctx"), None),
        P(("groups", "ctx"), None),
        P(),
        P(("groups", "ctx"), None),
        P(("groups", "ctx"), None),
        P(None, "ctx"),
        P(None, "ctx"),
        P("ctx", None),
    )
    return jax.shard_map(
        functools.partial(per_device, mesh.shape["ctx"] // 2),
        mesh=mesh,
        in_specs=placed,
        out_specs=(P(("groups", "ctx"), None), P(("groups", "ctx"), None)),
        check_vma=False,
    )
```

```python
import functools
import math

import jax
import jax.numpy as jnp
from jax import lax
from jax.experimental import pallas as pl
from jax.experimental.pallas import tpu as pltpu
from jax.sharding import PartitionSpec as P

HQ = 64
HK = 8
DH = 128
CAP = 16
GROUP = HQ // HK
WIDE = GROUP * DH
LOG_SCALE = math.log2(math.e) / math.sqrt(DH)
MASKED = -1e30
PIECES = 2
SUM_LIMIT = 2.0**100
PARTS = 3
STACK = 4
MIB = 1 << 20


def in_hbm(x):
    return pltpu.with_memory_space_constraint(x, pltpu.HBM)


def ring_order(chips):
    return list(range(0, chips, 2)) + list(range(1, chips, 2))[::-1]


def permutations(chips):
    order = ring_order(chips)
    right, left = [], []
    for place in range(chips):
        here, there = order[place], order[(place + 1) % chips]
        for core in range(2):
            right.append((2 * here + core, 2 * there + core))
            left.append((2 * there + core, 2 * here + core))
    sibling = [(i, i ^ 1) for i in range(2 * chips)]
    return right, left, sibling


def chip_at(me, step, chips):
    chip = me // 2
    place = jnp.where(chip % 2 == 0, chip // 2, chips - 1 - chip // 2)
    source = (place - step + 2 * chips) % chips
    return jnp.where(source < chips // 2, 2 * source, 2 * (chips - 1 - source) + 1)


def head_rows(queries, first):
    return jnp.concatenate(
        [queries[:, h * DH : (h + 1) * DH] for h in range(first, first + STACK)], axis=0
    )


def with_ones(values):
    return jnp.concatenate([values, jnp.ones_like(values)], axis=1)


def scores_of(queries, keys):
    return LOG_SCALE * lax.dot_general(
        queries, keys, (((1,), (1,)), ((), ())), preferred_element_type=jnp.float32
    )


def weights_of(scores, shift):
    return jnp.exp2(scores - jnp.concatenate([shift] * (scores.shape[1] // DH), axis=1))


def row_top(scores):
    return jnp.broadcast_to(jnp.max(scores, axis=1, keepdims=True), (scores.shape[0], DH))


def diagonal(tokens):
    shape = (STACK * tokens, tokens)
    token = lax.broadcasted_iota(jnp.int32, shape, 0) % tokens
    return lax.broadcasted_iota(jnp.int32, shape, 1) <= token


def head_group(q_ref, group):
    return q_ref[:, pl.ds(pl.multiple_of(group * WIDE, WIDE), WIDE)]


def for_groups(body):
    def step(group, carry):
        body(group, pl.ds(pl.multiple_of(group * DH, DH), DH))
        return carry

    lax.fori_loop(0, HK, step, 0)


def own_kernel(q_ref, own_ref, acc_ref, total_ref, shift_ref):
    tokens = q_ref.shape[0]
    allowed = diagonal(tokens)

    def one_group(group, columns):
        keys, values = own_ref[:tokens, columns], with_ones(own_ref[tokens:, columns])
        queries = head_group(q_ref, group)
        for first in range(0, GROUP, STACK):
            rows = slice(first * tokens, (first + STACK) * tokens)
            scores = jnp.where(allowed, scores_of(head_rows(queries, first), keys), MASKED)
            shift = row_top(scores)
            weights = weights_of(scores, shift).astype(jnp.bfloat16)
            update = jnp.dot(weights, values, preferred_element_type=jnp.float32)
            acc_ref[group, rows, :] = update[:, :DH]
            total_ref[group, rows, :] = update[:, DH:]
            shift_ref[group, rows, :] = shift

    for_groups(one_group)


def fold(queries, first, keys, values, shift):
    weights = weights_of(scores_of(head_rows(queries, first), keys), shift).astype(jnp.bfloat16)
    return jnp.dot(weights, values, preferred_element_type=jnp.float32)


def block_factors(earlier):
    return [jnp.where(flag, 1.0, 0.0).astype(jnp.bfloat16) for flag in earlier]


def join_blocks(blocks, factors, columns):
    pairs = [block(columns) for block in blocks]
    keys = jnp.concatenate([key for key, _ in pairs], axis=0)
    values = [with_ones(value) * factor for (_, value), factor in zip(pairs, factors)]
    return keys, jnp.concatenate(values, axis=0)


def fold_blocks(q_ref, blocks, earlier, shift_ref, acc_ref, total_ref):
    tokens = q_ref.shape[0]

    @pl.when(functools.reduce(jnp.logical_or, earlier))
    def _():
        factors = block_factors(earlier)

        def one_group(group, columns):
            keys, values = join_blocks(blocks, factors, columns)
            queries = head_group(q_ref, group)
            for first in range(0, GROUP, STACK):
                rows = slice(first * tokens, (first + STACK) * tokens)
                update = fold(queries, first, keys, values, shift_ref[group, rows, :])
                acc_ref[group, rows, :] += update[:, :DH]
                total_ref[group, rows, :] += update[:, DH:]

        for_groups(one_group)


def in_one(ref):
    tokens = ref.shape[0] // 2
    return lambda columns: (ref[:tokens, columns], ref[tokens:, columns])


def in_two(key_ref, value_ref):
    return lambda columns: (key_ref[:, columns], value_ref[:, columns])


def is_earlier(me, place, sibling, chips):
    core = 1 - me % 2 if sibling else me % 2
    return 2 * chip_at(me, place, chips) + core < me


def step_kernel(chips, places, me_ref, q_ref, *refs):
    count = len(places)
    blocks, shift_ref, state = refs[:count], refs[count], refs[count + 3 :]
    me = me_ref[0]
    earlier = [is_earlier(me, place, sibling, chips) for place, sibling in places]
    fold_blocks(q_ref, [in_one(ref) for ref in blocks], earlier, shift_ref, *state)


def allowed_in(chip, me, tokens):
    shape = (STACK * tokens, 2 * tokens)
    token = lax.broadcasted_iota(jnp.int32, shape, 0) % tokens
    column = lax.broadcasted_iota(jnp.int32, shape, 1)
    sibling = jnp.where(jnp.logical_or(me % 2 == 1, chip < me // 2), 2 * tokens, 0)
    own = jnp.where(chip < me // 2, 2 * tokens, token)
    return column <= jnp.where(column < tokens, own, sibling)


def running_attention(chips, me, sources, q_ref, out_ref, rows_ref, table_ref, scratch, sem):
    keys_ref, values_ref, acc_ref, total_ref, top_ref = scratch
    tokens = q_ref.shape[0]
    half = chips // 2
    places = [0] + [p for step in range(1, half) for p in (step, -step)] + [half]

    def fetch(source, target):
        copy = pltpu.make_async_copy(source, target, sem)
        copy.start()
        copy.wait()

    def one_head(head, carry):
        columns = pl.ds(pl.multiple_of(head * DH, DH), DH)
        queries = head_group(q_ref, head)
        for i, place in enumerate(places):
            if place != half:
                for core in range(2):
                    rows = pl.ds(core * tokens, tokens)
                    block = sources[2 * i + core]
                    fetch(block.at[pl.ds(0, tokens), columns], keys_ref.at[i, rows])
                    fetch(block.at[pl.ds(tokens, tokens), columns], values_ref.at[i, rows])
            else:
                key, value, sib_key, sib_value = sources[2 * i :]
                for core, (k, v) in enumerate(((key, value), (sib_key, sib_value))):
                    rows = pl.ds(core * tokens, tokens)
                    fetch(k.at[:, columns], keys_ref.at[i, rows])
                    fetch(v.at[:, columns], values_ref.at[i, rows])
        acc_ref[...] = jnp.zeros_like(acc_ref)
        total_ref[...] = jnp.zeros_like(total_ref)
        top_ref[...] = jnp.full_like(top_ref, 2 * MASKED)

        def one_chip(i, inner):
            forward = (i + 1) // 2
            place = jnp.where(i % 2 == 1, forward, -forward)
            chip = chip_at(me, place, chips)

            @pl.when(chip <= me // 2)
            def _():
                allowed = allowed_in(chip, me, tokens)
                keys, values = keys_ref[i], with_ones(values_ref[i])
                for first in range(0, GROUP, STACK):
                    rows = slice(first * tokens, (first + STACK) * tokens)
                    scores = jnp.where(allowed, scores_of(head_rows(queries, first), keys), MASKED)
                    old = top_ref[rows, :]
                    top = jnp.maximum(old, row_top(scores))
                    factor = jnp.exp2(old - top)
                    weights = weights_of(scores, top).astype(jnp.bfloat16)
                    update = jnp.dot(weights, values, preferred_element_type=jnp.float32)
                    acc_ref[rows, :] = acc_ref[rows, :] * factor + update[:, :DH]
                    total_ref[rows, :] = total_ref[rows, :] * factor + update[:, DH:]
                    top_ref[rows, :] = top

            return inner

        lax.fori_loop(0, chips, one_chip, 0)
        put_heads(out_ref, rows_ref, table_ref, head, divide(acc_ref[...], total_ref[...]))
        return carry

    lax.fori_loop(0, HK, one_head, 0)


def divide(acc, total):
    inverse = pl.reciprocal(total, approx=True)
    inverse = inverse * (2.0 - total * inverse)
    return (acc * inverse).astype(jnp.bfloat16)


def put_heads(out_ref, rows_ref, table_ref, group, result):
    tokens = out_ref.shape[0]
    columns = pl.ds(pl.multiple_of(group * WIDE, WIDE), WIDE)
    result = jnp.concatenate([result[h * tokens : (h + 1) * tokens] for h in range(GROUP)], axis=1)
    out_ref[:, columns] = result
    rows_ref[:, columns] = jnp.dot(table_ref[...], result, preferred_element_type=jnp.float32)


def last_kernel(chips, me_ref, q_ref, *refs):
    late_left, late_right, key, value, sib_key, sib_value, shift_ref = refs[:7]
    acc_ref, total_ref, gain_ref, table_ref = refs[7:11]
    sources = refs[11 : 13 + 2 * chips]
    keep_ref, give_ref, result_ref = refs[13 + 2 * chips : 16 + 2 * chips]
    out_ref, rows_ref, worst_ref, sem, out_sems, *scratch = refs[16 + 2 * chips :]
    tokens, width = q_ref.shape
    me = me_ref[0]
    half = chips // 2
    places = [(half - 1, True), (1 - half, True), (half, False), (half, True)]
    blocks = [in_one(late_left), in_one(late_right), in_two(key, value), in_two(sib_key, sib_value)]
    factors = block_factors([is_earlier(me, *place, chips) for place in places])
    worst_ref[...] = jnp.zeros_like(worst_ref)

    def write_out(group):
        columns = pl.ds(pl.multiple_of(group * WIDE, WIDE), WIDE)
        return pltpu.make_async_copy(
            out_ref.at[:, columns], result_ref.at[:, columns], out_sems.at[group]
        )

    def one_group(group, columns):
        keys, values = join_blocks(blocks, factors, columns)
        queries = head_group(q_ref, group)
        results = []
        for first in range(0, GROUP, STACK):
            rows = slice(first * tokens, (first + STACK) * tokens)
            update = fold(queries, first, keys, values, shift_ref[group, rows, :])
            total = total_ref[group, rows, :] + update[:, DH:]
            worst_ref[...] = jnp.maximum(worst_ref[...], total)
            results.append(divide(acc_ref[group, rows, :] + update[:, :DH], total))
        put_heads(out_ref, rows_ref, table_ref, group, jnp.concatenate(results, axis=0))
        write_out(group).start()

    for_groups(one_group)

    def norm_rows():
        core = me % 2
        squares = rows_ref[...] * rows_ref[...]
        scale = lax.rsqrt(jnp.sum(squares, axis=1, keepdims=True) / width + 1e-05)
        for side, ref in ((core, keep_ref), (1 - core, give_ref)):
            columns = pl.ds(pl.multiple_of(side * (width // 2), width // 2), width // 2)
            ref[...] = (rows_ref[:, columns] * scale * gain_ref[:, columns]).astype(jnp.bfloat16)

    norm_rows()
    fits = jnp.max(worst_ref[...]) <= SUM_LIMIT
    for group in range(HK):
        write_out(group).wait()

    @pl.when(jnp.logical_not(fits))
    def _():
        running_attention(chips, me, sources, q_ref, out_ref, rows_ref, table_ref, scratch, sem)
        for group in range(HK):
            write_out(group).start()
        for group in range(HK):
            write_out(group).wait()
        norm_rows()


class Attention:
    def __init__(self, me, queries, chips):
        self.me, self.queries, self.chips = me, queries, chips
        tokens = queries.shape[0]
        self.state_shape = pltpu.VMEM((HK, GROUP * tokens, DH), jnp.float32)

    def call(self, kernel, name, args, others, out_shape, out_others, scratch, aliases=None):
        tokens, width = self.queries.shape
        vmem, anywhere = pl.BlockSpec(memory_space=pltpu.VMEM), pl.BlockSpec(memory_space=pl.ANY)
        smem = pl.BlockSpec(memory_space=pltpu.SMEM)
        return pl.pallas_call(
            kernel,
            in_specs=[smem if x is self.me else vmem for x in args] + [anywhere] * len(others),
            out_specs=[vmem] * len(out_shape) + [anywhere] * len(out_others),
            out_shape=[*out_shape, *out_others],
            scratch_shapes=scratch,
            input_output_aliases=aliases or {},
            compiler_params=pltpu.CompilerParams(vmem_limit_bytes=12 * MIB),
            cost_estimate=pl.CostEstimate(
                flops=4 * tokens * width * tokens, bytes_accessed=4 * MIB, transcendentals=0
            ),
            name=name,
        )(*args, *others)

    def own(self, own):
        *state, shift = self.call(
            own_kernel, "attend_own", (self.queries, own), (), [self.state_shape] * 3, (), ()
        )
        return state, shift

    def step(self, blocks, places, shift, state):
        count = len(blocks)
        return self.call(
            functools.partial(step_kernel, self.chips, places),
            "attend_step",
            (self.me, self.queries, *blocks, shift, *state),
            (),
            [self.state_shape] * 2,
            (),
            (),
            {count + 3: 0, count + 4: 1},
        )

    def last(self, late, pieces, shift, state, gain, table, sources):
        tokens, width = self.queries.shape
        rows = GROUP * tokens
        out = jax.ShapeDtypeStruct((tokens, width), jnp.bfloat16)
        picked = pltpu.VMEM((CAP, width // 2), jnp.bfloat16)
        return self.call(
            functools.partial(last_kernel, self.chips),
            "attend_last",
            (self.me, self.queries, *late, *pieces, shift, *state, gain, table),
            sources,
            [picked, picked],
            [out],
            [
                pltpu.VMEM((tokens, width), jnp.bfloat16),
                pltpu.VMEM((CAP, width), jnp.float32),
                pltpu.VMEM((STACK * tokens, DH), jnp.float32),
                pltpu.SemaphoreType.DMA,
                pltpu.SemaphoreType.DMA((HK,)),
                pltpu.VMEM((self.chips, 2 * tokens, DH), jnp.bfloat16),
                pltpu.VMEM((self.chips, 2 * tokens, DH), jnp.bfloat16),
            ]
            + [pltpu.VMEM((rows, DH), jnp.float32)] * 3,
        )


def stack_kernel(upper_ref, lower_ref, out_ref, sems):
    rows = upper_ref.shape[0]
    copies = [
        pltpu.make_async_copy(ref, out_ref.at[pl.ds(i * rows, rows)], sems.at[i])
        for i, ref in enumerate((upper_ref, lower_ref))
    ]
    for copy in copies:
        copy.start()
    for copy in copies:
        copy.wait()


def stack(upper, lower):
    anywhere = pl.BlockSpec(memory_space=pl.ANY)
    return pl.pallas_call(
        stack_kernel,
        in_specs=[anywhere] * 2,
        out_specs=anywhere,
        out_shape=pltpu.VMEM((2 * upper.shape[0], upper.shape[1]), upper.dtype),
        scratch_shapes=[pltpu.SemaphoreType.DMA((2,))],
        compiler_params=pltpu.CompilerParams(vmem_limit_bytes=MIB),
        name="stack",
    )(in_hbm(upper), in_hbm(lower))


def load_kernel(start, source_ref, target_ref, sem):
    columns = pl.ds(start, target_ref.shape[1])
    copy = pltpu.make_async_copy(source_ref.at[:, columns], target_ref, sem)
    copy.start()
    copy.wait()


def load(x, piece=0, pieces=1):
    rows, width = x.shape[0], x.shape[1] // pieces
    return pl.pallas_call(
        functools.partial(load_kernel, piece * width),
        in_specs=[pl.BlockSpec(memory_space=pl.ANY)],
        out_specs=pl.BlockSpec(memory_space=pl.ANY),
        out_shape=pltpu.VMEM((rows, width), x.dtype),
        scratch_shapes=[pltpu.SemaphoreType.DMA],
        compiler_params=pltpu.CompilerParams(vmem_limit_bytes=MIB),
        cost_estimate=pl.CostEstimate(flops=0, bytes_accessed=rows * width, transcendentals=0),
        name="load",
    )(in_hbm(x))


def gather_kernel(*refs):
    blocks, out_ref = refs[:-1], refs[-1]
    middle = out_ref.shape[0] // 2
    parts = [(ref[:CAP], ref[CAP:]) for ref in blocks[:-2]] + [(blocks[-2][...], blocks[-1][...])]
    for j, (mine, other) in enumerate(parts):
        out_ref[j * CAP : (j + 1) * CAP] = mine
        out_ref[middle + j * CAP : middle + (j + 1) * CAP] = other


def gather(blocks):
    vmem = pl.BlockSpec(memory_space=pltpu.VMEM)
    width = blocks[0].shape[1]
    return pl.pallas_call(
        gather_kernel,
        in_specs=[vmem] * len(blocks),
        out_specs=vmem,
        out_shape=pltpu.VMEM((2 * CAP * (len(blocks) - 1), width), jnp.bfloat16),
        compiler_params=pltpu.CompilerParams(vmem_limit_bytes=4 * MIB),
        name="gather",
    )(*blocks)


def hidden_kernel(second, me_ref, rows_ref, gate_ref, up_ref, *refs):
    half = rows_ref.shape[1]
    middle = rows_ref.shape[0] // 2
    depth = min(1024, half)
    if second:
        gate_in, up_in, out_ref, gate_sum, up_sum = refs
        gate_sum[...] = gate_in[...]
        up_sum[...] = up_in[...]
    else:
        gate_sum, up_sum = refs
        gate_sum[...] = jnp.zeros_like(gate_sum)
        up_sum[...] = jnp.zeros_like(up_sum)
    side = 1 - me_ref[0] % 2 if second else me_ref[0] % 2

    def one_part(step, carry):
        part = rows_ref[:, pl.ds(pl.multiple_of(step * depth, depth), depth)]
        if second:
            part = jnp.concatenate([part[middle:], part[:middle]], axis=0)
        place = pl.ds(pl.multiple_of(side * half + step * depth, depth), depth)
        gate_sum[...] += jnp.dot(part, gate_ref[place, :], preferred_element_type=jnp.float32)
        up_sum[...] += jnp.dot(part, up_ref[place, :], preferred_element_type=jnp.float32)
        return carry

    lax.fori_loop(0, half // depth, one_part, 0)
    if second:
        gate = gate_sum[...]
        out_ref[...] = (gate / (1.0 + jnp.exp(-gate)) * up_sum[...]).astype(jnp.bfloat16)


def hidden_call(me, rows, w_gate, w_up, sums=None):
    count, half = rows.shape
    units = w_gate.shape[1]
    vmem = pl.BlockSpec(memory_space=pltpu.VMEM)
    sum_shape = pltpu.VMEM((count, units), jnp.float32)
    second = sums is not None
    return pl.pallas_call(
        functools.partial(hidden_kernel, second),
        in_specs=[pl.BlockSpec(memory_space=pltpu.SMEM)] + [vmem] * (5 if second else 3),
        out_specs=vmem if second else [vmem] * 2,
        out_shape=pltpu.VMEM((count, units), jnp.bfloat16) if second else [sum_shape] * 2,
        scratch_shapes=[sum_shape] * (2 if second else 0),
        compiler_params=pltpu.CompilerParams(vmem_limit_bytes=16 * MIB),
        cost_estimate=pl.CostEstimate(
            flops=4 * count * half * units,
            bytes_accessed=4 * half * units + 2 * count * half,
            transcendentals=count * units,
        ),
        name="hidden",
    )(me, rows, w_gate, w_up, *(sums or ()))


def down_kernel(hidden_ref, down_ref, own_ref, sib_ref):
    middle, width = own_ref.shape
    cols = min(1024, width)

    def one_part(step, carry):
        columns = pl.ds(pl.multiple_of(step * cols, cols), cols)
        part = jnp.dot(hidden_ref[...], down_ref[:, columns], preferred_element_type=jnp.float32)
        part = part.astype(jnp.bfloat16)
        own_ref[:, columns] = part[:middle]
        sib_ref[:, columns] = part[middle:]
        return carry

    lax.fori_loop(0, width // cols, one_part, 0)


def down_call(hidden, w_down):
    rows, units = hidden.shape
    width = w_down.shape[1]
    vmem = pl.BlockSpec(memory_space=pltpu.VMEM)
    return pl.pallas_call(
        down_kernel,
        in_specs=[vmem] * 2,
        out_specs=[vmem] * 2,
        out_shape=[pltpu.VMEM((rows // 2, width), jnp.bfloat16)] * 2,
        compiler_params=pltpu.CompilerParams(vmem_limit_bytes=16 * MIB),
        cost_estimate=pl.CostEstimate(
            flops=2 * rows * width * units,
            bytes_accessed=2 * width * units + 2 * rows * width,
            transcendentals=0,
        ),
        name="down",
    )(hidden, w_down)


def spread_kernel(a_ref, b_ref, c_ref, d_ref, table_ref, *rest):
    out_ref = rest[-1]
    total = a_ref[...].astype(jnp.float32) + b_ref[...].astype(jnp.float32)
    total += c_ref[...].astype(jnp.float32) + d_ref[...].astype(jnp.float32)
    total = total.astype(jnp.bfloat16)
    out_ref[...] = lax.dot_general(
        table_ref[...],
        jnp.concatenate([total] * PARTS, axis=0),
        (((0,), (0,)), ((), ())),
        preferred_element_type=jnp.float32,
    ).astype(jnp.bfloat16)


def spread_call(parts, table, piece, pieces, previous):
    tokens = table.shape[1]
    piece_width = parts[0].shape[1]
    cols = min(2048, piece_width)
    steps = piece_width // cols
    earlier = [] if previous is None else [previous]
    return pl.pallas_call(
        spread_kernel,
        grid=(steps,),
        in_specs=[pl.BlockSpec((CAP, cols), lambda i: (0, i))] * 4
        + [pl.BlockSpec((PARTS * CAP, tokens), lambda i: (0, 0))]
        + [pl.BlockSpec(memory_space=pl.ANY)] * len(earlier),
        out_specs=pl.BlockSpec((tokens, cols), lambda i: (0, piece * steps + i)),
        out_shape=jax.ShapeDtypeStruct((tokens, piece_width * pieces), jnp.bfloat16),
        input_output_aliases={5: 0} if earlier else {},
        compiler_params=pltpu.CompilerParams(
            dimension_semantics=("arbitrary",), vmem_limit_bytes=16 * MIB
        ),
        name="spread",
    )(*parts, table, *earlier)


def reduce_chip_rows(mine, other, half, chips, go_right, go_left):
    middle = mine.shape[1] // 2

    def block(index):
        rows = slice(index * CAP, (index + 1) * CAP)
        return mine[rows].astype(jnp.float32) + other[rows].astype(jnp.float32)

    far = block(chips - 1).astype(jnp.bfloat16)
    ahead, back = far[:, :middle], far[:, middle:]
    for distance in range(half - 1, -1, -1):
        ahead, back = lax.optimization_barrier((ahead, back))
        to_right, to_left = go_right(ahead), go_left(back)
        yield
        if distance == 0:
            break
        ahead, back = block(half - 1 + distance), block(distance)
        if distance == half - 1:
            ahead = jnp.concatenate(
                [ahead[:, :middle] + to_right.astype(jnp.float32), ahead[:, middle:]], axis=1
            )
            back = jnp.concatenate(
                [back[:, :middle], back[:, middle:] + to_left.astype(jnp.float32)], axis=1
            )
        else:
            ahead = ahead + to_right.astype(jnp.float32)
            back = back + to_left.astype(jnp.float32)
        ahead, back = ahead.astype(jnp.bfloat16), back.astype(jnp.bfloat16)
    return (mine, other, to_right, to_left)


def run_together(generators):
    results = [None] * len(generators)
    active = list(range(len(generators)))
    while active:
        for i in list(active):
            try:
                next(generators[i])
            except StopIteration as stop:
                results[i] = stop.value
                active.remove(i)
    return results


def per_device(chips, queries, keys, values, norm_gain, expert_ids, gates, w_gate, w_up, w_down):
    right, left, sibling = permutations(chips)
    half = chips // 2
    go_right = lambda x: lax.ppermute(x, "ctx", right)
    go_left = lambda x: lax.ppermute(x, "ctx", left)
    swap = lambda x: lax.ppermute(x, "ctx", sibling)

    me = lax.axis_index("ctx").astype(jnp.int32).reshape(1)
    tokens = queries.shape[0]
    hits = (expert_ids == 0).astype(jnp.float32)
    chosen = jnp.sum(hits, axis=1)
    position = jnp.arange(tokens, dtype=jnp.int32)
    before = (position[None, :] < position[:, None]).astype(jnp.float32)
    slot = jnp.sum(before * chosen[None, :], axis=1).astype(jnp.int32)
    table = jnp.logical_and(
        slot[None, :] == jnp.arange(CAP, dtype=jnp.int32)[:, None], chosen[None, :] > 0
    ).astype(jnp.float32)
    rest = jnp.sum(gates * hits, axis=1)
    weights = []
    for _ in range(PARTS):
        part = lax.reduce_precision(rest, 8, 7)
        weights.append(table * part[None, :])
        rest = rest - part
    weighted = jnp.concatenate(weights, axis=0).astype(jnp.bfloat16)
    table = table.astype(jnp.bfloat16)

    own = stack(keys, values)
    own, me = lax.optimization_barrier((own, me))
    attention = Attention(me, load(queries), chips)
    from_left, from_right = go_right(own), go_left(own)
    late, late_places = [swap(own)], [(0, True)]
    state, shift = attention.own(own)
    state, w_down = lax.optimization_barrier((state, w_down))
    downs = [load(w_down, piece, PIECES) for piece in range(PIECES)]
    mine, others = [own], []
    for step in range(1, half):
        from_left, from_right, state, late, downs = lax.optimization_barrier(
            (from_left, from_right, state, late, downs)
        )
        blocks = [from_left, from_right, *late]
        places = [(step, False), (-step, False), *late_places]
        mine += [from_left, from_right]
        others += late
        late = [swap(from_left), swap(from_right)]
        late_places = [(step, True), (-step, True)]
        if step < half - 1:
            from_left, from_right = go_right(from_left), go_left(from_right)
        else:
            far_keys, far_values = go_right(from_left[:tokens]), go_left(from_right[tokens:])
        state = attention.step(blocks, places, shift, state)
    others += late
    far_keys, far_values, state = lax.optimization_barrier((far_keys, far_values, state))
    opposite = (far_keys, far_values, swap(far_keys), swap(far_values))
    sources = [x for pair in zip(mine, others) for x in pair] + list(opposite)
    keep, give, result = attention.last(
        late, opposite, shift, state, norm_gain[None, :], table, sources
    )

    keep, give, w_gate, w_up = lax.optimization_barrier((keep, give, w_gate, w_up))
    block = jnp.concatenate([keep, swap(give)], axis=0)
    from_left, from_right = block, block
    blocks_right, blocks_left = [block], []
    for step in range(1, half):
        from_left, from_right = go_right(from_left), go_left(from_right)
        if step == 1:
            w_gate = load(w_gate)
        elif step == 2:
            w_up = load(w_up)
        from_left, from_right, w_gate, w_up = lax.optimization_barrier(
            (from_left, from_right, w_gate, w_up)
        )
        blocks_right.append(from_left)
        blocks_left.append(from_right)
    far = [go_right(from_left[:CAP]), go_left(from_right[CAP:])]
    rows = gather(blocks_right + blocks_left + far)
    other_rows = swap(rows)
    hidden = hidden_call(me, other_rows, w_gate, w_up, hidden_call(me, rows, w_gate, w_up))

    sums = []
    for piece in range(PIECES):
        mine, theirs = down_call(hidden, downs[piece])
        sums.append(reduce_chip_rows(mine, swap(theirs), half, chips, go_right, go_left))
    mixed = None
    for piece, parts in enumerate(run_together(sums)):
        mixed = spread_call(parts, weighted, piece, PIECES, mixed)
    return (result, mixed)


def solution(mesh):
    placed = (
        P(("groups", "ctx"), None),
        P(("groups", "ctx"), None),
        P(("groups", "ctx"), None),
        P(),
        P(("groups", "ctx"), None),
        P(("groups", "ctx"), None),
        P(None, "ctx"),
        P(None, "ctx"),
        P("ctx", None),
    )
    return jax.shard_map(
        functools.partial(per_device, mesh.shape["ctx"] // 2),
        mesh=mesh,
        in_specs=placed,
        out_specs=(P(("groups", "ctx"), None), P(("groups", "ctx"), None)),
        check_vma=False,
    )
```

```python
import functools
import math

import jax
import jax.numpy as jnp
from jax import lax
from jax.experimental import pallas as pl
from jax.experimental.pallas import tpu as pltpu
from jax.sharding import PartitionSpec as P

HQ = 64
HK = 8
DH = 128
CAP = 16
GROUP = HQ // HK
WIDE = GROUP * DH
LOG_SCALE = math.log2(math.e) / math.sqrt(DH)
MASKED = -1e30
PIECES = 2
ATTEND_MIB = 14
SUM_LIMIT = 2.0**100
PARTS = 3
STACK = 4
MIB = 1 << 20


def in_hbm(x):
    return pltpu.with_memory_space_constraint(x, pltpu.HBM)


def ring_order(chips):
    return list(range(0, chips, 2)) + list(range(1, chips, 2))[::-1]


def permutations(chips):
    order = ring_order(chips)
    right, left = [], []
    for place in range(chips):
        here, there = order[place], order[(place + 1) % chips]
        for core in range(2):
            right.append((2 * here + core, 2 * there + core))
            left.append((2 * there + core, 2 * here + core))
    sibling = [(i, i ^ 1) for i in range(2 * chips)]
    return right, left, sibling


def chip_at(me, step, chips):
    chip = me // 2
    place = jnp.where(chip % 2 == 0, chip // 2, chips - 1 - chip // 2)
    source = (place - step + 2 * chips) % chips
    return jnp.where(source < chips // 2, 2 * source, 2 * (chips - 1 - source) + 1)


def head_rows(own, sib, first):
    pieces = []
    for h in range(first, first + STACK):
        columns = slice(h * DH, (h + 1) * DH)
        pieces += [own[:, columns], sib[:, columns]]
    return jnp.concatenate(pieces, axis=0)


def with_ones(values):
    return jnp.concatenate([values, jnp.ones_like(values)], axis=1)


def scores_of(queries, keys):
    return LOG_SCALE * lax.dot_general(
        queries, keys, (((1,), (1,)), ((), ())), preferred_element_type=jnp.float32
    )


def weights_of(scores, shift):
    return jnp.exp2(scores - jnp.concatenate([shift] * (scores.shape[1] // DH), axis=1))


def row_top(scores):
    return jnp.broadcast_to(jnp.max(scores, axis=1, keepdims=True), (scores.shape[0], DH))


def allowed_here(core, tokens):
    rows, columns = STACK * 2 * tokens, 2 * tokens

    def position(axis):
        place = lax.broadcasted_iota(jnp.int32, (rows, columns), axis) % (2 * tokens)
        return jnp.where(place < tokens, core * tokens + place, (1 - core) * tokens + place - tokens)

    return position(1) <= position(0)


def group_queries(queries, group):
    columns = pl.ds(pl.multiple_of(group * WIDE, WIDE), WIDE)
    return [ref[:, columns] for ref in queries]


def for_groups(body):
    def step(group, carry):
        body(group, pl.ds(pl.multiple_of(group * DH, DH), DH))
        return carry

    lax.fori_loop(0, HK // 2, step, 0)


def fold(queries, first, keys, values, shift):
    scores = scores_of(head_rows(*queries, first), keys)
    return jnp.dot(
        weights_of(scores, shift).astype(jnp.bfloat16), values, preferred_element_type=jnp.float32
    )


def block_of(ref, columns):
    tokens = ref.shape[0] // 2
    return ref[:tokens, columns], ref[tokens:, columns]


def join_blocks(refs, factors, columns):
    pairs = [block_of(ref, columns) for ref in refs]
    keys = jnp.concatenate([key for key, _ in pairs], axis=0)
    values = [with_ones(value) * factor for (_, value), factor in zip(pairs, factors)]
    return keys, jnp.concatenate(values, axis=0)


def factors_of(me, places, chips):
    flags = [chip_at(me, place, chips) < me // 2 for place in places]
    return flags, [jnp.where(flag, 1.0, 0.0).astype(jnp.bfloat16) for flag in flags]


def chunks(tokens):
    size = STACK * 2 * tokens
    return [(first, slice(first // STACK * size, (first // STACK + 1) * size)) for first in range(0, GROUP, STACK)]


def own_kernel(loads, me_ref, q_ref, sib_q_ref, own_ref, sib_ref, *refs):
    acc_ref, total_ref, shift_ref = refs[loads : loads + 3]
    copies = start_loads(loads, refs[:loads], refs[loads + 3 :])
    tokens = q_ref.shape[0]
    allowed = allowed_here(me_ref[0] % 2, tokens)

    def one_group(group, columns):
        keys, values = join_blocks((own_ref, sib_ref), (1, 1), columns)
        queries = group_queries((q_ref, sib_q_ref), group)
        for first, rows in chunks(tokens):
            scores = jnp.where(allowed, scores_of(head_rows(*queries, first), keys), MASKED)
            shift = row_top(scores)
            weights = weights_of(scores, shift).astype(jnp.bfloat16)
            update = jnp.dot(weights, values, preferred_element_type=jnp.float32)
            acc_ref[group, rows, :] = update[:, :DH]
            total_ref[group, rows, :] = update[:, DH:]
            shift_ref[group, rows, :] = shift

    for_groups(one_group)
    for copy in copies:
        copy.wait()


def start_loads(loads, sources, rest):
    copies = [
        pltpu.make_async_copy(source, target, sem)
        for source, target, sem in zip(sources, rest[:loads], rest[loads : 2 * loads])
    ]
    for copy in copies:
        copy.start()
    return copies


def step_kernel(chips, places, loads, me_ref, q_ref, sib_q_ref, *refs):
    count = len(places)
    blocks, shift_ref = refs[:count], refs[count]
    refs = refs[count + 3 :]
    acc_ref, total_ref = refs[loads : loads + 2]
    copies = start_loads(loads, refs[:loads], refs[loads + 2 :])
    tokens = q_ref.shape[0]
    flags, factors = factors_of(me_ref[0], places, chips)

    @pl.when(functools.reduce(jnp.logical_or, flags))
    def _():
        def one_group(group, columns):
            keys, values = join_blocks(blocks, factors, columns)
            queries = group_queries((q_ref, sib_q_ref), group)
            for first, rows in chunks(tokens):
                update = fold(queries, first, keys, values, shift_ref[group, rows, :])
                acc_ref[group, rows, :] += update[:, :DH]
                total_ref[group, rows, :] += update[:, DH:]

        for_groups(one_group)

    for copy in copies:
        copy.wait()


def divide(acc, total):
    inverse = pl.reciprocal(total, approx=True)
    inverse = inverse * (2.0 - total * inverse)
    return (acc * inverse).astype(jnp.bfloat16)


def put_heads(out_refs, rows_ref, tables, group, result):
    tokens = out_refs[0].shape[0]
    columns = pl.ds(pl.multiple_of(group * WIDE, WIDE), WIDE)
    for i, (out_ref, table) in enumerate(zip(out_refs, tables)):
        pieces = [
            result[(2 * h + i) * tokens : (2 * h + i + 1) * tokens] for h in range(GROUP)
        ]
        piece = jnp.concatenate(pieces, axis=1)
        out_ref[:, columns] = piece
        rows_ref[i * CAP : (i + 1) * CAP, columns] = jnp.dot(
            table[...], piece, preferred_element_type=jnp.float32
        )


def running_attention(chips, me, sources, q_refs, put, scratch, sem):
    keys_ref, values_ref, acc_ref, total_ref, top_ref = scratch
    tokens = q_refs[0].shape[0]

    def fetch(source, target):
        copy = pltpu.make_async_copy(source, target, sem)
        copy.start()
        copy.wait()

    def one_group(group, columns):
        queries = group_queries(q_refs, group)
        for i in range(chips):
            for j, block in enumerate(sources[2 * i : 2 * i + 2]):
                rows = pl.ds(j * tokens, tokens)
                fetch(block.at[pl.ds(0, tokens), columns], keys_ref.at[i, rows])
                fetch(block.at[pl.ds(tokens, tokens), columns], values_ref.at[i, rows])
        acc_ref[...] = jnp.zeros_like(acc_ref)
        total_ref[...] = jnp.zeros_like(total_ref)
        top_ref[...] = jnp.full_like(top_ref, 2 * MASKED)

        def one_chip(i, inner):
            place = jnp.where(i % 2 == 1, (i + 1) // 2, -(i // 2))
            chip = chip_at(me, place, chips)

            @pl.when(chip <= me // 2)
            def _():
                keys, values = keys_ref[i], with_ones(values_ref[i])
                barred = jnp.where(chip == me // 2, MASKED, 0.0)
                bias = jnp.where(allowed_here(me % 2, tokens), 0.0, barred)
                for first, rows in chunks(tokens):
                    scores = scores_of(head_rows(*queries, first), keys)
                    scores = jnp.where(bias < 0.0, MASKED, scores)
                    old = top_ref[rows, :]
                    top = jnp.maximum(old, row_top(scores))
                    factor = jnp.exp2(old - top)
                    weights = weights_of(scores, top).astype(jnp.bfloat16)
                    update = jnp.dot(weights, values, preferred_element_type=jnp.float32)
                    acc_ref[rows, :] = acc_ref[rows, :] * factor + update[:, :DH]
                    total_ref[rows, :] = total_ref[rows, :] * factor + update[:, DH:]
                    top_ref[rows, :] = top

            return inner

        lax.fori_loop(0, chips, one_chip, 0)
        put(group, divide(acc_ref[...], total_ref[...]))

    for_groups(one_group)


def last_kernel(chips, me_ref, q_ref, sib_q_ref, *refs):
    blocks, (shift_ref, acc_ref, total_ref, gain_ref) = refs[:2], refs[2:6]
    tables, sources = refs[6:8], refs[8 : 8 + 2 * chips]
    out_refs, picked_refs = refs[8 + 2 * chips : 10 + 2 * chips], refs[10 + 2 * chips : 12 + 2 * chips]
    rows_ref, worst_ref, sem, *scratch = refs[12 + 2 * chips :]
    q_refs = (q_ref, sib_q_ref)
    tokens, half_width = q_ref.shape
    me = me_ref[0]
    _, factors = factors_of(me, [chips // 2] * 2, chips)
    worst_ref[...] = jnp.zeros_like(worst_ref)

    def put(group, result):
        put_heads(out_refs, rows_ref, tables, group, result)

    def one_group(group, columns):
        keys, values = join_blocks(blocks, factors, columns)
        queries = group_queries(q_refs, group)
        results = []
        for first, rows in chunks(tokens):
            update = fold(queries, first, keys, values, shift_ref[group, rows, :])
            total = total_ref[group, rows, :] + update[:, DH:]
            worst_ref[...] = jnp.maximum(worst_ref[...], total)
            results.append(divide(acc_ref[group, rows, :] + update[:, :DH], total))
        put(group, jnp.concatenate(results, axis=0))

    for_groups(one_group)
    fits = jnp.max(worst_ref[...]) <= SUM_LIMIT

    @pl.when(jnp.logical_not(fits))
    def _():
        running_attention(chips, me, sources, q_refs, put, scratch, sem)

    columns = pl.ds(pl.multiple_of(me % 2 * half_width, half_width), half_width)
    gain = gain_ref[:, columns]
    for i, ref in enumerate(picked_refs):
        rows = rows_ref[i * CAP : (i + 1) * CAP, :]
        squares = jnp.broadcast_to(jnp.sum(rows * rows, axis=1, keepdims=True), (CAP, DH))
        upper = squares.astype(jnp.bfloat16)
        lower = (squares - upper.astype(jnp.float32)).astype(jnp.bfloat16)
        lane = lax.broadcasted_iota(jnp.int32, (CAP, DH), 1)
        both = jnp.where(lane < DH // 2, upper.astype(jnp.float32), lower.astype(jnp.float32))
        ref[:, :half_width] = (rows * gain).astype(jnp.bfloat16)
        ref[:, half_width:] = both.astype(jnp.bfloat16)


class Attention:
    def __init__(self, me, queries, chips):
        self.me, self.queries, self.chips = me, queries, chips
        self.tokens, self.width = queries[0].shape
        self.rows = 2 * GROUP * self.tokens
        self.state_shape = pltpu.VMEM((HK // 2, self.rows, DH), jnp.float32)

    def call(self, kernel, name, args, others, out_shape, out_others, scratch, aliases=None):
        vmem, anywhere = pl.BlockSpec(memory_space=pltpu.VMEM), pl.BlockSpec(memory_space=pl.ANY)
        return pl.pallas_call(
            kernel,
            in_specs=[pl.BlockSpec(memory_space=pltpu.SMEM)]
            + [vmem] * (2 + len(args))
            + [anywhere] * len(others),
            out_specs=[vmem] * len(out_shape) + [anywhere] * len(out_others),
            out_shape=[*out_shape, *out_others],
            scratch_shapes=scratch,
            input_output_aliases=aliases or {},
            compiler_params=pltpu.CompilerParams(vmem_limit_bytes=ATTEND_MIB * MIB),
            cost_estimate=pl.CostEstimate(
                flops=4 * self.tokens * self.width * self.tokens,
                bytes_accessed=4 * MIB,
                transcendentals=0,
            ),
            name=name,
        )(self.me, *self.queries, *args, *others)

    def own(self, own, sib, weights=()):
        loads = len(weights)
        results = self.call(
            functools.partial(own_kernel, loads),
            "attend_own",
            (own, sib),
            [in_hbm(x) for x in weights],
            [self.state_shape] * 3,
            [pltpu.VMEM(x.shape, x.dtype) for x in weights],
            [pltpu.SemaphoreType.DMA] * loads,
        )
        return list(results[:2]), results[2], results[3:]

    def step(self, blocks, places, shift, state, weights=()):
        count, loads = len(blocks), len(weights)
        results = self.call(
            functools.partial(step_kernel, self.chips, places, loads),
            "attend_step",
            (*blocks, shift, *state),
            [in_hbm(x) for x in weights],
            [self.state_shape] * 2,
            [pltpu.VMEM(x.shape, x.dtype) for x in weights],
            [pltpu.SemaphoreType.DMA] * loads,
            {count + 4: 0, count + 5: 1},
        )
        return list(results[:2]), results[2:]

    def last(self, blocks, shift, state, gain, tables, sources):
        out = pltpu.VMEM((self.tokens, self.width), jnp.bfloat16)
        picked = pltpu.VMEM((CAP, self.width + DH), jnp.bfloat16)
        kept = pltpu.VMEM((self.chips, 2 * self.tokens, DH), jnp.bfloat16)
        sums = pltpu.VMEM((self.rows, DH), jnp.float32)
        return self.call(
            functools.partial(last_kernel, self.chips),
            "attend_last",
            (*blocks, shift, *state, gain, *tables),
            sources,
            [out, out, picked, picked],
            [],
            [
                pltpu.VMEM((2 * CAP, self.width), jnp.float32),
                pltpu.VMEM((STACK * 2 * self.tokens, DH), jnp.float32),
                pltpu.SemaphoreType.DMA,
                kept,
                kept,
                sums,
                sums,
                sums,
            ],
        )


def halves_kernel(me_ref, *refs):
    count = len(refs) - 3
    sources, (keep_ref, give_ref, sems) = refs[:count], refs[count:]
    rows, width = sources[0].shape
    core = me_ref[0] % 2
    copies = []
    for side, target in ((core, keep_ref), (1 - core, give_ref)):
        columns = pl.ds(pl.multiple_of(side * (width // 2), width // 2), width // 2)
        for i, source in enumerate(sources):
            copies.append((source.at[:, columns], target.at[pl.ds(i * rows, rows)]))
    copies = [pltpu.make_async_copy(*ends, sems.at[i]) for i, ends in enumerate(copies)]
    for copy in copies:
        copy.start()
    for copy in copies:
        copy.wait()


def halves(me, *arrays):
    rows, width = arrays[0].shape
    anywhere = pl.BlockSpec(memory_space=pl.ANY)
    out = pltpu.VMEM((len(arrays) * rows, width // 2), arrays[0].dtype)
    return pl.pallas_call(
        halves_kernel,
        in_specs=[pl.BlockSpec(memory_space=pltpu.SMEM)] + [anywhere] * len(arrays),
        out_specs=[anywhere] * 2,
        out_shape=[out, out],
        scratch_shapes=[pltpu.SemaphoreType.DMA((2 * len(arrays),))],
        compiler_params=pltpu.CompilerParams(vmem_limit_bytes=MIB),
        name="halves",
    )(me, *(in_hbm(x) for x in arrays))


def beside_kernel(me_ref, keep_ref, other_ref, out_ref, sems):
    width = keep_ref.shape[1]
    core = me_ref[0] % 2
    copies = []
    for i, (side, source) in enumerate(((core, keep_ref), (1 - core, other_ref))):
        columns = pl.ds(pl.multiple_of(side * width, width), width)
        copies.append(pltpu.make_async_copy(source, out_ref.at[:, columns], sems.at[i]))
    for copy in copies:
        copy.start()
    for copy in copies:
        copy.wait()


def beside(me, keep, other):
    rows, width = keep.shape
    anywhere = pl.BlockSpec(memory_space=pl.ANY)
    return pl.pallas_call(
        beside_kernel,
        in_specs=[pl.BlockSpec(memory_space=pltpu.SMEM)] + [anywhere] * 2,
        out_specs=anywhere,
        out_shape=jax.ShapeDtypeStruct((rows, 2 * width), keep.dtype),
        scratch_shapes=[pltpu.SemaphoreType.DMA((2,))],
        compiler_params=pltpu.CompilerParams(vmem_limit_bytes=MIB),
        name="beside",
    )(me, keep, other)


def gather_kernel(*refs):
    for j, ref in enumerate(refs[:-1]):
        refs[-1][j * CAP : (j + 1) * CAP] = ref[...]


def gather(blocks):
    vmem = pl.BlockSpec(memory_space=pltpu.VMEM)
    return pl.pallas_call(
        gather_kernel,
        in_specs=[vmem] * len(blocks),
        out_specs=vmem,
        out_shape=pltpu.VMEM((CAP * len(blocks), blocks[0].shape[1]), jnp.bfloat16),
        compiler_params=pltpu.CompilerParams(vmem_limit_bytes=4 * MIB),
        name="gather",
    )(*blocks)


def hidden_kernel(second, me_ref, rows_ref, gate_ref, up_ref, *refs):
    half = rows_ref.shape[1] - DH
    middle = rows_ref.shape[0] // 2
    depth = min(1024, half)
    if second:
        own_ref, gate_in, up_in, source_ref, out_ref, target_ref, gate_sum, up_sum, sem = refs
        gate_sum[...] = gate_in[...]
        up_sum[...] = up_in[...]
    else:
        source_ref, gate_sum, up_sum, target_ref, sem = refs
        gate_sum[...] = jnp.zeros_like(gate_sum)
        up_sum[...] = jnp.zeros_like(up_sum)
    side = 1 - me_ref[0] % 2 if second else me_ref[0] % 2
    columns = pl.ds(target_ref.shape[1] if second else 0, target_ref.shape[1])
    load = pltpu.make_async_copy(source_ref.at[:, columns], target_ref, sem)
    load.start()

    def one_part(step, carry):
        part = rows_ref[:, pl.ds(pl.multiple_of(step * depth, depth), depth)]
        if second:
            part = jnp.concatenate([part[middle:], part[:middle]], axis=0)
        place = pl.ds(pl.multiple_of(side * half + step * depth, depth), depth)
        gate_sum[...] += jnp.dot(part, gate_ref[place, :], preferred_element_type=jnp.float32)
        up_sum[...] += jnp.dot(part, up_ref[place, :], preferred_element_type=jnp.float32)
        return carry

    lax.fori_loop(0, half // depth, one_part, 0)
    if second:
        squares = own_ref[:, half:].astype(jnp.float32)
        others = rows_ref[:, half:].astype(jnp.float32)
        squares += jnp.concatenate([others[middle:], others[:middle]], axis=0)
        squares = squares[:, :1] + squares[:, DH // 2 : DH // 2 + 1]
        factor = lax.rsqrt(squares / (2 * half) + 1e-05)
        gate = gate_sum[...] * factor
        out_ref[...] = (gate / (1.0 + jnp.exp(-gate)) * (up_sum[...] * factor)).astype(jnp.bfloat16)
    load.wait()


def hidden_call(me, rows, w_gate, w_up, w_down, own=None, sums=()):
    count, half = rows.shape[0], rows.shape[1] - DH
    units, width = w_down.shape
    vmem, anywhere = pl.BlockSpec(memory_space=pltpu.VMEM), pl.BlockSpec(memory_space=pl.ANY)
    sum_shape = pltpu.VMEM((count, units), jnp.float32)
    second = own is not None
    more = (own, *sums) if second else ()
    outs = [pltpu.VMEM((count, units), jnp.bfloat16)] if second else [sum_shape] * 2
    return pl.pallas_call(
        functools.partial(hidden_kernel, second),
        in_specs=[pl.BlockSpec(memory_space=pltpu.SMEM)] + [vmem] * (3 + len(more)) + [anywhere],
        out_specs=[vmem] * len(outs) + [anywhere],
        out_shape=outs + [pltpu.VMEM((units, width // 2), w_down.dtype)],
        scratch_shapes=[sum_shape] * (2 if second else 0) + [pltpu.SemaphoreType.DMA],
        compiler_params=pltpu.CompilerParams(vmem_limit_bytes=12 * MIB),
        cost_estimate=pl.CostEstimate(
            flops=4 * count * half * units,
            bytes_accessed=4 * half * units + 2 * count * half,
            transcendentals=count * units,
        ),
        name="hidden",
    )(me, rows, w_gate, w_up, *more, in_hbm(w_down))


def down_kernel(hidden_ref, down_ref, own_ref, sib_ref):
    middle, width = own_ref.shape
    cols = min(1024, width)

    def one_part(step, carry):
        columns = pl.ds(pl.multiple_of(step * cols, cols), cols)
        part = jnp.dot(hidden_ref[...], down_ref[:, columns], preferred_element_type=jnp.float32)
        part = part.astype(jnp.bfloat16)
        own_ref[:, columns] = part[:middle]
        sib_ref[:, columns] = part[middle:]
        return carry

    lax.fori_loop(0, width // cols, one_part, 0)


def down_call(hidden, w_down):
    rows, units = hidden.shape
    width = w_down.shape[1]
    vmem = pl.BlockSpec(memory_space=pltpu.VMEM)
    return pl.pallas_call(
        down_kernel,
        in_specs=[vmem] * 2,
        out_specs=[vmem] * 2,
        out_shape=[pltpu.VMEM((rows // 2, width), jnp.bfloat16)] * 2,
        compiler_params=pltpu.CompilerParams(vmem_limit_bytes=16 * MIB),
        cost_estimate=pl.CostEstimate(
            flops=2 * rows * width * units,
            bytes_accessed=2 * width * units + 2 * rows * width,
            transcendentals=0,
        ),
        name="down",
    )(hidden, w_down)


def spread_kernel(a_ref, b_ref, c_ref, d_ref, table_ref, *rest):
    out_ref = rest[-1]
    total = a_ref[...].astype(jnp.float32) + b_ref[...].astype(jnp.float32)
    total += c_ref[...].astype(jnp.float32) + d_ref[...].astype(jnp.float32)
    total = total.astype(jnp.bfloat16)
    out_ref[...] = lax.dot_general(
        table_ref[...],
        jnp.concatenate([total] * PARTS, axis=0),
        (((0,), (0,)), ((), ())),
        preferred_element_type=jnp.float32,
    ).astype(jnp.bfloat16)


def spread_call(parts, table, piece, pieces, previous):
    tokens = table.shape[1]
    piece_width = parts[0].shape[1]
    cols = min(2048, piece_width)
    steps = piece_width // cols
    earlier = [] if previous is None else [previous]
    return pl.pallas_call(
        spread_kernel,
        grid=(steps,),
        in_specs=[pl.BlockSpec((CAP, cols), lambda i: (0, i))] * 4
        + [pl.BlockSpec((PARTS * CAP, tokens), lambda i: (0, 0))]
        + [pl.BlockSpec(memory_space=pl.ANY)] * len(earlier),
        out_specs=pl.BlockSpec((tokens, cols), lambda i: (0, piece * steps + i)),
        out_shape=jax.ShapeDtypeStruct((tokens, piece_width * pieces), jnp.bfloat16),
        input_output_aliases={5: 0} if earlier else {},
        compiler_params=pltpu.CompilerParams(
            dimension_semantics=("arbitrary",), vmem_limit_bytes=16 * MIB
        ),
        name="spread",
    )(*parts, table, *earlier)


def reduce_chip_rows(mine, other, half, chips, go_right, go_left):
    middle = mine.shape[1] // 2

    def block(index):
        rows = slice(index * CAP, (index + 1) * CAP)
        return mine[rows].astype(jnp.float32) + other[rows].astype(jnp.float32)

    far = block(chips - 1).astype(jnp.bfloat16)
    ahead, back = far[:, :middle], far[:, middle:]
    for distance in range(half - 1, -1, -1):
        ahead, back = lax.optimization_barrier((ahead, back))
        to_right, to_left = go_right(ahead), go_left(back)
        yield
        if distance == 0:
            break
        ahead, back = block(half - 1 + distance), block(distance)
        if distance == half - 1:
            ahead = jnp.concatenate(
                [ahead[:, :middle] + to_right.astype(jnp.float32), ahead[:, middle:]], axis=1
            )
            back = jnp.concatenate(
                [back[:, :middle], back[:, middle:] + to_left.astype(jnp.float32)], axis=1
            )
        else:
            ahead = ahead + to_right.astype(jnp.float32)
            back = back + to_left.astype(jnp.float32)
        ahead, back = ahead.astype(jnp.bfloat16), back.astype(jnp.bfloat16)
    return (mine, other, to_right, to_left)


def run_together(generators):
    results = [None] * len(generators)
    active = list(range(len(generators)))
    while active:
        for i in list(active):
            try:
                next(generators[i])
            except StopIteration as stop:
                results[i] = stop.value
                active.remove(i)
    return results


def per_device(chips, queries, keys, values, norm_gain, expert_ids, gates, w_gate, w_up, w_down):
    right, left, sibling = permutations(chips)
    half = chips // 2
    go_right = lambda x: lax.ppermute(x, "ctx", right)
    go_left = lambda x: lax.ppermute(x, "ctx", left)
    swap = lambda x: lax.ppermute(x, "ctx", sibling)

    me = lax.axis_index("ctx").astype(jnp.int32).reshape(1)
    tokens = queries.shape[0]
    hits = (expert_ids == 0).astype(jnp.float32)
    chosen = jnp.sum(hits, axis=1)
    position = jnp.arange(tokens, dtype=jnp.int32)
    before = (position[None, :] < position[:, None]).astype(jnp.float32)
    slot = jnp.sum(before * chosen[None, :], axis=1).astype(jnp.int32)
    table = jnp.logical_and(
        slot[None, :] == jnp.arange(CAP, dtype=jnp.int32)[:, None], chosen[None, :] > 0
    ).astype(jnp.float32)
    rest = jnp.sum(gates * hits, axis=1)
    weights = []
    for _ in range(PARTS):
        part = lax.reduce_precision(rest, 8, 7)
        weights.append(table * part[None, :])
        rest = rest - part
    weighted = jnp.concatenate(weights, axis=0).astype(jnp.bfloat16)
    table = table.astype(jnp.bfloat16)

    own, give = halves(me, keys, values)
    sib = swap(give)
    from_left, from_right = [go_right(own)], [go_left(own)]
    q_own, q_give = halves(me, queries)
    from_left.append(go_right(sib))
    from_right.append(go_left(sib))
    q_sib = swap(q_give)
    sib_table = swap(table)
    attention = Attention(me, (q_own, q_sib), chips)
    state, shift, (w_gate,) = attention.own(own, sib, (w_gate,))
    sources = [own, sib]
    for step in range(1, half):
        from_left, from_right, state = lax.optimization_barrier((from_left, from_right, state))
        blocks, places = from_left + from_right, [step, step, -step, -step]
        sources += blocks
        if step < half - 1:
            from_left, from_right = [go_right(x) for x in from_left], [go_left(x) for x in from_right]
        else:
            opposite = [go_right(from_left[0]), go_left(from_right[1])]
        if step == 2:
            state, (w_up,) = attention.step(blocks, places, shift, state, (w_up,))
        else:
            state, _ = attention.step(blocks, places, shift, state)
    opposite, state = lax.optimization_barrier((opposite, state))
    sources += opposite
    mine, theirs, *picked = attention.last(
        opposite, shift, state, norm_gain[None, :], (table, sib_table), sources
    )

    from_left, from_right = list(picked), list(picked)
    blocks_right, blocks_left = [picked], []
    result = None
    for step in range(1, half):
        from_left, from_right = [go_right(x) for x in from_left], [go_left(x) for x in from_right]
        from_left, from_right, mine, theirs = lax.optimization_barrier(
            (from_left, from_right, mine, theirs)
        )
        if step == 1:
            theirs = swap(theirs)
        elif step == 2:
            theirs = beside(me, mine, theirs)
        blocks_right.append(from_left)
        blocks_left.append(from_right)
    result = theirs
    far = [go_right(from_left[0]), go_left(from_right[1])]
    blocks = blocks_right + blocks_left + [far]
    rows = gather([own for own, _ in blocks] + [sib for _, sib in blocks])
    *first, down_low = hidden_call(me, rows, w_gate, w_up, w_down)
    hidden, down_high = hidden_call(me, swap(rows), w_gate, w_up, w_down, rows, first)
    downs = [down_low, down_high]

    sums = []
    for piece in range(PIECES):
        mine, theirs = down_call(hidden, downs[piece])
        sums.append(reduce_chip_rows(mine, swap(theirs), half, chips, go_right, go_left))
    mixed = None
    for piece, parts in enumerate(run_together(sums)):
        mixed = spread_call(parts, weighted, piece, PIECES, mixed)
    return (result, mixed)


def solution(mesh):
    placed = (
        P(("groups", "ctx"), None),
        P(("groups", "ctx"), None),
        P(("groups", "ctx"), None),
        P(),
        P(("groups", "ctx"), None),
        P(("groups", "ctx"), None),
        P(None, "ctx"),
        P(None, "ctx"),
        P("ctx", None),
    )
    return jax.shard_map(
        functools.partial(per_device, mesh.shape["ctx"] // 2),
        mesh=mesh,
        in_specs=placed,
        out_specs=(P(("groups", "ctx"), None), P(("groups", "ctx"), None)),
        check_vma=False,
    )
```

```python
import functools
import math

import jax
import jax.numpy as jnp
from jax import lax
from jax.experimental import pallas as pl
from jax.experimental.pallas import tpu as pltpu
from jax.sharding import PartitionSpec as P

HQ = 64
HK = 8
DH = 128
CAP = 16
GROUP = HQ // HK
WIDE = GROUP * DH
LOG_SCALE = math.log2(math.e) / math.sqrt(DH)
MASKED = -1e30
PIECES = 2
ATTEND_MIB = 11
SMALL = pl.CostEstimate(flops=1, bytes_accessed=1, transcendentals=0)
SUM_LIMIT = 2.0**100
PARTS = 3
STACK = 4
MIB = 1 << 20


def in_hbm(x):
    return pltpu.with_memory_space_constraint(x, pltpu.HBM)


def ring_order(chips):
    return list(range(0, chips, 2)) + list(range(1, chips, 2))[::-1]


def permutations(chips):
    order = ring_order(chips)
    right, left = [], []
    for place in range(chips):
        here, there = order[place], order[(place + 1) % chips]
        for core in range(2):
            right.append((2 * here + core, 2 * there + core))
            left.append((2 * there + core, 2 * here + core))
    sibling = [(i, i ^ 1) for i in range(2 * chips)]
    return right, left, sibling


def chip_at(me, step, chips):
    chip = me // 2
    place = jnp.where(chip % 2 == 0, chip // 2, chips - 1 - chip // 2)
    source = (place - step + 2 * chips) % chips
    return jnp.where(source < chips // 2, 2 * source, 2 * (chips - 1 - source) + 1)


def head_rows(own, sib, first):
    pieces = []
    for h in range(first, first + STACK):
        columns = slice(h * DH, (h + 1) * DH)
        pieces += [own[:, columns], sib[:, columns]]
    return jnp.concatenate(pieces, axis=0)


def with_ones(values):
    return jnp.concatenate([values, jnp.ones_like(values)], axis=1)


def scores_of(queries, keys):
    return LOG_SCALE * lax.dot_general(
        queries, keys, (((1,), (1,)), ((), ())), preferred_element_type=jnp.float32
    )


def weights_of(scores, shift):
    return jnp.exp2(scores - jnp.concatenate([shift] * (scores.shape[1] // DH), axis=1))


def row_top(scores):
    return jnp.broadcast_to(jnp.max(scores, axis=1, keepdims=True), (scores.shape[0], DH))


def allowed_here(core, tokens):
    rows, columns = STACK * 2 * tokens, 2 * tokens

    def position(axis):
        place = lax.broadcasted_iota(jnp.int32, (rows, columns), axis) % (2 * tokens)
        return jnp.where(place < tokens, core * tokens + place, (1 - core) * tokens + place - tokens)

    return position(1) <= position(0)


def group_queries(queries, group):
    columns = pl.ds(pl.multiple_of(group * WIDE, WIDE), WIDE)
    return [ref[:, columns] for ref in queries]


def for_groups(body):
    def step(group, carry):
        body(group, pl.ds(pl.multiple_of(group * DH, DH), DH))
        return carry

    lax.fori_loop(0, HK // 2, step, 0)


def fold(queries, first, keys, values, shift):
    scores = scores_of(head_rows(*queries, first), keys)
    return jnp.dot(
        weights_of(scores, shift).astype(jnp.bfloat16), values, preferred_element_type=jnp.float32
    )


def block_of(ref, columns):
    tokens = ref.shape[0] // 2
    return ref[:tokens, columns], ref[tokens:, columns]


def join_blocks(refs, factors, columns):
    pairs = [block_of(ref, columns) for ref in refs]
    keys = jnp.concatenate([key for key, _ in pairs], axis=0)
    values = [with_ones(value) * factor for (_, value), factor in zip(pairs, factors)]
    return keys, jnp.concatenate(values, axis=0)


def factors_of(me, places, chips):
    flags = [chip_at(me, place, chips) < me // 2 for place in places]
    return flags, [jnp.where(flag, 1.0, 0.0).astype(jnp.bfloat16) for flag in flags]


def chunks(tokens):
    size = STACK * 2 * tokens
    return [(first, slice(first // STACK * size, (first // STACK + 1) * size)) for first in range(0, GROUP, STACK)]


def own_kernel(loads, me_ref, q_ref, sib_q_ref, own_ref, sib_ref, *refs):
    acc_ref, total_ref, shift_ref = refs[loads : loads + 3]
    copies = start_loads(loads, refs[:loads], refs[loads + 3 :])
    tokens = q_ref.shape[0]
    allowed = allowed_here(me_ref[0] % 2, tokens)

    def one_group(group, columns):
        keys, values = join_blocks((own_ref, sib_ref), (1, 1), columns)
        queries = group_queries((q_ref, sib_q_ref), group)
        for first, rows in chunks(tokens):
            scores = jnp.where(allowed, scores_of(head_rows(*queries, first), keys), MASKED)
            shift = row_top(scores)
            weights = weights_of(scores, shift).astype(jnp.bfloat16)
            update = jnp.dot(weights, values, preferred_element_type=jnp.float32)
            acc_ref[group, rows, :] = update[:, :DH]
            total_ref[group, rows, :] = update[:, DH:]
            shift_ref[group, rows, :] = shift

    for_groups(one_group)
    for copy in copies:
        copy.wait()


def start_loads(loads, sources, rest):
    copies = [
        pltpu.make_async_copy(source, target, sem)
        for source, target, sem in zip(sources, rest[:loads], rest[loads : 2 * loads])
    ]
    for copy in copies:
        copy.start()
    return copies


def step_kernel(chips, places, loads, me_ref, q_ref, sib_q_ref, *refs):
    count = len(places)
    blocks, shift_ref = refs[:count], refs[count]
    refs = refs[count + 3 :]
    acc_ref, total_ref = refs[loads : loads + 2]
    copies = start_loads(loads, refs[:loads], refs[loads + 2 :])
    tokens = q_ref.shape[0]
    flags, factors = factors_of(me_ref[0], places, chips)

    @pl.when(functools.reduce(jnp.logical_or, flags))
    def _():
        def one_group(group, columns):
            keys, values = join_blocks(blocks, factors, columns)
            queries = group_queries((q_ref, sib_q_ref), group)
            for first, rows in chunks(tokens):
                update = fold(queries, first, keys, values, shift_ref[group, rows, :])
                acc_ref[group, rows, :] += update[:, :DH]
                total_ref[group, rows, :] += update[:, DH:]

        for_groups(one_group)

    for copy in copies:
        copy.wait()


def divide(acc, total):
    inverse = pl.reciprocal(total, approx=True)
    inverse = inverse * (2.0 - total * inverse)
    return (acc * inverse).astype(jnp.bfloat16)


def put_heads(out_refs, rows_ref, tables, group, result):
    tokens = out_refs[0].shape[0]
    columns = pl.ds(pl.multiple_of(group * WIDE, WIDE), WIDE)
    for i, (out_ref, table) in enumerate(zip(out_refs, tables)):
        pieces = [
            result[(2 * h + i) * tokens : (2 * h + i + 1) * tokens] for h in range(GROUP)
        ]
        piece = jnp.concatenate(pieces, axis=1)
        out_ref[:, columns] = piece
        rows_ref[i * CAP : (i + 1) * CAP, columns] = jnp.dot(
            table[...], piece, preferred_element_type=jnp.float32
        )


def running_attention(chips, me, sources, q_refs, put, scratch, sem):
    keys_ref, values_ref, acc_ref, total_ref, top_ref = scratch
    tokens = q_refs[0].shape[0]

    def fetch(source, target):
        copy = pltpu.make_async_copy(source, target, sem)
        copy.start()
        copy.wait()

    def one_group(group, columns):
        queries = group_queries(q_refs, group)
        for i in range(chips):
            for j, block in enumerate(sources[2 * i : 2 * i + 2]):
                rows = pl.ds(j * tokens, tokens)
                fetch(block.at[pl.ds(0, tokens), columns], keys_ref.at[i, rows])
                fetch(block.at[pl.ds(tokens, tokens), columns], values_ref.at[i, rows])
        acc_ref[...] = jnp.zeros_like(acc_ref)
        total_ref[...] = jnp.zeros_like(total_ref)
        top_ref[...] = jnp.full_like(top_ref, 2 * MASKED)

        def one_chip(i, inner):
            place = jnp.where(i % 2 == 1, (i + 1) // 2, -(i // 2))
            chip = chip_at(me, place, chips)

            @pl.when(chip <= me // 2)
            def _():
                keys, values = keys_ref[i], with_ones(values_ref[i])
                barred = jnp.where(chip == me // 2, MASKED, 0.0)
                bias = jnp.where(allowed_here(me % 2, tokens), 0.0, barred)
                for first, rows in chunks(tokens):
                    scores = scores_of(head_rows(*queries, first), keys)
                    scores = jnp.where(bias < 0.0, MASKED, scores)
                    old = top_ref[rows, :]
                    top = jnp.maximum(old, row_top(scores))
                    factor = jnp.exp2(old - top)
                    weights = weights_of(scores, top).astype(jnp.bfloat16)
                    update = jnp.dot(weights, values, preferred_element_type=jnp.float32)
                    acc_ref[rows, :] = acc_ref[rows, :] * factor + update[:, :DH]
                    total_ref[rows, :] = total_ref[rows, :] * factor + update[:, DH:]
                    top_ref[rows, :] = top

            return inner

        lax.fori_loop(0, chips, one_chip, 0)
        put(group, divide(acc_ref[...], total_ref[...]))

    for_groups(one_group)


def last_kernel(chips, me_ref, q_ref, sib_q_ref, *refs):
    blocks, (shift_ref, acc_ref, total_ref, gain_ref) = refs[:2], refs[2:6]
    tables, sources = refs[6:8], refs[8 : 8 + 2 * chips]
    refs = refs[8 + 2 * chips :]
    out_refs, picked_ref = refs[:2], refs[2]
    rows_ref, worst_ref, sem, *scratch = refs[3:]
    q_refs = (q_ref, sib_q_ref)
    tokens, half_width = q_ref.shape
    me = me_ref[0]
    _, factors = factors_of(me, [chips // 2] * 2, chips)
    worst_ref[...] = jnp.zeros_like(worst_ref)

    def put(group, result):
        put_heads(out_refs, rows_ref, tables, group, result)

    def one_group(group, columns):
        keys, values = join_blocks(blocks, factors, columns)
        queries = group_queries(q_refs, group)
        results = []
        for first, rows in chunks(tokens):
            update = fold(queries, first, keys, values, shift_ref[group, rows, :])
            total = total_ref[group, rows, :] + update[:, DH:]
            worst_ref[...] = jnp.maximum(worst_ref[...], total)
            results.append(divide(acc_ref[group, rows, :] + update[:, :DH], total))
        put(group, jnp.concatenate(results, axis=0))

    for_groups(one_group)
    fits = jnp.max(worst_ref[...]) <= SUM_LIMIT

    @pl.when(jnp.logical_not(fits))
    def _():
        running_attention(chips, me, sources, q_refs, put, scratch, sem)

    columns = pl.ds(pl.multiple_of(me % 2 * half_width, half_width), half_width)
    rows = rows_ref[...]
    squares = jnp.broadcast_to(jnp.sum(rows * rows, axis=1, keepdims=True), (2 * CAP, DH))
    upper = squares.astype(jnp.bfloat16).astype(jnp.float32)
    lower = (squares - upper).astype(jnp.bfloat16).astype(jnp.float32)
    lane = lax.broadcasted_iota(jnp.int32, squares.shape, 1)
    picked_ref[:, :half_width] = (rows * gain_ref[:, columns]).astype(jnp.bfloat16)
    picked_ref[:, half_width:] = jnp.where(lane < DH // 2, upper, lower).astype(jnp.bfloat16)


class Attention:
    def __init__(self, me, queries, chips):
        self.me, self.queries, self.chips = me, queries, chips
        self.tokens, self.width = queries[0].shape
        self.rows = 2 * GROUP * self.tokens
        self.state_shape = pltpu.VMEM((HK // 2, self.rows, DH), jnp.float32)

    def call(self, kernel, name, args, others, out_shape, out_others, scratch, aliases=None):
        vmem, anywhere = pl.BlockSpec(memory_space=pltpu.VMEM), pl.BlockSpec(memory_space=pl.ANY)
        return pl.pallas_call(
            kernel,
            in_specs=[pl.BlockSpec(memory_space=pltpu.SMEM)]
            + [vmem] * (2 + len(args))
            + [anywhere] * len(others),
            out_specs=[vmem] * len(out_shape) + [anywhere] * len(out_others),
            out_shape=[*out_shape, *out_others],
            scratch_shapes=scratch,
            input_output_aliases=aliases or {},
            compiler_params=pltpu.CompilerParams(vmem_limit_bytes=ATTEND_MIB * MIB),
            cost_estimate=SMALL,
            name=name,
        )(self.me, *self.queries, *args, *others)

    def own(self, own, sib, weights=()):
        loads = len(weights)
        results = self.call(
            functools.partial(own_kernel, loads),
            "attend_own",
            (own, sib),
            [in_hbm(x) for x in weights],
            [self.state_shape] * 3,
            [pltpu.VMEM(x.shape, x.dtype) for x in weights],
            [pltpu.SemaphoreType.DMA] * loads,
        )
        return list(results[:2]), results[2], results[3:]

    def step(self, blocks, places, shift, state, weights=()):
        count, loads = len(blocks), len(weights)
        results = self.call(
            functools.partial(step_kernel, self.chips, places, loads),
            "attend_step",
            (*blocks, shift, *state),
            [in_hbm(x) for x in weights],
            [self.state_shape] * 2,
            [pltpu.VMEM(x.shape, x.dtype) for x in weights],
            [pltpu.SemaphoreType.DMA] * loads,
            {count + 4: 0, count + 5: 1},
        )
        return list(results[:2]), results[2:]

    def last(self, blocks, shift, state, gain, tables, sources):
        out = pltpu.VMEM((self.tokens, self.width), jnp.bfloat16)
        picked = pltpu.VMEM((2 * CAP, self.width + DH), jnp.bfloat16)
        kept = pltpu.VMEM((self.chips, 2 * self.tokens, DH), jnp.bfloat16)
        sums = pltpu.VMEM((self.rows, DH), jnp.float32)
        return self.call(
            functools.partial(last_kernel, self.chips),
            "attend_last",
            (*blocks, shift, *state, gain, *tables),
            sources,
            [out, out, picked],
            [],
            [
                pltpu.VMEM((2 * CAP, self.width), jnp.float32),
                pltpu.VMEM((STACK * 2 * self.tokens, DH), jnp.float32),
                pltpu.SemaphoreType.DMA,
                kept,
                kept,
                sums,
                sums,
                sums,
            ],
        )


def halves_kernel(stacks, me_ref, *refs):
    count = sum(stacks)
    sources, outs, sems = list(refs[:count]), refs[count:-1], refs[-1]
    core = me_ref[0] % 2
    copies = []
    for size, keep_ref, give_ref in zip(stacks, outs[::2], outs[1::2]):
        for i in range(size):
            source = sources.pop(0)
            rows, width = source.shape
            for side, target in ((core, keep_ref), (1 - core, give_ref)):
                columns = pl.ds(pl.multiple_of(side * (width // 2), width // 2), width // 2)
                copies.append((source.at[:, columns], target.at[pl.ds(i * rows, rows)]))
    copies = [pltpu.make_async_copy(*ends, sems.at[i]) for i, ends in enumerate(copies)]
    for copy in copies:
        copy.start()
    for copy in copies:
        copy.wait()


def halves(me, *stacks):
    anywhere = pl.BlockSpec(memory_space=pl.ANY)
    arrays = [x for stack in stacks for x in stack]
    outs = []
    for stack in stacks:
        rows, width = stack[0].shape
        outs += [pltpu.VMEM((len(stack) * rows, width // 2), stack[0].dtype)] * 2
    return pl.pallas_call(
        functools.partial(halves_kernel, [len(stack) for stack in stacks]),
        in_specs=[pl.BlockSpec(memory_space=pltpu.SMEM)] + [anywhere] * len(arrays),
        out_specs=[anywhere] * len(outs),
        out_shape=outs,
        scratch_shapes=[pltpu.SemaphoreType.DMA((2 * len(arrays),))],
        compiler_params=pltpu.CompilerParams(vmem_limit_bytes=MIB),
        cost_estimate=SMALL,
        name="halves",
    )(me, *(in_hbm(x) for x in arrays))


def beside_kernel(me_ref, keep_ref, other_ref, out_ref, sems):
    width = keep_ref.shape[1]
    core = me_ref[0] % 2
    copies = []
    for i, (side, source) in enumerate(((core, keep_ref), (1 - core, other_ref))):
        columns = pl.ds(pl.multiple_of(side * width, width), width)
        copies.append(pltpu.make_async_copy(source, out_ref.at[:, columns], sems.at[i]))
    for copy in copies:
        copy.start()
    for copy in copies:
        copy.wait()


def beside(me, keep, other):
    rows, width = keep.shape
    anywhere = pl.BlockSpec(memory_space=pl.ANY)
    return pl.pallas_call(
        beside_kernel,
        in_specs=[pl.BlockSpec(memory_space=pltpu.SMEM)] + [anywhere] * 2,
        out_specs=anywhere,
        out_shape=jax.ShapeDtypeStruct((rows, 2 * width), keep.dtype),
        scratch_shapes=[pltpu.SemaphoreType.DMA((2,))],
        compiler_params=pltpu.CompilerParams(vmem_limit_bytes=MIB),
        cost_estimate=SMALL,
        name="beside",
    )(me, keep, other)


def load_kernel(source_ref, target_ref, sem):
    copy = pltpu.make_async_copy(source_ref, target_ref, sem)
    copy.start()
    copy.wait()


def load(x):
    return pl.pallas_call(
        load_kernel,
        in_specs=[pl.BlockSpec(memory_space=pl.ANY)],
        out_specs=pl.BlockSpec(memory_space=pl.ANY),
        out_shape=pltpu.VMEM(x.shape, x.dtype),
        scratch_shapes=[pltpu.SemaphoreType.DMA],
        compiler_params=pltpu.CompilerParams(vmem_limit_bytes=MIB),
        cost_estimate=SMALL,
        name="load",
    )(in_hbm(x))


def gather_kernel(*refs):
    blocks, out_ref = refs[:-1], refs[-1]
    middle = out_ref.shape[0] // 2
    parts = [(ref[:CAP], ref[CAP:]) for ref in blocks[:-2]] + [(blocks[-2][...], blocks[-1][...])]
    for j, (mine, other) in enumerate(parts):
        out_ref[j * CAP : (j + 1) * CAP] = mine
        out_ref[middle + j * CAP : middle + (j + 1) * CAP] = other


def gather(blocks):
    vmem = pl.BlockSpec(memory_space=pltpu.VMEM)
    return pl.pallas_call(
        gather_kernel,
        in_specs=[vmem] * len(blocks),
        out_specs=vmem,
        out_shape=pltpu.VMEM((2 * CAP * (len(blocks) - 1), blocks[0].shape[1]), jnp.bfloat16),
        compiler_params=pltpu.CompilerParams(vmem_limit_bytes=4 * MIB),
        cost_estimate=SMALL,
        name="gather",
    )(*blocks)


def hidden_kernel(second, me_ref, rows_ref, gate_ref, up_ref, *refs):
    half = rows_ref.shape[1] - DH
    middle = rows_ref.shape[0] // 2
    depth = min(1024, half)
    if second:
        own_ref, gate_in, up_in, source_ref, out_ref, target_ref, gate_sum, up_sum, sem = refs
        gate_sum[...] = gate_in[...]
        up_sum[...] = up_in[...]
    else:
        source_ref, gate_sum, up_sum, target_ref, sem = refs
        gate_sum[...] = jnp.zeros_like(gate_sum)
        up_sum[...] = jnp.zeros_like(up_sum)
    side = 1 - me_ref[0] % 2 if second else me_ref[0] % 2
    columns = pl.ds(target_ref.shape[1] if second else 0, target_ref.shape[1])
    load = pltpu.make_async_copy(source_ref.at[:, columns], target_ref, sem)
    load.start()

    def one_part(step, carry):
        part = rows_ref[:, pl.ds(pl.multiple_of(step * depth, depth), depth)]
        if second:
            part = jnp.concatenate([part[middle:], part[:middle]], axis=0)
        place = pl.ds(pl.multiple_of(side * half + step * depth, depth), depth)
        gate_sum[...] += jnp.dot(part, gate_ref[place, :], preferred_element_type=jnp.float32)
        up_sum[...] += jnp.dot(part, up_ref[place, :], preferred_element_type=jnp.float32)
        return carry

    lax.fori_loop(0, half // depth, one_part, 0)
    if second:
        squares = own_ref[:, half:].astype(jnp.float32)
        others = rows_ref[:, half:].astype(jnp.float32)
        squares += jnp.concatenate([others[middle:], others[:middle]], axis=0)
        squares = squares[:, :1] + squares[:, DH // 2 : DH // 2 + 1]
        factor = lax.rsqrt(squares / (2 * half) + 1e-05)
        gate = gate_sum[...] * factor
        out_ref[...] = (gate / (1.0 + jnp.exp(-gate)) * (up_sum[...] * factor)).astype(jnp.bfloat16)
    load.wait()


def hidden_call(me, rows, w_gate, w_up, w_down, own=None, sums=()):
    count, half = rows.shape[0], rows.shape[1] - DH
    units, width = w_down.shape
    vmem, anywhere = pl.BlockSpec(memory_space=pltpu.VMEM), pl.BlockSpec(memory_space=pl.ANY)
    sum_shape = pltpu.VMEM((count, units), jnp.float32)
    second = own is not None
    more = (own, *sums) if second else ()
    outs = [pltpu.VMEM((count, units), jnp.bfloat16)] if second else [sum_shape] * 2
    return pl.pallas_call(
        functools.partial(hidden_kernel, second),
        in_specs=[pl.BlockSpec(memory_space=pltpu.SMEM)] + [vmem] * (3 + len(more)) + [anywhere],
        out_specs=[vmem] * len(outs) + [anywhere],
        out_shape=outs + [pltpu.VMEM((units, width // 2), w_down.dtype)],
        scratch_shapes=[sum_shape] * (2 if second else 0) + [pltpu.SemaphoreType.DMA],
        compiler_params=pltpu.CompilerParams(vmem_limit_bytes=8 * MIB),
        cost_estimate=pl.CostEstimate(
            flops=4 * count * half * units,
            bytes_accessed=4 * half * units + 2 * count * half,
            transcendentals=count * units,
        ),
        name="hidden",
    )(me, rows, w_gate, w_up, *more, in_hbm(w_down))


def down_kernel(hidden_ref, down_ref, own_ref, sib_ref):
    middle, width = own_ref.shape
    cols = min(1024, width)

    def one_part(step, carry):
        columns = pl.ds(pl.multiple_of(step * cols, cols), cols)
        part = jnp.dot(hidden_ref[...], down_ref[:, columns], preferred_element_type=jnp.float32)
        part = part.astype(jnp.bfloat16)
        own_ref[:, columns] = part[:middle]
        sib_ref[:, columns] = part[middle:]
        return carry

    lax.fori_loop(0, width // cols, one_part, 0)


def down_call(hidden, w_down):
    rows, units = hidden.shape
    width = w_down.shape[1]
    vmem = pl.BlockSpec(memory_space=pltpu.VMEM)
    return pl.pallas_call(
        down_kernel,
        in_specs=[vmem] * 2,
        out_specs=[vmem] * 2,
        out_shape=[pltpu.VMEM((rows // 2, width), jnp.bfloat16)] * 2,
        compiler_params=pltpu.CompilerParams(vmem_limit_bytes=8 * MIB),
        cost_estimate=pl.CostEstimate(
            flops=2 * rows * width * units,
            bytes_accessed=2 * width * units + 2 * rows * width,
            transcendentals=0,
        ),
        name="down",
    )(hidden, w_down)


def spread_kernel(a_ref, b_ref, c_ref, d_ref, table_ref, *rest):
    out_ref = rest[-1]
    total = a_ref[...].astype(jnp.float32) + b_ref[...].astype(jnp.float32)
    total += c_ref[...].astype(jnp.float32) + d_ref[...].astype(jnp.float32)
    total = total.astype(jnp.bfloat16)
    out_ref[...] = lax.dot_general(
        table_ref[...],
        jnp.concatenate([total] * PARTS, axis=0),
        (((0,), (0,)), ((), ())),
        preferred_element_type=jnp.float32,
    ).astype(jnp.bfloat16)


def spread_call(parts, table, piece, pieces, previous):
    tokens = table.shape[1]
    piece_width = parts[0].shape[1]
    cols = min(2048, piece_width)
    steps = piece_width // cols
    earlier = [] if previous is None else [previous]
    return pl.pallas_call(
        spread_kernel,
        grid=(steps,),
        in_specs=[pl.BlockSpec((CAP, cols), lambda i: (0, i))] * 4
        + [pl.BlockSpec((PARTS * CAP, tokens), lambda i: (0, 0))]
        + [pl.BlockSpec(memory_space=pl.ANY)] * len(earlier),
        out_specs=pl.BlockSpec((tokens, cols), lambda i: (0, piece * steps + i)),
        out_shape=jax.ShapeDtypeStruct((tokens, piece_width * pieces), jnp.bfloat16),
        input_output_aliases={5: 0} if earlier else {},
        compiler_params=pltpu.CompilerParams(
            dimension_semantics=("arbitrary",), vmem_limit_bytes=16 * MIB
        ),
        name="spread",
    )(*parts, table, *earlier)


def reduce_chip_rows(mine, other, half, chips, go_right, go_left):
    middle = mine.shape[1] // 2

    def block(index):
        rows = slice(index * CAP, (index + 1) * CAP)
        return mine[rows].astype(jnp.float32) + other[rows].astype(jnp.float32)

    far = block(chips - 1).astype(jnp.bfloat16)
    ahead, back = far[:, :middle], far[:, middle:]
    for distance in range(half - 1, -1, -1):
        ahead, back = lax.optimization_barrier((ahead, back))
        to_right, to_left = go_right(ahead), go_left(back)
        yield
        if distance == 0:
            break
        ahead, back = block(half - 1 + distance), block(distance)
        if distance == half - 1:
            ahead = jnp.concatenate(
                [ahead[:, :middle] + to_right.astype(jnp.float32), ahead[:, middle:]], axis=1
            )
            back = jnp.concatenate(
                [back[:, :middle], back[:, middle:] + to_left.astype(jnp.float32)], axis=1
            )
        else:
            ahead = ahead + to_right.astype(jnp.float32)
            back = back + to_left.astype(jnp.float32)
        ahead, back = ahead.astype(jnp.bfloat16), back.astype(jnp.bfloat16)
    return (mine, other, to_right, to_left)


def run_together(generators):
    results = [None] * len(generators)
    active = list(range(len(generators)))
    while active:
        for i in list(active):
            try:
                next(generators[i])
            except StopIteration as stop:
                results[i] = stop.value
                active.remove(i)
    return results


def per_device(chips, queries, keys, values, norm_gain, expert_ids, gates, w_gate, w_up, w_down):
    right, left, sibling = permutations(chips)
    half = chips // 2
    go_right = lambda x: lax.ppermute(x, "ctx", right)
    go_left = lambda x: lax.ppermute(x, "ctx", left)
    swap = lambda x: lax.ppermute(x, "ctx", sibling)

    me = lax.axis_index("ctx").astype(jnp.int32).reshape(1)
    tokens = queries.shape[0]
    hits = (expert_ids == 0).astype(jnp.float32)
    chosen = jnp.sum(hits, axis=1)
    position = jnp.arange(tokens, dtype=jnp.int32)
    before = (position[None, :] < position[:, None]).astype(jnp.float32)
    slot = jnp.sum(before * chosen[None, :], axis=1).astype(jnp.int32)
    table = jnp.logical_and(
        slot[None, :] == jnp.arange(CAP, dtype=jnp.int32)[:, None], chosen[None, :] > 0
    ).astype(jnp.float32)
    rest = jnp.sum(gates * hits, axis=1)
    weights = []
    for _ in range(PARTS):
        part = lax.reduce_precision(rest, 8, 7)
        weights.append(table * part[None, :])
        rest = rest - part
    weighted = jnp.concatenate(weights, axis=0).astype(jnp.bfloat16)
    table = table.astype(jnp.bfloat16)

    own, give, q_own, q_give = halves(me, (keys, values), (queries,))
    across_right, across_left = [
        lax.ppermute(give, "ctx", [(i, j ^ 1) for i, j in pairs]) for pairs in (right, left)
    ]
    chains = [(go_right(own), go_left(own)), (across_right, across_left)]
    sib, q_sib = swap(give), swap(q_give)
    sib_table = swap(table)
    attention = Attention(me, (q_own, q_sib), chips)
    state, shift, _ = attention.own(own, sib)
    sources = [own, sib]
    for step in range(1, half):
        *chains[0], state = lax.optimization_barrier((*chains[0], state))
        chains[1], _, state = lax.optimization_barrier((chains[1], chains[0], state))
        blocks = [chain[side] for side in range(2) for chain in chains]
        sources += blocks
        if step < half - 1:
            chains = [(go_right(chain[0]), go_left(chain[1])) for chain in chains]
        else:
            opposite = [go_right(chains[0][0]), go_left(chains[1][1])]
        state, _ = attention.step(blocks, [step, step, -step, -step], shift, state)
    opposite, state = lax.optimization_barrier((opposite, state))
    sources += opposite
    mine, theirs, picked = attention.last(
        opposite, shift, state, norm_gain[None, :], (table, sib_table), sources
    )

    picked, w_gate = lax.optimization_barrier((picked, w_gate))
    from_left, from_right, blocks_right, blocks_left = picked, picked, [picked], []
    for step in range(1, half):
        from_left, from_right = go_right(from_left), go_left(from_right)
        if step == 1:
            w_gate = load(w_gate)
        elif step == 2:
            w_up = load(w_up)
            theirs = swap(theirs)
        from_left, from_right, w_gate, w_up, theirs = lax.optimization_barrier(
            (from_left, from_right, w_gate, w_up, theirs)
        )
        blocks_right.append(from_left)
        blocks_left.append(from_right)
    far = [go_right(from_left[:CAP]), go_left(from_right[CAP:])]
    result = beside(me, mine, theirs)
    far, result = lax.optimization_barrier((far, result))
    rows = gather(blocks_right + blocks_left + far)
    *first, down_low = hidden_call(me, rows, w_gate, w_up, w_down)
    hidden, down_high = hidden_call(me, swap(rows), w_gate, w_up, w_down, rows, first)
    downs = [down_low, down_high]

    sums = []
    for piece in range(PIECES):
        mine, theirs = down_call(hidden, downs[piece])
        sums.append(reduce_chip_rows(mine, swap(theirs), half, chips, go_right, go_left))
    mixed = None
    for piece, parts in enumerate(run_together(sums)):
        mixed = spread_call(parts, weighted, piece, PIECES, mixed)
    return (result, mixed)


def solution(mesh):
    placed = (
        P(("groups", "ctx"), None),
        P(("groups", "ctx"), None),
        P(("groups", "ctx"), None),
        P(),
        P(("groups", "ctx"), None),
        P(("groups", "ctx"), None),
        P(None, "ctx"),
        P(None, "ctx"),
        P("ctx", None),
    )
    return jax.shard_map(
        functools.partial(per_device, mesh.shape["ctx"] // 2),
        mesh=mesh,
        in_specs=placed,
        out_specs=(P(("groups", "ctx"), None), P(("groups", "ctx"), None)),
        check_vma=False,
    )
```

```python
import functools
import math

import jax
import jax.numpy as jnp
from jax import lax
from jax.experimental import pallas as pl
from jax.experimental.pallas import tpu as pltpu
from jax.sharding import PartitionSpec as P

HQ = 64
HK = 8
DH = 128
CAP = 16
GROUP = HQ // HK
WIDE = GROUP * DH
LOG_SCALE = math.log2(math.e) / math.sqrt(DH)
MASKED = -1e30
PIECES = 2
ATTEND_MIB = 11
SMALL = pl.CostEstimate(flops=1, bytes_accessed=1, transcendentals=0)
SUM_LIMIT = 2.0**100
PARTS = 3
STACK = 4
MIB = 1 << 20


def in_hbm(x):
    return pltpu.with_memory_space_constraint(x, pltpu.HBM)


def ring_order(chips):
    return list(range(0, chips, 2)) + list(range(1, chips, 2))[::-1]


def permutations(chips):
    order = ring_order(chips)
    right, left = [], []
    for place in range(chips):
        here, there = order[place], order[(place + 1) % chips]
        for core in range(2):
            right.append((2 * here + core, 2 * there + core))
            left.append((2 * there + core, 2 * here + core))
    sibling = [(i, i ^ 1) for i in range(2 * chips)]
    return right, left, sibling


def chip_at(me, step, chips):
    chip = me // 2
    place = jnp.where(chip % 2 == 0, chip // 2, chips - 1 - chip // 2)
    source = (place - step + 2 * chips) % chips
    return jnp.where(source < chips // 2, 2 * source, 2 * (chips - 1 - source) + 1)


def head_rows(own, sib, first):
    pieces = []
    for h in range(first, first + STACK):
        columns = slice(h * DH, (h + 1) * DH)
        pieces += [own[:, columns], sib[:, columns]]
    return jnp.concatenate(pieces, axis=0)


def with_ones(values):
    return jnp.concatenate([values, jnp.ones_like(values)], axis=1)


def scores_of(queries, keys):
    return LOG_SCALE * lax.dot_general(
        queries, keys, (((1,), (1,)), ((), ())), preferred_element_type=jnp.float32
    )


def weights_of(scores, shift):
    return jnp.exp2(scores - jnp.concatenate([shift] * (scores.shape[1] // DH), axis=1))


def row_top(scores):
    return jnp.broadcast_to(jnp.max(scores, axis=1, keepdims=True), (scores.shape[0], DH))


def allowed_here(core, tokens):
    rows, columns = STACK * 2 * tokens, 2 * tokens

    def position(axis):
        place = lax.broadcasted_iota(jnp.int32, (rows, columns), axis) % (2 * tokens)
        return jnp.where(place < tokens, core * tokens + place, (1 - core) * tokens + place - tokens)

    return position(1) <= position(0)


def group_queries(queries, group):
    columns = pl.ds(pl.multiple_of(group * WIDE, WIDE), WIDE)
    return [ref[:, columns] for ref in queries]


def for_groups(body):
    def step(group, carry):
        body(group, pl.ds(pl.multiple_of(group * DH, DH), DH))
        return carry

    lax.fori_loop(0, HK // 2, step, 0)


def fold(queries, first, keys, values, shift):
    scores = scores_of(head_rows(*queries, first), keys)
    return jnp.dot(
        weights_of(scores, shift).astype(jnp.bfloat16), values, preferred_element_type=jnp.float32
    )


def block_of(ref, columns):
    if isinstance(ref, tuple):
        return ref[0][:, columns], ref[1][:, columns]
    tokens = ref.shape[0] // 2
    return ref[:tokens, columns], ref[tokens:, columns]


def join_blocks(refs, factors, columns):
    pairs = [block_of(ref, columns) for ref in refs]
    keys = jnp.concatenate([key for key, _ in pairs], axis=0)
    values = [with_ones(value) * factor for (_, value), factor in zip(pairs, factors)]
    return keys, jnp.concatenate(values, axis=0)


def factors_of(me, places, chips):
    flags = [chip_at(me, place, chips) < me // 2 for place in places]
    return flags, [jnp.where(flag, 1.0, 0.0).astype(jnp.bfloat16) for flag in flags]


def chunks(tokens):
    size = STACK * 2 * tokens
    return [(first, slice(first // STACK * size, (first // STACK + 1) * size)) for first in range(0, GROUP, STACK)]


def own_kernel(loads, me_ref, q_ref, sib_q_ref, own_ref, sib_ref, *refs):
    acc_ref, total_ref, shift_ref = refs[loads : loads + 3]
    copies = start_loads(loads, refs[:loads], refs[loads + 3 :])
    tokens = q_ref.shape[0]
    allowed = allowed_here(me_ref[0] % 2, tokens)

    def one_group(group, columns):
        keys, values = join_blocks((own_ref, sib_ref), (1, 1), columns)
        queries = group_queries((q_ref, sib_q_ref), group)
        for first, rows in chunks(tokens):
            scores = jnp.where(allowed, scores_of(head_rows(*queries, first), keys), MASKED)
            shift = row_top(scores)
            weights = weights_of(scores, shift).astype(jnp.bfloat16)
            update = jnp.dot(weights, values, preferred_element_type=jnp.float32)
            acc_ref[group, rows, :] = update[:, :DH]
            total_ref[group, rows, :] = update[:, DH:]
            shift_ref[group, rows, :] = shift

    for_groups(one_group)
    for copy in copies:
        copy.wait()


def start_loads(loads, sources, rest):
    copies = [
        pltpu.make_async_copy(source, target, sem)
        for source, target, sem in zip(sources, rest[:loads], rest[loads : 2 * loads])
    ]
    for copy in copies:
        copy.start()
    return copies


def step_kernel(chips, places, loads, me_ref, q_ref, sib_q_ref, *refs):
    count = len(places)
    blocks, shift_ref = refs[:count], refs[count]
    refs = refs[count + 3 :]
    acc_ref, total_ref = refs[loads : loads + 2]
    copies = start_loads(loads, refs[:loads], refs[loads + 2 :])
    tokens = q_ref.shape[0]
    flags, factors = factors_of(me_ref[0], places, chips)

    @pl.when(functools.reduce(jnp.logical_or, flags))
    def _():
        def one_group(group, columns):
            keys, values = join_blocks(blocks, factors, columns)
            queries = group_queries((q_ref, sib_q_ref), group)
            for first, rows in chunks(tokens):
                update = fold(queries, first, keys, values, shift_ref[group, rows, :])
                acc_ref[group, rows, :] += update[:, :DH]
                total_ref[group, rows, :] += update[:, DH:]

        for_groups(one_group)

    for copy in copies:
        copy.wait()


def divide(acc, total):
    inverse = pl.reciprocal(total, approx=True)
    inverse = inverse * (2.0 - total * inverse)
    return (acc * inverse).astype(jnp.bfloat16)


def put_heads(out_refs, rows_ref, tables, group, result):
    tokens = out_refs[0].shape[0]
    columns = pl.ds(pl.multiple_of(group * WIDE, WIDE), WIDE)
    for i, (out_ref, table) in enumerate(zip(out_refs, tables)):
        pieces = [
            result[(2 * h + i) * tokens : (2 * h + i + 1) * tokens] for h in range(GROUP)
        ]
        piece = jnp.concatenate(pieces, axis=1)
        out_ref[:, columns] = piece
        rows_ref[i * CAP : (i + 1) * CAP, columns] = jnp.dot(
            table[...], piece, preferred_element_type=jnp.float32
        )


def running_attention(chips, me, sources, q_refs, put, scratch, sem):
    keys_ref, values_ref, acc_ref, total_ref, top_ref = scratch
    tokens = q_refs[0].shape[0]

    def fetch(source, target):
        copy = pltpu.make_async_copy(source, target, sem)
        copy.start()
        copy.wait()

    def one_group(group, columns):
        queries = group_queries(q_refs, group)
        for i in range(chips - 1):
            for j, block in enumerate(sources[2 * i : 2 * i + 2]):
                rows = pl.ds(j * tokens, tokens)
                fetch(block.at[pl.ds(0, tokens), columns], keys_ref.at[i, rows])
                fetch(block.at[pl.ds(tokens, tokens), columns], values_ref.at[i, rows])
        for j, block in enumerate(sources[2 * chips - 2 :]):
            target = (values_ref if j % 2 else keys_ref).at[chips - 1, pl.ds(j // 2 * tokens, tokens)]
            fetch(block.at[:, columns], target)
        acc_ref[...] = jnp.zeros_like(acc_ref)
        total_ref[...] = jnp.zeros_like(total_ref)
        top_ref[...] = jnp.full_like(top_ref, 2 * MASKED)

        def one_chip(i, inner):
            place = jnp.where(i % 2 == 1, (i + 1) // 2, -(i // 2))
            chip = chip_at(me, place, chips)

            @pl.when(chip <= me // 2)
            def _():
                keys, values = keys_ref[i], with_ones(values_ref[i])
                barred = jnp.where(chip == me // 2, MASKED, 0.0)
                bias = jnp.where(allowed_here(me % 2, tokens), 0.0, barred)
                for first, rows in chunks(tokens):
                    scores = scores_of(head_rows(*queries, first), keys)
                    scores = jnp.where(bias < 0.0, MASKED, scores)
                    old = top_ref[rows, :]
                    top = jnp.maximum(old, row_top(scores))
                    factor = jnp.exp2(old - top)
                    weights = weights_of(scores, top).astype(jnp.bfloat16)
                    update = jnp.dot(weights, values, preferred_element_type=jnp.float32)
                    acc_ref[rows, :] = acc_ref[rows, :] * factor + update[:, :DH]
                    total_ref[rows, :] = total_ref[rows, :] * factor + update[:, DH:]
                    top_ref[rows, :] = top

            return inner

        lax.fori_loop(0, chips, one_chip, 0)
        put(group, divide(acc_ref[...], total_ref[...]))

    for_groups(one_group)


def last_kernel(chips, me_ref, q_ref, sib_q_ref, *refs):
    blocks, (shift_ref, acc_ref, total_ref, gain_ref) = (refs[:2], refs[2:4]), refs[4:8]
    tables, sources = refs[8:10], refs[10 : 12 + 2 * chips]
    refs = refs[12 + 2 * chips :]
    out_refs, picked_refs = refs[:2], refs[2:4]
    rows_ref, worst_ref, sem, *scratch = refs[4:]
    q_refs = (q_ref, sib_q_ref)
    tokens, half_width = q_ref.shape
    me = me_ref[0]
    _, factors = factors_of(me, [chips // 2] * 2, chips)
    worst_ref[...] = jnp.zeros_like(worst_ref)

    def put(group, result):
        put_heads(out_refs, rows_ref, tables, group, result)

    def one_group(group, columns):
        keys, values = join_blocks(blocks, factors, columns)
        queries = group_queries(q_refs, group)
        results = []
        for first, rows in chunks(tokens):
            update = fold(queries, first, keys, values, shift_ref[group, rows, :])
            total = total_ref[group, rows, :] + update[:, DH:]
            worst_ref[...] = jnp.maximum(worst_ref[...], total)
            results.append(divide(acc_ref[group, rows, :] + update[:, :DH], total))
        put(group, jnp.concatenate(results, axis=0))

    for_groups(one_group)
    fits = jnp.max(worst_ref[...]) <= SUM_LIMIT

    @pl.when(jnp.logical_not(fits))
    def _():
        running_attention(chips, me, sources, q_refs, put, scratch, sem)

    columns = pl.ds(pl.multiple_of(me % 2 * half_width, half_width), half_width)
    rows = rows_ref[...]
    squares = jnp.broadcast_to(jnp.sum(rows * rows, axis=1, keepdims=True), (2 * CAP, DH))
    upper = squares.astype(jnp.bfloat16).astype(jnp.float32)
    lower = (squares - upper).astype(jnp.bfloat16).astype(jnp.float32)
    lane = lax.broadcasted_iota(jnp.int32, squares.shape, 1)
    rows = (rows * gain_ref[:, columns]).astype(jnp.bfloat16)
    squares = jnp.where(lane < DH // 2, upper, lower).astype(jnp.bfloat16)
    for i, ref in enumerate(picked_refs):
        ref[:, :half_width] = rows[i * CAP : (i + 1) * CAP]
        ref[:, half_width:] = squares[i * CAP : (i + 1) * CAP]


class Attention:
    def __init__(self, me, queries, chips):
        self.me, self.queries, self.chips = me, queries, chips
        self.tokens, self.width = queries[0].shape
        self.rows = 2 * GROUP * self.tokens
        self.state_shape = pltpu.VMEM((HK // 2, self.rows, DH), jnp.float32)

    def call(self, kernel, name, args, others, out_shape, out_others, scratch, aliases=None):
        vmem, anywhere = pl.BlockSpec(memory_space=pltpu.VMEM), pl.BlockSpec(memory_space=pl.ANY)
        return pl.pallas_call(
            kernel,
            in_specs=[pl.BlockSpec(memory_space=pltpu.SMEM)]
            + [vmem] * (2 + len(args))
            + [anywhere] * len(others),
            out_specs=[vmem] * len(out_shape) + [anywhere] * len(out_others),
            out_shape=[*out_shape, *out_others],
            scratch_shapes=scratch,
            input_output_aliases=aliases or {},
            compiler_params=pltpu.CompilerParams(vmem_limit_bytes=ATTEND_MIB * MIB),
            cost_estimate=SMALL,
            name=name,
        )(self.me, *self.queries, *args, *others)

    def own(self, own, sib, weights=()):
        loads = len(weights)
        results = self.call(
            functools.partial(own_kernel, loads),
            "attend_own",
            (own, sib),
            [in_hbm(x) for x in weights],
            [self.state_shape] * 3,
            [pltpu.VMEM(x.shape, x.dtype) for x in weights],
            [pltpu.SemaphoreType.DMA] * loads,
        )
        return list(results[:2]), results[2], results[3:]

    def step(self, blocks, places, shift, state, weights=()):
        count, loads = len(blocks), len(weights)
        results = self.call(
            functools.partial(step_kernel, self.chips, places, loads),
            "attend_step",
            (*blocks, shift, *state),
            [in_hbm(x) for x in weights],
            [self.state_shape] * 2,
            [pltpu.VMEM(x.shape, x.dtype) for x in weights],
            [pltpu.SemaphoreType.DMA] * loads,
            {count + 4: 0, count + 5: 1},
        )
        return list(results[:2]), results[2:]

    def last(self, blocks, shift, state, gain, tables, sources):
        out = pltpu.VMEM((self.tokens, self.width), jnp.bfloat16)
        picked = pltpu.VMEM((CAP, self.width + DH), jnp.bfloat16)
        kept = pltpu.VMEM((self.chips, 2 * self.tokens, DH), jnp.bfloat16)
        sums = pltpu.VMEM((self.rows, DH), jnp.float32)
        return self.call(
            functools.partial(last_kernel, self.chips),
            "attend_last",
            (*blocks, shift, *state, gain, *tables),
            sources,
            [out, out, picked, picked],
            [],
            [
                pltpu.VMEM((2 * CAP, self.width), jnp.float32),
                pltpu.VMEM((STACK * 2 * self.tokens, DH), jnp.float32),
                pltpu.SemaphoreType.DMA,
                kept,
                kept,
                sums,
                sums,
                sums,
            ],
        )


def halves_kernel(stacks, me_ref, *refs):
    count = sum(stacks)
    sources, outs, sems = list(refs[:count]), refs[count:-1], refs[-1]
    core = me_ref[0] % 2
    copies = []
    for size, keep_ref, give_ref in zip(stacks, outs[::2], outs[1::2]):
        for i in range(size):
            source = sources.pop(0)
            rows, width = source.shape
            for side, target in ((core, keep_ref), (1 - core, give_ref)):
                columns = pl.ds(pl.multiple_of(side * (width // 2), width // 2), width // 2)
                copies.append((source.at[:, columns], target.at[pl.ds(i * rows, rows)]))
    copies = [pltpu.make_async_copy(*ends, sems.at[i]) for i, ends in enumerate(copies)]
    for copy in copies:
        copy.start()
    for copy in copies:
        copy.wait()


def halves(me, *stacks):
    anywhere = pl.BlockSpec(memory_space=pl.ANY)
    arrays = [x for stack in stacks for x in stack]
    outs = []
    for stack in stacks:
        rows, width = stack[0].shape
        outs += [pltpu.VMEM((len(stack) * rows, width // 2), stack[0].dtype)] * 2
    return pl.pallas_call(
        functools.partial(halves_kernel, [len(stack) for stack in stacks]),
        in_specs=[pl.BlockSpec(memory_space=pltpu.SMEM)] + [anywhere] * len(arrays),
        out_specs=[anywhere] * len(outs),
        out_shape=outs,
        scratch_shapes=[pltpu.SemaphoreType.DMA((2 * len(arrays),))],
        compiler_params=pltpu.CompilerParams(vmem_limit_bytes=MIB),
        cost_estimate=SMALL,
        name="halves",
    )(me, *(in_hbm(x) for x in arrays))


def beside_kernel(me_ref, keep_ref, other_ref, out_ref, sems):
    width = keep_ref.shape[1]
    core = me_ref[0] % 2
    copies = []
    for i, (side, source) in enumerate(((core, keep_ref), (1 - core, other_ref))):
        columns = pl.ds(pl.multiple_of(side * width, width), width)
        copies.append(pltpu.make_async_copy(source, out_ref.at[:, columns], sems.at[i]))
    for copy in copies:
        copy.start()
    for copy in copies:
        copy.wait()


def beside(me, keep, other):
    rows, width = keep.shape
    anywhere = pl.BlockSpec(memory_space=pl.ANY)
    return pl.pallas_call(
        beside_kernel,
        in_specs=[pl.BlockSpec(memory_space=pltpu.SMEM)] + [anywhere] * 2,
        out_specs=anywhere,
        out_shape=jax.ShapeDtypeStruct((rows, 2 * width), keep.dtype),
        scratch_shapes=[pltpu.SemaphoreType.DMA((2,))],
        compiler_params=pltpu.CompilerParams(vmem_limit_bytes=MIB),
        cost_estimate=SMALL,
        name="beside",
    )(me, keep, other)


def load_kernel(me_ref, source_ref, target_ref, sem):
    copy = pltpu.make_async_copy(half_rows(me_ref, source_ref, False), target_ref, sem)
    copy.start()
    copy.wait()


def half_rows(me_ref, ref, sibling):
    half = ref.shape[0] // 2
    side = 1 - me_ref[0] % 2 if sibling else me_ref[0] % 2
    return ref.at[pl.ds(pl.multiple_of(side * half, half), half), :]


def load(me, x):
    return pl.pallas_call(
        load_kernel,
        in_specs=[pl.BlockSpec(memory_space=pltpu.SMEM), pl.BlockSpec(memory_space=pl.ANY)],
        out_specs=pl.BlockSpec(memory_space=pl.ANY),
        out_shape=pltpu.VMEM((x.shape[0] // 2, x.shape[1]), x.dtype),
        scratch_shapes=[pltpu.SemaphoreType.DMA],
        compiler_params=pltpu.CompilerParams(vmem_limit_bytes=MIB),
        cost_estimate=SMALL,
        name="load",
    )(me, in_hbm(x))


def place_kernel(spots, *refs):
    blocks, out_ref = refs[: len(spots)], refs[-1]
    for (row, column), ref in zip(spots, blocks):
        out_ref[row : row + ref.shape[0], column : column + ref.shape[1]] = ref[...]


def place(blocks, spots, shape, rows=None):
    vmem = pl.BlockSpec(memory_space=pltpu.VMEM)
    earlier = [] if rows is None else [rows]
    return pl.pallas_call(
        functools.partial(place_kernel, spots),
        in_specs=[vmem] * (len(blocks) + len(earlier)),
        out_specs=vmem,
        out_shape=pltpu.VMEM(shape, jnp.bfloat16),
        input_output_aliases={len(blocks): 0} if earlier else {},
        compiler_params=pltpu.CompilerParams(vmem_limit_bytes=4 * MIB),
        cost_estimate=SMALL,
        name="place",
    )(*blocks, *earlier)


def contract(rows_ref, gate_ref, up_ref, gate_sum, up_sum, order):
    half = gate_ref.shape[0]
    depth = min(1024, half)

    def one_part(step, carry):
        columns = pl.ds(pl.multiple_of(step * depth, depth), depth)
        part = order(rows_ref[:, columns])
        gate_sum[...] += jnp.dot(part, gate_ref[columns, :], preferred_element_type=jnp.float32)
        up_sum[...] += jnp.dot(part, up_ref[columns, :], preferred_element_type=jnp.float32)
        return carry

    lax.fori_loop(0, half // depth, one_part, 0)


def first_kernel(me_ref, rows_ref, gate_ref, up_ref, *refs):
    sources, (gate_sum, up_sum), targets, sems = refs[:2], refs[2:4], refs[4:6], refs[6]
    copies = [
        pltpu.make_async_copy(half_rows(me_ref, source, True), target, sems.at[i])
        for i, (source, target) in enumerate(zip(sources, targets))
    ]
    for copy in copies:
        copy.start()
    gate_sum[...] = jnp.zeros_like(gate_sum)
    up_sum[...] = jnp.zeros_like(up_sum)
    contract(rows_ref, gate_ref, up_ref, gate_sum, up_sum, lambda part: part)
    for copy in copies:
        copy.wait()


def second_kernel(rows_ref, gate_ref, up_ref, own_ref, gate_in, up_in, source_ref, out_ref, *refs):
    targets, (gate_sum, up_sum, sems) = refs[:PIECES], refs[PIECES:]
    piece = targets[0].shape[1]
    copies = [
        pltpu.make_async_copy(source_ref.at[:, pl.ds(i * piece, piece)], target, sems.at[i])
        for i, target in enumerate(targets)
    ]
    for copy in copies:
        copy.start()
    middle, half = rows_ref.shape[0] // 2, gate_ref.shape[0]

    def order(part):
        return jnp.concatenate([part[middle:], part[:middle]], axis=0)

    gate_sum[...] = gate_in[...]
    up_sum[...] = up_in[...]
    contract(rows_ref, gate_ref, up_ref, gate_sum, up_sum, order)
    squares = own_ref[:, half:].astype(jnp.float32) + order(rows_ref[:, half:].astype(jnp.float32))
    squares = squares[:, :1] + squares[:, DH // 2 : DH // 2 + 1]
    factor = lax.rsqrt(squares / (2 * half) + 1e-05)
    gate = gate_sum[...] * factor
    out_ref[...] = (gate / (1.0 + jnp.exp(-gate)) * (up_sum[...] * factor)).astype(jnp.bfloat16)
    for copy in copies:
        copy.wait()


def hidden_calls(me, rows, other_rows, loaded, w_gate, w_up, w_down):
    count, units, width = rows.shape[0], w_down.shape[0], w_down.shape[1]
    vmem, anywhere = pl.BlockSpec(memory_space=pltpu.VMEM), pl.BlockSpec(memory_space=pl.ANY)
    sums = [pltpu.VMEM((count, units), jnp.float32)] * 2
    params = pltpu.CompilerParams(vmem_limit_bytes=8 * MIB)
    cost = pl.CostEstimate(
        flops=2 * count * width * units, bytes_accessed=2 * width * units, transcendentals=count * units
    )
    *partial, gate, up = pl.pallas_call(
        first_kernel,
        in_specs=[pl.BlockSpec(memory_space=pltpu.SMEM)] + [vmem] * 3 + [anywhere] * 2,
        out_specs=[vmem] * 2 + [anywhere] * 2,
        out_shape=sums + [pltpu.VMEM((width // 2, units), w_gate.dtype)] * 2,
        scratch_shapes=[pltpu.SemaphoreType.DMA((2,))],
        compiler_params=params,
        cost_estimate=cost,
        name="hidden_first",
    )(me, rows, *loaded, in_hbm(w_gate), in_hbm(w_up))
    hidden, *downs = pl.pallas_call(
        second_kernel,
        in_specs=[vmem] * 6 + [anywhere],
        out_specs=[vmem] + [anywhere] * PIECES,
        out_shape=[pltpu.VMEM((count, units), jnp.bfloat16)]
        + [pltpu.VMEM((units, width // PIECES), w_down.dtype)] * PIECES,
        scratch_shapes=sums + [pltpu.SemaphoreType.DMA((PIECES,))],
        compiler_params=params,
        cost_estimate=cost,
        name="hidden_second",
    )(other_rows, gate, up, rows, *partial, in_hbm(w_down))
    return hidden, downs


def down_kernel(hidden_ref, down_ref, own_ref, sib_ref):
    middle, width = own_ref.shape
    cols = min(1024, width)

    def one_part(step, carry):
        columns = pl.ds(pl.multiple_of(step * cols, cols), cols)
        part = jnp.dot(hidden_ref[...], down_ref[:, columns], preferred_element_type=jnp.float32)
        part = part.astype(jnp.bfloat16)
        own_ref[:, columns] = part[:middle]
        sib_ref[:, columns] = part[middle:]
        return carry

    lax.fori_loop(0, width // cols, one_part, 0)


def down_call(hidden, w_down):
    rows, units = hidden.shape
    width = w_down.shape[1]
    vmem = pl.BlockSpec(memory_space=pltpu.VMEM)
    return pl.pallas_call(
        down_kernel,
        in_specs=[vmem] * 2,
        out_specs=[vmem] * 2,
        out_shape=[pltpu.VMEM((rows // 2, width), jnp.bfloat16)] * 2,
        compiler_params=pltpu.CompilerParams(vmem_limit_bytes=8 * MIB),
        cost_estimate=pl.CostEstimate(
            flops=2 * rows * width * units,
            bytes_accessed=2 * width * units + 2 * rows * width,
            transcendentals=0,
        ),
        name="down",
    )(hidden, w_down)


def spread_kernel(a_ref, b_ref, c_ref, d_ref, table_ref, *rest):
    out_ref = rest[-1]
    total = a_ref[...].astype(jnp.float32) + b_ref[...].astype(jnp.float32)
    total += c_ref[...].astype(jnp.float32) + d_ref[...].astype(jnp.float32)
    total = total.astype(jnp.bfloat16)
    out_ref[...] = lax.dot_general(
        table_ref[...],
        jnp.concatenate([total] * PARTS, axis=0),
        (((0,), (0,)), ((), ())),
        preferred_element_type=jnp.float32,
    ).astype(jnp.bfloat16)


def spread_call(parts, table, piece, pieces, previous):
    tokens = table.shape[1]
    piece_width = parts[0].shape[1]
    cols = min(2048, piece_width)
    steps = piece_width // cols
    earlier = [] if previous is None else [previous]
    return pl.pallas_call(
        spread_kernel,
        grid=(steps,),
        in_specs=[pl.BlockSpec((CAP, cols), lambda i: (0, i))] * 4
        + [pl.BlockSpec((PARTS * CAP, tokens), lambda i: (0, 0))]
        + [pl.BlockSpec(memory_space=pl.ANY)] * len(earlier),
        out_specs=pl.BlockSpec((tokens, cols), lambda i: (0, piece * steps + i)),
        out_shape=jax.ShapeDtypeStruct((tokens, piece_width * pieces), jnp.bfloat16),
        input_output_aliases={5: 0} if earlier else {},
        compiler_params=pltpu.CompilerParams(
            dimension_semantics=("arbitrary",), vmem_limit_bytes=16 * MIB
        ),
        name="spread",
    )(*parts, table, *earlier)


def reduce_chip_rows(mine, other, half, chips, go_right, go_left):
    middle = mine.shape[1] // 2

    def block(index):
        rows = slice(index * CAP, (index + 1) * CAP)
        return mine[rows].astype(jnp.float32) + other[rows].astype(jnp.float32)

    far = block(chips - 1).astype(jnp.bfloat16)
    ahead, back = far[:, :middle], far[:, middle:]
    for distance in range(half - 1, -1, -1):
        ahead, back = lax.optimization_barrier((ahead, back))
        to_right, to_left = go_right(ahead), go_left(back)
        yield
        if distance == 0:
            break
        ahead, back = block(half - 1 + distance), block(distance)
        if distance == half - 1:
            ahead = jnp.concatenate(
                [ahead[:, :middle] + to_right.astype(jnp.float32), ahead[:, middle:]], axis=1
            )
            back = jnp.concatenate(
                [back[:, :middle], back[:, middle:] + to_left.astype(jnp.float32)], axis=1
            )
        else:
            ahead = ahead + to_right.astype(jnp.float32)
            back = back + to_left.astype(jnp.float32)
        ahead, back = ahead.astype(jnp.bfloat16), back.astype(jnp.bfloat16)
    return (mine, other, to_right, to_left)


def run_together(generators):
    results = [None] * len(generators)
    active = list(range(len(generators)))
    while active:
        for i in list(active):
            try:
                next(generators[i])
            except StopIteration as stop:
                results[i] = stop.value
                active.remove(i)
    return results


def per_device(chips, queries, keys, values, norm_gain, expert_ids, gates, w_gate, w_up, w_down):
    right, left, sibling = permutations(chips)
    half = chips // 2
    go_right = lambda x: lax.ppermute(x, "ctx", right)
    go_left = lambda x: lax.ppermute(x, "ctx", left)
    swap = lambda x: lax.ppermute(x, "ctx", sibling)

    me = lax.axis_index("ctx").astype(jnp.int32).reshape(1)
    tokens = queries.shape[0]
    hits = (expert_ids == 0).astype(jnp.float32)
    chosen = jnp.sum(hits, axis=1)
    position = jnp.arange(tokens, dtype=jnp.int32)
    before = (position[None, :] < position[:, None]).astype(jnp.float32)
    slot = jnp.sum(before * chosen[None, :], axis=1).astype(jnp.int32)
    table = jnp.logical_and(
        slot[None, :] == jnp.arange(CAP, dtype=jnp.int32)[:, None], chosen[None, :] > 0
    ).astype(jnp.float32)
    rest = jnp.sum(gates * hits, axis=1)
    weights = []
    for _ in range(PARTS):
        part = lax.reduce_precision(rest, 8, 7)
        weights.append(table * part[None, :])
        rest = rest - part
    weighted = jnp.concatenate(weights, axis=0).astype(jnp.bfloat16)
    table = table.astype(jnp.bfloat16)

    own, give, q_own, q_give = halves(me, (keys, values), (queries,))
    across_right, across_left = [
        lax.ppermute(give, "ctx", [(i, j ^ 1) for i, j in pairs]) for pairs in (right, left)
    ]
    chains = [(go_right(own), go_left(own)), (across_right, across_left)]
    sib, q_sib = swap(give), swap(q_give)
    sib_table = swap(table)
    attention = Attention(me, (q_own, q_sib), chips)
    state, shift, _ = attention.own(own, sib)
    sources = [own, sib]
    for step in range(1, half):
        *chains[0], state = lax.optimization_barrier((*chains[0], state))
        chains[1], _, state = lax.optimization_barrier((chains[1], chains[0], state))
        blocks = [chain[side] for side in range(2) for chain in chains]
        sources += blocks
        if step < half - 1:
            chains = [(go_right(chain[0]), go_left(chain[1])) for chain in chains]
        else:
            opposite = [
                part for chain in chains for part in (go_right(chain[0][:tokens]), go_left(chain[1][tokens:]))
            ]
        state, _ = attention.step(blocks, [step, step, -step, -step], shift, state)
    opposite, state = lax.optimization_barrier((opposite, state))
    sources += opposite
    mine, theirs, *picked = attention.last(
        opposite, shift, state, norm_gain[None, :], (table, sib_table), sources
    )

    picked, w_gate = lax.optimization_barrier((picked, w_gate))
    chains = [(go_right(x), go_left(x)) for x in picked]
    width = picked[0].shape[1]
    middle = width // DH // 2 * DH
    shape = (2 * chips * CAP, width)
    spots = lambda index: [(index * CAP, 0), ((chips + index) * CAP, 0)]
    rows = place(picked, spots(0), shape)
    loaded = [load(me, w_gate)]
    for step in range(1, half):
        if step == 1:
            chains, rows, loaded = lax.optimization_barrier((chains, rows, loaded))
        *chains[0], rows, loaded = lax.optimization_barrier((*chains[0], rows, loaded))
        chains[1], _, rows, theirs = lax.optimization_barrier((chains[1], chains[0], rows, theirs))
        blocks = [chain[side] for side in range(2) for chain in chains]
        if step < half - 1:
            chains = [(go_right(chain[0]), go_left(chain[1])) for chain in chains]
        else:
            far = [
                part
                for chain in chains
                for part in (go_right(chain[0][:, :middle]), go_left(chain[1][:, middle:]))
            ]
        rows = place(blocks, spots(step) + spots(half - 1 + step), shape, rows)
        if step == 1:
            loaded = loaded + [load(me, w_up)]
        elif step == 2:
            theirs = swap(theirs)
    result = beside(me, mine, theirs)
    far, rows, result = lax.optimization_barrier((far, rows, result))
    places = [(row, column) for row, _ in spots(chips - 1) for column in (0, middle)]
    rows = place(far, places, shape, rows)
    hidden, downs = hidden_calls(me, rows, swap(rows), loaded, w_gate, w_up, w_down)

    sums = []
    for piece in range(PIECES):
        mine, theirs = down_call(hidden, downs[piece])
        sums.append(reduce_chip_rows(mine, swap(theirs), half, chips, go_right, go_left))
    mixed = None
    for piece, parts in enumerate(run_together(sums)):
        mixed = spread_call(parts, weighted, piece, PIECES, mixed)
    return (result, mixed)


def solution(mesh):
    placed = (
        P(("groups", "ctx"), None),
        P(("groups", "ctx"), None),
        P(("groups", "ctx"), None),
        P(),
        P(("groups", "ctx"), None),
        P(("groups", "ctx"), None),
        P(None, "ctx"),
        P(None, "ctx"),
        P("ctx", None),
    )
    return jax.shard_map(
        functools.partial(per_device, mesh.shape["ctx"] // 2),
        mesh=mesh,
        in_specs=placed,
        out_specs=(P(("groups", "ctx"), None), P(("groups", "ctx"), None)),
        check_vma=False,
    )
```

```python
import functools
import math

import jax
import jax.numpy as jnp
from jax import lax
from jax.experimental import pallas as pl
from jax.experimental.pallas import tpu as pltpu
from jax.sharding import PartitionSpec as P

HQ = 64
HK = 8
DH = 128
CAP = 16
GROUP = HQ // HK
WIDE = GROUP * DH
LOG_SCALE = math.log2(math.e) / math.sqrt(DH)
MASKED = -1e30
PIECES = 2
ATTEND_MIB = 11
SMALL = pl.CostEstimate(flops=1, bytes_accessed=1, transcendentals=0)
SUM_LIMIT = 2.0**100
PARTS = 3
STACK = 4
MIB = 1 << 20


def in_hbm(x):
    return pltpu.with_memory_space_constraint(x, pltpu.HBM)


def ring_order(chips):
    return list(range(0, chips, 2)) + list(range(1, chips, 2))[::-1]


def permutations(chips):
    order = ring_order(chips)
    right, left = [], []
    for place in range(chips):
        here, there = order[place], order[(place + 1) % chips]
        for core in range(2):
            right.append((2 * here + core, 2 * there + core))
            left.append((2 * there + core, 2 * here + core))
    sibling = [(i, i ^ 1) for i in range(2 * chips)]
    return right, left, sibling


def chip_at(me, step, chips):
    chip = me // 2
    place = jnp.where(chip % 2 == 0, chip // 2, chips - 1 - chip // 2)
    source = (place - step + 2 * chips) % chips
    return jnp.where(source < chips // 2, 2 * source, 2 * (chips - 1 - source) + 1)


def head_rows(own, sib, first):
    pieces = []
    for h in range(first, first + STACK):
        columns = slice(h * DH, (h + 1) * DH)
        pieces += [own[:, columns], sib[:, columns]]
    return jnp.concatenate(pieces, axis=0)


def with_ones(values):
    return jnp.concatenate([values, jnp.ones_like(values)], axis=1)


def scores_of(queries, keys):
    return LOG_SCALE * lax.dot_general(
        queries, keys, (((1,), (1,)), ((), ())), preferred_element_type=jnp.float32
    )


def weights_of(scores, shift):
    return jnp.exp2(scores - jnp.concatenate([shift] * (scores.shape[1] // DH), axis=1))


def row_top(scores):
    return jnp.broadcast_to(jnp.max(scores, axis=1, keepdims=True), (scores.shape[0], DH))


def allowed_here(core, tokens):
    rows, columns = STACK * 2 * tokens, 2 * tokens

    def position(axis):
        place = lax.broadcasted_iota(jnp.int32, (rows, columns), axis) % (2 * tokens)
        return jnp.where(place < tokens, core * tokens + place, (1 - core) * tokens + place - tokens)

    return position(1) <= position(0)


def group_queries(queries, group):
    columns = pl.ds(pl.multiple_of(group * WIDE, WIDE), WIDE)
    return [ref[:, columns] for ref in queries]


def for_groups(body):
    def step(group, carry):
        body(group, pl.ds(pl.multiple_of(group * DH, DH), DH))
        return carry

    lax.fori_loop(0, HK // 2, step, 0)


def fold(queries, first, keys, values, shift):
    scores = scores_of(head_rows(*queries, first), keys)
    return jnp.dot(
        weights_of(scores, shift).astype(jnp.bfloat16), values, preferred_element_type=jnp.float32
    )


def block_of(ref, columns):
    if isinstance(ref, tuple):
        return ref[0][:, columns], ref[1][:, columns]
    tokens = ref.shape[0] // 2
    return ref[:tokens, columns], ref[tokens:, columns]


def join_blocks(refs, factors, columns):
    pairs = [block_of(ref, columns) for ref in refs]
    keys = jnp.concatenate([key for key, _ in pairs], axis=0)
    values = [with_ones(value) * factor for (_, value), factor in zip(pairs, factors)]
    return keys, jnp.concatenate(values, axis=0)


def factors_of(me, places, chips):
    flags = [chip_at(me, place, chips) < me // 2 for place in places]
    return flags, [jnp.where(flag, 1.0, 0.0).astype(jnp.bfloat16) for flag in flags]


def chunks(tokens):
    size = STACK * 2 * tokens
    return [(first, slice(first // STACK * size, (first // STACK + 1) * size)) for first in range(0, GROUP, STACK)]


def own_kernel(loads, me_ref, q_ref, sib_q_ref, own_ref, sib_ref, *refs):
    acc_ref, total_ref, shift_ref = refs[loads : loads + 3]
    copies = start_loads(loads, refs[:loads], refs[loads + 3 :])
    tokens = q_ref.shape[0]
    allowed = allowed_here(me_ref[0] % 2, tokens)

    def one_group(group, columns):
        keys, values = join_blocks((own_ref, sib_ref), (1, 1), columns)
        queries = group_queries((q_ref, sib_q_ref), group)
        for first, rows in chunks(tokens):
            scores = jnp.where(allowed, scores_of(head_rows(*queries, first), keys), MASKED)
            shift = row_top(scores)
            weights = weights_of(scores, shift).astype(jnp.bfloat16)
            update = jnp.dot(weights, values, preferred_element_type=jnp.float32)
            acc_ref[group, rows, :] = update[:, :DH]
            total_ref[group, rows, :] = update[:, DH:]
            shift_ref[group, rows, :] = shift

    for_groups(one_group)
    for copy in copies:
        copy.wait()


def start_loads(loads, sources, rest):
    copies = [
        pltpu.make_async_copy(source, target, sem)
        for source, target, sem in zip(sources, rest[:loads], rest[loads : 2 * loads])
    ]
    for copy in copies:
        copy.start()
    return copies


def step_kernel(chips, places, loads, me_ref, q_ref, sib_q_ref, *refs):
    count = len(places)
    blocks, shift_ref = refs[:count], refs[count]
    refs = refs[count + 3 :]
    acc_ref, total_ref = refs[loads : loads + 2]
    copies = start_loads(loads, refs[:loads], refs[loads + 2 :])
    tokens = q_ref.shape[0]
    flags, factors = factors_of(me_ref[0], places, chips)

    @pl.when(functools.reduce(jnp.logical_or, flags))
    def _():
        def one_group(group, columns):
            keys, values = join_blocks(blocks, factors, columns)
            queries = group_queries((q_ref, sib_q_ref), group)
            for first, rows in chunks(tokens):
                update = fold(queries, first, keys, values, shift_ref[group, rows, :])
                acc_ref[group, rows, :] += update[:, :DH]
                total_ref[group, rows, :] += update[:, DH:]

        for_groups(one_group)

    for copy in copies:
        copy.wait()


def divide(acc, total):
    inverse = pl.reciprocal(total, approx=True)
    inverse = inverse * (2.0 - total * inverse)
    return (acc * inverse).astype(jnp.bfloat16)


def put_heads(out_refs, rows_ref, tables, group, result):
    tokens = out_refs[0].shape[0]
    columns = pl.ds(pl.multiple_of(group * WIDE, WIDE), WIDE)
    for i, (out_ref, table) in enumerate(zip(out_refs, tables)):
        pieces = [
            result[(2 * h + i) * tokens : (2 * h + i + 1) * tokens] for h in range(GROUP)
        ]
        piece = jnp.concatenate(pieces, axis=1)
        out_ref[:, columns] = piece
        rows_ref[i * CAP : (i + 1) * CAP, columns] = jnp.dot(
            table[...], piece, preferred_element_type=jnp.float32
        )


def running_attention(chips, me, sources, q_refs, put, scratch, sem):
    keys_ref, values_ref, acc_ref, total_ref, top_ref = scratch
    tokens = q_refs[0].shape[0]

    def fetch(source, target):
        copy = pltpu.make_async_copy(source, target, sem)
        copy.start()
        copy.wait()

    def one_group(group, columns):
        queries = group_queries(q_refs, group)
        for i in range(chips - 1):
            for j, block in enumerate(sources[2 * i : 2 * i + 2]):
                rows = pl.ds(j * tokens, tokens)
                fetch(block.at[pl.ds(0, tokens), columns], keys_ref.at[i, rows])
                fetch(block.at[pl.ds(tokens, tokens), columns], values_ref.at[i, rows])
        for j, block in enumerate(sources[2 * chips - 2 :]):
            target = (values_ref if j % 2 else keys_ref).at[chips - 1, pl.ds(j // 2 * tokens, tokens)]
            fetch(block.at[:, columns], target)
        acc_ref[...] = jnp.zeros_like(acc_ref)
        total_ref[...] = jnp.zeros_like(total_ref)
        top_ref[...] = jnp.full_like(top_ref, 2 * MASKED)

        def one_chip(i, inner):
            place = jnp.where(i % 2 == 1, (i + 1) // 2, -(i // 2))
            chip = chip_at(me, place, chips)

            @pl.when(chip <= me // 2)
            def _():
                keys, values = keys_ref[i], with_ones(values_ref[i])
                barred = jnp.where(chip == me // 2, MASKED, 0.0)
                bias = jnp.where(allowed_here(me % 2, tokens), 0.0, barred)
                for first, rows in chunks(tokens):
                    scores = scores_of(head_rows(*queries, first), keys)
                    scores = jnp.where(bias < 0.0, MASKED, scores)
                    old = top_ref[rows, :]
                    top = jnp.maximum(old, row_top(scores))
                    factor = jnp.exp2(old - top)
                    weights = weights_of(scores, top).astype(jnp.bfloat16)
                    update = jnp.dot(weights, values, preferred_element_type=jnp.float32)
                    acc_ref[rows, :] = acc_ref[rows, :] * factor + update[:, :DH]
                    total_ref[rows, :] = total_ref[rows, :] * factor + update[:, DH:]
                    top_ref[rows, :] = top

            return inner

        lax.fori_loop(0, chips, one_chip, 0)
        put(group, divide(acc_ref[...], total_ref[...]))

    for_groups(one_group)


def last_kernel(chips, me_ref, q_ref, sib_q_ref, *refs):
    blocks, (shift_ref, acc_ref, total_ref, gain_ref) = (refs[:2], refs[2:4]), refs[4:8]
    tables, sources = refs[8:10], refs[10 : 12 + 2 * chips]
    refs = refs[12 + 2 * chips :]
    out_refs, picked_ref = refs[:2], refs[2]
    rows_ref, worst_ref, sem, *scratch = refs[3:]
    q_refs = (q_ref, sib_q_ref)
    tokens, half_width = q_ref.shape
    me = me_ref[0]
    _, factors = factors_of(me, [chips // 2] * 2, chips)
    worst_ref[...] = jnp.zeros_like(worst_ref)

    def put(group, result):
        put_heads(out_refs, rows_ref, tables, group, result)

    def one_group(group, columns):
        keys, values = join_blocks(blocks, factors, columns)
        queries = group_queries(q_refs, group)
        results = []
        for first, rows in chunks(tokens):
            update = fold(queries, first, keys, values, shift_ref[group, rows, :])
            total = total_ref[group, rows, :] + update[:, DH:]
            worst_ref[...] = jnp.maximum(worst_ref[...], total)
            results.append(divide(acc_ref[group, rows, :] + update[:, :DH], total))
        put(group, jnp.concatenate(results, axis=0))

    for_groups(one_group)
    fits = jnp.max(worst_ref[...]) <= SUM_LIMIT

    @pl.when(jnp.logical_not(fits))
    def _():
        running_attention(chips, me, sources, q_refs, put, scratch, sem)

    columns = pl.ds(pl.multiple_of(me % 2 * half_width, half_width), half_width)
    rows = rows_ref[...]
    squares = jnp.broadcast_to(jnp.sum(rows * rows, axis=1, keepdims=True), (2 * CAP, DH))
    upper = squares.astype(jnp.bfloat16).astype(jnp.float32)
    lower = (squares - upper).astype(jnp.bfloat16).astype(jnp.float32)
    lane = lax.broadcasted_iota(jnp.int32, squares.shape, 1)
    picked_ref[:, :half_width] = (rows * gain_ref[:, columns]).astype(jnp.bfloat16)
    picked_ref[:, half_width:] = jnp.where(lane < DH // 2, upper, lower).astype(jnp.bfloat16)


class Attention:
    def __init__(self, me, queries, chips):
        self.me, self.queries, self.chips = me, queries, chips
        self.tokens, self.width = queries[0].shape
        self.rows = 2 * GROUP * self.tokens
        self.state_shape = pltpu.VMEM((HK // 2, self.rows, DH), jnp.float32)

    def call(self, kernel, name, args, others, out_shape, out_others, scratch, aliases=None):
        vmem, anywhere = pl.BlockSpec(memory_space=pltpu.VMEM), pl.BlockSpec(memory_space=pl.ANY)
        return pl.pallas_call(
            kernel,
            in_specs=[pl.BlockSpec(memory_space=pltpu.SMEM)]
            + [vmem] * (2 + len(args))
            + [anywhere] * len(others),
            out_specs=[vmem] * len(out_shape) + [anywhere] * len(out_others),
            out_shape=[*out_shape, *out_others],
            scratch_shapes=scratch,
            input_output_aliases=aliases or {},
            compiler_params=pltpu.CompilerParams(vmem_limit_bytes=ATTEND_MIB * MIB),
            cost_estimate=SMALL,
            name=name,
        )(self.me, *self.queries, *args, *others)

    def own(self, own, sib, weights=()):
        loads = len(weights)
        results = self.call(
            functools.partial(own_kernel, loads),
            "attend_own",
            (own, sib),
            [in_hbm(x) for x in weights],
            [self.state_shape] * 3,
            [pltpu.VMEM(x.shape, x.dtype) for x in weights],
            [pltpu.SemaphoreType.DMA] * loads,
        )
        return list(results[:2]), results[2], results[3:]

    def step(self, blocks, places, shift, state, weights=()):
        count, loads = len(blocks), len(weights)
        results = self.call(
            functools.partial(step_kernel, self.chips, places, loads),
            "attend_step",
            (*blocks, shift, *state),
            [in_hbm(x) for x in weights],
            [self.state_shape] * 2,
            [pltpu.VMEM(x.shape, x.dtype) for x in weights],
            [pltpu.SemaphoreType.DMA] * loads,
            {count + 4: 0, count + 5: 1},
        )
        return list(results[:2]), results[2:]

    def last(self, blocks, shift, state, gain, tables, sources):
        out = pltpu.VMEM((self.tokens, self.width), jnp.bfloat16)
        picked = pltpu.VMEM((2 * CAP, self.width + DH), jnp.bfloat16)
        kept = pltpu.VMEM((self.chips, 2 * self.tokens, DH), jnp.bfloat16)
        sums = pltpu.VMEM((self.rows, DH), jnp.float32)
        return self.call(
            functools.partial(last_kernel, self.chips),
            "attend_last",
            (*blocks, shift, *state, gain, *tables),
            sources,
            [out, out, picked],
            [],
            [
                pltpu.VMEM((2 * CAP, self.width), jnp.float32),
                pltpu.VMEM((STACK * 2 * self.tokens, DH), jnp.float32),
                pltpu.SemaphoreType.DMA,
                kept,
                kept,
                sums,
                sums,
                sums,
            ],
        )


def halves_kernel(stacks, me_ref, *refs):
    count = sum(stacks)
    sources, outs, sems = list(refs[:count]), refs[count:-1], refs[-1]
    core = me_ref[0] % 2
    copies = []
    for size, keep_ref, give_ref in zip(stacks, outs[::2], outs[1::2]):
        for i in range(size):
            source = sources.pop(0)
            rows, width = source.shape
            for side, target in ((core, keep_ref), (1 - core, give_ref)):
                columns = pl.ds(pl.multiple_of(side * (width // 2), width // 2), width // 2)
                copies.append((source.at[:, columns], target.at[pl.ds(i * rows, rows)]))
    copies = [pltpu.make_async_copy(*ends, sems.at[i]) for i, ends in enumerate(copies)]
    for copy in copies:
        copy.start()
    for copy in copies:
        copy.wait()


def halves(me, *stacks):
    anywhere = pl.BlockSpec(memory_space=pl.ANY)
    arrays = [x for stack in stacks for x in stack]
    outs = []
    for stack in stacks:
        rows, width = stack[0].shape
        outs += [pltpu.VMEM((len(stack) * rows, width // 2), stack[0].dtype)] * 2
    return pl.pallas_call(
        functools.partial(halves_kernel, [len(stack) for stack in stacks]),
        in_specs=[pl.BlockSpec(memory_space=pltpu.SMEM)] + [anywhere] * len(arrays),
        out_specs=[anywhere] * len(outs),
        out_shape=outs,
        scratch_shapes=[pltpu.SemaphoreType.DMA((2 * len(arrays),))],
        compiler_params=pltpu.CompilerParams(vmem_limit_bytes=MIB),
        cost_estimate=SMALL,
        name="halves",
    )(me, *(in_hbm(x) for x in arrays))


def load_kernel(me_ref, source_ref, target_ref, sem):
    copy = pltpu.make_async_copy(half_rows(me_ref, source_ref, False), target_ref, sem)
    copy.start()
    copy.wait()


def half_rows(me_ref, ref, sibling):
    half = ref.shape[0] // 2
    side = 1 - me_ref[0] % 2 if sibling else me_ref[0] % 2
    return ref.at[pl.ds(pl.multiple_of(side * half, half), half), :]


def load(me, x):
    return pl.pallas_call(
        load_kernel,
        in_specs=[pl.BlockSpec(memory_space=pltpu.SMEM), pl.BlockSpec(memory_space=pl.ANY)],
        out_specs=pl.BlockSpec(memory_space=pl.ANY),
        out_shape=pltpu.VMEM((x.shape[0] // 2, x.shape[1]), x.dtype),
        scratch_shapes=[pltpu.SemaphoreType.DMA],
        compiler_params=pltpu.CompilerParams(vmem_limit_bytes=MIB),
        cost_estimate=SMALL,
        name="load",
    )(me, in_hbm(x))


def place_kernel(spots, *refs):
    blocks, out_ref = refs[: len(spots)], refs[-1]
    middle = out_ref.shape[0] // 2
    for index, ref in zip(spots, blocks):
        for core in range(2):
            row = core * middle + index * CAP
            out_ref[row : row + CAP] = ref[core * CAP : (core + 1) * CAP]


def place(blocks, spots, rows):
    vmem = pl.BlockSpec(memory_space=pltpu.VMEM)
    earlier = [] if isinstance(rows, tuple) else [rows]
    shape = rows.shape if earlier else rows
    return pl.pallas_call(
        functools.partial(place_kernel, spots),
        in_specs=[vmem] * (len(blocks) + len(earlier)),
        out_specs=vmem,
        out_shape=pltpu.VMEM(shape, jnp.bfloat16),
        input_output_aliases={len(blocks): 0} if earlier else {},
        compiler_params=pltpu.CompilerParams(vmem_limit_bytes=4 * MIB),
        cost_estimate=SMALL,
        name="place",
    )(*blocks, *earlier)


def place_far_kernel(low_ref, high_ref, _, out_ref):
    middle, row = out_ref.shape[0] // 2, out_ref.shape[0] // 2 - CAP
    out_ref[row : row + CAP] = low_ref[...]
    out_ref[middle + row : middle + row + CAP] = high_ref[...]


def place_far(low, high, rows):
    vmem = pl.BlockSpec(memory_space=pltpu.VMEM)
    return pl.pallas_call(
        place_far_kernel,
        in_specs=[vmem] * 3,
        out_specs=vmem,
        out_shape=pltpu.VMEM(rows.shape, jnp.bfloat16),
        input_output_aliases={2: 0},
        compiler_params=pltpu.CompilerParams(vmem_limit_bytes=4 * MIB),
        cost_estimate=SMALL,
        name="place",
    )(low, high, rows)


def contract(rows_ref, gate_ref, up_ref, gate_sum, up_sum, order):
    half = gate_ref.shape[0]
    depth = min(1024, half)

    def one_part(step, carry):
        columns = pl.ds(pl.multiple_of(step * depth, depth), depth)
        part = order(rows_ref[:, columns])
        gate_sum[...] += jnp.dot(part, gate_ref[columns, :], preferred_element_type=jnp.float32)
        up_sum[...] += jnp.dot(part, up_ref[columns, :], preferred_element_type=jnp.float32)
        return carry

    lax.fori_loop(0, half // depth, one_part, 0)


def first_kernel(me_ref, rows_ref, gate_ref, up_ref, *refs):
    sources, (gate_sum, up_sum), targets, sems = refs[:2], refs[2:4], refs[4:6], refs[6]
    copies = [
        pltpu.make_async_copy(half_rows(me_ref, source, True), target, sems.at[i])
        for i, (source, target) in enumerate(zip(sources, targets))
    ]
    for copy in copies:
        copy.start()
    gate_sum[...] = jnp.zeros_like(gate_sum)
    up_sum[...] = jnp.zeros_like(up_sum)
    contract(rows_ref, gate_ref, up_ref, gate_sum, up_sum, lambda part: part)
    for copy in copies:
        copy.wait()


def second_kernel(rows_ref, gate_ref, up_ref, own_ref, gate_in, up_in, source_ref, out_ref, *refs):
    targets, (gate_sum, up_sum, sems) = refs[:PIECES], refs[PIECES:]
    piece = targets[0].shape[1]
    copies = [
        pltpu.make_async_copy(source_ref.at[:, pl.ds(i * piece, piece)], target, sems.at[i])
        for i, target in enumerate(targets)
    ]
    for copy in copies:
        copy.start()
    middle, half = rows_ref.shape[0] // 2, gate_ref.shape[0]

    def order(part):
        return jnp.concatenate([part[middle:], part[:middle]], axis=0)

    gate_sum[...] = gate_in[...]
    up_sum[...] = up_in[...]
    contract(rows_ref, gate_ref, up_ref, gate_sum, up_sum, order)
    squares = own_ref[:, half:].astype(jnp.float32) + order(rows_ref[:, half:].astype(jnp.float32))
    squares = squares[:, :1] + squares[:, DH // 2 : DH // 2 + 1]
    factor = lax.rsqrt(squares / (2 * half) + 1e-05)
    gate = gate_sum[...] * factor
    out_ref[...] = (gate / (1.0 + jnp.exp(-gate)) * (up_sum[...] * factor)).astype(jnp.bfloat16)
    for copy in copies:
        copy.wait()


def hidden_calls(me, rows, other_rows, loaded, w_gate, w_up, w_down):
    count, units, width = rows.shape[0], w_down.shape[0], w_down.shape[1]
    vmem, anywhere = pl.BlockSpec(memory_space=pltpu.VMEM), pl.BlockSpec(memory_space=pl.ANY)
    sums = [pltpu.VMEM((count, units), jnp.float32)] * 2
    params = pltpu.CompilerParams(vmem_limit_bytes=8 * MIB)
    cost = pl.CostEstimate(
        flops=2 * count * width * units, bytes_accessed=2 * width * units, transcendentals=count * units
    )
    *partial, gate, up = pl.pallas_call(
        first_kernel,
        in_specs=[pl.BlockSpec(memory_space=pltpu.SMEM)] + [vmem] * 3 + [anywhere] * 2,
        out_specs=[vmem] * 2 + [anywhere] * 2,
        out_shape=sums + [pltpu.VMEM((width // 2, units), w_gate.dtype)] * 2,
        scratch_shapes=[pltpu.SemaphoreType.DMA((2,))],
        compiler_params=params,
        cost_estimate=cost,
        name="hidden_first",
    )(me, rows, *loaded, in_hbm(w_gate), in_hbm(w_up))
    hidden, *downs = pl.pallas_call(
        second_kernel,
        in_specs=[vmem] * 6 + [anywhere],
        out_specs=[vmem] + [anywhere] * PIECES,
        out_shape=[pltpu.VMEM((count, units), jnp.bfloat16)]
        + [pltpu.VMEM((units, width // PIECES), w_down.dtype)] * PIECES,
        scratch_shapes=sums + [pltpu.SemaphoreType.DMA((PIECES,))],
        compiler_params=params,
        cost_estimate=cost,
        name="hidden_second",
    )(other_rows, gate, up, rows, *partial, in_hbm(w_down))
    return hidden, downs


def down_kernel(hidden_ref, down_ref, *refs):
    copies = []
    if len(refs) == 2:
        own_ref, sib_ref = refs
    else:
        me_ref, *parts, own_ref, sib_ref, result_ref, sems = refs
        width = parts[0].shape[1]
        core = me_ref[0] % 2
        for i, (side, source) in enumerate(zip((core, 1 - core), parts)):
            columns = pl.ds(pl.multiple_of(side * width, width), width)
            copies.append(pltpu.make_async_copy(source, result_ref.at[:, columns], sems.at[i]))
    for copy in copies:
        copy.start()
    middle, width = own_ref.shape
    cols = min(1024, width)

    def one_part(step, carry):
        columns = pl.ds(pl.multiple_of(step * cols, cols), cols)
        part = jnp.dot(hidden_ref[...], down_ref[:, columns], preferred_element_type=jnp.float32)
        part = part.astype(jnp.bfloat16)
        own_ref[:, columns] = part[:middle]
        sib_ref[:, columns] = part[middle:]
        return carry

    lax.fori_loop(0, width // cols, one_part, 0)
    for copy in copies:
        copy.wait()


def down_call(hidden, w_down, halves=()):
    rows, units = hidden.shape
    width = w_down.shape[1]
    vmem, anywhere = pl.BlockSpec(memory_space=pltpu.VMEM), pl.BlockSpec(memory_space=pl.ANY)
    more = [pl.BlockSpec(memory_space=pltpu.SMEM), anywhere, anywhere] if halves else []
    outs = [pltpu.VMEM((rows // 2, width), jnp.bfloat16)] * 2
    if halves:
        tokens, part = halves[1].shape
        outs.append(jax.ShapeDtypeStruct((tokens, 2 * part), jnp.bfloat16))
    return pl.pallas_call(
        down_kernel,
        in_specs=[vmem] * 2 + more,
        out_specs=[vmem] * 2 + [anywhere] * (len(outs) - 2),
        out_shape=outs,
        scratch_shapes=[pltpu.SemaphoreType.DMA((2,))] if halves else [],
        compiler_params=pltpu.CompilerParams(vmem_limit_bytes=8 * MIB),
        cost_estimate=pl.CostEstimate(
            flops=2 * rows * width * units,
            bytes_accessed=2 * width * units + 2 * rows * width,
            transcendentals=0,
        ),
        name="down",
    )(hidden, w_down, *halves)


def spread_kernel(a_ref, b_ref, c_ref, d_ref, table_ref, *rest):
    out_ref = rest[-1]
    total = a_ref[...].astype(jnp.float32) + b_ref[...].astype(jnp.float32)
    total += c_ref[...].astype(jnp.float32) + d_ref[...].astype(jnp.float32)
    total = total.astype(jnp.bfloat16)
    out_ref[...] = lax.dot_general(
        table_ref[...],
        jnp.concatenate([total] * PARTS, axis=0),
        (((0,), (0,)), ((), ())),
        preferred_element_type=jnp.float32,
    ).astype(jnp.bfloat16)


def spread_call(parts, table, piece, pieces, previous):
    tokens = table.shape[1]
    piece_width = parts[0].shape[1]
    cols = min(2048, piece_width)
    steps = piece_width // cols
    earlier = [] if previous is None else [previous]
    return pl.pallas_call(
        spread_kernel,
        grid=(steps,),
        in_specs=[pl.BlockSpec((CAP, cols), lambda i: (0, i))] * 4
        + [pl.BlockSpec((PARTS * CAP, tokens), lambda i: (0, 0))]
        + [pl.BlockSpec(memory_space=pl.ANY)] * len(earlier),
        out_specs=pl.BlockSpec((tokens, cols), lambda i: (0, piece * steps + i)),
        out_shape=jax.ShapeDtypeStruct((tokens, piece_width * pieces), jnp.bfloat16),
        input_output_aliases={5: 0} if earlier else {},
        compiler_params=pltpu.CompilerParams(
            dimension_semantics=("arbitrary",), vmem_limit_bytes=16 * MIB
        ),
        name="spread",
    )(*parts, table, *earlier)


def reduce_chip_rows(mine, other, half, chips, go_right, go_left):
    middle = mine.shape[1] // 2

    def block(index):
        rows = slice(index * CAP, (index + 1) * CAP)
        return mine[rows].astype(jnp.float32) + other[rows].astype(jnp.float32)

    far = block(chips - 1).astype(jnp.bfloat16)
    ahead, back = far[:, :middle], far[:, middle:]
    for distance in range(half - 1, -1, -1):
        ahead, back = lax.optimization_barrier((ahead, back))
        to_right, to_left = go_right(ahead), go_left(back)
        yield
        if distance == 0:
            break
        ahead, back = block(half - 1 + distance), block(distance)
        if distance == half - 1:
            ahead = jnp.concatenate(
                [ahead[:, :middle] + to_right.astype(jnp.float32), ahead[:, middle:]], axis=1
            )
            back = jnp.concatenate(
                [back[:, :middle], back[:, middle:] + to_left.astype(jnp.float32)], axis=1
            )
        else:
            ahead = ahead + to_right.astype(jnp.float32)
            back = back + to_left.astype(jnp.float32)
        ahead, back = ahead.astype(jnp.bfloat16), back.astype(jnp.bfloat16)
    return (mine, other, to_right, to_left)


def run_together(generators):
    results = [None] * len(generators)
    active = list(range(len(generators)))
    while active:
        for i in list(active):
            try:
                next(generators[i])
            except StopIteration as stop:
                results[i] = stop.value
                active.remove(i)
    return results


def per_device(chips, queries, keys, values, norm_gain, expert_ids, gates, w_gate, w_up, w_down):
    right, left, sibling = permutations(chips)
    half = chips // 2
    go_right = lambda x: lax.ppermute(x, "ctx", right)
    go_left = lambda x: lax.ppermute(x, "ctx", left)
    swap = lambda x: lax.ppermute(x, "ctx", sibling)

    me = lax.axis_index("ctx").astype(jnp.int32).reshape(1)
    tokens = queries.shape[0]
    hits = (expert_ids == 0).astype(jnp.float32)
    chosen = jnp.sum(hits, axis=1)
    position = jnp.arange(tokens, dtype=jnp.int32)
    before = (position[None, :] < position[:, None]).astype(jnp.float32)
    slot = jnp.sum(before * chosen[None, :], axis=1).astype(jnp.int32)
    table = jnp.logical_and(
        slot[None, :] == jnp.arange(CAP, dtype=jnp.int32)[:, None], chosen[None, :] > 0
    ).astype(jnp.float32)
    rest = jnp.sum(gates * hits, axis=1)
    weights = []
    for _ in range(PARTS):
        part = lax.reduce_precision(rest, 8, 7)
        weights.append(table * part[None, :])
        rest = rest - part
    weighted = jnp.concatenate(weights, axis=0).astype(jnp.bfloat16)
    table = table.astype(jnp.bfloat16)

    own, give, q_own, q_give = halves(me, (keys, values), (queries,))
    across_right, across_left = [
        lax.ppermute(give, "ctx", [(i, j ^ 1) for i, j in pairs]) for pairs in (right, left)
    ]
    chains = [(go_right(own), go_left(own)), (across_right, across_left)]
    sib, q_sib = swap(give), swap(q_give)
    sib_table = swap(table)
    attention = Attention(me, (q_own, q_sib), chips)
    state, shift, _ = attention.own(own, sib)
    sources = [own, sib]
    for step in range(1, half):
        *chains[0], state = lax.optimization_barrier((*chains[0], state))
        chains[1], _, state = lax.optimization_barrier((chains[1], chains[0], state))
        blocks = [chain[side] for side in range(2) for chain in chains]
        sources += blocks
        if step < half - 1:
            chains = [(go_right(chain[0]), go_left(chain[1])) for chain in chains]
        else:
            opposite = [
                part for chain in chains for part in (go_right(chain[0][:tokens]), go_left(chain[1][tokens:]))
            ]
        state, _ = attention.step(blocks, [step, step, -step, -step], shift, state)
    opposite, state = lax.optimization_barrier((opposite, state))
    sources += opposite
    mine, theirs, picked = attention.last(
        opposite, shift, state, norm_gain[None, :], (table, sib_table), sources
    )

    picked, w_gate = lax.optimization_barrier((picked, w_gate))
    from_left, from_right = go_right(picked), go_left(picked)
    rows = place([picked], [0], (2 * chips * CAP, picked.shape[1]))
    loaded, theirs = [load(me, w_gate)], swap(theirs)
    for step in range(1, half):
        from_left, rows, loaded = lax.optimization_barrier((from_left, rows, loaded))
        from_right, _, rows = lax.optimization_barrier((from_right, from_left, rows))
        blocks = [from_left, from_right]
        if step < half - 1:
            from_left, from_right = go_right(from_left), go_left(from_right)
        else:
            far = go_right(from_left[:CAP]), go_left(from_right[CAP:])
        rows = place(blocks, [step, half - 1 + step], rows)
        if step == 1:
            rows, w_up = lax.optimization_barrier((rows, w_up))
            loaded = loaded + [load(me, w_up)]
    far, rows = lax.optimization_barrier((far, rows))
    rows = place_far(*far, rows)
    hidden, downs = hidden_calls(me, rows, swap(rows), loaded, w_gate, w_up, w_down)

    sums = []
    for piece in range(PIECES):
        if piece == 0:
            own, sib, result = down_call(hidden, downs[piece], (me, mine, theirs))
        else:
            own, sib = down_call(hidden, downs[piece])
        sums.append(reduce_chip_rows(own, swap(sib), half, chips, go_right, go_left))
    mixed = None
    for piece, parts in enumerate(run_together(sums)):
        mixed = spread_call(parts, weighted, piece, PIECES, mixed)
    return (result, mixed)


def solution(mesh):
    placed = (
        P(("groups", "ctx"), None),
        P(("groups", "ctx"), None),
        P(("groups", "ctx"), None),
        P(),
        P(("groups", "ctx"), None),
        P(("groups", "ctx"), None),
        P(None, "ctx"),
        P(None, "ctx"),
        P("ctx", None),
    )
    return jax.shard_map(
        functools.partial(per_device, mesh.shape["ctx"] // 2),
        mesh=mesh,
        in_specs=placed,
        out_specs=(P(("groups", "ctx"), None), P(("groups", "ctx"), None)),
        check_vma=False,
    )
```

```python
import functools
import math

import jax
import jax.numpy as jnp
from jax import lax
from jax.experimental import pallas as pl
from jax.experimental.pallas import tpu as pltpu
from jax.sharding import PartitionSpec as P

HQ = 64
HK = 8
DH = 128
CAP = 16
GROUP = HQ // HK
WIDE = GROUP * DH
LOG_SCALE = math.log2(math.e) / math.sqrt(DH)
MASKED = -1e30
PIECES = 2
ATTEND_MIB = 11
SMALL = pl.CostEstimate(flops=1, bytes_accessed=1, transcendentals=0)
SUM_LIMIT = 2.0**100
PARTS = 3
STACK = 4
MIB = 1 << 20


def in_hbm(x):
    return pltpu.with_memory_space_constraint(x, pltpu.HBM)


def ring_order(chips):
    return list(range(0, chips, 2)) + list(range(1, chips, 2))[::-1]


def permutations(chips):
    order = ring_order(chips)
    right, left = [], []
    for place in range(chips):
        here, there = order[place], order[(place + 1) % chips]
        for core in range(2):
            right.append((2 * here + core, 2 * there + core))
            left.append((2 * there + core, 2 * here + core))
    sibling = [(i, i ^ 1) for i in range(2 * chips)]
    return right, left, sibling


def chip_at(me, step, chips):
    chip = me // 2
    place = jnp.where(chip % 2 == 0, chip // 2, chips - 1 - chip // 2)
    source = (place - step + 2 * chips) % chips
    return jnp.where(source < chips // 2, 2 * source, 2 * (chips - 1 - source) + 1)


def head_rows(own, sib, first):
    pieces = []
    for h in range(first, first + STACK):
        columns = slice(h * DH, (h + 1) * DH)
        pieces += [own[:, columns], sib[:, columns]]
    return jnp.concatenate(pieces, axis=0)


def with_ones(values):
    return jnp.concatenate([values, jnp.ones_like(values)], axis=1)


def scores_of(queries, keys):
    return LOG_SCALE * lax.dot_general(
        queries, keys, (((1,), (1,)), ((), ())), preferred_element_type=jnp.float32
    )


def weights_of(scores, shift):
    return jnp.exp2(scores - jnp.concatenate([shift] * (scores.shape[1] // DH), axis=1))


def row_top(scores):
    return jnp.broadcast_to(jnp.max(scores, axis=1, keepdims=True), (scores.shape[0], DH))


def allowed_here(core, tokens):
    rows, columns = STACK * 2 * tokens, 2 * tokens

    def position(axis):
        place = lax.broadcasted_iota(jnp.int32, (rows, columns), axis) % (2 * tokens)
        return jnp.where(place < tokens, core * tokens + place, (1 - core) * tokens + place - tokens)

    return position(1) <= position(0)


def group_queries(queries, group):
    columns = pl.ds(pl.multiple_of(group * WIDE, WIDE), WIDE)
    return [ref[:, columns] for ref in queries]


def for_groups(body):
    def step(group, carry):
        body(group, pl.ds(pl.multiple_of(group * DH, DH), DH))
        return carry

    lax.fori_loop(0, HK // 2, step, 0)


def fold(queries, first, keys, values, shift):
    scores = scores_of(head_rows(*queries, first), keys)
    return jnp.dot(
        weights_of(scores, shift).astype(jnp.bfloat16), values, preferred_element_type=jnp.float32
    )


def block_of(ref, columns):
    if isinstance(ref, tuple):
        return ref[0][:, columns], ref[1][:, columns]
    tokens = ref.shape[0] // 2
    return ref[:tokens, columns], ref[tokens:, columns]


def join_blocks(refs, factors, columns):
    pairs = [block_of(ref, columns) for ref in refs]
    keys = jnp.concatenate([key for key, _ in pairs], axis=0)
    values = [with_ones(value) * factor for (_, value), factor in zip(pairs, factors)]
    return keys, jnp.concatenate(values, axis=0)


def factors_of(me, places, chips):
    flags = [chip_at(me, place, chips) < me // 2 for place in places]
    return flags, [jnp.where(flag, 1.0, 0.0).astype(jnp.bfloat16) for flag in flags]


def chunks(tokens):
    size = STACK * 2 * tokens
    return [(first, slice(first // STACK * size, (first // STACK + 1) * size)) for first in range(0, GROUP, STACK)]


def own_kernel(loads, me_ref, q_ref, sib_q_ref, own_ref, sib_ref, *refs):
    acc_ref, total_ref, shift_ref = refs[loads : loads + 3]
    copies = start_loads(loads, refs[:loads], refs[loads + 3 :])
    tokens = q_ref.shape[0]
    allowed = allowed_here(me_ref[0] % 2, tokens)

    def one_group(group, columns):
        keys, values = join_blocks((own_ref, sib_ref), (1, 1), columns)
        queries = group_queries((q_ref, sib_q_ref), group)
        for first, rows in chunks(tokens):
            scores = jnp.where(allowed, scores_of(head_rows(*queries, first), keys), MASKED)
            shift = row_top(scores)
            weights = weights_of(scores, shift).astype(jnp.bfloat16)
            update = jnp.dot(weights, values, preferred_element_type=jnp.float32)
            acc_ref[group, rows, :] = update[:, :DH]
            total_ref[group, rows, :] = update[:, DH:]
            shift_ref[group, rows, :] = shift

    for_groups(one_group)
    for copy in copies:
        copy.wait()


def start_loads(loads, sources, rest):
    copies = [
        pltpu.make_async_copy(source, target, sem)
        for source, target, sem in zip(sources, rest[:loads], rest[loads : 2 * loads])
    ]
    for copy in copies:
        copy.start()
    return copies


def step_kernel(chips, places, loads, me_ref, q_ref, sib_q_ref, *refs):
    count = len(places)
    blocks, shift_ref = refs[:count], refs[count]
    refs = refs[count + 3 :]
    acc_ref, total_ref = refs[loads : loads + 2]
    copies = start_loads(loads, refs[:loads], refs[loads + 2 :])
    tokens = q_ref.shape[0]
    flags, factors = factors_of(me_ref[0], places, chips)

    @pl.when(functools.reduce(jnp.logical_or, flags))
    def _():
        def one_group(group, columns):
            keys, values = join_blocks(blocks, factors, columns)
            queries = group_queries((q_ref, sib_q_ref), group)
            for first, rows in chunks(tokens):
                update = fold(queries, first, keys, values, shift_ref[group, rows, :])
                acc_ref[group, rows, :] += update[:, :DH]
                total_ref[group, rows, :] += update[:, DH:]

        for_groups(one_group)

    for copy in copies:
        copy.wait()


def divide(acc, total):
    inverse = pl.reciprocal(total, approx=True)
    inverse = inverse * (2.0 - total * inverse)
    return (acc * inverse).astype(jnp.bfloat16)


def put_heads(out_refs, rows_ref, tables, group, result):
    tokens = out_refs[0].shape[0]
    columns = pl.ds(pl.multiple_of(group * WIDE, WIDE), WIDE)
    for i, (out_ref, table) in enumerate(zip(out_refs, tables)):
        pieces = [
            result[(2 * h + i) * tokens : (2 * h + i + 1) * tokens] for h in range(GROUP)
        ]
        piece = jnp.concatenate(pieces, axis=1)
        out_ref[:, columns] = piece
        rows_ref[i * CAP : (i + 1) * CAP, columns] = jnp.dot(
            table[...], piece, preferred_element_type=jnp.float32
        )


def running_attention(chips, me, sources, q_refs, put, scratch, sem):
    keys_ref, values_ref, acc_ref, total_ref, top_ref = scratch
    tokens = q_refs[0].shape[0]

    def fetch(source, target):
        copy = pltpu.make_async_copy(source, target, sem)
        copy.start()
        copy.wait()

    def one_group(group, columns):
        queries = group_queries(q_refs, group)
        for i in range(chips - 1):
            for j, block in enumerate(sources[2 * i : 2 * i + 2]):
                rows = pl.ds(j * tokens, tokens)
                fetch(block.at[pl.ds(0, tokens), columns], keys_ref.at[i, rows])
                fetch(block.at[pl.ds(tokens, tokens), columns], values_ref.at[i, rows])
        whole, key, value = sources[2 * chips - 2 :]
        own, sib = pl.ds(0, tokens), pl.ds(tokens, tokens)
        fetch(whole.at[own, columns], keys_ref.at[chips - 1, own])
        fetch(whole.at[sib, columns], values_ref.at[chips - 1, own])
        fetch(key.at[:, columns], keys_ref.at[chips - 1, sib])
        fetch(value.at[:, columns], values_ref.at[chips - 1, sib])
        acc_ref[...] = jnp.zeros_like(acc_ref)
        total_ref[...] = jnp.zeros_like(total_ref)
        top_ref[...] = jnp.full_like(top_ref, 2 * MASKED)

        def one_chip(i, inner):
            place = jnp.where(i % 2 == 1, (i + 1) // 2, -(i // 2))
            chip = chip_at(me, place, chips)

            @pl.when(chip <= me // 2)
            def _():
                keys, values = keys_ref[i], with_ones(values_ref[i])
                barred = jnp.where(chip == me // 2, MASKED, 0.0)
                bias = jnp.where(allowed_here(me % 2, tokens), 0.0, barred)
                for first, rows in chunks(tokens):
                    scores = scores_of(head_rows(*queries, first), keys)
                    scores = jnp.where(bias < 0.0, MASKED, scores)
                    old = top_ref[rows, :]
                    top = jnp.maximum(old, row_top(scores))
                    factor = jnp.exp2(old - top)
                    weights = weights_of(scores, top).astype(jnp.bfloat16)
                    update = jnp.dot(weights, values, preferred_element_type=jnp.float32)
                    acc_ref[rows, :] = acc_ref[rows, :] * factor + update[:, :DH]
                    total_ref[rows, :] = total_ref[rows, :] * factor + update[:, DH:]
                    top_ref[rows, :] = top

            return inner

        lax.fori_loop(0, chips, one_chip, 0)
        put(group, divide(acc_ref[...], total_ref[...]))

    for_groups(one_group)


def last_kernel(chips, me_ref, q_ref, sib_q_ref, *refs):
    blocks, (shift_ref, acc_ref, total_ref, gain_ref) = (refs[0], refs[1:3]), refs[3:7]
    tables, sources = refs[7:9], refs[9 : 10 + 2 * chips]
    refs = refs[10 + 2 * chips :]
    out_refs, picked_ref = refs[:2], refs[2]
    rows_ref, worst_ref, sem, *scratch = refs[3:]
    q_refs = (q_ref, sib_q_ref)
    tokens, half_width = q_ref.shape
    me = me_ref[0]
    _, factors = factors_of(me, [chips // 2] * 2, chips)
    worst_ref[...] = jnp.zeros_like(worst_ref)

    def put(group, result):
        put_heads(out_refs, rows_ref, tables, group, result)

    def one_group(group, columns):
        keys, values = join_blocks(blocks, factors, columns)
        queries = group_queries(q_refs, group)
        results = []
        for first, rows in chunks(tokens):
            update = fold(queries, first, keys, values, shift_ref[group, rows, :])
            total = total_ref[group, rows, :] + update[:, DH:]
            worst_ref[...] = jnp.maximum(worst_ref[...], total)
            results.append(divide(acc_ref[group, rows, :] + update[:, :DH], total))
        put(group, jnp.concatenate(results, axis=0))

    for_groups(one_group)
    fits = jnp.max(worst_ref[...]) <= SUM_LIMIT

    @pl.when(jnp.logical_not(fits))
    def _():
        running_attention(chips, me, sources, q_refs, put, scratch, sem)

    columns = pl.ds(pl.multiple_of(me % 2 * half_width, half_width), half_width)
    rows = rows_ref[...]
    squares = jnp.broadcast_to(jnp.sum(rows * rows, axis=1, keepdims=True), (2 * CAP, DH))
    upper = squares.astype(jnp.bfloat16).astype(jnp.float32)
    lower = (squares - upper).astype(jnp.bfloat16).astype(jnp.float32)
    lane = lax.broadcasted_iota(jnp.int32, squares.shape, 1)
    picked_ref[:, :half_width] = (rows * gain_ref[:, columns]).astype(jnp.bfloat16)
    picked_ref[:, half_width:] = jnp.where(lane < DH // 2, upper, lower).astype(jnp.bfloat16)


class Attention:
    def __init__(self, me, queries, chips):
        self.me, self.queries, self.chips = me, queries, chips
        self.tokens, self.width = queries[0].shape
        self.rows = 2 * GROUP * self.tokens
        self.state_shape = pltpu.VMEM((HK // 2, self.rows, DH), jnp.float32)

    def call(self, kernel, name, args, others, out_shape, out_others, scratch, aliases=None):
        vmem, anywhere = pl.BlockSpec(memory_space=pltpu.VMEM), pl.BlockSpec(memory_space=pl.ANY)
        return pl.pallas_call(
            kernel,
            in_specs=[pl.BlockSpec(memory_space=pltpu.SMEM)]
            + [vmem] * (2 + len(args))
            + [anywhere] * len(others),
            out_specs=[vmem] * len(out_shape) + [anywhere] * len(out_others),
            out_shape=[*out_shape, *out_others],
            scratch_shapes=scratch,
            input_output_aliases=aliases or {},
            compiler_params=pltpu.CompilerParams(vmem_limit_bytes=ATTEND_MIB * MIB),
            cost_estimate=SMALL,
            name=name,
        )(self.me, *self.queries, *args, *others)

    def own(self, own, sib, weights=()):
        loads = len(weights)
        results = self.call(
            functools.partial(own_kernel, loads),
            "attend_own",
            (own, sib),
            [in_hbm(x) for x in weights],
            [self.state_shape] * 3,
            [pltpu.VMEM(x.shape, x.dtype) for x in weights],
            [pltpu.SemaphoreType.DMA] * loads,
        )
        return list(results[:2]), results[2], results[3:]

    def step(self, blocks, places, shift, state, weights=()):
        count, loads = len(blocks), len(weights)
        results = self.call(
            functools.partial(step_kernel, self.chips, places, loads),
            "attend_step",
            (*blocks, shift, *state),
            [in_hbm(x) for x in weights],
            [self.state_shape] * 2,
            [pltpu.VMEM(x.shape, x.dtype) for x in weights],
            [pltpu.SemaphoreType.DMA] * loads,
            {count + 4: 0, count + 5: 1},
        )
        return list(results[:2]), results[2:]

    def last(self, blocks, shift, state, gain, tables, sources):
        out = pltpu.VMEM((self.tokens, self.width), jnp.bfloat16)
        picked = pltpu.VMEM((2 * CAP, self.width + DH), jnp.bfloat16)
        kept = pltpu.VMEM((self.chips, 2 * self.tokens, DH), jnp.bfloat16)
        sums = pltpu.VMEM((self.rows, DH), jnp.float32)
        return self.call(
            functools.partial(last_kernel, self.chips),
            "attend_last",
            (*blocks, shift, *state, gain, *tables),
            sources,
            [out, out, picked],
            [],
            [
                pltpu.VMEM((2 * CAP, self.width), jnp.float32),
                pltpu.VMEM((STACK * 2 * self.tokens, DH), jnp.float32),
                pltpu.SemaphoreType.DMA,
                kept,
                kept,
                sums,
                sums,
                sums,
            ],
        )


def halves_kernel(stacks, me_ref, *refs):
    count = sum(stacks)
    sources, outs, sems = list(refs[:count]), refs[count:-1], refs[-1]
    core = me_ref[0] % 2
    copies = []
    for size, keep_ref, give_ref in zip(stacks, outs[::2], outs[1::2]):
        for i in range(size):
            source = sources.pop(0)
            rows, width = source.shape
            for side, target in ((core, keep_ref), (1 - core, give_ref)):
                columns = pl.ds(pl.multiple_of(side * (width // 2), width // 2), width // 2)
                copies.append((source.at[:, columns], target.at[pl.ds(i * rows, rows)]))
    copies = [pltpu.make_async_copy(*ends, sems.at[i]) for i, ends in enumerate(copies)]
    for copy in copies:
        copy.start()
    for copy in copies:
        copy.wait()


def halves(me, *stacks):
    anywhere = pl.BlockSpec(memory_space=pl.ANY)
    arrays = [x for stack in stacks for x in stack]
    outs = []
    for stack in stacks:
        rows, width = stack[0].shape
        outs += [pltpu.VMEM((len(stack) * rows, width // 2), stack[0].dtype)] * 2
    return pl.pallas_call(
        functools.partial(halves_kernel, [len(stack) for stack in stacks]),
        in_specs=[pl.BlockSpec(memory_space=pltpu.SMEM)] + [anywhere] * len(arrays),
        out_specs=[anywhere] * len(outs),
        out_shape=outs,
        scratch_shapes=[pltpu.SemaphoreType.DMA((2 * len(arrays),))],
        compiler_params=pltpu.CompilerParams(vmem_limit_bytes=MIB),
        cost_estimate=SMALL,
        name="halves",
    )(me, *(in_hbm(x) for x in arrays))


def load_kernel(me_ref, source_ref, target_ref, sem):
    copy = pltpu.make_async_copy(half_rows(me_ref, source_ref, False), target_ref, sem)
    copy.start()
    copy.wait()


def half_rows(me_ref, ref, sibling):
    half = ref.shape[0] // 2
    side = 1 - me_ref[0] % 2 if sibling else me_ref[0] % 2
    return ref.at[pl.ds(pl.multiple_of(side * half, half), half), :]


def load(me, x):
    return pl.pallas_call(
        load_kernel,
        in_specs=[pl.BlockSpec(memory_space=pltpu.SMEM), pl.BlockSpec(memory_space=pl.ANY)],
        out_specs=pl.BlockSpec(memory_space=pl.ANY),
        out_shape=pltpu.VMEM((x.shape[0] // 2, x.shape[1]), x.dtype),
        scratch_shapes=[pltpu.SemaphoreType.DMA],
        compiler_params=pltpu.CompilerParams(vmem_limit_bytes=MIB),
        cost_estimate=SMALL,
        name="load",
    )(me, in_hbm(x))


def place_kernel(spots, *refs):
    blocks, out_ref = refs[: len(spots)], refs[-1]
    middle = out_ref.shape[0] // 2
    for index, ref in zip(spots, blocks):
        for core in range(2):
            row = core * middle + index * CAP
            out_ref[row : row + CAP] = ref[core * CAP : (core + 1) * CAP]


def place(blocks, spots, rows):
    vmem = pl.BlockSpec(memory_space=pltpu.VMEM)
    earlier = [] if isinstance(rows, tuple) else [rows]
    shape = rows.shape if earlier else rows
    return pl.pallas_call(
        functools.partial(place_kernel, spots),
        in_specs=[vmem] * (len(blocks) + len(earlier)),
        out_specs=vmem,
        out_shape=pltpu.VMEM(shape, jnp.bfloat16),
        input_output_aliases={len(blocks): 0} if earlier else {},
        compiler_params=pltpu.CompilerParams(vmem_limit_bytes=4 * MIB),
        cost_estimate=SMALL,
        name="place",
    )(*blocks, *earlier)


def place_far_kernel(low_ref, high_ref, _, out_ref):
    middle, row = out_ref.shape[0] // 2, out_ref.shape[0] // 2 - CAP
    out_ref[row : row + CAP] = low_ref[...]
    out_ref[middle + row : middle + row + CAP] = high_ref[...]


def place_far(low, high, rows):
    vmem = pl.BlockSpec(memory_space=pltpu.VMEM)
    return pl.pallas_call(
        place_far_kernel,
        in_specs=[vmem] * 3,
        out_specs=vmem,
        out_shape=pltpu.VMEM(rows.shape, jnp.bfloat16),
        input_output_aliases={2: 0},
        compiler_params=pltpu.CompilerParams(vmem_limit_bytes=4 * MIB),
        cost_estimate=SMALL,
        name="place",
    )(low, high, rows)


def contract(rows_ref, gate_ref, up_ref, gate_sum, up_sum, order):
    half = gate_ref.shape[0]
    depth = min(1024, half)

    def one_part(step, carry):
        columns = pl.ds(pl.multiple_of(step * depth, depth), depth)
        part = order(rows_ref[:, columns])
        gate_sum[...] += jnp.dot(part, gate_ref[columns, :], preferred_element_type=jnp.float32)
        up_sum[...] += jnp.dot(part, up_ref[columns, :], preferred_element_type=jnp.float32)
        return carry

    lax.fori_loop(0, half // depth, one_part, 0)


def first_kernel(me_ref, rows_ref, gate_ref, up_ref, *refs):
    sources, (gate_sum, up_sum), targets, sems = refs[:2], refs[2:4], refs[4:6], refs[6]
    copies = [
        pltpu.make_async_copy(half_rows(me_ref, source, True), target, sems.at[i])
        for i, (source, target) in enumerate(zip(sources, targets))
    ]
    for copy in copies:
        copy.start()
    gate_sum[...] = jnp.zeros_like(gate_sum)
    up_sum[...] = jnp.zeros_like(up_sum)
    contract(rows_ref, gate_ref, up_ref, gate_sum, up_sum, lambda part: part)
    for copy in copies:
        copy.wait()


def second_kernel(rows_ref, gate_ref, up_ref, own_ref, gate_in, up_in, source_ref, out_ref, *refs):
    targets, (gate_sum, up_sum, sems) = refs[:PIECES], refs[PIECES:]
    piece = targets[0].shape[1]
    copies = [
        pltpu.make_async_copy(source_ref.at[:, pl.ds(i * piece, piece)], target, sems.at[i])
        for i, target in enumerate(targets)
    ]
    for copy in copies:
        copy.start()
    middle, half = rows_ref.shape[0] // 2, gate_ref.shape[0]

    def order(part):
        return jnp.concatenate([part[middle:], part[:middle]], axis=0)

    gate_sum[...] = gate_in[...]
    up_sum[...] = up_in[...]
    contract(rows_ref, gate_ref, up_ref, gate_sum, up_sum, order)
    squares = own_ref[:, half:].astype(jnp.float32) + order(rows_ref[:, half:].astype(jnp.float32))
    squares = squares[:, :1] + squares[:, DH // 2 : DH // 2 + 1]
    factor = lax.rsqrt(squares / (2 * half) + 1e-05)
    gate = gate_sum[...] * factor
    out_ref[...] = (gate / (1.0 + jnp.exp(-gate)) * (up_sum[...] * factor)).astype(jnp.bfloat16)
    for copy in copies:
        copy.wait()


def hidden_calls(me, rows, other_rows, loaded, w_gate, w_up, w_down):
    count, units, width = rows.shape[0], w_down.shape[0], w_down.shape[1]
    vmem, anywhere = pl.BlockSpec(memory_space=pltpu.VMEM), pl.BlockSpec(memory_space=pl.ANY)
    sums = [pltpu.VMEM((count, units), jnp.float32)] * 2
    params = pltpu.CompilerParams(vmem_limit_bytes=8 * MIB)
    cost = pl.CostEstimate(
        flops=2 * count * width * units, bytes_accessed=2 * width * units, transcendentals=count * units
    )
    *partial, gate, up = pl.pallas_call(
        first_kernel,
        in_specs=[pl.BlockSpec(memory_space=pltpu.SMEM)] + [vmem] * 3 + [anywhere] * 2,
        out_specs=[vmem] * 2 + [anywhere] * 2,
        out_shape=sums + [pltpu.VMEM((width // 2, units), w_gate.dtype)] * 2,
        scratch_shapes=[pltpu.SemaphoreType.DMA((2,))],
        compiler_params=params,
        cost_estimate=cost,
        name="hidden_first",
    )(me, rows, *loaded, in_hbm(w_gate), in_hbm(w_up))
    hidden, *downs = pl.pallas_call(
        second_kernel,
        in_specs=[vmem] * 6 + [anywhere],
        out_specs=[vmem] + [anywhere] * PIECES,
        out_shape=[pltpu.VMEM((count, units), jnp.bfloat16)]
        + [pltpu.VMEM((units, width // PIECES), w_down.dtype)] * PIECES,
        scratch_shapes=sums + [pltpu.SemaphoreType.DMA((PIECES,))],
        compiler_params=params,
        cost_estimate=cost,
        name="hidden_second",
    )(other_rows, gate, up, rows, *partial, in_hbm(w_down))
    return hidden, downs


def down_kernel(hidden_ref, down_ref, *refs):
    copies = []
    if len(refs) == 2:
        own_ref, sib_ref = refs
    else:
        me_ref, *parts, own_ref, sib_ref, result_ref, sems = refs
        width = parts[0].shape[1]
        core = me_ref[0] % 2
        for i, (side, source) in enumerate(zip((core, 1 - core), parts)):
            columns = pl.ds(pl.multiple_of(side * width, width), width)
            copies.append(pltpu.make_async_copy(source, result_ref.at[:, columns], sems.at[i]))
    for copy in copies:
        copy.start()
    middle, width = own_ref.shape
    cols = min(1024, width)

    def one_part(step, carry):
        columns = pl.ds(pl.multiple_of(step * cols, cols), cols)
        part = jnp.dot(hidden_ref[...], down_ref[:, columns], preferred_element_type=jnp.float32)
        part = part.astype(jnp.bfloat16)
        own_ref[:, columns] = part[:middle]
        sib_ref[:, columns] = part[middle:]
        return carry

    lax.fori_loop(0, width // cols, one_part, 0)
    for copy in copies:
        copy.wait()


def down_call(hidden, w_down, halves=()):
    rows, units = hidden.shape
    width = w_down.shape[1]
    vmem, anywhere = pl.BlockSpec(memory_space=pltpu.VMEM), pl.BlockSpec(memory_space=pl.ANY)
    more = [pl.BlockSpec(memory_space=pltpu.SMEM), anywhere, anywhere] if halves else []
    outs = [pltpu.VMEM((rows // 2, width), jnp.bfloat16)] * 2
    if halves:
        tokens, part = halves[1].shape
        outs.append(jax.ShapeDtypeStruct((tokens, 2 * part), jnp.bfloat16))
    return pl.pallas_call(
        down_kernel,
        in_specs=[vmem] * 2 + more,
        out_specs=[vmem] * 2 + [anywhere] * (len(outs) - 2),
        out_shape=outs,
        scratch_shapes=[pltpu.SemaphoreType.DMA((2,))] if halves else [],
        compiler_params=pltpu.CompilerParams(vmem_limit_bytes=8 * MIB),
        cost_estimate=pl.CostEstimate(
            flops=2 * rows * width * units,
            bytes_accessed=2 * width * units + 2 * rows * width,
            transcendentals=0,
        ),
        name="down",
    )(hidden, w_down, *halves)


def spread_kernel(a_ref, b_ref, c_ref, d_ref, table_ref, *rest):
    out_ref = rest[-1]
    total = a_ref[...].astype(jnp.float32) + b_ref[...].astype(jnp.float32)
    total += c_ref[...].astype(jnp.float32) + d_ref[...].astype(jnp.float32)
    total = total.astype(jnp.bfloat16)
    out_ref[...] = lax.dot_general(
        table_ref[...],
        jnp.concatenate([total] * PARTS, axis=0),
        (((0,), (0,)), ((), ())),
        preferred_element_type=jnp.float32,
    ).astype(jnp.bfloat16)


def spread_call(parts, table, piece, pieces, previous):
    tokens = table.shape[1]
    piece_width = parts[0].shape[1]
    cols = min(2048, piece_width)
    steps = piece_width // cols
    earlier = [] if previous is None else [previous]
    return pl.pallas_call(
        spread_kernel,
        grid=(steps,),
        in_specs=[pl.BlockSpec((CAP, cols), lambda i: (0, i))] * 4
        + [pl.BlockSpec((PARTS * CAP, tokens), lambda i: (0, 0))]
        + [pl.BlockSpec(memory_space=pl.ANY)] * len(earlier),
        out_specs=pl.BlockSpec((tokens, cols), lambda i: (0, piece * steps + i)),
        out_shape=jax.ShapeDtypeStruct((tokens, piece_width * pieces), jnp.bfloat16),
        input_output_aliases={5: 0} if earlier else {},
        compiler_params=pltpu.CompilerParams(
            dimension_semantics=("arbitrary",), vmem_limit_bytes=16 * MIB
        ),
        name="spread",
    )(*parts, table, *earlier)


def add_kernel(row, columns, place, mine_ref, other_ref, *refs):
    received_ref, out_ref = (refs[0] if len(refs) > 1 else None), refs[-1]
    rows = slice(row, row + CAP)
    total = mine_ref[rows, columns].astype(jnp.float32) + other_ref[rows, columns].astype(jnp.float32)
    if received_ref is None:
        out_ref[...] = total.astype(jnp.bfloat16)
        return
    start, width = place, received_ref.shape[1]
    part = total[:, start : start + width] + received_ref[...].astype(jnp.float32)
    out_ref[:, start : start + width] = part.astype(jnp.bfloat16)
    if width < out_ref.shape[1]:
        rest = slice(width, None) if start == 0 else slice(0, start)
        out_ref[:, rest] = total[:, rest].astype(jnp.bfloat16)


def add_call(mine, other, index, columns, received=None, place=0):
    vmem = pl.BlockSpec(memory_space=pltpu.VMEM)
    more = () if received is None else (received,)
    return pl.pallas_call(
        functools.partial(add_kernel, index * CAP, columns, place),
        in_specs=[vmem] * (2 + len(more)),
        out_specs=vmem,
        out_shape=pltpu.VMEM((CAP, columns.stop - columns.start), jnp.bfloat16),
        compiler_params=pltpu.CompilerParams(vmem_limit_bytes=4 * MIB),
        cost_estimate=SMALL,
        name="add",
    )(mine, other, *more)


def reduce_chip_rows(pieces, half, chips, moves, token):
    width = pieces[0][0].shape[1]
    middle = width // 2
    chains = [(piece, side) for piece in range(len(pieces)) for side in range(2)]
    received = [None] * len(chains)
    for distance in range(half, 0, -1):
        for i, (piece, side) in enumerate(chains):
            mine, other = pieces[piece]
            if distance == half:
                columns = slice(side * middle, (side + 1) * middle)
                total = add_call(mine, other, chips - 1, columns)
            else:
                received[i], token = lax.optimization_barrier((received[i], token))
                index = distance if side else half - 1 + distance
                place = side * middle if distance == half - 1 else 0
                total = add_call(mine, other, index, slice(0, width), received[i], place)
            received[i] = moves[side](total)
    return [(*pieces[p], *received[2 * p : 2 * p + 2]) for p in range(len(pieces))]


def per_device(chips, queries, keys, values, norm_gain, expert_ids, gates, w_gate, w_up, w_down):
    right, left, sibling = permutations(chips)
    half = chips // 2
    go_right = lambda x: lax.ppermute(x, "ctx", right)
    go_left = lambda x: lax.ppermute(x, "ctx", left)
    swap = lambda x: lax.ppermute(x, "ctx", sibling)

    me = lax.axis_index("ctx").astype(jnp.int32).reshape(1)
    tokens = queries.shape[0]
    hits = (expert_ids == 0).astype(jnp.float32)
    chosen = jnp.sum(hits, axis=1)
    position = jnp.arange(tokens, dtype=jnp.int32)
    before = (position[None, :] < position[:, None]).astype(jnp.float32)
    slot = jnp.sum(before * chosen[None, :], axis=1).astype(jnp.int32)
    table = jnp.logical_and(
        slot[None, :] == jnp.arange(CAP, dtype=jnp.int32)[:, None], chosen[None, :] > 0
    ).astype(jnp.float32)
    rest = jnp.sum(gates * hits, axis=1)
    weights = []
    for _ in range(PARTS):
        part = lax.reduce_precision(rest, 8, 7)
        weights.append(table * part[None, :])
        rest = rest - part
    weighted = jnp.concatenate(weights, axis=0).astype(jnp.bfloat16)
    table = table.astype(jnp.bfloat16)

    own, give, q_own, q_give = halves(me, (keys, values), (queries,))
    across_right, across_left = [
        lax.ppermute(give, "ctx", [(i, j ^ 1) for i, j in pairs]) for pairs in (right, left)
    ]
    chains = [(go_right(own), go_left(own)), (across_right, across_left)]
    sib, q_sib = swap(give), swap(q_give)
    sib_table = swap(table)
    attention = Attention(me, (q_own, q_sib), chips)
    state, shift, _ = attention.own(own, sib)
    sources = [own, sib]
    for step in range(1, half):
        *chains[0], state = lax.optimization_barrier((*chains[0], state))
        chains[1], _, state = lax.optimization_barrier((chains[1], chains[0], state))
        blocks = [chain[side] for side in range(2) for chain in chains]
        sources += blocks
        if step < half - 1:
            chains = [(go_right(chain[0]), go_left(chain[1])) for chain in chains]
        else:
            far_sib = go_right(chains[1][0][:tokens]), go_left(chains[1][1][tokens:])
            opposite = [go_right(chains[0][0]), *far_sib]
        state, _ = attention.step(blocks, [step, step, -step, -step], shift, state)
    opposite, state = lax.optimization_barrier((opposite, state))
    sources += opposite
    mine, theirs, picked = attention.last(
        opposite, shift, state, norm_gain[None, :], (table, sib_table), sources
    )

    picked, w_gate = lax.optimization_barrier((picked, w_gate))
    from_left, from_right = go_right(picked), go_left(picked)
    rows = place([picked], [0], (2 * chips * CAP, picked.shape[1]))
    loaded, theirs = [load(me, w_gate)], swap(theirs)
    for step in range(1, half):
        from_left, rows, loaded = lax.optimization_barrier((from_left, rows, loaded))
        from_right, _, rows = lax.optimization_barrier((from_right, from_left, rows))
        blocks = [from_left, from_right]
        if step < half - 1:
            from_left, from_right = go_right(from_left), go_left(from_right)
        else:
            far = go_right(from_left[:CAP]), go_left(from_right[CAP:])
        rows = place(blocks, [step, half - 1 + step], rows)
        if step == 1:
            rows, w_up = lax.optimization_barrier((rows, w_up))
            loaded = loaded + [load(me, w_up)]
    far, rows = lax.optimization_barrier((far, rows))
    rows = place_far(*far, rows)
    hidden, downs = hidden_calls(me, rows, swap(rows), loaded, w_gate, w_up, w_down)

    partial = []
    for piece in range(PIECES):
        if piece == 0:
            own, sib, result = down_call(hidden, downs[piece], (me, mine, theirs))
        else:
            own, sib = down_call(hidden, downs[piece])
        partial.append((own, swap(sib)))
    mixed = None
    for piece, parts in enumerate(reduce_chip_rows(partial, half, chips, (go_right, go_left), weighted)):
        mixed = spread_call(parts, weighted, piece, PIECES, mixed)
    return (result, mixed)


def solution(mesh):
    placed = (
        P(("groups", "ctx"), None),
        P(("groups", "ctx"), None),
        P(("groups", "ctx"), None),
        P(),
        P(("groups", "ctx"), None),
        P(("groups", "ctx"), None),
        P(None, "ctx"),
        P(None, "ctx"),
        P("ctx", None),
    )
    return jax.shard_map(
        functools.partial(per_device, mesh.shape["ctx"] // 2),
        mesh=mesh,
        in_specs=placed,
        out_specs=(P(("groups", "ctx"), None), P(("groups", "ctx"), None)),
        check_vma=False,
    )
```

```python
import functools
import math

import jax
import jax.numpy as jnp
from jax import lax
from jax.experimental import pallas as pl
from jax.experimental.pallas import tpu as pltpu
from jax.sharding import PartitionSpec as P

HQ = 64
HK = 8
DH = 128
CAP = 16
GROUP = HQ // HK
WIDE = GROUP * DH
LOG_SCALE = math.log2(math.e) / math.sqrt(DH)
MASKED = -1e30
PIECES = 2
ATTEND_MIB = 11
SMALL = pl.CostEstimate(flops=1, bytes_accessed=1, transcendentals=0)
SUM_LIMIT = 2.0**100
PARTS = 3
STACK = 4
MIB = 1 << 20


def in_hbm(x):
    return pltpu.with_memory_space_constraint(x, pltpu.HBM)


def ring_order(chips):
    return list(range(0, chips, 2)) + list(range(1, chips, 2))[::-1]


def permutations(chips):
    order = ring_order(chips)
    right, left = [], []
    for place in range(chips):
        here, there = order[place], order[(place + 1) % chips]
        for core in range(2):
            right.append((2 * here + core, 2 * there + core))
            left.append((2 * there + core, 2 * here + core))
    sibling = [(i, i ^ 1) for i in range(2 * chips)]
    return right, left, sibling


def chip_at(me, step, chips):
    chip = me // 2
    place = jnp.where(chip % 2 == 0, chip // 2, chips - 1 - chip // 2)
    source = (place - step + 2 * chips) % chips
    return jnp.where(source < chips // 2, 2 * source, 2 * (chips - 1 - source) + 1)


def head_rows(own, sib, first):
    pieces = []
    for h in range(first, first + STACK):
        columns = slice(h * DH, (h + 1) * DH)
        pieces += [own[:, columns], sib[:, columns]]
    return jnp.concatenate(pieces, axis=0)


def with_ones(values):
    return jnp.concatenate([values, jnp.ones_like(values)], axis=1)


def scores_of(queries, keys):
    return LOG_SCALE * lax.dot_general(
        queries, keys, (((1,), (1,)), ((), ())), preferred_element_type=jnp.float32
    )


def weights_of(scores, shift):
    return jnp.exp2(scores - jnp.concatenate([shift] * (scores.shape[1] // DH), axis=1))


def row_top(scores):
    return jnp.broadcast_to(jnp.max(scores, axis=1, keepdims=True), (scores.shape[0], DH))


def allowed_here(core, tokens):
    rows, columns = STACK * 2 * tokens, 2 * tokens

    def position(axis):
        place = lax.broadcasted_iota(jnp.int32, (rows, columns), axis) % (2 * tokens)
        return jnp.where(place < tokens, core * tokens + place, (1 - core) * tokens + place - tokens)

    return position(1) <= position(0)


def group_queries(queries, group):
    columns = pl.ds(pl.multiple_of(group * WIDE, WIDE), WIDE)
    return [ref[:, columns] for ref in queries]


def for_groups(body):
    def step(group, carry):
        body(group, pl.ds(pl.multiple_of(group * DH, DH), DH))
        return carry

    lax.fori_loop(0, HK // 2, step, 0)


def fold(queries, first, keys, values, shift):
    scores = scores_of(head_rows(*queries, first), keys)
    return jnp.dot(
        weights_of(scores, shift).astype(jnp.bfloat16), values, preferred_element_type=jnp.float32
    )


def block_of(ref, columns):
    if isinstance(ref, tuple):
        return ref[0][:, columns], ref[1][:, columns]
    tokens = ref.shape[0] // 2
    return ref[:tokens, columns], ref[tokens:, columns]


def join_blocks(refs, factors, columns):
    pairs = [block_of(ref, columns) for ref in refs]
    keys = jnp.concatenate([key for key, _ in pairs], axis=0)
    values = [with_ones(value) * factor for (_, value), factor in zip(pairs, factors)]
    return keys, jnp.concatenate(values, axis=0)


def factors_of(me, places, chips):
    flags = [chip_at(me, place, chips) < me // 2 for place in places]
    return flags, [jnp.where(flag, 1.0, 0.0).astype(jnp.bfloat16) for flag in flags]


def chunks(tokens):
    size = STACK * 2 * tokens
    return [(first, slice(first // STACK * size, (first // STACK + 1) * size)) for first in range(0, GROUP, STACK)]


def own_kernel(loads, me_ref, q_ref, sib_q_ref, own_ref, sib_ref, *refs):
    acc_ref, total_ref, shift_ref = refs[loads : loads + 3]
    copies = start_loads(loads, refs[:loads], refs[loads + 3 :])
    tokens = q_ref.shape[0]
    allowed = allowed_here(me_ref[0] % 2, tokens)

    def one_group(group, columns):
        keys, values = join_blocks((own_ref, sib_ref), (1, 1), columns)
        queries = group_queries((q_ref, sib_q_ref), group)
        for first, rows in chunks(tokens):
            scores = jnp.where(allowed, scores_of(head_rows(*queries, first), keys), MASKED)
            shift = row_top(scores)
            weights = weights_of(scores, shift).astype(jnp.bfloat16)
            update = jnp.dot(weights, values, preferred_element_type=jnp.float32)
            acc_ref[group, rows, :] = update[:, :DH]
            total_ref[group, rows, :] = update[:, DH:]
            shift_ref[group, rows, :] = shift

    for_groups(one_group)
    for copy in copies:
        copy.wait()


def start_loads(loads, sources, rest):
    copies = [
        pltpu.make_async_copy(source, target, sem)
        for source, target, sem in zip(sources, rest[:loads], rest[loads : 2 * loads])
    ]
    for copy in copies:
        copy.start()
    return copies


def step_kernel(chips, places, loads, me_ref, q_ref, sib_q_ref, *refs):
    count = len(places)
    blocks, shift_ref = refs[:count], refs[count]
    refs = refs[count + 3 :]
    acc_ref, total_ref = refs[loads : loads + 2]
    copies = start_loads(loads, refs[:loads], refs[loads + 2 :])
    tokens = q_ref.shape[0]
    flags, factors = factors_of(me_ref[0], places, chips)

    @pl.when(functools.reduce(jnp.logical_or, flags))
    def _():
        def one_group(group, columns):
            keys, values = join_blocks(blocks, factors, columns)
            queries = group_queries((q_ref, sib_q_ref), group)
            for first, rows in chunks(tokens):
                update = fold(queries, first, keys, values, shift_ref[group, rows, :])
                acc_ref[group, rows, :] += update[:, :DH]
                total_ref[group, rows, :] += update[:, DH:]

        for_groups(one_group)

    for copy in copies:
        copy.wait()


def divide(acc, total):
    inverse = pl.reciprocal(total, approx=True)
    inverse = inverse * (2.0 - total * inverse)
    return (acc * inverse).astype(jnp.bfloat16)


def put_heads(out_refs, rows_ref, tables, group, result):
    tokens = out_refs[0].shape[0]
    columns = pl.ds(pl.multiple_of(group * WIDE, WIDE), WIDE)
    for i, (out_ref, table) in enumerate(zip(out_refs, tables)):
        pieces = [
            result[(2 * h + i) * tokens : (2 * h + i + 1) * tokens] for h in range(GROUP)
        ]
        piece = jnp.concatenate(pieces, axis=1)
        out_ref[:, columns] = piece
        rows_ref[i * CAP : (i + 1) * CAP, columns] = jnp.dot(
            table[...], piece, preferred_element_type=jnp.float32
        )


def running_attention(chips, me, sources, q_refs, put, scratch, sem):
    keys_ref, values_ref, acc_ref, total_ref, top_ref = scratch
    tokens = q_refs[0].shape[0]

    def fetch(source, target):
        copy = pltpu.make_async_copy(source, target, sem)
        copy.start()
        copy.wait()

    def one_group(group, columns):
        queries = group_queries(q_refs, group)
        for i in range(chips - 1):
            for j, block in enumerate(sources[2 * i : 2 * i + 2]):
                rows = pl.ds(j * tokens, tokens)
                fetch(block.at[pl.ds(0, tokens), columns], keys_ref.at[i, rows])
                fetch(block.at[pl.ds(tokens, tokens), columns], values_ref.at[i, rows])
        whole, key, value = sources[2 * chips - 2 :]
        own, sib = pl.ds(0, tokens), pl.ds(tokens, tokens)
        fetch(whole.at[own, columns], keys_ref.at[chips - 1, own])
        fetch(whole.at[sib, columns], values_ref.at[chips - 1, own])
        fetch(key.at[:, columns], keys_ref.at[chips - 1, sib])
        fetch(value.at[:, columns], values_ref.at[chips - 1, sib])
        acc_ref[...] = jnp.zeros_like(acc_ref)
        total_ref[...] = jnp.zeros_like(total_ref)
        top_ref[...] = jnp.full_like(top_ref, 2 * MASKED)

        def one_chip(i, inner):
            place = jnp.where(i % 2 == 1, (i + 1) // 2, -(i // 2))
            chip = chip_at(me, place, chips)

            @pl.when(chip <= me // 2)
            def _():
                keys, values = keys_ref[i], with_ones(values_ref[i])
                barred = jnp.where(chip == me // 2, MASKED, 0.0)
                bias = jnp.where(allowed_here(me % 2, tokens), 0.0, barred)
                for first, rows in chunks(tokens):
                    scores = scores_of(head_rows(*queries, first), keys)
                    scores = jnp.where(bias < 0.0, MASKED, scores)
                    old = top_ref[rows, :]
                    top = jnp.maximum(old, row_top(scores))
                    factor = jnp.exp2(old - top)
                    weights = weights_of(scores, top).astype(jnp.bfloat16)
                    update = jnp.dot(weights, values, preferred_element_type=jnp.float32)
                    acc_ref[rows, :] = acc_ref[rows, :] * factor + update[:, :DH]
                    total_ref[rows, :] = total_ref[rows, :] * factor + update[:, DH:]
                    top_ref[rows, :] = top

            return inner

        lax.fori_loop(0, chips, one_chip, 0)
        put(group, divide(acc_ref[...], total_ref[...]))

    for_groups(one_group)


def last_kernel(chips, me_ref, q_ref, sib_q_ref, *refs):
    blocks, (shift_ref, acc_ref, total_ref, gain_ref) = (refs[0], refs[1:3]), refs[3:7]
    tables, sources = refs[7:9], refs[9 : 10 + 2 * chips]
    refs = refs[10 + 2 * chips :]
    weights, refs = refs[:2], refs[2:]
    out_refs, picked_refs, loaded = refs[:2], refs[2:4], refs[4:6]
    rows_ref, worst_ref, sem, load_sems, *scratch = refs[6:]
    loads = [
        pltpu.make_async_copy(half_rows(me_ref, weight, False), target, load_sems.at[i])
        for i, (weight, target) in enumerate(zip(weights, loaded))
    ]
    for load in loads:
        load.start()
    q_refs = (q_ref, sib_q_ref)
    tokens, half_width = q_ref.shape
    me = me_ref[0]
    _, factors = factors_of(me, [chips // 2] * 2, chips)
    worst_ref[...] = jnp.zeros_like(worst_ref)

    def put(group, result):
        put_heads(out_refs, rows_ref, tables, group, result)

    def one_group(group, columns):
        keys, values = join_blocks(blocks, factors, columns)
        queries = group_queries(q_refs, group)
        results = []
        for first, rows in chunks(tokens):
            update = fold(queries, first, keys, values, shift_ref[group, rows, :])
            total = total_ref[group, rows, :] + update[:, DH:]
            worst_ref[...] = jnp.maximum(worst_ref[...], total)
            results.append(divide(acc_ref[group, rows, :] + update[:, :DH], total))
        put(group, jnp.concatenate(results, axis=0))

    for_groups(one_group)
    fits = jnp.max(worst_ref[...]) <= SUM_LIMIT

    @pl.when(jnp.logical_not(fits))
    def _():
        running_attention(chips, me, sources, q_refs, put, scratch, sem)

    columns = pl.ds(pl.multiple_of(me % 2 * half_width, half_width), half_width)
    rows = rows_ref[...]
    squares = jnp.broadcast_to(jnp.sum(rows * rows, axis=1, keepdims=True), (2 * CAP, DH))
    upper = squares.astype(jnp.bfloat16).astype(jnp.float32)
    lower = (squares - upper).astype(jnp.bfloat16).astype(jnp.float32)
    lane = lax.broadcasted_iota(jnp.int32, squares.shape, 1)
    rows = (rows * gain_ref[:, columns]).astype(jnp.bfloat16)
    squares = jnp.where(lane < DH // 2, upper, lower).astype(jnp.bfloat16)
    for i, ref in enumerate(picked_refs):
        ref[:, :half_width] = rows[i * CAP : (i + 1) * CAP]
        ref[:, half_width:] = squares[i * CAP : (i + 1) * CAP]
    for load in loads:
        load.wait()


class Attention:
    def __init__(self, me, queries, chips):
        self.me, self.queries, self.chips = me, queries, chips
        self.tokens, self.width = queries[0].shape
        self.rows = 2 * GROUP * self.tokens
        self.state_shape = pltpu.VMEM((HK // 2, self.rows, DH), jnp.float32)

    def call(self, kernel, name, args, others, out_shape, out_others, scratch, aliases=None):
        vmem, anywhere = pl.BlockSpec(memory_space=pltpu.VMEM), pl.BlockSpec(memory_space=pl.ANY)
        return pl.pallas_call(
            kernel,
            in_specs=[pl.BlockSpec(memory_space=pltpu.SMEM)]
            + [vmem] * (2 + len(args))
            + [anywhere] * len(others),
            out_specs=[vmem] * len(out_shape) + [anywhere] * len(out_others),
            out_shape=[*out_shape, *out_others],
            scratch_shapes=scratch,
            input_output_aliases=aliases or {},
            compiler_params=pltpu.CompilerParams(vmem_limit_bytes=ATTEND_MIB * MIB),
            cost_estimate=SMALL,
            name=name,
        )(self.me, *self.queries, *args, *others)

    def own(self, own, sib, weights=()):
        loads = len(weights)
        results = self.call(
            functools.partial(own_kernel, loads),
            "attend_own",
            (own, sib),
            [in_hbm(x) for x in weights],
            [self.state_shape] * 3,
            [pltpu.VMEM(x.shape, x.dtype) for x in weights],
            [pltpu.SemaphoreType.DMA] * loads,
        )
        return list(results[:2]), results[2], results[3:]

    def step(self, blocks, places, shift, state, weights=()):
        count, loads = len(blocks), len(weights)
        results = self.call(
            functools.partial(step_kernel, self.chips, places, loads),
            "attend_step",
            (*blocks, shift, *state),
            [in_hbm(x) for x in weights],
            [self.state_shape] * 2,
            [pltpu.VMEM(x.shape, x.dtype) for x in weights],
            [pltpu.SemaphoreType.DMA] * loads,
            {count + 4: 0, count + 5: 1},
        )
        return list(results[:2]), results[2:]

    def last(self, blocks, shift, state, gain, tables, sources, weights):
        out = pltpu.VMEM((self.tokens, self.width), jnp.bfloat16)
        picked = pltpu.VMEM((CAP, self.width + DH), jnp.bfloat16)
        loaded = [pltpu.VMEM((x.shape[0] // 2, x.shape[1]), x.dtype) for x in weights]
        kept = pltpu.VMEM((self.chips, 2 * self.tokens, DH), jnp.bfloat16)
        sums = pltpu.VMEM((self.rows, DH), jnp.float32)
        return self.call(
            functools.partial(last_kernel, self.chips),
            "attend_last",
            (*blocks, shift, *state, gain, *tables),
            (*sources, *(in_hbm(x) for x in weights)),
            [out, out, picked, picked],
            loaded,
            [
                pltpu.VMEM((2 * CAP, self.width), jnp.float32),
                pltpu.VMEM((STACK * 2 * self.tokens, DH), jnp.float32),
                pltpu.SemaphoreType.DMA,
                pltpu.SemaphoreType.DMA((len(weights),)),
                kept,
                kept,
                sums,
                sums,
                sums,
            ],
        )


def halves_kernel(stacks, me_ref, *refs):
    count = sum(stacks)
    sources, outs, sems = list(refs[:count]), refs[count:-1], refs[-1]
    core = me_ref[0] % 2
    copies = []
    for size, keep_ref, give_ref in zip(stacks, outs[::2], outs[1::2]):
        for i in range(size):
            source = sources.pop(0)
            rows, width = source.shape
            for side, target in ((core, keep_ref), (1 - core, give_ref)):
                columns = pl.ds(pl.multiple_of(side * (width // 2), width // 2), width // 2)
                copies.append((source.at[:, columns], target.at[pl.ds(i * rows, rows)]))
    copies = [pltpu.make_async_copy(*ends, sems.at[i]) for i, ends in enumerate(copies)]
    for copy in copies:
        copy.start()
    for copy in copies:
        copy.wait()


def halves(me, *stacks):
    anywhere = pl.BlockSpec(memory_space=pl.ANY)
    arrays = [x for stack in stacks for x in stack]
    outs = []
    for stack in stacks:
        rows, width = stack[0].shape
        outs += [pltpu.VMEM((len(stack) * rows, width // 2), stack[0].dtype)] * 2
    return pl.pallas_call(
        functools.partial(halves_kernel, [len(stack) for stack in stacks]),
        in_specs=[pl.BlockSpec(memory_space=pltpu.SMEM)] + [anywhere] * len(arrays),
        out_specs=[anywhere] * len(outs),
        out_shape=outs,
        scratch_shapes=[pltpu.SemaphoreType.DMA((2 * len(arrays),))],
        compiler_params=pltpu.CompilerParams(vmem_limit_bytes=MIB),
        cost_estimate=SMALL,
        name="halves",
    )(me, *(in_hbm(x) for x in arrays))


def half_rows(me_ref, ref, sibling):
    half = ref.shape[0] // 2
    side = 1 - me_ref[0] % 2 if sibling else me_ref[0] % 2
    return ref.at[pl.ds(pl.multiple_of(side * half, half), half), :]


def place_kernel(spots, *refs):
    blocks, out_ref = refs[: len(spots)], refs[-1]
    for index, ref in zip(spots, blocks):
        out_ref[index * CAP : (index + 1) * CAP] = ref[...]


def place(blocks, spots, rows):
    vmem = pl.BlockSpec(memory_space=pltpu.VMEM)
    earlier = [] if isinstance(rows, tuple) else [rows]
    shape = rows.shape if earlier else rows
    return pl.pallas_call(
        functools.partial(place_kernel, spots),
        in_specs=[vmem] * (len(blocks) + len(earlier)),
        out_specs=vmem,
        out_shape=pltpu.VMEM(shape, jnp.bfloat16),
        input_output_aliases={len(blocks): 0} if earlier else {},
        compiler_params=pltpu.CompilerParams(vmem_limit_bytes=4 * MIB),
        cost_estimate=SMALL,
        name="place",
    )(*blocks, *earlier)


def contract(rows_ref, gate_ref, up_ref, gate_sum, up_sum, order):
    half = gate_ref.shape[0]
    depth = min(1024, half)

    def one_part(step, carry):
        columns = pl.ds(pl.multiple_of(step * depth, depth), depth)
        part = order(rows_ref[:, columns])
        gate_sum[...] += jnp.dot(part, gate_ref[columns, :], preferred_element_type=jnp.float32)
        up_sum[...] += jnp.dot(part, up_ref[columns, :], preferred_element_type=jnp.float32)
        return carry

    lax.fori_loop(0, half // depth, one_part, 0)


def first_kernel(me_ref, rows_ref, gate_ref, up_ref, *refs):
    sources, (gate_sum, up_sum), targets, sems = refs[:2], refs[2:4], refs[4:6], refs[6]
    copies = [
        pltpu.make_async_copy(half_rows(me_ref, source, True), target, sems.at[i])
        for i, (source, target) in enumerate(zip(sources, targets))
    ]
    for copy in copies:
        copy.start()
    gate_sum[...] = jnp.zeros_like(gate_sum)
    up_sum[...] = jnp.zeros_like(up_sum)
    contract(rows_ref, gate_ref, up_ref, gate_sum, up_sum, lambda part: part)
    for copy in copies:
        copy.wait()


def second_kernel(rows_ref, gate_ref, up_ref, own_ref, gate_in, up_in, source_ref, out_ref, *refs):
    targets, (gate_sum, up_sum, sems) = refs[:PIECES], refs[PIECES:]
    piece = targets[0].shape[1]
    copies = [
        pltpu.make_async_copy(source_ref.at[:, pl.ds(i * piece, piece)], target, sems.at[i])
        for i, target in enumerate(targets)
    ]
    for copy in copies:
        copy.start()
    middle, half = rows_ref.shape[0] // 2, gate_ref.shape[0]

    def order(part):
        return jnp.concatenate([part[middle:], part[:middle]], axis=0)

    gate_sum[...] = gate_in[...]
    up_sum[...] = up_in[...]
    contract(rows_ref, gate_ref, up_ref, gate_sum, up_sum, order)
    squares = own_ref[:, half:].astype(jnp.float32) + order(rows_ref[:, half:].astype(jnp.float32))
    squares = squares[:, :1] + squares[:, DH // 2 : DH // 2 + 1]
    factor = lax.rsqrt(squares / (2 * half) + 1e-05)
    gate = gate_sum[...] * factor
    out_ref[...] = (gate / (1.0 + jnp.exp(-gate)) * (up_sum[...] * factor)).astype(jnp.bfloat16)
    for copy in copies:
        copy.wait()


def hidden_calls(me, rows, other_rows, loaded, w_gate, w_up, w_down):
    count, units, width = rows.shape[0], w_down.shape[0], w_down.shape[1]
    vmem, anywhere = pl.BlockSpec(memory_space=pltpu.VMEM), pl.BlockSpec(memory_space=pl.ANY)
    sums = [pltpu.VMEM((count, units), jnp.float32)] * 2
    params = pltpu.CompilerParams(vmem_limit_bytes=8 * MIB)
    cost = pl.CostEstimate(
        flops=2 * count * width * units, bytes_accessed=2 * width * units, transcendentals=count * units
    )
    *partial, gate, up = pl.pallas_call(
        first_kernel,
        in_specs=[pl.BlockSpec(memory_space=pltpu.SMEM)] + [vmem] * 3 + [anywhere] * 2,
        out_specs=[vmem] * 2 + [anywhere] * 2,
        out_shape=sums + [pltpu.VMEM((width // 2, units), w_gate.dtype)] * 2,
        scratch_shapes=[pltpu.SemaphoreType.DMA((2,))],
        compiler_params=params,
        cost_estimate=cost,
        name="hidden_first",
    )(me, rows, *loaded, in_hbm(w_gate), in_hbm(w_up))
    hidden, *downs = pl.pallas_call(
        second_kernel,
        in_specs=[vmem] * 6 + [anywhere],
        out_specs=[vmem] + [anywhere] * PIECES,
        out_shape=[pltpu.VMEM((count, units), jnp.bfloat16)]
        + [pltpu.VMEM((units, width // PIECES), w_down.dtype)] * PIECES,
        scratch_shapes=sums + [pltpu.SemaphoreType.DMA((PIECES,))],
        compiler_params=params,
        cost_estimate=cost,
        name="hidden_second",
    )(other_rows, gate, up, rows, *partial, in_hbm(w_down))
    return hidden, downs


def down_kernel(hidden_ref, down_ref, *refs):
    copies = []
    if len(refs) == 2:
        own_ref, sib_ref = refs
    else:
        me_ref, *parts, own_ref, sib_ref, result_ref, sems = refs
        width = parts[0].shape[1]
        core = me_ref[0] % 2
        for i, (side, source) in enumerate(zip((core, 1 - core), parts)):
            columns = pl.ds(pl.multiple_of(side * width, width), width)
            copies.append(pltpu.make_async_copy(source, result_ref.at[:, columns], sems.at[i]))
    for copy in copies:
        copy.start()
    middle, width = own_ref.shape
    cols = min(1024, width)

    def one_part(step, carry):
        columns = pl.ds(pl.multiple_of(step * cols, cols), cols)
        part = jnp.dot(hidden_ref[...], down_ref[:, columns], preferred_element_type=jnp.float32)
        part = part.astype(jnp.bfloat16)
        own_ref[:, columns] = part[:middle]
        sib_ref[:, columns] = part[middle:]
        return carry

    lax.fori_loop(0, width // cols, one_part, 0)
    for copy in copies:
        copy.wait()


def down_call(hidden, w_down, halves=()):
    rows, units = hidden.shape
    width = w_down.shape[1]
    vmem, anywhere = pl.BlockSpec(memory_space=pltpu.VMEM), pl.BlockSpec(memory_space=pl.ANY)
    more = [pl.BlockSpec(memory_space=pltpu.SMEM), anywhere, anywhere] if halves else []
    outs = [pltpu.VMEM((rows // 2, width), jnp.bfloat16)] * 2
    if halves:
        tokens, part = halves[1].shape
        outs.append(jax.ShapeDtypeStruct((tokens, 2 * part), jnp.bfloat16))
    return pl.pallas_call(
        down_kernel,
        in_specs=[vmem] * 2 + more,
        out_specs=[vmem] * 2 + [anywhere] * (len(outs) - 2),
        out_shape=outs,
        scratch_shapes=[pltpu.SemaphoreType.DMA((2,))] if halves else [],
        compiler_params=pltpu.CompilerParams(vmem_limit_bytes=8 * MIB),
        cost_estimate=pl.CostEstimate(
            flops=2 * rows * width * units,
            bytes_accessed=2 * width * units + 2 * rows * width,
            transcendentals=0,
        ),
        name="down",
    )(hidden, w_down, *halves)


def spread_kernel(a_ref, b_ref, c_ref, d_ref, table_ref, *rest):
    out_ref = rest[-1]
    total = a_ref[...].astype(jnp.float32) + b_ref[...].astype(jnp.float32)
    total += c_ref[...].astype(jnp.float32) + d_ref[...].astype(jnp.float32)
    total = total.astype(jnp.bfloat16)
    out_ref[...] = lax.dot_general(
        table_ref[...],
        jnp.concatenate([total] * PARTS, axis=0),
        (((0,), (0,)), ((), ())),
        preferred_element_type=jnp.float32,
    ).astype(jnp.bfloat16)


def spread_call(parts, table, piece, pieces, previous):
    tokens = table.shape[1]
    piece_width = parts[0].shape[1]
    cols = min(2048, piece_width)
    steps = piece_width // cols
    earlier = [] if previous is None else [previous]
    return pl.pallas_call(
        spread_kernel,
        grid=(steps,),
        in_specs=[pl.BlockSpec((CAP, cols), lambda i: (0, i))] * 4
        + [pl.BlockSpec((PARTS * CAP, tokens), lambda i: (0, 0))]
        + [pl.BlockSpec(memory_space=pl.ANY)] * len(earlier),
        out_specs=pl.BlockSpec((tokens, cols), lambda i: (0, piece * steps + i)),
        out_shape=jax.ShapeDtypeStruct((tokens, piece_width * pieces), jnp.bfloat16),
        input_output_aliases={5: 0} if earlier else {},
        compiler_params=pltpu.CompilerParams(
            dimension_semantics=("arbitrary",), vmem_limit_bytes=16 * MIB
        ),
        name="spread",
    )(*parts, table, *earlier)


def add_kernel(row, mine_ref, other_ref, *refs):
    rows = slice(row, row + CAP)
    total = mine_ref[rows].astype(jnp.float32) + other_ref[rows].astype(jnp.float32)
    for ref in refs[:-1]:
        total += ref[...].astype(jnp.float32)
    refs[-1][...] = total.astype(jnp.bfloat16)


def add_call(mine, other, index, received=None):
    vmem = pl.BlockSpec(memory_space=pltpu.VMEM)
    more = () if received is None else (received,)
    return pl.pallas_call(
        functools.partial(add_kernel, index * CAP),
        in_specs=[vmem] * (2 + len(more)),
        out_specs=vmem,
        out_shape=pltpu.VMEM((CAP, mine.shape[1]), jnp.bfloat16),
        compiler_params=pltpu.CompilerParams(vmem_limit_bytes=4 * MIB),
        cost_estimate=SMALL,
        name="add",
    )(mine, other, *more)


def reduce_chip_rows(pieces, half, chips, moves, token):
    chains = [(piece, side) for piece in range(len(pieces)) for side in range(2)]
    received = [None] * len(chains)
    for distance in range(half, 0, -1):
        for i, (piece, side) in enumerate(chains):
            if distance == half and piece % 2 != side:
                continue
            if received[i] is not None:
                received[i], token = lax.optimization_barrier((received[i], token))
            index = chips - 1 if distance == half else distance if side else half - 1 + distance
            received[i] = moves[side](add_call(*pieces[piece], index, received[i]))
    return [(*pieces[p], *received[2 * p : 2 * p + 2]) for p in range(len(pieces))]


def per_device(chips, queries, keys, values, norm_gain, expert_ids, gates, w_gate, w_up, w_down):
    right, left, sibling = permutations(chips)
    half = chips // 2
    go_right = lambda x: lax.ppermute(x, "ctx", right)
    go_left = lambda x: lax.ppermute(x, "ctx", left)
    swap = lambda x: lax.ppermute(x, "ctx", sibling)

    me = lax.axis_index("ctx").astype(jnp.int32).reshape(1)
    tokens = queries.shape[0]
    hits = (expert_ids == 0).astype(jnp.float32)
    chosen = jnp.sum(hits, axis=1)
    position = jnp.arange(tokens, dtype=jnp.int32)
    before = (position[None, :] < position[:, None]).astype(jnp.float32)
    slot = jnp.sum(before * chosen[None, :], axis=1).astype(jnp.int32)
    table = jnp.logical_and(
        slot[None, :] == jnp.arange(CAP, dtype=jnp.int32)[:, None], chosen[None, :] > 0
    ).astype(jnp.float32)
    rest = jnp.sum(gates * hits, axis=1)
    weights = []
    for _ in range(PARTS):
        part = lax.reduce_precision(rest, 8, 7)
        weights.append(table * part[None, :])
        rest = rest - part
    weighted = jnp.concatenate(weights, axis=0).astype(jnp.bfloat16)
    table = table.astype(jnp.bfloat16)

    own, give, q_own, q_give = halves(me, (keys, values), (queries,))
    across_right, across_left = [
        lax.ppermute(give, "ctx", [(i, j ^ 1) for i, j in pairs]) for pairs in (right, left)
    ]
    chains = [(go_right(own), go_left(own)), (across_right, across_left)]
    sib, q_sib = swap(give), swap(q_give)
    sib_table = swap(table)
    attention = Attention(me, (q_own, q_sib), chips)
    state, shift, _ = attention.own(own, sib)
    sources = [own, sib]
    for step in range(1, half):
        *chains[0], state = lax.optimization_barrier((*chains[0], state))
        chains[1], _, state = lax.optimization_barrier((chains[1], chains[0], state))
        blocks = [chain[side] for side in range(2) for chain in chains]
        sources += blocks
        if step < half - 1:
            chains = [(go_right(chain[0]), go_left(chain[1])) for chain in chains]
        else:
            far_sib = go_right(chains[1][0][:tokens]), go_left(chains[1][1][tokens:])
            opposite = [go_right(chains[0][0]), *far_sib]
        state, _ = attention.step(blocks, [step, step, -step, -step], shift, state)
    opposite, state = lax.optimization_barrier((opposite, state))
    sources += opposite
    mine, theirs, *picked, gate, up = attention.last(
        opposite, shift, state, norm_gain[None, :], (table, sib_table), sources, (w_gate, w_up)
    )

    moves = (go_right, go_left, go_right, go_left)
    received = [move(picked[i // 2]) for i, move in enumerate(moves)]
    rows = place(picked, [0, chips], (2 * chips * CAP, picked[0].shape[1]))
    theirs = swap(theirs)
    for step in range(1, half):
        blocks, far = [], []
        for i, move in enumerate(moves):
            block, rows = lax.optimization_barrier((received[i], rows))
            blocks.append(block)
            if step < half - 1:
                received[i] = move(block)
            elif i in (0, 3):
                far.append(move(block))
        spots = [core * chips + side * (half - 1) + step for core in range(2) for side in range(2)]
        rows = place(blocks, spots, rows)
    far, rows = lax.optimization_barrier((far, rows))
    rows = place(far, [chips - 1, 2 * chips - 1], rows)
    hidden, downs = hidden_calls(me, rows, swap(rows), (gate, up), w_gate, w_up, w_down)

    partial = []
    for piece in range(PIECES):
        if piece == 0:
            own, sib, result = down_call(hidden, downs[piece], (me, mine, theirs))
        else:
            own, sib = down_call(hidden, downs[piece])
        partial.append((own, swap(sib)))
    mixed = None
    for piece, parts in enumerate(reduce_chip_rows(partial, half, chips, (go_right, go_left), weighted)):
        mixed = spread_call(parts, weighted, piece, PIECES, mixed)
    return (result, mixed)


def solution(mesh):
    placed = (
        P(("groups", "ctx"), None),
        P(("groups", "ctx"), None),
        P(("groups", "ctx"), None),
        P(),
        P(("groups", "ctx"), None),
        P(("groups", "ctx"), None),
        P(None, "ctx"),
        P(None, "ctx"),
        P("ctx", None),
    )
    return jax.shard_map(
        functools.partial(per_device, mesh.shape["ctx"] // 2),
        mesh=mesh,
        in_specs=placed,
        out_specs=(P(("groups", "ctx"), None), P(("groups", "ctx"), None)),
        check_vma=False,
    )
```

```python
import functools
import math

import jax
import jax.numpy as jnp
from jax import lax
from jax.experimental import pallas as pl
from jax.experimental.pallas import tpu as pltpu
from jax.sharding import PartitionSpec as P

HQ = 64
HK = 8
DH = 128
CAP = 16
GROUP = HQ // HK
WIDE = GROUP * DH
LOG_SCALE = math.log2(math.e) / math.sqrt(DH)
MASKED = -1e30
PIECES = 2
ATTEND_MIB = 11
SMALL = pl.CostEstimate(flops=1, bytes_accessed=1, transcendentals=0)
SUM_LIMIT = 2.0**100
PARTS = 3
STACK = 4
MIB = 1 << 20


def in_hbm(x):
    return pltpu.with_memory_space_constraint(x, pltpu.HBM)


def ring_order(chips):
    return list(range(0, chips, 2)) + list(range(1, chips, 2))[::-1]


def permutations(chips):
    order = ring_order(chips)
    right, left = [], []
    for place in range(chips):
        here, there = order[place], order[(place + 1) % chips]
        for core in range(2):
            right.append((2 * here + core, 2 * there + core))
            left.append((2 * there + core, 2 * here + core))
    sibling = [(i, i ^ 1) for i in range(2 * chips)]
    return right, left, sibling


def chip_at(me, step, chips):
    chip = me // 2
    place = jnp.where(chip % 2 == 0, chip // 2, chips - 1 - chip // 2)
    source = (place - step + 2 * chips) % chips
    return jnp.where(source < chips // 2, 2 * source, 2 * (chips - 1 - source) + 1)


def head_rows(own, sib, first):
    pieces = []
    for h in range(first, first + STACK):
        columns = slice(h * DH, (h + 1) * DH)
        pieces += [own[:, columns], sib[:, columns]]
    return jnp.concatenate(pieces, axis=0)


def with_ones(values):
    return jnp.concatenate([values, jnp.ones_like(values)], axis=1)


def scores_of(queries, keys):
    return LOG_SCALE * lax.dot_general(
        queries, keys, (((1,), (1,)), ((), ())), preferred_element_type=jnp.float32
    )


def weights_of(scores, shift):
    return jnp.exp2(scores - jnp.concatenate([shift] * (scores.shape[1] // DH), axis=1))


def row_top(scores):
    return jnp.broadcast_to(jnp.max(scores, axis=1, keepdims=True), (scores.shape[0], DH))


def allowed_here(core, tokens):
    rows, columns = STACK * 2 * tokens, 2 * tokens

    def position(axis):
        place = lax.broadcasted_iota(jnp.int32, (rows, columns), axis) % (2 * tokens)
        return jnp.where(place < tokens, core * tokens + place, (1 - core) * tokens + place - tokens)

    return position(1) <= position(0)


def group_queries(queries, group):
    columns = pl.ds(pl.multiple_of(group * WIDE, WIDE), WIDE)
    return [ref[:, columns] for ref in queries]


def for_groups(body):
    def step(group, carry):
        body(group, pl.ds(pl.multiple_of(group * DH, DH), DH))
        return carry

    lax.fori_loop(0, HK // 2, step, 0)


def fold(queries, first, keys, values, shift):
    scores = scores_of(head_rows(*queries, first), keys)
    return jnp.dot(
        weights_of(scores, shift).astype(jnp.bfloat16), values, preferred_element_type=jnp.float32
    )


def block_of(ref, columns):
    if isinstance(ref, tuple):
        return ref[0][:, columns], ref[1][:, columns]
    tokens = ref.shape[0] // 2
    return ref[:tokens, columns], ref[tokens:, columns]


def join_blocks(refs, factors, columns):
    pairs = [block_of(ref, columns) for ref in refs]
    keys = jnp.concatenate([key for key, _ in pairs], axis=0)
    values = [with_ones(value) * factor for (_, value), factor in zip(pairs, factors)]
    return keys, jnp.concatenate(values, axis=0)


def factors_of(me, places, chips):
    flags = [chip_at(me, place, chips) < me // 2 for place in places]
    return flags, [jnp.where(flag, 1.0, 0.0).astype(jnp.bfloat16) for flag in flags]


def chunks(tokens):
    size = STACK * 2 * tokens
    return [(first, slice(first // STACK * size, (first // STACK + 1) * size)) for first in range(0, GROUP, STACK)]


def own_kernel(loads, me_ref, q_ref, sib_q_ref, own_ref, sib_ref, *refs):
    acc_ref, total_ref, shift_ref = refs[loads : loads + 3]
    copies = start_loads(loads, refs[:loads], refs[loads + 3 :])
    tokens = q_ref.shape[0]
    allowed = allowed_here(me_ref[0] % 2, tokens)

    def one_group(group, columns):
        keys, values = join_blocks((own_ref, sib_ref), (1, 1), columns)
        queries = group_queries((q_ref, sib_q_ref), group)
        for first, rows in chunks(tokens):
            scores = jnp.where(allowed, scores_of(head_rows(*queries, first), keys), MASKED)
            shift = row_top(scores)
            weights = weights_of(scores, shift).astype(jnp.bfloat16)
            update = jnp.dot(weights, values, preferred_element_type=jnp.float32)
            acc_ref[group, rows, :] = update[:, :DH]
            total_ref[group, rows, :] = update[:, DH:]
            shift_ref[group, rows, :] = shift

    for_groups(one_group)
    for copy in copies:
        copy.wait()


def start_loads(loads, sources, rest):
    copies = [
        pltpu.make_async_copy(source, target, sem)
        for source, target, sem in zip(sources, rest[:loads], rest[loads : 2 * loads])
    ]
    for copy in copies:
        copy.start()
    return copies


def step_kernel(chips, places, loads, me_ref, q_ref, sib_q_ref, *refs):
    count = len(places)
    blocks, shift_ref = refs[:count], refs[count]
    refs = refs[count + 3 :]
    acc_ref, total_ref = refs[loads : loads + 2]
    copies = start_loads(loads, refs[:loads], refs[loads + 2 :])
    tokens = q_ref.shape[0]
    flags, factors = factors_of(me_ref[0], places, chips)

    @pl.when(functools.reduce(jnp.logical_or, flags))
    def _():
        def one_group(group, columns):
            keys, values = join_blocks(blocks, factors, columns)
            queries = group_queries((q_ref, sib_q_ref), group)
            for first, rows in chunks(tokens):
                update = fold(queries, first, keys, values, shift_ref[group, rows, :])
                acc_ref[group, rows, :] += update[:, :DH]
                total_ref[group, rows, :] += update[:, DH:]

        for_groups(one_group)

    for copy in copies:
        copy.wait()


def divide(acc, total):
    inverse = pl.reciprocal(total, approx=True)
    inverse = inverse * (2.0 - total * inverse)
    return (acc * inverse).astype(jnp.bfloat16)


def put_heads(out_refs, rows_ref, tables, group, result):
    tokens = out_refs[0].shape[0]
    columns = pl.ds(pl.multiple_of(group * WIDE, WIDE), WIDE)
    for i, (out_ref, table) in enumerate(zip(out_refs, tables)):
        pieces = [
            result[(2 * h + i) * tokens : (2 * h + i + 1) * tokens] for h in range(GROUP)
        ]
        piece = jnp.concatenate(pieces, axis=1)
        out_ref[:, columns] = piece
        rows_ref[i * CAP : (i + 1) * CAP, columns] = jnp.dot(
            table[...], piece, preferred_element_type=jnp.float32
        )


def running_attention(chips, me, sources, q_refs, put, scratch, sem):
    keys_ref, values_ref, acc_ref, total_ref, top_ref = scratch
    tokens = q_refs[0].shape[0]

    def fetch(source, target):
        copy = pltpu.make_async_copy(source, target, sem)
        copy.start()
        copy.wait()

    def one_group(group, columns):
        queries = group_queries(q_refs, group)
        for i in range(chips - 1):
            for j, block in enumerate(sources[2 * i : 2 * i + 2]):
                rows = pl.ds(j * tokens, tokens)
                fetch(block.at[pl.ds(0, tokens), columns], keys_ref.at[i, rows])
                fetch(block.at[pl.ds(tokens, tokens), columns], values_ref.at[i, rows])
        whole, key, value = sources[2 * chips - 2 :]
        own, sib = pl.ds(0, tokens), pl.ds(tokens, tokens)
        fetch(whole.at[own, columns], keys_ref.at[chips - 1, own])
        fetch(whole.at[sib, columns], values_ref.at[chips - 1, own])
        fetch(key.at[:, columns], keys_ref.at[chips - 1, sib])
        fetch(value.at[:, columns], values_ref.at[chips - 1, sib])
        acc_ref[...] = jnp.zeros_like(acc_ref)
        total_ref[...] = jnp.zeros_like(total_ref)
        top_ref[...] = jnp.full_like(top_ref, 2 * MASKED)

        def one_chip(i, inner):
            place = jnp.where(i % 2 == 1, (i + 1) // 2, -(i // 2))
            chip = chip_at(me, place, chips)

            @pl.when(chip <= me // 2)
            def _():
                keys, values = keys_ref[i], with_ones(values_ref[i])
                barred = jnp.where(chip == me // 2, MASKED, 0.0)
                bias = jnp.where(allowed_here(me % 2, tokens), 0.0, barred)
                for first, rows in chunks(tokens):
                    scores = scores_of(head_rows(*queries, first), keys)
                    scores = jnp.where(bias < 0.0, MASKED, scores)
                    old = top_ref[rows, :]
                    top = jnp.maximum(old, row_top(scores))
                    factor = jnp.exp2(old - top)
                    weights = weights_of(scores, top).astype(jnp.bfloat16)
                    update = jnp.dot(weights, values, preferred_element_type=jnp.float32)
                    acc_ref[rows, :] = acc_ref[rows, :] * factor + update[:, :DH]
                    total_ref[rows, :] = total_ref[rows, :] * factor + update[:, DH:]
                    top_ref[rows, :] = top

            return inner

        lax.fori_loop(0, chips, one_chip, 0)
        put(group, divide(acc_ref[...], total_ref[...]))

    for_groups(one_group)


def last_kernel(chips, me_ref, q_ref, sib_q_ref, *refs):
    blocks, (shift_ref, acc_ref, total_ref, gain_ref) = (refs[0], refs[1:3]), refs[3:7]
    tables, sources = refs[7:9], refs[9 : 10 + 2 * chips]
    refs = refs[10 + 2 * chips :]
    weights, refs = refs[:2], refs[2:]
    out_refs, picked_refs, loaded = refs[:2], refs[2:4], refs[4:6]
    rows_ref, worst_ref, sem, load_sems, *scratch = refs[6:]
    loads = [
        pltpu.make_async_copy(half_rows(me_ref, weight, False), target, load_sems.at[i])
        for i, (weight, target) in enumerate(zip(weights, loaded))
    ]
    for load in loads:
        load.start()
    q_refs = (q_ref, sib_q_ref)
    tokens, half_width = q_ref.shape
    me = me_ref[0]
    _, factors = factors_of(me, [chips // 2] * 2, chips)
    worst_ref[...] = jnp.zeros_like(worst_ref)

    def put(group, result):
        put_heads(out_refs, rows_ref, tables, group, result)

    def one_group(group, columns):
        keys, values = join_blocks(blocks, factors, columns)
        queries = group_queries(q_refs, group)
        results = []
        for first, rows in chunks(tokens):
            update = fold(queries, first, keys, values, shift_ref[group, rows, :])
            total = total_ref[group, rows, :] + update[:, DH:]
            worst_ref[...] = jnp.maximum(worst_ref[...], total)
            results.append(divide(acc_ref[group, rows, :] + update[:, :DH], total))
        put(group, jnp.concatenate(results, axis=0))

    for_groups(one_group)
    fits = jnp.max(worst_ref[...]) <= SUM_LIMIT

    @pl.when(jnp.logical_not(fits))
    def _():
        running_attention(chips, me, sources, q_refs, put, scratch, sem)

    columns = pl.ds(pl.multiple_of(me % 2 * half_width, half_width), half_width)
    rows = rows_ref[...]
    squares = jnp.broadcast_to(jnp.sum(rows * rows, axis=1, keepdims=True), (2 * CAP, DH))
    upper = squares.astype(jnp.bfloat16).astype(jnp.float32)
    lower = (squares - upper).astype(jnp.bfloat16).astype(jnp.float32)
    lane = lax.broadcasted_iota(jnp.int32, squares.shape, 1)
    rows = (rows * gain_ref[:, columns]).astype(jnp.bfloat16)
    squares = jnp.where(lane < DH // 2, upper, lower).astype(jnp.bfloat16)
    for i, ref in enumerate(picked_refs):
        ref[:, :half_width] = rows[i * CAP : (i + 1) * CAP]
        ref[:, half_width:] = squares[i * CAP : (i + 1) * CAP]
    for load in loads:
        load.wait()


class Attention:
    def __init__(self, me, queries, chips):
        self.me, self.queries, self.chips = me, queries, chips
        self.tokens, self.width = queries[0].shape
        self.rows = 2 * GROUP * self.tokens
        self.state_shape = pltpu.VMEM((HK // 2, self.rows, DH), jnp.float32)

    def call(self, kernel, name, args, others, out_shape, out_others, scratch, aliases=None):
        vmem, anywhere = pl.BlockSpec(memory_space=pltpu.VMEM), pl.BlockSpec(memory_space=pl.ANY)
        return pl.pallas_call(
            kernel,
            in_specs=[pl.BlockSpec(memory_space=pltpu.SMEM)]
            + [vmem] * (2 + len(args))
            + [anywhere] * len(others),
            out_specs=[vmem] * len(out_shape) + [anywhere] * len(out_others),
            out_shape=[*out_shape, *out_others],
            scratch_shapes=scratch,
            input_output_aliases=aliases or {},
            compiler_params=pltpu.CompilerParams(vmem_limit_bytes=ATTEND_MIB * MIB),
            cost_estimate=SMALL,
            name=name,
        )(self.me, *self.queries, *args, *others)

    def own(self, own, sib, weights=()):
        loads = len(weights)
        results = self.call(
            functools.partial(own_kernel, loads),
            "attend_own",
            (own, sib),
            [in_hbm(x) for x in weights],
            [self.state_shape] * 3,
            [pltpu.VMEM(x.shape, x.dtype) for x in weights],
            [pltpu.SemaphoreType.DMA] * loads,
        )
        return list(results[:2]), results[2], results[3:]

    def step(self, blocks, places, shift, state, weights=()):
        count, loads = len(blocks), len(weights)
        results = self.call(
            functools.partial(step_kernel, self.chips, places, loads),
            "attend_step",
            (*blocks, shift, *state),
            [in_hbm(x) for x in weights],
            [self.state_shape] * 2,
            [pltpu.VMEM(x.shape, x.dtype) for x in weights],
            [pltpu.SemaphoreType.DMA] * loads,
            {count + 4: 0, count + 5: 1},
        )
        return list(results[:2]), results[2:]

    def last(self, blocks, shift, state, gain, tables, sources, weights):
        out = pltpu.VMEM((self.tokens, self.width), jnp.bfloat16)
        picked = pltpu.VMEM((CAP, self.width + DH), jnp.bfloat16)
        loaded = [pltpu.VMEM((x.shape[0] // 2, x.shape[1]), x.dtype) for x in weights]
        kept = pltpu.VMEM((self.chips, 2 * self.tokens, DH), jnp.bfloat16)
        sums = pltpu.VMEM((self.rows, DH), jnp.float32)
        return self.call(
            functools.partial(last_kernel, self.chips),
            "attend_last",
            (*blocks, shift, *state, gain, *tables),
            (*sources, *(in_hbm(x) for x in weights)),
            [out, out, picked, picked],
            loaded,
            [
                pltpu.VMEM((2 * CAP, self.width), jnp.float32),
                pltpu.VMEM((STACK * 2 * self.tokens, DH), jnp.float32),
                pltpu.SemaphoreType.DMA,
                pltpu.SemaphoreType.DMA((len(weights),)),
                kept,
                kept,
                sums,
                sums,
                sums,
            ],
        )


def halves_kernel(stacks, me_ref, *refs):
    count = sum(stacks)
    sources, outs, sems = list(refs[:count]), refs[count:-1], refs[-1]
    core = me_ref[0] % 2
    copies = []
    for size, keep_ref, give_ref in zip(stacks, outs[::2], outs[1::2]):
        for i in range(size):
            source = sources.pop(0)
            rows, width = source.shape
            for side, target in ((core, keep_ref), (1 - core, give_ref)):
                columns = pl.ds(pl.multiple_of(side * (width // 2), width // 2), width // 2)
                copies.append((source.at[:, columns], target.at[pl.ds(i * rows, rows)]))
    copies = [pltpu.make_async_copy(*ends, sems.at[i]) for i, ends in enumerate(copies)]
    for copy in copies:
        copy.start()
    for copy in copies:
        copy.wait()


def halves(me, *stacks):
    anywhere = pl.BlockSpec(memory_space=pl.ANY)
    arrays = [x for stack in stacks for x in stack]
    outs = []
    for stack in stacks:
        rows, width = stack[0].shape
        outs += [pltpu.VMEM((len(stack) * rows, width // 2), stack[0].dtype)] * 2
    return pl.pallas_call(
        functools.partial(halves_kernel, [len(stack) for stack in stacks]),
        in_specs=[pl.BlockSpec(memory_space=pltpu.SMEM)] + [anywhere] * len(arrays),
        out_specs=[anywhere] * len(outs),
        out_shape=outs,
        scratch_shapes=[pltpu.SemaphoreType.DMA((2 * len(arrays),))],
        compiler_params=pltpu.CompilerParams(vmem_limit_bytes=MIB),
        cost_estimate=SMALL,
        name="halves",
    )(me, *(in_hbm(x) for x in arrays))


def half_rows(me_ref, ref, sibling):
    half = ref.shape[0] // 2
    side = 1 - me_ref[0] % 2 if sibling else me_ref[0] % 2
    return ref.at[pl.ds(pl.multiple_of(side * half, half), half), :]


def place_kernel(spots, *refs):
    blocks, out_ref = refs[: len(spots)], refs[-1]
    for index, ref in zip(spots, blocks):
        out_ref[index * CAP : (index + 1) * CAP] = ref[...]


def place(blocks, spots, rows):
    vmem = pl.BlockSpec(memory_space=pltpu.VMEM)
    earlier = [] if isinstance(rows, tuple) else [rows]
    shape = rows.shape if earlier else rows
    return pl.pallas_call(
        functools.partial(place_kernel, spots),
        in_specs=[vmem] * (len(blocks) + len(earlier)),
        out_specs=vmem,
        out_shape=pltpu.VMEM(shape, jnp.bfloat16),
        input_output_aliases={len(blocks): 0} if earlier else {},
        compiler_params=pltpu.CompilerParams(vmem_limit_bytes=4 * MIB),
        cost_estimate=SMALL,
        name="place",
    )(*blocks, *earlier)


def contract(rows_ref, gate_ref, up_ref, gate_sum, up_sum, order):
    half = gate_ref.shape[0]
    depth = min(1024, half)

    def one_part(step, carry):
        columns = pl.ds(pl.multiple_of(step * depth, depth), depth)
        part = order(rows_ref[:, columns])
        gate_sum[...] += jnp.dot(part, gate_ref[columns, :], preferred_element_type=jnp.float32)
        up_sum[...] += jnp.dot(part, up_ref[columns, :], preferred_element_type=jnp.float32)
        return carry

    lax.fori_loop(0, half // depth, one_part, 0)


def first_kernel(me_ref, rows_ref, gate_ref, up_ref, *refs):
    sources, (gate_sum, up_sum), targets, sems = refs[:2], refs[2:4], refs[4:6], refs[6]
    copies = [
        pltpu.make_async_copy(half_rows(me_ref, source, True), target, sems.at[i])
        for i, (source, target) in enumerate(zip(sources, targets))
    ]
    for copy in copies:
        copy.start()
    gate_sum[...] = jnp.zeros_like(gate_sum)
    up_sum[...] = jnp.zeros_like(up_sum)
    contract(rows_ref, gate_ref, up_ref, gate_sum, up_sum, lambda part: part)
    for copy in copies:
        copy.wait()


def second_kernel(rows_ref, gate_ref, up_ref, own_ref, gate_in, up_in, source_ref, out_ref, *refs):
    targets, (gate_sum, up_sum, sems) = refs[:PIECES], refs[PIECES:]
    piece = targets[0].shape[1]
    copies = [
        pltpu.make_async_copy(source_ref.at[:, pl.ds(i * piece, piece)], target, sems.at[i])
        for i, target in enumerate(targets)
    ]
    for copy in copies:
        copy.start()
    middle, half = rows_ref.shape[0] // 2, gate_ref.shape[0]

    def order(part):
        return jnp.concatenate([part[middle:], part[:middle]], axis=0)

    gate_sum[...] = gate_in[...]
    up_sum[...] = up_in[...]
    contract(rows_ref, gate_ref, up_ref, gate_sum, up_sum, order)
    squares = own_ref[:, half:].astype(jnp.float32) + order(rows_ref[:, half:].astype(jnp.float32))
    squares = squares[:, :1] + squares[:, DH // 2 : DH // 2 + 1]
    factor = lax.rsqrt(squares / (2 * half) + 1e-05)
    gate = gate_sum[...] * factor
    out_ref[...] = (gate / (1.0 + jnp.exp(-gate)) * (up_sum[...] * factor)).astype(jnp.bfloat16)
    for copy in copies:
        copy.wait()


def hidden_calls(me, rows, other_rows, loaded, w_gate, w_up, w_down):
    count, units, width = rows.shape[0], w_down.shape[0], w_down.shape[1]
    vmem, anywhere = pl.BlockSpec(memory_space=pltpu.VMEM), pl.BlockSpec(memory_space=pl.ANY)
    sums = [pltpu.VMEM((count, units), jnp.float32)] * 2
    params = pltpu.CompilerParams(vmem_limit_bytes=8 * MIB)
    cost = pl.CostEstimate(
        flops=2 * count * width * units, bytes_accessed=2 * width * units, transcendentals=count * units
    )
    *partial, gate, up = pl.pallas_call(
        first_kernel,
        in_specs=[pl.BlockSpec(memory_space=pltpu.SMEM)] + [vmem] * 3 + [anywhere] * 2,
        out_specs=[vmem] * 2 + [anywhere] * 2,
        out_shape=sums + [pltpu.VMEM((width // 2, units), w_gate.dtype)] * 2,
        scratch_shapes=[pltpu.SemaphoreType.DMA((2,))],
        compiler_params=params,
        cost_estimate=cost,
        name="hidden_first",
    )(me, rows, *loaded, in_hbm(w_gate), in_hbm(w_up))
    hidden, *downs = pl.pallas_call(
        second_kernel,
        in_specs=[vmem] * 6 + [anywhere],
        out_specs=[vmem] + [anywhere] * PIECES,
        out_shape=[pltpu.VMEM((count, units), jnp.bfloat16)]
        + [pltpu.VMEM((units, width // PIECES), w_down.dtype)] * PIECES,
        scratch_shapes=sums + [pltpu.SemaphoreType.DMA((PIECES,))],
        compiler_params=params,
        cost_estimate=cost,
        name="hidden_second",
    )(other_rows, gate, up, rows, *partial, in_hbm(w_down))
    return hidden, downs


def down_kernel(hidden_ref, down_ref, *refs):
    copies = []
    if len(refs) == 2:
        own_ref, sib_ref = refs
    else:
        me_ref, *parts, own_ref, sib_ref, result_ref, sems = refs
        width = parts[0].shape[1]
        core = me_ref[0] % 2
        for i, (side, source) in enumerate(zip((core, 1 - core), parts)):
            columns = pl.ds(pl.multiple_of(side * width, width), width)
            copies.append(pltpu.make_async_copy(source, result_ref.at[:, columns], sems.at[i]))
    for copy in copies:
        copy.start()
    middle, width = own_ref.shape
    cols = min(1024, width)

    def one_part(step, carry):
        columns = pl.ds(pl.multiple_of(step * cols, cols), cols)
        part = jnp.dot(hidden_ref[...], down_ref[:, columns], preferred_element_type=jnp.float32)
        part = part.astype(jnp.bfloat16)
        own_ref[:, columns] = part[:middle]
        sib_ref[:, columns] = part[middle:]
        return carry

    lax.fori_loop(0, width // cols, one_part, 0)
    for copy in copies:
        copy.wait()


def down_call(hidden, w_down, halves=()):
    rows, units = hidden.shape
    width = w_down.shape[1]
    vmem, anywhere = pl.BlockSpec(memory_space=pltpu.VMEM), pl.BlockSpec(memory_space=pl.ANY)
    more = [pl.BlockSpec(memory_space=pltpu.SMEM), anywhere, anywhere] if halves else []
    outs = [pltpu.VMEM((rows // 2, width), jnp.bfloat16)] * 2
    if halves:
        tokens, part = halves[1].shape
        outs.append(jax.ShapeDtypeStruct((tokens, 2 * part), jnp.bfloat16))
    return pl.pallas_call(
        down_kernel,
        in_specs=[vmem] * 2 + more,
        out_specs=[vmem] * 2 + [anywhere] * (len(outs) - 2),
        out_shape=outs,
        scratch_shapes=[pltpu.SemaphoreType.DMA((2,))] if halves else [],
        compiler_params=pltpu.CompilerParams(vmem_limit_bytes=8 * MIB),
        cost_estimate=pl.CostEstimate(
            flops=2 * rows * width * units,
            bytes_accessed=2 * width * units + 2 * rows * width,
            transcendentals=0,
        ),
        name="down",
    )(hidden, w_down, *halves)


def spread_kernel(a_ref, b_ref, c_ref, d_ref, table_ref, *rest):
    out_ref = rest[-1]
    total = a_ref[...].astype(jnp.float32) + b_ref[...].astype(jnp.float32)
    total += c_ref[...].astype(jnp.float32) + d_ref[...].astype(jnp.float32)
    total = total.astype(jnp.bfloat16)
    out_ref[...] = lax.dot_general(
        table_ref[...],
        jnp.concatenate([total] * PARTS, axis=0),
        (((0,), (0,)), ((), ())),
        preferred_element_type=jnp.float32,
    ).astype(jnp.bfloat16)


def spread_call(parts, table, piece, pieces, previous):
    tokens = table.shape[1]
    piece_width = parts[0].shape[1]
    cols = min(2048, piece_width)
    steps = piece_width // cols
    earlier = [] if previous is None else [previous]
    return pl.pallas_call(
        spread_kernel,
        grid=(steps,),
        in_specs=[pl.BlockSpec((CAP, cols), lambda i: (0, i))] * 4
        + [pl.BlockSpec((PARTS * CAP, tokens), lambda i: (0, 0))]
        + [pl.BlockSpec(memory_space=pl.ANY)] * len(earlier),
        out_specs=pl.BlockSpec((tokens, cols), lambda i: (0, piece * steps + i)),
        out_shape=jax.ShapeDtypeStruct((tokens, piece_width * pieces), jnp.bfloat16),
        input_output_aliases={5: 0} if earlier else {},
        compiler_params=pltpu.CompilerParams(
            dimension_semantics=("arbitrary",), vmem_limit_bytes=16 * MIB
        ),
        name="spread",
    )(*parts, table, *earlier)


def add_kernel(row, columns, place, mine_ref, other_ref, *refs):
    received_ref, out_ref = (refs[0] if len(refs) > 1 else None), refs[-1]
    rows = slice(row, row + CAP)
    total = mine_ref[rows, columns].astype(jnp.float32) + other_ref[rows, columns].astype(jnp.float32)
    if received_ref is None:
        out_ref[...] = total.astype(jnp.bfloat16)
        return
    start, width = place, received_ref.shape[1]
    part = total[:, start : start + width] + received_ref[...].astype(jnp.float32)
    out_ref[:, start : start + width] = part.astype(jnp.bfloat16)
    if width < out_ref.shape[1]:
        rest = slice(width, None) if start == 0 else slice(0, start)
        out_ref[:, rest] = total[:, rest].astype(jnp.bfloat16)


def add_call(mine, other, index, columns, received=None, place=0):
    vmem = pl.BlockSpec(memory_space=pltpu.VMEM)
    more = () if received is None else (received,)
    return pl.pallas_call(
        functools.partial(add_kernel, index * CAP, columns, place),
        in_specs=[vmem] * (2 + len(more)),
        out_specs=vmem,
        out_shape=pltpu.VMEM((CAP, columns.stop - columns.start), jnp.bfloat16),
        compiler_params=pltpu.CompilerParams(vmem_limit_bytes=4 * MIB),
        cost_estimate=SMALL,
        name="add",
    )(mine, other, *more)


def reduce_chip_rows(pieces, half, chips, moves, token):
    width = pieces[0][0].shape[1]
    middle = width // 2
    chains = [(piece, side) for piece in range(len(pieces)) for side in range(2)]
    received = [None] * len(chains)
    for distance in range(half, 0, -1):
        for i, (piece, side) in enumerate(chains):
            mine, other = pieces[piece]
            if distance == half:
                columns = slice(side * middle, (side + 1) * middle)
                total = add_call(mine, other, chips - 1, columns)
            else:
                received[i], token = lax.optimization_barrier((received[i], token))
                index = distance if side else half - 1 + distance
                place = side * middle if distance == half - 1 else 0
                total = add_call(mine, other, index, slice(0, width), received[i], place)
            received[i] = moves[side](total)
    return [(*pieces[p], *received[2 * p : 2 * p + 2]) for p in range(len(pieces))]


def per_device(chips, queries, keys, values, norm_gain, expert_ids, gates, w_gate, w_up, w_down):
    right, left, sibling = permutations(chips)
    half = chips // 2
    go_right = lambda x: lax.ppermute(x, "ctx", right)
    go_left = lambda x: lax.ppermute(x, "ctx", left)
    swap = lambda x: lax.ppermute(x, "ctx", sibling)

    me = lax.axis_index("ctx").astype(jnp.int32).reshape(1)
    tokens = queries.shape[0]
    hits = (expert_ids == 0).astype(jnp.float32)
    chosen = jnp.sum(hits, axis=1)
    position = jnp.arange(tokens, dtype=jnp.int32)
    before = (position[None, :] < position[:, None]).astype(jnp.float32)
    slot = jnp.sum(before * chosen[None, :], axis=1).astype(jnp.int32)
    table = jnp.logical_and(
        slot[None, :] == jnp.arange(CAP, dtype=jnp.int32)[:, None], chosen[None, :] > 0
    ).astype(jnp.float32)
    rest = jnp.sum(gates * hits, axis=1)
    weights = []
    for _ in range(PARTS):
        part = lax.reduce_precision(rest, 8, 7)
        weights.append(table * part[None, :])
        rest = rest - part
    weighted = jnp.concatenate(weights, axis=0).astype(jnp.bfloat16)
    table = table.astype(jnp.bfloat16)

    own, give, q_own, q_give = halves(me, (keys, values), (queries,))
    across_right, across_left = [
        lax.ppermute(give, "ctx", [(i, j ^ 1) for i, j in pairs]) for pairs in (right, left)
    ]
    chains = [(go_right(own), go_left(own)), (across_right, across_left)]
    sib, q_sib = swap(give), swap(q_give)
    sib_table = swap(table)
    attention = Attention(me, (q_own, q_sib), chips)
    state, shift, _ = attention.own(own, sib)
    sources = [own, sib]
    for step in range(1, half):
        *chains[0], state = lax.optimization_barrier((*chains[0], state))
        chains[1], _, state = lax.optimization_barrier((chains[1], chains[0], state))
        blocks = [chain[side] for side in range(2) for chain in chains]
        sources += blocks
        if step < half - 1:
            chains = [(go_right(chain[0]), go_left(chain[1])) for chain in chains]
        else:
            far_sib = go_right(chains[1][0][:tokens]), go_left(chains[1][1][tokens:])
            opposite = [go_right(chains[0][0]), *far_sib]
        state, _ = attention.step(blocks, [step, step, -step, -step], shift, state)
    opposite, state = lax.optimization_barrier((opposite, state))
    sources += opposite
    mine, theirs, *picked, gate, up = attention.last(
        opposite, shift, state, norm_gain[None, :], (table, sib_table), sources, (w_gate, w_up)
    )

    chains = [(0, 1), (1, 0), (0, 0), (1, 1)]
    moves = [(go_right, go_left)[side] for _, side in chains]
    received = [move(picked[core]) for move, (core, _) in zip(moves, chains)]
    rows = place(picked, [0, chips], (2 * chips * CAP, picked[0].shape[1]))
    theirs = swap(theirs)
    for step in range(1, half):
        spots = [core * chips + side * (half - 1) + step for core, side in chains]
        blocks = list(received)
        for i, move in enumerate(moves):
            if step < half - 1 or i < 2:
                blocks[i], rows = lax.optimization_barrier((received[i], rows))
                received[i] = move(blocks[i])
        if step < half - 1:
            rows = place(blocks, spots, rows)
    rows = place(blocks + received[:2], spots + [chips - 1, 2 * chips - 1], rows)
    hidden, downs = hidden_calls(me, rows, swap(rows), (gate, up), w_gate, w_up, w_down)

    partial = []
    for piece in range(PIECES):
        if piece == 0:
            own, sib, result = down_call(hidden, downs[piece], (me, mine, theirs))
        else:
            own, sib = down_call(hidden, downs[piece])
        partial.append((own, swap(sib)))
    mixed = None
    for piece, parts in enumerate(reduce_chip_rows(partial, half, chips, (go_right, go_left), weighted)):
        mixed = spread_call(parts, weighted, piece, PIECES, mixed)
    return (result, mixed)


def solution(mesh):
    placed = (
        P(("groups", "ctx"), None),
        P(("groups", "ctx"), None),
        P(("groups", "ctx"), None),
        P(),
        P(("groups", "ctx"), None),
        P(("groups", "ctx"), None),
        P(None, "ctx"),
        P(None, "ctx"),
        P("ctx", None),
    )
    return jax.shard_map(
        functools.partial(per_device, mesh.shape["ctx"] // 2),
        mesh=mesh,
        in_specs=placed,
        out_specs=(P(("groups", "ctx"), None), P(("groups", "ctx"), None)),
        check_vma=False,
    )
```

```python
import functools
import math

import jax
import jax.numpy as jnp
from jax import lax
from jax.experimental import pallas as pl
from jax.experimental.pallas import tpu as pltpu
from jax.sharding import PartitionSpec as P

HQ = 64
HK = 8
DH = 128
CAP = 16
GROUP = HQ // HK
WIDE = GROUP * DH
LOG_SCALE = math.log2(math.e) / math.sqrt(DH)
MASKED = -1e30
PIECES = 2
ATTEND_MIB = 11
SMALL = pl.CostEstimate(flops=1, bytes_accessed=1, transcendentals=0)
SUM_LIMIT = 2.0**100
PARTS = 3
STACK = 4
MIB = 1 << 20


def in_hbm(x):
    return pltpu.with_memory_space_constraint(x, pltpu.HBM)


def ring_order(chips):
    return list(range(0, chips, 2)) + list(range(1, chips, 2))[::-1]


def permutations(chips, step=1):
    order = ring_order(chips)
    right, left = [], []
    for place in range(chips):
        here, there = order[place], order[(place + step) % chips]
        for core in range(2):
            right.append((2 * here + core, 2 * there + core))
            left.append((2 * there + core, 2 * here + core))
    sibling = [(i, i ^ 1) for i in range(2 * chips)]
    return right, left, sibling


def chip_at(me, step, chips):
    chip = me // 2
    place = jnp.where(chip % 2 == 0, chip // 2, chips - 1 - chip // 2)
    source = (place - step + 2 * chips) % chips
    return jnp.where(source < chips // 2, 2 * source, 2 * (chips - 1 - source) + 1)


def head_rows(own, sib, first):
    pieces = []
    for h in range(first, first + STACK):
        columns = slice(h * DH, (h + 1) * DH)
        pieces += [own[:, columns], sib[:, columns]]
    return jnp.concatenate(pieces, axis=0)


def with_ones(values):
    return jnp.concatenate([values, jnp.ones_like(values)], axis=1)


def scores_of(queries, keys):
    return LOG_SCALE * lax.dot_general(
        queries, keys, (((1,), (1,)), ((), ())), preferred_element_type=jnp.float32
    )


def weights_of(scores, shift):
    return jnp.exp2(scores - jnp.concatenate([shift] * (scores.shape[1] // DH), axis=1))


def row_top(scores):
    return jnp.broadcast_to(jnp.max(scores, axis=1, keepdims=True), (scores.shape[0], DH))


def allowed_here(core, tokens):
    rows, columns = STACK * 2 * tokens, 2 * tokens

    def position(axis):
        place = lax.broadcasted_iota(jnp.int32, (rows, columns), axis) % (2 * tokens)
        return jnp.where(place < tokens, core * tokens + place, (1 - core) * tokens + place - tokens)

    return position(1) <= position(0)


def group_queries(queries, group):
    columns = pl.ds(pl.multiple_of(group * WIDE, WIDE), WIDE)
    return [ref[:, columns] for ref in queries]


def for_groups(body):
    def step(group, carry):
        body(group, pl.ds(pl.multiple_of(group * DH, DH), DH))
        return carry

    lax.fori_loop(0, HK // 2, step, 0)


def fold(queries, first, keys, values, shift):
    scores = scores_of(head_rows(*queries, first), keys)
    return jnp.dot(
        weights_of(scores, shift).astype(jnp.bfloat16), values, preferred_element_type=jnp.float32
    )


def block_of(ref, columns):
    if isinstance(ref, tuple):
        return ref[0][:, columns], ref[1][:, columns]
    tokens = ref.shape[0] // 2
    return ref[:tokens, columns], ref[tokens:, columns]


def join_blocks(refs, factors, columns):
    pairs = [block_of(ref, columns) for ref in refs]
    keys = jnp.concatenate([key for key, _ in pairs], axis=0)
    values = [with_ones(value) * factor for (_, value), factor in zip(pairs, factors)]
    return keys, jnp.concatenate(values, axis=0)


def factors_of(me, places, chips):
    flags = [chip_at(me, place, chips) < me // 2 for place in places]
    return flags, [jnp.where(flag, 1.0, 0.0).astype(jnp.bfloat16) for flag in flags]


def chunks(tokens):
    size = STACK * 2 * tokens
    return [(first, slice(first // STACK * size, (first // STACK + 1) * size)) for first in range(0, GROUP, STACK)]


def own_kernel(loads, me_ref, q_ref, sib_q_ref, own_ref, sib_ref, *refs):
    acc_ref, total_ref, shift_ref = refs[loads : loads + 3]
    copies = start_loads(loads, refs[:loads], refs[loads + 3 :])
    tokens = q_ref.shape[0]
    allowed = allowed_here(me_ref[0] % 2, tokens)

    def one_group(group, columns):
        keys, values = join_blocks((own_ref, sib_ref), (1, 1), columns)
        queries = group_queries((q_ref, sib_q_ref), group)
        for first, rows in chunks(tokens):
            scores = jnp.where(allowed, scores_of(head_rows(*queries, first), keys), MASKED)
            shift = row_top(scores)
            weights = weights_of(scores, shift).astype(jnp.bfloat16)
            update = jnp.dot(weights, values, preferred_element_type=jnp.float32)
            acc_ref[group, rows, :] = update[:, :DH]
            total_ref[group, rows, :] = update[:, DH:]
            shift_ref[group, rows, :] = shift

    for_groups(one_group)
    for copy in copies:
        copy.wait()


def start_loads(loads, sources, rest):
    copies = [
        pltpu.make_async_copy(source, target, sem)
        for source, target, sem in zip(sources, rest[:loads], rest[loads : 2 * loads])
    ]
    for copy in copies:
        copy.start()
    return copies


def step_kernel(chips, places, loads, me_ref, q_ref, sib_q_ref, *refs):
    count = len(places)
    blocks, shift_ref = refs[:count], refs[count]
    refs = refs[count + 3 :]
    acc_ref, total_ref = refs[loads : loads + 2]
    copies = start_loads(loads, refs[:loads], refs[loads + 2 :])
    tokens = q_ref.shape[0]
    flags, factors = factors_of(me_ref[0], places, chips)

    @pl.when(functools.reduce(jnp.logical_or, flags))
    def _():
        def one_group(group, columns):
            keys, values = join_blocks(blocks, factors, columns)
            queries = group_queries((q_ref, sib_q_ref), group)
            for first, rows in chunks(tokens):
                update = fold(queries, first, keys, values, shift_ref[group, rows, :])
                acc_ref[group, rows, :] += update[:, :DH]
                total_ref[group, rows, :] += update[:, DH:]

        for_groups(one_group)

    for copy in copies:
        copy.wait()


def divide(acc, total):
    inverse = pl.reciprocal(total, approx=True)
    inverse = inverse * (2.0 - total * inverse)
    return (acc * inverse).astype(jnp.bfloat16)


def put_heads(out_refs, rows_ref, tables, group, result):
    tokens = out_refs[0].shape[0]
    columns = pl.ds(pl.multiple_of(group * WIDE, WIDE), WIDE)
    for i, (out_ref, table) in enumerate(zip(out_refs, tables)):
        pieces = [
            result[(2 * h + i) * tokens : (2 * h + i + 1) * tokens] for h in range(GROUP)
        ]
        piece = jnp.concatenate(pieces, axis=1)
        out_ref[:, columns] = piece
        rows_ref[i * CAP : (i + 1) * CAP, columns] = jnp.dot(
            table[...], piece, preferred_element_type=jnp.float32
        )


def running_attention(chips, me, sources, q_refs, put, scratch, sem):
    keys_ref, values_ref, acc_ref, total_ref, top_ref = scratch
    tokens = q_refs[0].shape[0]

    def fetch(source, target):
        copy = pltpu.make_async_copy(source, target, sem)
        copy.start()
        copy.wait()

    def one_group(group, columns):
        queries = group_queries(q_refs, group)
        for i in range(chips - 1):
            for j, block in enumerate(sources[2 * i : 2 * i + 2]):
                rows = pl.ds(j * tokens, tokens)
                fetch(block.at[pl.ds(0, tokens), columns], keys_ref.at[i, rows])
                fetch(block.at[pl.ds(tokens, tokens), columns], values_ref.at[i, rows])
        whole, key, value = sources[2 * chips - 2 :]
        own, sib = pl.ds(0, tokens), pl.ds(tokens, tokens)
        fetch(whole.at[own, columns], keys_ref.at[chips - 1, own])
        fetch(whole.at[sib, columns], values_ref.at[chips - 1, own])
        fetch(key.at[:, columns], keys_ref.at[chips - 1, sib])
        fetch(value.at[:, columns], values_ref.at[chips - 1, sib])
        acc_ref[...] = jnp.zeros_like(acc_ref)
        total_ref[...] = jnp.zeros_like(total_ref)
        top_ref[...] = jnp.full_like(top_ref, 2 * MASKED)

        def one_chip(i, inner):
            place = jnp.where(i % 2 == 1, (i + 1) // 2, -(i // 2))
            chip = chip_at(me, place, chips)

            @pl.when(chip <= me // 2)
            def _():
                keys, values = keys_ref[i], with_ones(values_ref[i])
                barred = jnp.where(chip == me // 2, MASKED, 0.0)
                bias = jnp.where(allowed_here(me % 2, tokens), 0.0, barred)
                for first, rows in chunks(tokens):
                    scores = scores_of(head_rows(*queries, first), keys)
                    scores = jnp.where(bias < 0.0, MASKED, scores)
                    old = top_ref[rows, :]
                    top = jnp.maximum(old, row_top(scores))
                    factor = jnp.exp2(old - top)
                    weights = weights_of(scores, top).astype(jnp.bfloat16)
                    update = jnp.dot(weights, values, preferred_element_type=jnp.float32)
                    acc_ref[rows, :] = acc_ref[rows, :] * factor + update[:, :DH]
                    total_ref[rows, :] = total_ref[rows, :] * factor + update[:, DH:]
                    top_ref[rows, :] = top

            return inner

        lax.fori_loop(0, chips, one_chip, 0)
        put(group, divide(acc_ref[...], total_ref[...]))

    for_groups(one_group)


def last_kernel(chips, me_ref, q_ref, sib_q_ref, *refs):
    blocks, (shift_ref, acc_ref, total_ref, gain_ref) = (refs[0], refs[1:3]), refs[3:7]
    tables, sources = refs[7:9], refs[9 : 10 + 2 * chips]
    refs = refs[10 + 2 * chips :]
    weights, refs = refs[:2], refs[2:]
    out_refs, picked_refs, loaded = refs[:2], refs[2:4], refs[4:6]
    rows_ref, worst_ref, sem, load_sems, *scratch = refs[6:]
    loads = [
        pltpu.make_async_copy(half_rows(me_ref, weight, False), target, load_sems.at[i])
        for i, (weight, target) in enumerate(zip(weights, loaded))
    ]
    for load in loads:
        load.start()
    q_refs = (q_ref, sib_q_ref)
    tokens, half_width = q_ref.shape
    me = me_ref[0]
    _, factors = factors_of(me, [chips // 2] * 2, chips)
    worst_ref[...] = jnp.zeros_like(worst_ref)

    def put(group, result):
        put_heads(out_refs, rows_ref, tables, group, result)

    def one_group(group, columns):
        keys, values = join_blocks(blocks, factors, columns)
        queries = group_queries(q_refs, group)
        results = []
        for first, rows in chunks(tokens):
            update = fold(queries, first, keys, values, shift_ref[group, rows, :])
            total = total_ref[group, rows, :] + update[:, DH:]
            worst_ref[...] = jnp.maximum(worst_ref[...], total)
            results.append(divide(acc_ref[group, rows, :] + update[:, :DH], total))
        put(group, jnp.concatenate(results, axis=0))

    for_groups(one_group)
    fits = jnp.max(worst_ref[...]) <= SUM_LIMIT

    @pl.when(jnp.logical_not(fits))
    def _():
        running_attention(chips, me, sources, q_refs, put, scratch, sem)

    columns = pl.ds(pl.multiple_of(me % 2 * half_width, half_width), half_width)
    rows = rows_ref[...]
    squares = jnp.broadcast_to(jnp.sum(rows * rows, axis=1, keepdims=True), (2 * CAP, DH))
    upper = squares.astype(jnp.bfloat16).astype(jnp.float32)
    lower = (squares - upper).astype(jnp.bfloat16).astype(jnp.float32)
    lane = lax.broadcasted_iota(jnp.int32, squares.shape, 1)
    rows = (rows * gain_ref[:, columns]).astype(jnp.bfloat16)
    squares = jnp.where(lane < DH // 2, upper, lower).astype(jnp.bfloat16)
    for i, ref in enumerate(picked_refs):
        ref[:, :half_width] = rows[i * CAP : (i + 1) * CAP]
        ref[:, half_width:] = squares[i * CAP : (i + 1) * CAP]
    for load in loads:
        load.wait()


class Attention:
    def __init__(self, me, queries, chips):
        self.me, self.queries, self.chips = me, queries, chips
        self.tokens, self.width = queries[0].shape
        self.rows = 2 * GROUP * self.tokens
        self.state_shape = pltpu.VMEM((HK // 2, self.rows, DH), jnp.float32)

    def call(self, kernel, name, args, others, out_shape, out_others, scratch, aliases=None):
        vmem, anywhere = pl.BlockSpec(memory_space=pltpu.VMEM), pl.BlockSpec(memory_space=pl.ANY)
        return pl.pallas_call(
            kernel,
            in_specs=[pl.BlockSpec(memory_space=pltpu.SMEM)]
            + [vmem] * (2 + len(args))
            + [anywhere] * len(others),
            out_specs=[vmem] * len(out_shape) + [anywhere] * len(out_others),
            out_shape=[*out_shape, *out_others],
            scratch_shapes=scratch,
            input_output_aliases=aliases or {},
            compiler_params=pltpu.CompilerParams(vmem_limit_bytes=ATTEND_MIB * MIB),
            cost_estimate=SMALL,
            name=name,
        )(self.me, *self.queries, *args, *others)

    def own(self, own, sib, weights=()):
        loads = len(weights)
        results = self.call(
            functools.partial(own_kernel, loads),
            "attend_own",
            (own, sib),
            [in_hbm(x) for x in weights],
            [self.state_shape] * 3,
            [pltpu.VMEM(x.shape, x.dtype) for x in weights],
            [pltpu.SemaphoreType.DMA] * loads,
        )
        return list(results[:2]), results[2], results[3:]

    def step(self, blocks, places, shift, state, weights=()):
        count, loads = len(blocks), len(weights)
        results = self.call(
            functools.partial(step_kernel, self.chips, places, loads),
            "attend_step",
            (*blocks, shift, *state),
            [in_hbm(x) for x in weights],
            [self.state_shape] * 2,
            [pltpu.VMEM(x.shape, x.dtype) for x in weights],
            [pltpu.SemaphoreType.DMA] * loads,
            {count + 4: 0, count + 5: 1},
        )
        return list(results[:2]), results[2:]

    def last(self, blocks, shift, state, gain, tables, sources, weights):
        out = pltpu.VMEM((self.tokens, self.width), jnp.bfloat16)
        picked = pltpu.VMEM((CAP, self.width + DH), jnp.bfloat16)
        loaded = [pltpu.VMEM((x.shape[0] // 2, x.shape[1]), x.dtype) for x in weights]
        kept = pltpu.VMEM((self.chips, 2 * self.tokens, DH), jnp.bfloat16)
        sums = pltpu.VMEM((self.rows, DH), jnp.float32)
        return self.call(
            functools.partial(last_kernel, self.chips),
            "attend_last",
            (*blocks, shift, *state, gain, *tables),
            (*sources, *(in_hbm(x) for x in weights)),
            [out, out, picked, picked],
            loaded,
            [
                pltpu.VMEM((2 * CAP, self.width), jnp.float32),
                pltpu.VMEM((STACK * 2 * self.tokens, DH), jnp.float32),
                pltpu.SemaphoreType.DMA,
                pltpu.SemaphoreType.DMA((len(weights),)),
                kept,
                kept,
                sums,
                sums,
                sums,
            ],
        )


def halves_kernel(stacks, me_ref, *refs):
    count = sum(stacks)
    sources, outs, sems = list(refs[:count]), refs[count:-1], refs[-1]
    core = me_ref[0] % 2
    copies = []
    for size, keep_ref, give_ref in zip(stacks, outs[::2], outs[1::2]):
        for i in range(size):
            source = sources.pop(0)
            rows, width = source.shape
            for side, target in ((core, keep_ref), (1 - core, give_ref)):
                columns = pl.ds(pl.multiple_of(side * (width // 2), width // 2), width // 2)
                copies.append((source.at[:, columns], target.at[pl.ds(i * rows, rows)]))
    copies = [pltpu.make_async_copy(*ends, sems.at[i]) for i, ends in enumerate(copies)]
    for copy in copies:
        copy.start()
    for copy in copies:
        copy.wait()


def halves(me, *stacks):
    anywhere = pl.BlockSpec(memory_space=pl.ANY)
    arrays = [x for stack in stacks for x in stack]
    outs = []
    for stack in stacks:
        rows, width = stack[0].shape
        outs += [pltpu.VMEM((len(stack) * rows, width // 2), stack[0].dtype)] * 2
    return pl.pallas_call(
        functools.partial(halves_kernel, [len(stack) for stack in stacks]),
        in_specs=[pl.BlockSpec(memory_space=pltpu.SMEM)] + [anywhere] * len(arrays),
        out_specs=[anywhere] * len(outs),
        out_shape=outs,
        scratch_shapes=[pltpu.SemaphoreType.DMA((2 * len(arrays),))],
        compiler_params=pltpu.CompilerParams(vmem_limit_bytes=MIB),
        cost_estimate=SMALL,
        name="halves",
    )(me, *(in_hbm(x) for x in arrays))


def half_rows(me_ref, ref, sibling):
    half = ref.shape[0] // 2
    side = 1 - me_ref[0] % 2 if sibling else me_ref[0] % 2
    return ref.at[pl.ds(pl.multiple_of(side * half, half), half), :]


def place_kernel(spots, *refs):
    blocks, out_ref = refs[: len(spots)], refs[-1]
    for index, ref in zip(spots, blocks):
        out_ref[index * CAP : (index + 1) * CAP] = ref[...]


def place(blocks, spots, rows):
    vmem = pl.BlockSpec(memory_space=pltpu.VMEM)
    earlier = [] if isinstance(rows, tuple) else [rows]
    shape = rows.shape if earlier else rows
    return pl.pallas_call(
        functools.partial(place_kernel, spots),
        in_specs=[vmem] * (len(blocks) + len(earlier)),
        out_specs=vmem,
        out_shape=pltpu.VMEM(shape, jnp.bfloat16),
        input_output_aliases={len(blocks): 0} if earlier else {},
        compiler_params=pltpu.CompilerParams(vmem_limit_bytes=4 * MIB),
        cost_estimate=SMALL,
        name="place",
    )(*blocks, *earlier)


def contract(rows_ref, gate_ref, up_ref, gate_sum, up_sum, order):
    half = gate_ref.shape[0]
    depth = min(1024, half)

    def one_part(step, carry):
        columns = pl.ds(pl.multiple_of(step * depth, depth), depth)
        part = order(rows_ref[:, columns])
        gate_sum[...] += jnp.dot(part, gate_ref[columns, :], preferred_element_type=jnp.float32)
        up_sum[...] += jnp.dot(part, up_ref[columns, :], preferred_element_type=jnp.float32)
        return carry

    lax.fori_loop(0, half // depth, one_part, 0)


def first_kernel(me_ref, rows_ref, gate_ref, up_ref, *refs):
    sources, (gate_sum, up_sum), targets, sems = refs[:2], refs[2:4], refs[4:6], refs[6]
    copies = [
        pltpu.make_async_copy(half_rows(me_ref, source, True), target, sems.at[i])
        for i, (source, target) in enumerate(zip(sources, targets))
    ]
    for copy in copies:
        copy.start()
    gate_sum[...] = jnp.zeros_like(gate_sum)
    up_sum[...] = jnp.zeros_like(up_sum)
    contract(rows_ref, gate_ref, up_ref, gate_sum, up_sum, lambda part: part)
    for copy in copies:
        copy.wait()


def second_kernel(rows_ref, gate_ref, up_ref, own_ref, gate_in, up_in, source_ref, out_ref, *refs):
    targets, (gate_sum, up_sum, sems) = refs[:PIECES], refs[PIECES:]
    piece = targets[0].shape[1]
    copies = [
        pltpu.make_async_copy(source_ref.at[:, pl.ds(i * piece, piece)], target, sems.at[i])
        for i, target in enumerate(targets)
    ]
    for copy in copies:
        copy.start()
    middle, half = rows_ref.shape[0] // 2, gate_ref.shape[0]

    def order(part):
        return jnp.concatenate([part[middle:], part[:middle]], axis=0)

    gate_sum[...] = gate_in[...]
    up_sum[...] = up_in[...]
    contract(rows_ref, gate_ref, up_ref, gate_sum, up_sum, order)
    squares = own_ref[:, half:].astype(jnp.float32) + order(rows_ref[:, half:].astype(jnp.float32))
    squares = squares[:, :1] + squares[:, DH // 2 : DH // 2 + 1]
    factor = lax.rsqrt(squares / (2 * half) + 1e-05)
    gate = gate_sum[...] * factor
    out_ref[...] = (gate / (1.0 + jnp.exp(-gate)) * (up_sum[...] * factor)).astype(jnp.bfloat16)
    for copy in copies:
        copy.wait()


def hidden_calls(me, rows, other_rows, loaded, w_gate, w_up, w_down):
    count, units, width = rows.shape[0], w_down.shape[0], w_down.shape[1]
    vmem, anywhere = pl.BlockSpec(memory_space=pltpu.VMEM), pl.BlockSpec(memory_space=pl.ANY)
    sums = [pltpu.VMEM((count, units), jnp.float32)] * 2
    params = pltpu.CompilerParams(vmem_limit_bytes=8 * MIB)
    cost = pl.CostEstimate(
        flops=2 * count * width * units, bytes_accessed=2 * width * units, transcendentals=count * units
    )
    *partial, gate, up = pl.pallas_call(
        first_kernel,
        in_specs=[pl.BlockSpec(memory_space=pltpu.SMEM)] + [vmem] * 3 + [anywhere] * 2,
        out_specs=[vmem] * 2 + [anywhere] * 2,
        out_shape=sums + [pltpu.VMEM((width // 2, units), w_gate.dtype)] * 2,
        scratch_shapes=[pltpu.SemaphoreType.DMA((2,))],
        compiler_params=params,
        cost_estimate=cost,
        name="hidden_first",
    )(me, rows, *loaded, in_hbm(w_gate), in_hbm(w_up))
    hidden, *downs = pl.pallas_call(
        second_kernel,
        in_specs=[vmem] * 6 + [anywhere],
        out_specs=[vmem] + [anywhere] * PIECES,
        out_shape=[pltpu.VMEM((count, units), jnp.bfloat16)]
        + [pltpu.VMEM((units, width // PIECES), w_down.dtype)] * PIECES,
        scratch_shapes=sums + [pltpu.SemaphoreType.DMA((PIECES,))],
        compiler_params=params,
        cost_estimate=cost,
        name="hidden_second",
    )(other_rows, gate, up, rows, *partial, in_hbm(w_down))
    return hidden, downs


def down_kernel(hidden_ref, down_ref, *refs):
    copies = []
    if len(refs) == 2:
        own_ref, sib_ref = refs
    else:
        me_ref, *parts, own_ref, sib_ref, result_ref, sems = refs
        width = parts[0].shape[1]
        core = me_ref[0] % 2
        for i, (side, source) in enumerate(zip((core, 1 - core), parts)):
            columns = pl.ds(pl.multiple_of(side * width, width), width)
            copies.append(pltpu.make_async_copy(source, result_ref.at[:, columns], sems.at[i]))
    for copy in copies:
        copy.start()
    middle, width = own_ref.shape
    cols = min(1024, width)

    def one_part(step, carry):
        columns = pl.ds(pl.multiple_of(step * cols, cols), cols)
        part = jnp.dot(hidden_ref[...], down_ref[:, columns], preferred_element_type=jnp.float32)
        part = part.astype(jnp.bfloat16)
        own_ref[:, columns] = part[:middle]
        sib_ref[:, columns] = part[middle:]
        return carry

    lax.fori_loop(0, width // cols, one_part, 0)
    for copy in copies:
        copy.wait()


def down_call(hidden, w_down, halves=()):
    rows, units = hidden.shape
    width = w_down.shape[1]
    vmem, anywhere = pl.BlockSpec(memory_space=pltpu.VMEM), pl.BlockSpec(memory_space=pl.ANY)
    more = [pl.BlockSpec(memory_space=pltpu.SMEM), anywhere, anywhere] if halves else []
    outs = [pltpu.VMEM((rows // 2, width), jnp.bfloat16)] * 2
    if halves:
        tokens, part = halves[1].shape
        outs.append(jax.ShapeDtypeStruct((tokens, 2 * part), jnp.bfloat16))
    return pl.pallas_call(
        down_kernel,
        in_specs=[vmem] * 2 + more,
        out_specs=[vmem] * 2 + [anywhere] * (len(outs) - 2),
        out_shape=outs,
        scratch_shapes=[pltpu.SemaphoreType.DMA((2,))] if halves else [],
        compiler_params=pltpu.CompilerParams(vmem_limit_bytes=8 * MIB),
        cost_estimate=pl.CostEstimate(
            flops=2 * rows * width * units,
            bytes_accessed=2 * width * units + 2 * rows * width,
            transcendentals=0,
        ),
        name="down",
    )(hidden, w_down, *halves)


def spread_kernel(start, *refs):
    parts, table_ref, out_ref, kept_ref, sems = refs[:4], refs[4], *refs[-3:]
    table = table_ref[...]
    width = kept_ref.shape[1]
    cols = min(1024, width)
    copies = []
    for i in range(width // cols):
        columns = slice(i * cols, (i + 1) * cols)
        total = sum(ref[:CAP, columns].astype(jnp.float32) for ref in parts).astype(jnp.bfloat16)
        kept_ref[:, columns] = lax.dot_general(
            table,
            jnp.concatenate([total] * PARTS, axis=0),
            (((0,), (0,)), ((), ())),
            preferred_element_type=jnp.float32,
        ).astype(jnp.bfloat16)
        target = out_ref.at[:, pl.ds(start + i * cols, cols)]
        copies.append(pltpu.make_async_copy(kept_ref.at[:, pl.ds(i * cols, cols)], target, sems.at[i]))
        copies[-1].start()
    for copy in copies:
        copy.wait()


def spread_call(parts, table, piece, pieces, previous):
    tokens = table.shape[1]
    width = parts[0].shape[1]
    earlier = [] if previous is None else [previous]
    vmem, anywhere = pl.BlockSpec(memory_space=pltpu.VMEM), pl.BlockSpec(memory_space=pl.ANY)
    return pl.pallas_call(
        functools.partial(spread_kernel, piece * width),
        in_specs=[vmem] * 5 + [anywhere] * len(earlier),
        out_specs=anywhere,
        out_shape=jax.ShapeDtypeStruct((tokens, width * pieces), jnp.bfloat16),
        input_output_aliases={5: 0} if earlier else {},
        scratch_shapes=[
            pltpu.VMEM((tokens, width), jnp.bfloat16),
            pltpu.SemaphoreType.DMA((max(1, width // 1024),)),
        ],
        compiler_params=pltpu.CompilerParams(vmem_limit_bytes=8 * MIB),
        cost_estimate=SMALL,
        name="spread",
    )(*parts, table, *earlier)


def add_kernel(row, mine_ref, other_ref, *refs):
    rows = slice(row, row + CAP)
    total = mine_ref[rows].astype(jnp.float32) + other_ref[rows].astype(jnp.float32)
    for ref in refs[:-1]:
        total += ref[...].astype(jnp.float32)
    refs[-1][...] = total.astype(jnp.bfloat16)


def add_call(mine, other, index, received=()):
    vmem = pl.BlockSpec(memory_space=pltpu.VMEM)
    return pl.pallas_call(
        functools.partial(add_kernel, index * CAP),
        in_specs=[vmem] * (2 + len(received)),
        out_specs=vmem,
        out_shape=pltpu.VMEM((CAP, mine.shape[1]), jnp.bfloat16),
        compiler_params=pltpu.CompilerParams(vmem_limit_bytes=4 * MIB),
        cost_estimate=SMALL,
        name="add",
    )(mine, other, *received)


def reduce_chip_rows(pieces, half, chips, moves, skips, token):
    chains = [(piece, side) for piece in range(len(pieces)) for side in range(2)]
    received, far = [()] * len(chains), {}
    for distance in range(half - 1, 0, -1):
        for i, (piece, side) in enumerate(chains):
            if received[i]:
                received[i], token = lax.optimization_barrier((received[i], token))
            more = received[i]
            if distance == half - 2 and piece % 2 == side:
                more = (*more, far[piece])
            index = distance if side else half - 1 + distance
            received[i] = (moves[side](add_call(*pieces[piece], index, more)),)
        if distance == half - 1:
            far = {p: skips[p % 2](add_call(*piece, chips - 1)) for p, piece in enumerate(pieces)}
    return [(*pieces[p], *received[2 * p], *received[2 * p + 1]) for p in range(len(pieces))]


def per_device(chips, queries, keys, values, norm_gain, expert_ids, gates, w_gate, w_up, w_down):
    right, left, sibling = permutations(chips)
    two_right, two_left, _ = permutations(chips, 2)
    half = chips // 2
    go_right = lambda x: lax.ppermute(x, "ctx", right)
    go_left = lambda x: lax.ppermute(x, "ctx", left)
    swap = lambda x: lax.ppermute(x, "ctx", sibling)
    skips = [lambda x, pairs=pairs: lax.ppermute(x, "ctx", pairs) for pairs in (two_right, two_left)]

    me = lax.axis_index("ctx").astype(jnp.int32).reshape(1)
    tokens = queries.shape[0]
    hits = (expert_ids == 0).astype(jnp.float32)
    chosen = jnp.sum(hits, axis=1)
    position = jnp.arange(tokens, dtype=jnp.int32)
    before = (position[None, :] < position[:, None]).astype(jnp.float32)
    slot = jnp.sum(before * chosen[None, :], axis=1).astype(jnp.int32)
    table = jnp.logical_and(
        slot[None, :] == jnp.arange(CAP, dtype=jnp.int32)[:, None], chosen[None, :] > 0
    ).astype(jnp.float32)
    rest = jnp.sum(gates * hits, axis=1)
    weights = []
    for _ in range(PARTS):
        part = lax.reduce_precision(rest, 8, 7)
        weights.append(table * part[None, :])
        rest = rest - part
    weighted = jnp.concatenate(weights, axis=0).astype(jnp.bfloat16)
    table = table.astype(jnp.bfloat16)

    own, give, q_own, q_give = halves(me, (keys, values), (queries,))
    across_right, across_left = [
        lax.ppermute(give, "ctx", [(i, j ^ 1) for i, j in pairs]) for pairs in (right, left)
    ]
    chains = [(go_right(own), go_left(own)), (across_right, across_left)]
    sib, q_sib = swap(give), swap(q_give)
    sib_table = swap(table)
    attention = Attention(me, (q_own, q_sib), chips)
    state, shift, _ = attention.own(own, sib)
    sources = [own, sib]
    for step in range(1, half):
        *chains[0], state = lax.optimization_barrier((*chains[0], state))
        chains[1], _, state = lax.optimization_barrier((chains[1], chains[0], state))
        blocks = [chain[side] for side in range(2) for chain in chains]
        sources += blocks
        if step < half - 1:
            chains = [(go_right(chain[0]), go_left(chain[1])) for chain in chains]
        else:
            far_sib = go_right(chains[1][0][:tokens]), go_left(chains[1][1][tokens:])
            opposite = [go_right(chains[0][0]), *far_sib]
        state, _ = attention.step(blocks, [step, step, -step, -step], shift, state)
    opposite, state = lax.optimization_barrier((opposite, state))
    sources += opposite
    mine, theirs, *picked, gate, up = attention.last(
        opposite, shift, state, norm_gain[None, :], (table, sib_table), sources, (w_gate, w_up)
    )

    chains = [(0, 1), (1, 0), (0, 0), (1, 1)]
    moves = [(go_right, go_left)[side] for _, side in chains]
    received = [move(picked[core]) for move, (core, _) in zip(moves, chains)]
    rows = place(picked, [0, chips], (2 * chips * CAP, picked[0].shape[1]))
    theirs = swap(theirs)
    far = []
    for step in range(1, half):
        spots = [core * chips + side * (half - 1) + step for core, side in chains]
        blocks = list(received)
        for i, move in enumerate(moves):
            if step == half - 1 and i == 1:
                far, rows = lax.optimization_barrier((far, rows))
            blocks[i], rows = lax.optimization_barrier((received[i], rows))
            if step < half - 1:
                received[i] = move(blocks[i])
            if step == half - 2 and i < 2:
                far.append(skips[chains[i][1]](blocks[i]))
        if step < half - 1:
            rows = place(blocks, spots, rows)
    rows = place(blocks + far, spots + [chips - 1, 2 * chips - 1], rows)
    hidden, downs = hidden_calls(me, rows, swap(rows), (gate, up), w_gate, w_up, w_down)

    partial = []
    for piece in range(PIECES):
        if piece == 0:
            own, sib, result = down_call(hidden, downs[piece], (me, mine, theirs))
        else:
            own, sib = down_call(hidden, downs[piece])
        partial.append((own, swap(sib)))
    mixed = None
    for piece, parts in enumerate(reduce_chip_rows(partial, half, chips, (go_right, go_left), skips, weighted)):
        mixed = spread_call(parts, weighted, piece, PIECES, mixed)
    return (result, mixed)


def solution(mesh):
    placed = (
        P(("groups", "ctx"), None),
        P(("groups", "ctx"), None),
        P(("groups", "ctx"), None),
        P(),
        P(("groups", "ctx"), None),
        P(("groups", "ctx"), None),
        P(None, "ctx"),
        P(None, "ctx"),
        P("ctx", None),
    )
    return jax.shard_map(
        functools.partial(per_device, mesh.shape["ctx"] // 2),
        mesh=mesh,
        in_specs=placed,
        out_specs=(P(("groups", "ctx"), None), P(("groups", "ctx"), None)),
        check_vma=False,
    )
```

```python
import functools
import math

import jax
import jax.numpy as jnp
from jax import lax
from jax.experimental import pallas as pl
from jax.experimental.pallas import tpu as pltpu
from jax.sharding import PartitionSpec as P

HQ = 64
HK = 8
DH = 128
CAP = 16
GROUP = HQ // HK
WIDE = GROUP * DH
LOG_SCALE = math.log2(math.e) / math.sqrt(DH)
MASKED = -1e30
PIECES = 2
ATTEND_MIB = 11
SMALL = pl.CostEstimate(flops=1, bytes_accessed=1, transcendentals=0)
SUM_LIMIT = 2.0**100
PARTS = 3
STACK = 4
MIB = 1 << 20


def in_hbm(x):
    return pltpu.with_memory_space_constraint(x, pltpu.HBM)


def ring_order(chips):
    return list(range(0, chips, 2)) + list(range(1, chips, 2))[::-1]


def permutations(chips):
    order = ring_order(chips)
    right, left = [], []
    for place in range(chips):
        here, there = order[place], order[(place + 1) % chips]
        for core in range(2):
            right.append((2 * here + core, 2 * there + core))
            left.append((2 * there + core, 2 * here + core))
    sibling = [(i, i ^ 1) for i in range(2 * chips)]
    return right, left, sibling


def chip_at(me, step, chips):
    chip = me // 2
    place = jnp.where(chip % 2 == 0, chip // 2, chips - 1 - chip // 2)
    source = (place - step + 2 * chips) % chips
    return jnp.where(source < chips // 2, 2 * source, 2 * (chips - 1 - source) + 1)


def head_rows(own, sib, first):
    pieces = []
    for h in range(first, first + STACK):
        columns = slice(h * DH, (h + 1) * DH)
        pieces += [own[:, columns], sib[:, columns]]
    return jnp.concatenate(pieces, axis=0)


def with_ones(values):
    return jnp.concatenate([values, jnp.ones_like(values)], axis=1)


def scores_of(queries, keys):
    return LOG_SCALE * lax.dot_general(
        queries, keys, (((1,), (1,)), ((), ())), preferred_element_type=jnp.float32
    )


def weights_of(scores, shift):
    return jnp.exp2(scores - jnp.concatenate([shift] * (scores.shape[1] // DH), axis=1))


def row_top(scores):
    return jnp.broadcast_to(jnp.max(scores, axis=1, keepdims=True), (scores.shape[0], DH))


def allowed_here(core, tokens):
    rows, columns = STACK * 2 * tokens, 2 * tokens

    def position(axis):
        place = lax.broadcasted_iota(jnp.int32, (rows, columns), axis) % (2 * tokens)
        return jnp.where(place < tokens, core * tokens + place, (1 - core) * tokens + place - tokens)

    return position(1) <= position(0)


def group_queries(queries, group):
    columns = pl.ds(pl.multiple_of(group * WIDE, WIDE), WIDE)
    return [ref[:, columns] for ref in queries]


def for_groups(body):
    def step(group, carry):
        body(group, pl.ds(pl.multiple_of(group * DH, DH), DH))
        return carry

    lax.fori_loop(0, HK // 2, step, 0)


def fold(queries, first, keys, values, shift):
    scores = scores_of(head_rows(*queries, first), keys)
    return jnp.dot(
        weights_of(scores, shift).astype(jnp.bfloat16), values, preferred_element_type=jnp.float32
    )


def block_of(ref, columns):
    if isinstance(ref, tuple):
        return ref[0][:, columns], ref[1][:, columns]
    tokens = ref.shape[0] // 2
    return ref[:tokens, columns], ref[tokens:, columns]


def join_blocks(refs, factors, columns):
    pairs = [block_of(ref, columns) for ref in refs]
    keys = jnp.concatenate([key for key, _ in pairs], axis=0)
    values = [with_ones(value) * factor for (_, value), factor in zip(pairs, factors)]
    return keys, jnp.concatenate(values, axis=0)


def factors_of(me, places, chips):
    flags = [chip_at(me, place, chips) < me // 2 for place in places]
    return flags, [jnp.where(flag, 1.0, 0.0).astype(jnp.bfloat16) for flag in flags]


def chunks(tokens):
    size = STACK * 2 * tokens
    return [(first, slice(first // STACK * size, (first // STACK + 1) * size)) for first in range(0, GROUP, STACK)]


def own_kernel(loads, me_ref, q_ref, sib_q_ref, own_ref, sib_ref, *refs):
    acc_ref, total_ref, shift_ref = refs[loads : loads + 3]
    copies = start_loads(loads, refs[:loads], refs[loads + 3 :])
    tokens = q_ref.shape[0]
    allowed = allowed_here(me_ref[0] % 2, tokens)

    def one_group(group, columns):
        keys, values = join_blocks((own_ref, sib_ref), (1, 1), columns)
        queries = group_queries((q_ref, sib_q_ref), group)
        for first, rows in chunks(tokens):
            scores = jnp.where(allowed, scores_of(head_rows(*queries, first), keys), MASKED)
            shift = row_top(scores)
            weights = weights_of(scores, shift).astype(jnp.bfloat16)
            update = jnp.dot(weights, values, preferred_element_type=jnp.float32)
            acc_ref[group, rows, :] = update[:, :DH]
            total_ref[group, rows, :] = update[:, DH:]
            shift_ref[group, rows, :] = shift

    for_groups(one_group)
    for copy in copies:
        copy.wait()


def start_loads(loads, sources, rest):
    copies = [
        pltpu.make_async_copy(source, target, sem)
        for source, target, sem in zip(sources, rest[:loads], rest[loads : 2 * loads])
    ]
    for copy in copies:
        copy.start()
    return copies


def step_kernel(chips, places, loads, me_ref, q_ref, sib_q_ref, *refs):
    count = len(places)
    blocks, shift_ref = refs[:count], refs[count]
    refs = refs[count + 3 :]
    acc_ref, total_ref = refs[loads : loads + 2]
    copies = start_loads(loads, refs[:loads], refs[loads + 2 :])
    tokens = q_ref.shape[0]
    flags, factors = factors_of(me_ref[0], places, chips)

    @pl.when(functools.reduce(jnp.logical_or, flags))
    def _():
        def one_group(group, columns):
            keys, values = join_blocks(blocks, factors, columns)
            queries = group_queries((q_ref, sib_q_ref), group)
            for first, rows in chunks(tokens):
                update = fold(queries, first, keys, values, shift_ref[group, rows, :])
                acc_ref[group, rows, :] += update[:, :DH]
                total_ref[group, rows, :] += update[:, DH:]

        for_groups(one_group)

    for copy in copies:
        copy.wait()


def divide(acc, total):
    inverse = pl.reciprocal(total, approx=True)
    inverse = inverse * (2.0 - total * inverse)
    return (acc * inverse).astype(jnp.bfloat16)


def put_heads(out_refs, rows_ref, tables, group, result):
    tokens = out_refs[0].shape[0]
    columns = pl.ds(pl.multiple_of(group * WIDE, WIDE), WIDE)
    for i, (out_ref, table) in enumerate(zip(out_refs, tables)):
        pieces = [
            result[(2 * h + i) * tokens : (2 * h + i + 1) * tokens] for h in range(GROUP)
        ]
        piece = jnp.concatenate(pieces, axis=1)
        out_ref[:, columns] = piece
        rows_ref[i * CAP : (i + 1) * CAP, columns] = jnp.dot(
            table[...], piece, preferred_element_type=jnp.float32
        )


def running_attention(chips, me, sources, q_refs, put, scratch, sem):
    keys_ref, values_ref, acc_ref, total_ref, top_ref = scratch
    tokens = q_refs[0].shape[0]

    def fetch(source, target):
        copy = pltpu.make_async_copy(source, target, sem)
        copy.start()
        copy.wait()

    def one_group(group, columns):
        queries = group_queries(q_refs, group)
        for i in range(chips - 1):
            for j, block in enumerate(sources[2 * i : 2 * i + 2]):
                rows = pl.ds(j * tokens, tokens)
                fetch(block.at[pl.ds(0, tokens), columns], keys_ref.at[i, rows])
                fetch(block.at[pl.ds(tokens, tokens), columns], values_ref.at[i, rows])
        whole, key, value = sources[2 * chips - 2 :]
        own, sib = pl.ds(0, tokens), pl.ds(tokens, tokens)
        fetch(whole.at[own, columns], keys_ref.at[chips - 1, own])
        fetch(whole.at[sib, columns], values_ref.at[chips - 1, own])
        fetch(key.at[:, columns], keys_ref.at[chips - 1, sib])
        fetch(value.at[:, columns], values_ref.at[chips - 1, sib])
        acc_ref[...] = jnp.zeros_like(acc_ref)
        total_ref[...] = jnp.zeros_like(total_ref)
        top_ref[...] = jnp.full_like(top_ref, 2 * MASKED)

        def one_chip(i, inner):
            place = jnp.where(i % 2 == 1, (i + 1) // 2, -(i // 2))
            chip = chip_at(me, place, chips)

            @pl.when(chip <= me // 2)
            def _():
                keys, values = keys_ref[i], with_ones(values_ref[i])
                barred = jnp.where(chip == me // 2, MASKED, 0.0)
                bias = jnp.where(allowed_here(me % 2, tokens), 0.0, barred)
                for first, rows in chunks(tokens):
                    scores = scores_of(head_rows(*queries, first), keys)
                    scores = jnp.where(bias < 0.0, MASKED, scores)
                    old = top_ref[rows, :]
                    top = jnp.maximum(old, row_top(scores))
                    factor = jnp.exp2(old - top)
                    weights = weights_of(scores, top).astype(jnp.bfloat16)
                    update = jnp.dot(weights, values, preferred_element_type=jnp.float32)
                    acc_ref[rows, :] = acc_ref[rows, :] * factor + update[:, :DH]
                    total_ref[rows, :] = total_ref[rows, :] * factor + update[:, DH:]
                    top_ref[rows, :] = top

            return inner

        lax.fori_loop(0, chips, one_chip, 0)
        put(group, divide(acc_ref[...], total_ref[...]))

    for_groups(one_group)


def last_kernel(chips, me_ref, q_ref, sib_q_ref, *refs):
    blocks, (shift_ref, acc_ref, total_ref, gain_ref) = (refs[0], refs[1:3]), refs[3:7]
    tables, sources = refs[7:9], refs[9 : 10 + 2 * chips]
    refs = refs[10 + 2 * chips :]
    weights, refs = refs[:2], refs[2:]
    out_refs, picked_refs, loaded = refs[:2], refs[2:4], refs[4:6]
    rows_ref, worst_ref, sem, load_sems, *scratch = refs[6:]
    loads = [
        pltpu.make_async_copy(half_rows(me_ref, weight, False), target, load_sems.at[i])
        for i, (weight, target) in enumerate(zip(weights, loaded))
    ]
    for load in loads:
        load.start()
    q_refs = (q_ref, sib_q_ref)
    tokens, half_width = q_ref.shape
    me = me_ref[0]
    _, factors = factors_of(me, [chips // 2] * 2, chips)
    worst_ref[...] = jnp.zeros_like(worst_ref)

    def put(group, result):
        put_heads(out_refs, rows_ref, tables, group, result)

    def one_group(group, columns):
        keys, values = join_blocks(blocks, factors, columns)
        queries = group_queries(q_refs, group)
        results = []
        for first, rows in chunks(tokens):
            update = fold(queries, first, keys, values, shift_ref[group, rows, :])
            total = total_ref[group, rows, :] + update[:, DH:]
            worst_ref[...] = jnp.maximum(worst_ref[...], total)
            results.append(divide(acc_ref[group, rows, :] + update[:, :DH], total))
        put(group, jnp.concatenate(results, axis=0))

    for_groups(one_group)
    fits = jnp.max(worst_ref[...]) <= SUM_LIMIT

    @pl.when(jnp.logical_not(fits))
    def _():
        running_attention(chips, me, sources, q_refs, put, scratch, sem)

    columns = pl.ds(pl.multiple_of(me % 2 * half_width, half_width), half_width)
    rows = rows_ref[...]
    squares = jnp.broadcast_to(jnp.sum(rows * rows, axis=1, keepdims=True), (2 * CAP, DH))
    upper = squares.astype(jnp.bfloat16).astype(jnp.float32)
    lower = (squares - upper).astype(jnp.bfloat16).astype(jnp.float32)
    lane = lax.broadcasted_iota(jnp.int32, squares.shape, 1)
    rows = (rows * gain_ref[:, columns]).astype(jnp.bfloat16)
    squares = jnp.where(lane < DH // 2, upper, lower).astype(jnp.bfloat16)
    for i, ref in enumerate(picked_refs):
        ref[:, :half_width] = rows[i * CAP : (i + 1) * CAP]
        ref[:, half_width:] = squares[i * CAP : (i + 1) * CAP]
    for load in loads:
        load.wait()


class Attention:
    def __init__(self, me, queries, chips):
        self.me, self.queries, self.chips = me, queries, chips
        self.tokens, self.width = queries[0].shape
        self.rows = 2 * GROUP * self.tokens
        self.state_shape = pltpu.VMEM((HK // 2, self.rows, DH), jnp.float32)

    def call(self, kernel, name, args, others, out_shape, out_others, scratch, aliases=None):
        vmem, anywhere = pl.BlockSpec(memory_space=pltpu.VMEM), pl.BlockSpec(memory_space=pl.ANY)
        return pl.pallas_call(
            kernel,
            in_specs=[pl.BlockSpec(memory_space=pltpu.SMEM)]
            + [vmem] * (2 + len(args))
            + [anywhere] * len(others),
            out_specs=[vmem] * len(out_shape) + [anywhere] * len(out_others),
            out_shape=[*out_shape, *out_others],
            scratch_shapes=scratch,
            input_output_aliases=aliases or {},
            compiler_params=pltpu.CompilerParams(vmem_limit_bytes=ATTEND_MIB * MIB),
            cost_estimate=SMALL,
            name=name,
        )(self.me, *self.queries, *args, *others)

    def own(self, own, sib, weights=()):
        loads = len(weights)
        results = self.call(
            functools.partial(own_kernel, loads),
            "attend_own",
            (own, sib),
            [in_hbm(x) for x in weights],
            [self.state_shape] * 3,
            [pltpu.VMEM(x.shape, x.dtype) for x in weights],
            [pltpu.SemaphoreType.DMA] * loads,
        )
        return list(results[:2]), results[2], results[3:]

    def step(self, blocks, places, shift, state, weights=()):
        count, loads = len(blocks), len(weights)
        results = self.call(
            functools.partial(step_kernel, self.chips, places, loads),
            "attend_step",
            (*blocks, shift, *state),
            [in_hbm(x) for x in weights],
            [self.state_shape] * 2,
            [pltpu.VMEM(x.shape, x.dtype) for x in weights],
            [pltpu.SemaphoreType.DMA] * loads,
            {count + 4: 0, count + 5: 1},
        )
        return list(results[:2]), results[2:]

    def last(self, blocks, shift, state, gain, tables, sources, weights):
        out = pltpu.VMEM((self.tokens, self.width), jnp.bfloat16)
        picked = pltpu.VMEM((CAP, self.width + DH), jnp.bfloat16)
        loaded = [pltpu.VMEM((x.shape[0] // 2, x.shape[1]), x.dtype) for x in weights]
        kept = pltpu.VMEM((self.chips, 2 * self.tokens, DH), jnp.bfloat16)
        sums = pltpu.VMEM((self.rows, DH), jnp.float32)
        return self.call(
            functools.partial(last_kernel, self.chips),
            "attend_last",
            (*blocks, shift, *state, gain, *tables),
            (*sources, *(in_hbm(x) for x in weights)),
            [out, out, picked, picked],
            loaded,
            [
                pltpu.VMEM((2 * CAP, self.width), jnp.float32),
                pltpu.VMEM((STACK * 2 * self.tokens, DH), jnp.float32),
                pltpu.SemaphoreType.DMA,
                pltpu.SemaphoreType.DMA((len(weights),)),
                kept,
                kept,
                sums,
                sums,
                sums,
            ],
        )


def halves_kernel(stacks, me_ref, *refs):
    count = sum(stacks)
    sources, outs, sems = list(refs[:count]), refs[count:-1], refs[-1]
    core = me_ref[0] % 2
    copies = []
    for size, keep_ref, give_ref in zip(stacks, outs[::2], outs[1::2]):
        for i in range(size):
            source = sources.pop(0)
            rows, width = source.shape
            for side, target in ((core, keep_ref), (1 - core, give_ref)):
                columns = pl.ds(pl.multiple_of(side * (width // 2), width // 2), width // 2)
                copies.append((source.at[:, columns], target.at[pl.ds(i * rows, rows)]))
    copies = [pltpu.make_async_copy(*ends, sems.at[i]) for i, ends in enumerate(copies)]
    for copy in copies:
        copy.start()
    for copy in copies:
        copy.wait()


def halves(me, *stacks):
    anywhere = pl.BlockSpec(memory_space=pl.ANY)
    arrays = [x for stack in stacks for x in stack]
    outs = []
    for stack in stacks:
        rows, width = stack[0].shape
        outs += [pltpu.VMEM((len(stack) * rows, width // 2), stack[0].dtype)] * 2
    return pl.pallas_call(
        functools.partial(halves_kernel, [len(stack) for stack in stacks]),
        in_specs=[pl.BlockSpec(memory_space=pltpu.SMEM)] + [anywhere] * len(arrays),
        out_specs=[anywhere] * len(outs),
        out_shape=outs,
        scratch_shapes=[pltpu.SemaphoreType.DMA((2 * len(arrays),))],
        compiler_params=pltpu.CompilerParams(vmem_limit_bytes=MIB),
        cost_estimate=SMALL,
        name="halves",
    )(me, *(in_hbm(x) for x in arrays))


def half_rows(me_ref, ref, sibling):
    half = ref.shape[0] // 2
    side = 1 - me_ref[0] % 2 if sibling else me_ref[0] % 2
    return ref.at[pl.ds(pl.multiple_of(side * half, half), half), :]


def place_kernel(spots, *refs):
    blocks, out_ref = refs[: len(spots)], refs[-1]
    for index, ref in zip(spots, blocks):
        out_ref[index * CAP : (index + 1) * CAP] = ref[...]


def place(blocks, spots, rows):
    vmem = pl.BlockSpec(memory_space=pltpu.VMEM)
    earlier = [] if isinstance(rows, tuple) else [rows]
    shape = rows.shape if earlier else rows
    return pl.pallas_call(
        functools.partial(place_kernel, spots),
        in_specs=[vmem] * (len(blocks) + len(earlier)),
        out_specs=vmem,
        out_shape=pltpu.VMEM(shape, jnp.bfloat16),
        input_output_aliases={len(blocks): 0} if earlier else {},
        compiler_params=pltpu.CompilerParams(vmem_limit_bytes=4 * MIB),
        cost_estimate=SMALL,
        name="place",
    )(*blocks, *earlier)


def contract(rows_ref, gate_ref, up_ref, gate_sum, up_sum, order):
    half = gate_ref.shape[0]
    depth = min(1024, half)

    def one_part(step, carry):
        columns = pl.ds(pl.multiple_of(step * depth, depth), depth)
        part = order(rows_ref[:, columns])
        gate_sum[...] += jnp.dot(part, gate_ref[columns, :], preferred_element_type=jnp.float32)
        up_sum[...] += jnp.dot(part, up_ref[columns, :], preferred_element_type=jnp.float32)
        return carry

    lax.fori_loop(0, half // depth, one_part, 0)


def first_kernel(me_ref, rows_ref, gate_ref, up_ref, *refs):
    sources, (gate_sum, up_sum), targets, sems = refs[:2], refs[2:4], refs[4:6], refs[6]
    copies = [
        pltpu.make_async_copy(half_rows(me_ref, source, True), target, sems.at[i])
        for i, (source, target) in enumerate(zip(sources, targets))
    ]
    for copy in copies:
        copy.start()
    gate_sum[...] = jnp.zeros_like(gate_sum)
    up_sum[...] = jnp.zeros_like(up_sum)
    contract(rows_ref, gate_ref, up_ref, gate_sum, up_sum, lambda part: part)
    for copy in copies:
        copy.wait()


def second_kernel(rows_ref, gate_ref, up_ref, own_ref, gate_in, up_in, source_ref, out_ref, *refs):
    targets, (gate_sum, up_sum, sems) = refs[:PIECES], refs[PIECES:]
    piece = targets[0].shape[1]
    copies = [
        pltpu.make_async_copy(source_ref.at[:, pl.ds(i * piece, piece)], target, sems.at[i])
        for i, target in enumerate(targets)
    ]
    for copy in copies:
        copy.start()
    middle, half = rows_ref.shape[0] // 2, gate_ref.shape[0]

    def order(part):
        return jnp.concatenate([part[middle:], part[:middle]], axis=0)

    gate_sum[...] = gate_in[...]
    up_sum[...] = up_in[...]
    contract(rows_ref, gate_ref, up_ref, gate_sum, up_sum, order)
    squares = own_ref[:, half:].astype(jnp.float32) + order(rows_ref[:, half:].astype(jnp.float32))
    squares = squares[:, :1] + squares[:, DH // 2 : DH // 2 + 1]
    factor = lax.rsqrt(squares / (2 * half) + 1e-05)
    gate = gate_sum[...] * factor
    out_ref[...] = (gate / (1.0 + jnp.exp(-gate)) * (up_sum[...] * factor)).astype(jnp.bfloat16)
    for copy in copies:
        copy.wait()


def hidden_calls(me, rows, other_rows, loaded, w_gate, w_up, w_down):
    count, units, width = rows.shape[0], w_down.shape[0], w_down.shape[1]
    vmem, anywhere = pl.BlockSpec(memory_space=pltpu.VMEM), pl.BlockSpec(memory_space=pl.ANY)
    sums = [pltpu.VMEM((count, units), jnp.float32)] * 2
    params = pltpu.CompilerParams(vmem_limit_bytes=8 * MIB)
    cost = pl.CostEstimate(
        flops=2 * count * width * units, bytes_accessed=2 * width * units, transcendentals=count * units
    )
    *partial, gate, up = pl.pallas_call(
        first_kernel,
        in_specs=[pl.BlockSpec(memory_space=pltpu.SMEM)] + [vmem] * 3 + [anywhere] * 2,
        out_specs=[vmem] * 2 + [anywhere] * 2,
        out_shape=sums + [pltpu.VMEM((width // 2, units), w_gate.dtype)] * 2,
        scratch_shapes=[pltpu.SemaphoreType.DMA((2,))],
        compiler_params=params,
        cost_estimate=cost,
        name="hidden_first",
    )(me, rows, *loaded, in_hbm(w_gate), in_hbm(w_up))
    hidden, *downs = pl.pallas_call(
        second_kernel,
        in_specs=[vmem] * 6 + [anywhere],
        out_specs=[vmem] + [anywhere] * PIECES,
        out_shape=[pltpu.VMEM((count, units), jnp.bfloat16)]
        + [pltpu.VMEM((units, width // PIECES), w_down.dtype)] * PIECES,
        scratch_shapes=sums + [pltpu.SemaphoreType.DMA((PIECES,))],
        compiler_params=params,
        cost_estimate=cost,
        name="hidden_second",
    )(other_rows, gate, up, rows, *partial, in_hbm(w_down))
    return hidden, downs


def down_kernel(hidden_ref, down_ref, *refs):
    copies = []
    if len(refs) == 2:
        own_ref, sib_ref = refs
    else:
        me_ref, *parts, own_ref, sib_ref, result_ref, sems = refs
        width = parts[0].shape[1]
        core = me_ref[0] % 2
        for i, (side, source) in enumerate(zip((core, 1 - core), parts)):
            columns = pl.ds(pl.multiple_of(side * width, width), width)
            copies.append(pltpu.make_async_copy(source, result_ref.at[:, columns], sems.at[i]))
    for copy in copies:
        copy.start()
    middle, width = own_ref.shape
    cols = min(1024, width)

    def one_part(step, carry):
        columns = pl.ds(pl.multiple_of(step * cols, cols), cols)
        part = jnp.dot(hidden_ref[...], down_ref[:, columns], preferred_element_type=jnp.float32)
        part = part.astype(jnp.bfloat16)
        own_ref[:, columns] = part[:middle]
        sib_ref[:, columns] = part[middle:]
        return carry

    lax.fori_loop(0, width // cols, one_part, 0)
    for copy in copies:
        copy.wait()


def down_call(hidden, w_down, halves=()):
    rows, units = hidden.shape
    width = w_down.shape[1]
    vmem, anywhere = pl.BlockSpec(memory_space=pltpu.VMEM), pl.BlockSpec(memory_space=pl.ANY)
    more = [pl.BlockSpec(memory_space=pltpu.SMEM), anywhere, anywhere] if halves else []
    outs = [pltpu.VMEM((rows // 2, width), jnp.bfloat16)] * 2
    if halves:
        tokens, part = halves[1].shape
        outs.append(jax.ShapeDtypeStruct((tokens, 2 * part), jnp.bfloat16))
    return pl.pallas_call(
        down_kernel,
        in_specs=[vmem] * 2 + more,
        out_specs=[vmem] * 2 + [anywhere] * (len(outs) - 2),
        out_shape=outs,
        scratch_shapes=[pltpu.SemaphoreType.DMA((2,))] if halves else [],
        compiler_params=pltpu.CompilerParams(vmem_limit_bytes=8 * MIB),
        cost_estimate=pl.CostEstimate(
            flops=2 * rows * width * units,
            bytes_accessed=2 * width * units + 2 * rows * width,
            transcendentals=0,
        ),
        name="down",
    )(hidden, w_down, *halves)


def spread_kernel(start, *refs):
    parts, table_ref, out_ref, kept_ref, sems = refs[:4], refs[4], *refs[-3:]
    table = table_ref[...]
    width = kept_ref.shape[1]
    cols = min(1024, width)
    copies = []
    for i in range(width // cols):
        columns = slice(i * cols, (i + 1) * cols)
        total = sum(ref[:CAP, columns].astype(jnp.float32) for ref in parts).astype(jnp.bfloat16)
        kept_ref[:, columns] = lax.dot_general(
            table,
            jnp.concatenate([total] * PARTS, axis=0),
            (((0,), (0,)), ((), ())),
            preferred_element_type=jnp.float32,
        ).astype(jnp.bfloat16)
        target = out_ref.at[:, pl.ds(start + i * cols, cols)]
        copies.append(pltpu.make_async_copy(kept_ref.at[:, pl.ds(i * cols, cols)], target, sems.at[i]))
        copies[-1].start()
    for copy in copies:
        copy.wait()


def spread_call(parts, table, piece, pieces, previous):
    tokens = table.shape[1]
    width = parts[0].shape[1]
    earlier = [] if previous is None else [previous]
    vmem, anywhere = pl.BlockSpec(memory_space=pltpu.VMEM), pl.BlockSpec(memory_space=pl.ANY)
    return pl.pallas_call(
        functools.partial(spread_kernel, piece * width),
        in_specs=[vmem] * 5 + [anywhere] * len(earlier),
        out_specs=anywhere,
        out_shape=jax.ShapeDtypeStruct((tokens, width * pieces), jnp.bfloat16),
        input_output_aliases={5: 0} if earlier else {},
        scratch_shapes=[
            pltpu.VMEM((tokens, width), jnp.bfloat16),
            pltpu.SemaphoreType.DMA((max(1, width // 1024),)),
        ],
        compiler_params=pltpu.CompilerParams(vmem_limit_bytes=8 * MIB),
        cost_estimate=SMALL,
        name="spread",
    )(*parts, table, *earlier)


def add_kernel(row, columns, place, mine_ref, other_ref, *refs):
    received_ref, out_ref = (refs[0] if len(refs) > 1 else None), refs[-1]
    rows = slice(row, row + CAP)
    total = mine_ref[rows, columns].astype(jnp.float32) + other_ref[rows, columns].astype(jnp.float32)
    if received_ref is None:
        out_ref[...] = total.astype(jnp.bfloat16)
        return
    start, width = place, received_ref.shape[1]
    part = total[:, start : start + width] + received_ref[...].astype(jnp.float32)
    out_ref[:, start : start + width] = part.astype(jnp.bfloat16)
    if width < out_ref.shape[1]:
        rest = slice(width, None) if start == 0 else slice(0, start)
        out_ref[:, rest] = total[:, rest].astype(jnp.bfloat16)


def add_call(mine, other, index, columns, received=None, place=0):
    vmem = pl.BlockSpec(memory_space=pltpu.VMEM)
    more = () if received is None else (received,)
    return pl.pallas_call(
        functools.partial(add_kernel, index * CAP, columns, place),
        in_specs=[vmem] * (2 + len(more)),
        out_specs=vmem,
        out_shape=pltpu.VMEM((CAP, columns.stop - columns.start), jnp.bfloat16),
        compiler_params=pltpu.CompilerParams(vmem_limit_bytes=4 * MIB),
        cost_estimate=SMALL,
        name="add",
    )(mine, other, *more)


def reduce_chip_rows(pieces, half, chips, moves, token):
    width = pieces[0][0].shape[1]
    middle = width // 2
    chains = [(piece, side) for piece in range(len(pieces)) for side in range(2)]
    received = [None] * len(chains)
    for distance in range(half, 0, -1):
        for i, (piece, side) in enumerate(chains):
            mine, other = pieces[piece]
            if distance == half:
                columns = slice(side * middle, (side + 1) * middle)
                total = add_call(mine, other, chips - 1, columns)
            else:
                received[i], token = lax.optimization_barrier((received[i], token))
                index = distance if side else half - 1 + distance
                place = side * middle if distance == half - 1 else 0
                total = add_call(mine, other, index, slice(0, width), received[i], place)
            received[i] = moves[side](total)
    return [(*pieces[p], *received[2 * p : 2 * p + 2]) for p in range(len(pieces))]


def per_device(chips, queries, keys, values, norm_gain, expert_ids, gates, w_gate, w_up, w_down):
    right, left, sibling = permutations(chips)
    half = chips // 2
    go_right = lambda x: lax.ppermute(x, "ctx", right)
    go_left = lambda x: lax.ppermute(x, "ctx", left)
    swap = lambda x: lax.ppermute(x, "ctx", sibling)

    me = lax.axis_index("ctx").astype(jnp.int32).reshape(1)
    tokens = queries.shape[0]
    hits = (expert_ids == 0).astype(jnp.float32)
    chosen = jnp.sum(hits, axis=1)
    position = jnp.arange(tokens, dtype=jnp.int32)
    before = (position[None, :] < position[:, None]).astype(jnp.float32)
    slot = jnp.sum(before * chosen[None, :], axis=1).astype(jnp.int32)
    table = jnp.logical_and(
        slot[None, :] == jnp.arange(CAP, dtype=jnp.int32)[:, None], chosen[None, :] > 0
    ).astype(jnp.float32)
    rest = jnp.sum(gates * hits, axis=1)
    weights = []
    for _ in range(PARTS):
        part = lax.reduce_precision(rest, 8, 7)
        weights.append(table * part[None, :])
        rest = rest - part
    weighted = jnp.concatenate(weights, axis=0).astype(jnp.bfloat16)
    table = table.astype(jnp.bfloat16)

    own, give, q_own, q_give = halves(me, (keys, values), (queries,))
    across_right, across_left = [
        lax.ppermute(give, "ctx", [(i, j ^ 1) for i, j in pairs]) for pairs in (right, left)
    ]
    chains = [(go_right(own), go_left(own)), (across_right, across_left)]
    sib, q_sib = swap(give), swap(q_give)
    sib_table = swap(table)
    attention = Attention(me, (q_own, q_sib), chips)
    state, shift, _ = attention.own(own, sib)
    sources = [own, sib]
    for step in range(1, half):
        *chains[0], state = lax.optimization_barrier((*chains[0], state))
        chains[1], _, state = lax.optimization_barrier((chains[1], chains[0], state))
        blocks = [chain[side] for side in range(2) for chain in chains]
        sources += blocks
        if step < half - 1:
            chains = [(go_right(chain[0]), go_left(chain[1])) for chain in chains]
        else:
            far_sib = go_right(chains[1][0][:tokens]), go_left(chains[1][1][tokens:])
            opposite = [go_right(chains[0][0]), *far_sib]
        state, _ = attention.step(blocks, [step, step, -step, -step], shift, state)
    opposite, state = lax.optimization_barrier((opposite, state))
    sources += opposite
    mine, theirs, *picked, gate, up = attention.last(
        opposite, shift, state, norm_gain[None, :], (table, sib_table), sources, (w_gate, w_up)
    )

    chains = [(0, 1), (1, 0), (0, 0), (1, 1)]
    moves = [(go_right, go_left)[side] for _, side in chains]
    received = [move(picked[core]) for move, (core, _) in zip(moves, chains)]
    rows = place(picked, [0, chips], (2 * chips * CAP, picked[0].shape[1]))
    theirs = swap(theirs)
    for step in range(1, half):
        spots = [core * chips + side * (half - 1) + step for core, side in chains]
        blocks = list(received)
        for i, move in enumerate(moves):
            if step < half - 1 or i < 2:
                blocks[i], rows = lax.optimization_barrier((received[i], rows))
                received[i] = move(blocks[i])
        if step < half - 1:
            rows = place(blocks, spots, rows)
    rows = place(blocks + received[:2], spots + [chips - 1, 2 * chips - 1], rows)
    hidden, downs = hidden_calls(me, rows, swap(rows), (gate, up), w_gate, w_up, w_down)

    partial = []
    for piece in range(PIECES):
        if piece == 0:
            own, sib, result = down_call(hidden, downs[piece], (me, mine, theirs))
        else:
            own, sib = down_call(hidden, downs[piece])
        partial.append((own, swap(sib)))
    mixed = None
    for piece, parts in enumerate(reduce_chip_rows(partial, half, chips, (go_right, go_left), weighted)):
        mixed = spread_call(parts, weighted, piece, PIECES, mixed)
    return (result, mixed)


def solution(mesh):
    placed = (
        P(("groups", "ctx"), None),
        P(("groups", "ctx"), None),
        P(("groups", "ctx"), None),
        P(),
        P(("groups", "ctx"), None),
        P(("groups", "ctx"), None),
        P(None, "ctx"),
        P(None, "ctx"),
        P("ctx", None),
    )
    return jax.shard_map(
        functools.partial(per_device, mesh.shape["ctx"] // 2),
        mesh=mesh,
        in_specs=placed,
        out_specs=(P(("groups", "ctx"), None), P(("groups", "ctx"), None)),
        check_vma=False,
    )
```

```python
import functools
import math

import jax
import jax.numpy as jnp
from jax import lax
from jax.experimental import pallas as pl
from jax.experimental.pallas import tpu as pltpu
from jax.sharding import PartitionSpec as P

HQ = 64
HK = 8
DH = 128
CAP = 16
GROUP = HQ // HK
WIDE = GROUP * DH
LOG_SCALE = math.log2(math.e) / math.sqrt(DH)
MASKED = -1e30
PIECES = 2
ATTEND_MIB = 11
SMALL = pl.CostEstimate(flops=1, bytes_accessed=1, transcendentals=0)
SUM_LIMIT = 2.0**100
PARTS = 3
STACK = 4
MIB = 1 << 20


def in_hbm(x):
    return pltpu.with_memory_space_constraint(x, pltpu.HBM)


def ring_order(chips):
    return list(range(0, chips, 2)) + list(range(1, chips, 2))[::-1]


def permutations(chips):
    order = ring_order(chips)
    right, left = [], []
    for place in range(chips):
        here, there = order[place], order[(place + 1) % chips]
        for core in range(2):
            right.append((2 * here + core, 2 * there + core))
            left.append((2 * there + core, 2 * here + core))
    sibling = [(i, i ^ 1) for i in range(2 * chips)]
    return right, left, sibling


def chip_at(me, step, chips):
    chip = me // 2
    place = jnp.where(chip % 2 == 0, chip // 2, chips - 1 - chip // 2)
    source = (place - step + 2 * chips) % chips
    return jnp.where(source < chips // 2, 2 * source, 2 * (chips - 1 - source) + 1)


def head_rows(own, sib, first):
    pieces = []
    for h in range(first, first + STACK):
        columns = slice(h * DH, (h + 1) * DH)
        pieces += [own[:, columns], sib[:, columns]]
    return jnp.concatenate(pieces, axis=0)


def with_ones(values):
    return jnp.concatenate([values, jnp.ones_like(values)], axis=1)


def scores_of(queries, keys):
    return LOG_SCALE * lax.dot_general(
        queries, keys, (((1,), (1,)), ((), ())), preferred_element_type=jnp.float32
    )


def weights_of(scores, shift):
    return jnp.exp2(scores - jnp.concatenate([shift] * (scores.shape[1] // DH), axis=1))


def row_top(scores):
    return jnp.broadcast_to(jnp.max(scores, axis=1, keepdims=True), (scores.shape[0], DH))


def allowed_here(core, tokens):
    rows, columns = STACK * 2 * tokens, 2 * tokens

    def position(axis):
        place = lax.broadcasted_iota(jnp.int32, (rows, columns), axis) % (2 * tokens)
        return jnp.where(place < tokens, core * tokens + place, (1 - core) * tokens + place - tokens)

    return position(1) <= position(0)


def group_queries(queries, group):
    columns = pl.ds(pl.multiple_of(group * WIDE, WIDE), WIDE)
    return [ref[:, columns] for ref in queries]


def for_groups(body, first=0, stop=HK // 2):
    def step(group, carry):
        body(group, pl.ds(pl.multiple_of(group * DH, DH), DH))
        return carry

    lax.fori_loop(first, stop, step, 0)


def fold(queries, first, keys, values, shift):
    scores = scores_of(head_rows(*queries, first), keys)
    return jnp.dot(
        weights_of(scores, shift).astype(jnp.bfloat16), values, preferred_element_type=jnp.float32
    )


def block_of(ref, columns):
    if isinstance(ref, tuple):
        return ref[0][:, columns], ref[1][:, columns]
    tokens = ref.shape[0] // 2
    return ref[:tokens, columns], ref[tokens:, columns]


def join_blocks(refs, factors, columns):
    pairs = [block_of(ref, columns) for ref in refs]
    keys = jnp.concatenate([key for key, _ in pairs], axis=0)
    values = [with_ones(value) * factor for (_, value), factor in zip(pairs, factors)]
    return keys, jnp.concatenate(values, axis=0)


def factors_of(me, places, chips):
    flags = [chip_at(me, place, chips) < me // 2 for place in places]
    return flags, [jnp.where(flag, 1.0, 0.0).astype(jnp.bfloat16) for flag in flags]


def chunks(tokens):
    size = STACK * 2 * tokens
    return [(first, slice(first // STACK * size, (first // STACK + 1) * size)) for first in range(0, GROUP, STACK)]


def own_kernel(loads, me_ref, q_ref, sib_q_ref, own_ref, sib_ref, *refs):
    acc_ref, total_ref, shift_ref = refs[loads : loads + 3]
    copies = start_loads(loads, refs[:loads], refs[loads + 3 :])
    tokens = q_ref.shape[0]
    allowed = allowed_here(me_ref[0] % 2, tokens)

    def one_group(group, columns):
        keys, values = join_blocks((own_ref, sib_ref), (1, 1), columns)
        queries = group_queries((q_ref, sib_q_ref), group)
        for first, rows in chunks(tokens):
            scores = jnp.where(allowed, scores_of(head_rows(*queries, first), keys), MASKED)
            shift = row_top(scores)
            weights = weights_of(scores, shift).astype(jnp.bfloat16)
            update = jnp.dot(weights, values, preferred_element_type=jnp.float32)
            acc_ref[group, rows, :] = update[:, :DH]
            total_ref[group, rows, :] = update[:, DH:]
            shift_ref[group, rows, :] = shift

    for_groups(one_group)
    for copy in copies:
        copy.wait()


def start_loads(loads, sources, rest):
    copies = [
        pltpu.make_async_copy(source, target, sem)
        for source, target, sem in zip(sources, rest[:loads], rest[loads : 2 * loads])
    ]
    for copy in copies:
        copy.start()
    return copies


def step_kernel(chips, places, groups, loads, me_ref, q_ref, sib_q_ref, *refs):
    count = len(places)
    blocks, shift_ref = refs[:count], refs[count]
    refs = refs[count + 3 :]
    acc_ref, total_ref = refs[loads : loads + 2]
    copies = start_loads(loads, refs[:loads], refs[loads + 2 :])
    tokens = q_ref.shape[0]
    flags, factors = factors_of(me_ref[0], places, chips)

    @pl.when(functools.reduce(jnp.logical_or, flags))
    def _():
        def one_group(group, columns):
            keys, values = join_blocks(blocks, factors, columns)
            queries = group_queries((q_ref, sib_q_ref), group)
            for first, rows in chunks(tokens):
                update = fold(queries, first, keys, values, shift_ref[group, rows, :])
                acc_ref[group, rows, :] += update[:, :DH]
                total_ref[group, rows, :] += update[:, DH:]

        for_groups(one_group, *groups)

    for copy in copies:
        copy.wait()


def divide(acc, total):
    inverse = pl.reciprocal(total, approx=True)
    inverse = inverse * (2.0 - total * inverse)
    return (acc * inverse).astype(jnp.bfloat16)


def put_heads(out_refs, rows_ref, tables, group, result):
    tokens = out_refs[0].shape[0]
    columns = pl.ds(pl.multiple_of(group * WIDE, WIDE), WIDE)
    for i, (out_ref, table) in enumerate(zip(out_refs, tables)):
        pieces = [
            result[(2 * h + i) * tokens : (2 * h + i + 1) * tokens] for h in range(GROUP)
        ]
        piece = jnp.concatenate(pieces, axis=1)
        out_ref[:, columns] = piece
        rows_ref[i * CAP : (i + 1) * CAP, columns] = jnp.dot(
            table[...], piece, preferred_element_type=jnp.float32
        )


def running_attention(chips, me, sources, q_refs, put, scratch, sem):
    keys_ref, values_ref, acc_ref, total_ref, top_ref = scratch
    tokens = q_refs[0].shape[0]

    def fetch(source, target):
        copy = pltpu.make_async_copy(source, target, sem)
        copy.start()
        copy.wait()

    def one_group(group, columns):
        queries = group_queries(q_refs, group)
        for i in range(chips - 1):
            for j, block in enumerate(sources[2 * i : 2 * i + 2]):
                rows = pl.ds(j * tokens, tokens)
                fetch(block.at[pl.ds(0, tokens), columns], keys_ref.at[i, rows])
                fetch(block.at[pl.ds(tokens, tokens), columns], values_ref.at[i, rows])
        whole, key, value = sources[2 * chips - 2 :]
        own, sib = pl.ds(0, tokens), pl.ds(tokens, tokens)
        fetch(whole.at[own, columns], keys_ref.at[chips - 1, own])
        fetch(whole.at[sib, columns], values_ref.at[chips - 1, own])
        fetch(key.at[:, columns], keys_ref.at[chips - 1, sib])
        fetch(value.at[:, columns], values_ref.at[chips - 1, sib])
        acc_ref[...] = jnp.zeros_like(acc_ref)
        total_ref[...] = jnp.zeros_like(total_ref)
        top_ref[...] = jnp.full_like(top_ref, 2 * MASKED)

        def one_chip(i, inner):
            place = jnp.where(i % 2 == 1, (i + 1) // 2, -(i // 2))
            chip = chip_at(me, place, chips)

            @pl.when(chip <= me // 2)
            def _():
                keys, values = keys_ref[i], with_ones(values_ref[i])
                barred = jnp.where(chip == me // 2, MASKED, 0.0)
                bias = jnp.where(allowed_here(me % 2, tokens), 0.0, barred)
                for first, rows in chunks(tokens):
                    scores = scores_of(head_rows(*queries, first), keys)
                    scores = jnp.where(bias < 0.0, MASKED, scores)
                    old = top_ref[rows, :]
                    top = jnp.maximum(old, row_top(scores))
                    factor = jnp.exp2(old - top)
                    weights = weights_of(scores, top).astype(jnp.bfloat16)
                    update = jnp.dot(weights, values, preferred_element_type=jnp.float32)
                    acc_ref[rows, :] = acc_ref[rows, :] * factor + update[:, :DH]
                    total_ref[rows, :] = total_ref[rows, :] * factor + update[:, DH:]
                    top_ref[rows, :] = top

            return inner

        lax.fori_loop(0, chips, one_chip, 0)
        put(group, divide(acc_ref[...], total_ref[...]))

    for_groups(one_group)


def last_kernel(chips, me_ref, q_ref, sib_q_ref, *refs):
    blocks, (shift_ref, acc_ref, total_ref, gain_ref) = (refs[0], refs[1:3]), refs[3:7]
    tables, sources = refs[7:9], refs[9 : 10 + 2 * chips]
    refs = refs[10 + 2 * chips :]
    weights, refs = refs[:2], refs[2:]
    out_refs, picked_refs, loaded = refs[:2], refs[2:4], refs[4:6]
    rows_ref, worst_ref, sem, load_sems, *scratch = refs[6:]
    loads = [
        pltpu.make_async_copy(half_rows(me_ref, weight, False), target, load_sems.at[i])
        for i, (weight, target) in enumerate(zip(weights, loaded))
    ]
    for load in loads:
        load.start()
    q_refs = (q_ref, sib_q_ref)
    tokens, half_width = q_ref.shape
    me = me_ref[0]
    _, factors = factors_of(me, [chips // 2] * 2, chips)
    worst_ref[...] = jnp.zeros_like(worst_ref)

    def put(group, result):
        put_heads(out_refs, rows_ref, tables, group, result)

    def one_group(group, columns):
        keys, values = join_blocks(blocks, factors, columns)
        queries = group_queries(q_refs, group)
        results = []
        for first, rows in chunks(tokens):
            update = fold(queries, first, keys, values, shift_ref[group, rows, :])
            total = total_ref[group, rows, :] + update[:, DH:]
            worst_ref[...] = jnp.maximum(worst_ref[...], total)
            results.append(divide(acc_ref[group, rows, :] + update[:, :DH], total))
        put(group, jnp.concatenate(results, axis=0))

    for_groups(one_group)
    fits = jnp.max(worst_ref[...]) <= SUM_LIMIT

    @pl.when(jnp.logical_not(fits))
    def _():
        running_attention(chips, me, sources, q_refs, put, scratch, sem)

    columns = pl.ds(pl.multiple_of(me % 2 * half_width, half_width), half_width)
    rows = rows_ref[...]
    squares = jnp.broadcast_to(jnp.sum(rows * rows, axis=1, keepdims=True), (2 * CAP, DH))
    upper = squares.astype(jnp.bfloat16).astype(jnp.float32)
    lower = (squares - upper).astype(jnp.bfloat16).astype(jnp.float32)
    lane = lax.broadcasted_iota(jnp.int32, squares.shape, 1)
    rows = (rows * gain_ref[:, columns]).astype(jnp.bfloat16)
    squares = jnp.where(lane < DH // 2, upper, lower).astype(jnp.bfloat16)
    for i, ref in enumerate(picked_refs):
        ref[:, :half_width] = rows[i * CAP : (i + 1) * CAP]
        ref[:, half_width:] = squares[i * CAP : (i + 1) * CAP]
    for load in loads:
        load.wait()


class Attention:
    def __init__(self, me, queries, chips):
        self.me, self.queries, self.chips = me, queries, chips
        self.tokens, self.width = queries[0].shape
        self.rows = 2 * GROUP * self.tokens
        self.state_shape = pltpu.VMEM((HK // 2, self.rows, DH), jnp.float32)

    def call(self, kernel, name, args, others, out_shape, out_others, scratch, aliases=None):
        vmem, anywhere = pl.BlockSpec(memory_space=pltpu.VMEM), pl.BlockSpec(memory_space=pl.ANY)
        return pl.pallas_call(
            kernel,
            in_specs=[pl.BlockSpec(memory_space=pltpu.SMEM)]
            + [vmem] * (2 + len(args))
            + [anywhere] * len(others),
            out_specs=[vmem] * len(out_shape) + [anywhere] * len(out_others),
            out_shape=[*out_shape, *out_others],
            scratch_shapes=scratch,
            input_output_aliases=aliases or {},
            compiler_params=pltpu.CompilerParams(vmem_limit_bytes=ATTEND_MIB * MIB),
            cost_estimate=SMALL,
            name=name,
        )(self.me, *self.queries, *args, *others)

    def own(self, own, sib, weights=()):
        loads = len(weights)
        results = self.call(
            functools.partial(own_kernel, loads),
            "attend_own",
            (own, sib),
            [in_hbm(x) for x in weights],
            [self.state_shape] * 3,
            [pltpu.VMEM(x.shape, x.dtype) for x in weights],
            [pltpu.SemaphoreType.DMA] * loads,
        )
        return list(results[:2]), results[2], results[3:]

    def step(self, blocks, places, groups, shift, state, weights=()):
        count, loads = len(blocks), len(weights)
        results = self.call(
            functools.partial(step_kernel, self.chips, places, groups, loads),
            "attend_step",
            (*blocks, shift, *state),
            [in_hbm(x) for x in weights],
            [self.state_shape] * 2,
            [pltpu.VMEM(x.shape, x.dtype) for x in weights],
            [pltpu.SemaphoreType.DMA] * loads,
            {count + 4: 0, count + 5: 1},
        )
        return list(results[:2]), results[2:]

    def last(self, blocks, shift, state, gain, tables, sources, weights):
        out = pltpu.VMEM((self.tokens, self.width), jnp.bfloat16)
        picked = pltpu.VMEM((CAP, self.width + DH), jnp.bfloat16)
        loaded = [pltpu.VMEM((x.shape[0] // 2, x.shape[1]), x.dtype) for x in weights]
        kept = pltpu.VMEM((self.chips, 2 * self.tokens, DH), jnp.bfloat16)
        sums = pltpu.VMEM((self.rows, DH), jnp.float32)
        return self.call(
            functools.partial(last_kernel, self.chips),
            "attend_last",
            (*blocks, shift, *state, gain, *tables),
            (*sources, *(in_hbm(x) for x in weights)),
            [out, out, picked, picked],
            loaded,
            [
                pltpu.VMEM((2 * CAP, self.width), jnp.float32),
                pltpu.VMEM((STACK * 2 * self.tokens, DH), jnp.float32),
                pltpu.SemaphoreType.DMA,
                pltpu.SemaphoreType.DMA((len(weights),)),
                kept,
                kept,
                sums,
                sums,
                sums,
            ],
        )


def halves_kernel(stacks, me_ref, *refs):
    count = sum(stacks)
    sources, outs, sems = list(refs[:count]), refs[count:-1], refs[-1]
    core = me_ref[0] % 2
    copies = []
    for size, keep_ref, give_ref in zip(stacks, outs[::2], outs[1::2]):
        for i in range(size):
            source = sources.pop(0)
            rows, width = source.shape
            for side, target in ((core, keep_ref), (1 - core, give_ref)):
                columns = pl.ds(pl.multiple_of(side * (width // 2), width // 2), width // 2)
                copies.append((source.at[:, columns], target.at[pl.ds(i * rows, rows)]))
    copies = [pltpu.make_async_copy(*ends, sems.at[i]) for i, ends in enumerate(copies)]
    for copy in copies:
        copy.start()
    for copy in copies:
        copy.wait()


def halves(me, *stacks):
    anywhere = pl.BlockSpec(memory_space=pl.ANY)
    arrays = [x for stack in stacks for x in stack]
    outs = []
    for stack in stacks:
        rows, width = stack[0].shape
        outs += [pltpu.VMEM((len(stack) * rows, width // 2), stack[0].dtype)] * 2
    return pl.pallas_call(
        functools.partial(halves_kernel, [len(stack) for stack in stacks]),
        in_specs=[pl.BlockSpec(memory_space=pltpu.SMEM)] + [anywhere] * len(arrays),
        out_specs=[anywhere] * len(outs),
        out_shape=outs,
        scratch_shapes=[pltpu.SemaphoreType.DMA((2 * len(arrays),))],
        compiler_params=pltpu.CompilerParams(vmem_limit_bytes=MIB),
        cost_estimate=SMALL,
        name="halves",
    )(me, *(in_hbm(x) for x in arrays))


def half_rows(me_ref, ref, sibling):
    half = ref.shape[0] // 2
    side = 1 - me_ref[0] % 2 if sibling else me_ref[0] % 2
    return ref.at[pl.ds(pl.multiple_of(side * half, half), half), :]


def place_kernel(spots, *refs):
    blocks, out_ref = refs[: len(spots)], refs[-1]
    for index, ref in zip(spots, blocks):
        out_ref[index * CAP : (index + 1) * CAP] = ref[...]


def place(blocks, spots, rows):
    vmem = pl.BlockSpec(memory_space=pltpu.VMEM)
    earlier = [] if isinstance(rows, tuple) else [rows]
    shape = rows.shape if earlier else rows
    return pl.pallas_call(
        functools.partial(place_kernel, spots),
        in_specs=[vmem] * (len(blocks) + len(earlier)),
        out_specs=vmem,
        out_shape=pltpu.VMEM(shape, jnp.bfloat16),
        input_output_aliases={len(blocks): 0} if earlier else {},
        compiler_params=pltpu.CompilerParams(vmem_limit_bytes=4 * MIB),
        cost_estimate=SMALL,
        name="place",
    )(*blocks, *earlier)


def contract(rows_ref, gate_ref, up_ref, gate_sum, up_sum, order):
    half = gate_ref.shape[0]
    depth = min(1024, half)

    def one_part(step, carry):
        columns = pl.ds(pl.multiple_of(step * depth, depth), depth)
        part = order(rows_ref[:, columns])
        gate_sum[...] += jnp.dot(part, gate_ref[columns, :], preferred_element_type=jnp.float32)
        up_sum[...] += jnp.dot(part, up_ref[columns, :], preferred_element_type=jnp.float32)
        return carry

    lax.fori_loop(0, half // depth, one_part, 0)


def first_kernel(me_ref, rows_ref, gate_ref, up_ref, *refs):
    sources, (gate_sum, up_sum), targets, sems = refs[:2], refs[2:4], refs[4:6], refs[6]
    copies = [
        pltpu.make_async_copy(half_rows(me_ref, source, True), target, sems.at[i])
        for i, (source, target) in enumerate(zip(sources, targets))
    ]
    for copy in copies:
        copy.start()
    gate_sum[...] = jnp.zeros_like(gate_sum)
    up_sum[...] = jnp.zeros_like(up_sum)
    contract(rows_ref, gate_ref, up_ref, gate_sum, up_sum, lambda part: part)
    for copy in copies:
        copy.wait()


def second_kernel(rows_ref, gate_ref, up_ref, own_ref, gate_in, up_in, source_ref, out_ref, *refs):
    targets, (gate_sum, up_sum, sems) = refs[:PIECES], refs[PIECES:]
    piece = targets[0].shape[1]
    copies = [
        pltpu.make_async_copy(source_ref.at[:, pl.ds(i * piece, piece)], target, sems.at[i])
        for i, target in enumerate(targets)
    ]
    for copy in copies:
        copy.start()
    middle, half = rows_ref.shape[0] // 2, gate_ref.shape[0]

    def order(part):
        return jnp.concatenate([part[middle:], part[:middle]], axis=0)

    gate_sum[...] = gate_in[...]
    up_sum[...] = up_in[...]
    contract(rows_ref, gate_ref, up_ref, gate_sum, up_sum, order)
    squares = own_ref[:, half:].astype(jnp.float32) + order(rows_ref[:, half:].astype(jnp.float32))
    squares = squares[:, :1] + squares[:, DH // 2 : DH // 2 + 1]
    factor = lax.rsqrt(squares / (2 * half) + 1e-05)
    gate = gate_sum[...] * factor
    out_ref[...] = (gate / (1.0 + jnp.exp(-gate)) * (up_sum[...] * factor)).astype(jnp.bfloat16)
    for copy in copies:
        copy.wait()


def hidden_calls(me, rows, other_rows, loaded, w_gate, w_up, w_down):
    count, units, width = rows.shape[0], w_down.shape[0], w_down.shape[1]
    vmem, anywhere = pl.BlockSpec(memory_space=pltpu.VMEM), pl.BlockSpec(memory_space=pl.ANY)
    sums = [pltpu.VMEM((count, units), jnp.float32)] * 2
    params = pltpu.CompilerParams(vmem_limit_bytes=8 * MIB)
    cost = pl.CostEstimate(
        flops=2 * count * width * units, bytes_accessed=2 * width * units, transcendentals=count * units
    )
    *partial, gate, up = pl.pallas_call(
        first_kernel,
        in_specs=[pl.BlockSpec(memory_space=pltpu.SMEM)] + [vmem] * 3 + [anywhere] * 2,
        out_specs=[vmem] * 2 + [anywhere] * 2,
        out_shape=sums + [pltpu.VMEM((width // 2, units), w_gate.dtype)] * 2,
        scratch_shapes=[pltpu.SemaphoreType.DMA((2,))],
        compiler_params=params,
        cost_estimate=cost,
        name="hidden_first",
    )(me, rows, *loaded, in_hbm(w_gate), in_hbm(w_up))
    hidden, *downs = pl.pallas_call(
        second_kernel,
        in_specs=[vmem] * 6 + [anywhere],
        out_specs=[vmem] + [anywhere] * PIECES,
        out_shape=[pltpu.VMEM((count, units), jnp.bfloat16)]
        + [pltpu.VMEM((units, width // PIECES), w_down.dtype)] * PIECES,
        scratch_shapes=sums + [pltpu.SemaphoreType.DMA((PIECES,))],
        compiler_params=params,
        cost_estimate=cost,
        name="hidden_second",
    )(other_rows, gate, up, rows, *partial, in_hbm(w_down))
    return hidden, downs


def down_kernel(hidden_ref, down_ref, *refs):
    copies = []
    if len(refs) == 2:
        own_ref, sib_ref = refs
    else:
        me_ref, *parts, own_ref, sib_ref, result_ref, sems = refs
        width = parts[0].shape[1]
        core = me_ref[0] % 2
        for i, (side, source) in enumerate(zip((core, 1 - core), parts)):
            columns = pl.ds(pl.multiple_of(side * width, width), width)
            copies.append(pltpu.make_async_copy(source, result_ref.at[:, columns], sems.at[i]))
    for copy in copies:
        copy.start()
    middle, width = own_ref.shape
    cols = min(1024, width)

    def one_part(step, carry):
        columns = pl.ds(pl.multiple_of(step * cols, cols), cols)
        part = jnp.dot(hidden_ref[...], down_ref[:, columns], preferred_element_type=jnp.float32)
        part = part.astype(jnp.bfloat16)
        own_ref[:, columns] = part[:middle]
        sib_ref[:, columns] = part[middle:]
        return carry

    lax.fori_loop(0, width // cols, one_part, 0)
    for copy in copies:
        copy.wait()


def down_call(hidden, w_down, halves=()):
    rows, units = hidden.shape
    width = w_down.shape[1]
    vmem, anywhere = pl.BlockSpec(memory_space=pltpu.VMEM), pl.BlockSpec(memory_space=pl.ANY)
    more = [pl.BlockSpec(memory_space=pltpu.SMEM), anywhere, anywhere] if halves else []
    outs = [pltpu.VMEM((rows // 2, width), jnp.bfloat16)] * 2
    if halves:
        tokens, part = halves[1].shape
        outs.append(jax.ShapeDtypeStruct((tokens, 2 * part), jnp.bfloat16))
    return pl.pallas_call(
        down_kernel,
        in_specs=[vmem] * 2 + more,
        out_specs=[vmem] * 2 + [anywhere] * (len(outs) - 2),
        out_shape=outs,
        scratch_shapes=[pltpu.SemaphoreType.DMA((2,))] if halves else [],
        compiler_params=pltpu.CompilerParams(vmem_limit_bytes=8 * MIB),
        cost_estimate=pl.CostEstimate(
            flops=2 * rows * width * units,
            bytes_accessed=2 * width * units + 2 * rows * width,
            transcendentals=0,
        ),
        name="down",
    )(hidden, w_down, *halves)


def spread_kernel(start, *refs):
    parts, table_ref, out_ref, kept_ref, sems = refs[:4], refs[4], *refs[-3:]
    table = table_ref[...]
    width = kept_ref.shape[1]
    cols = min(1024, width)
    copies = []
    for i in range(width // cols):
        columns = slice(i * cols, (i + 1) * cols)
        total = sum(ref[:CAP, columns].astype(jnp.float32) for ref in parts).astype(jnp.bfloat16)
        kept_ref[:, columns] = lax.dot_general(
            table,
            jnp.concatenate([total] * PARTS, axis=0),
            (((0,), (0,)), ((), ())),
            preferred_element_type=jnp.float32,
        ).astype(jnp.bfloat16)
        target = out_ref.at[:, pl.ds(start + i * cols, cols)]
        copies.append(pltpu.make_async_copy(kept_ref.at[:, pl.ds(i * cols, cols)], target, sems.at[i]))
        copies[-1].start()
    for copy in copies:
        copy.wait()


def spread_call(parts, table, piece, pieces, previous):
    tokens = table.shape[1]
    width = parts[0].shape[1]
    earlier = [] if previous is None else [previous]
    vmem, anywhere = pl.BlockSpec(memory_space=pltpu.VMEM), pl.BlockSpec(memory_space=pl.ANY)
    return pl.pallas_call(
        functools.partial(spread_kernel, piece * width),
        in_specs=[vmem] * 5 + [anywhere] * len(earlier),
        out_specs=anywhere,
        out_shape=jax.ShapeDtypeStruct((tokens, width * pieces), jnp.bfloat16),
        input_output_aliases={5: 0} if earlier else {},
        scratch_shapes=[
            pltpu.VMEM((tokens, width), jnp.bfloat16),
            pltpu.SemaphoreType.DMA((max(1, width // 1024),)),
        ],
        compiler_params=pltpu.CompilerParams(vmem_limit_bytes=8 * MIB),
        cost_estimate=SMALL,
        name="spread",
    )(*parts, table, *earlier)


def add_kernel(row, columns, place, mine_ref, other_ref, *refs):
    received_ref, out_ref = (refs[0] if len(refs) > 1 else None), refs[-1]
    rows = slice(row, row + CAP)
    total = mine_ref[rows, columns].astype(jnp.float32) + other_ref[rows, columns].astype(jnp.float32)
    if received_ref is None:
        out_ref[...] = total.astype(jnp.bfloat16)
        return
    start, width = place, received_ref.shape[1]
    part = total[:, start : start + width] + received_ref[...].astype(jnp.float32)
    out_ref[:, start : start + width] = part.astype(jnp.bfloat16)
    if width < out_ref.shape[1]:
        rest = slice(width, None) if start == 0 else slice(0, start)
        out_ref[:, rest] = total[:, rest].astype(jnp.bfloat16)


def add_call(mine, other, index, columns, received=None, place=0):
    vmem = pl.BlockSpec(memory_space=pltpu.VMEM)
    more = () if received is None else (received,)
    return pl.pallas_call(
        functools.partial(add_kernel, index * CAP, columns, place),
        in_specs=[vmem] * (2 + len(more)),
        out_specs=vmem,
        out_shape=pltpu.VMEM((CAP, columns.stop - columns.start), jnp.bfloat16),
        compiler_params=pltpu.CompilerParams(vmem_limit_bytes=4 * MIB),
        cost_estimate=SMALL,
        name="add",
    )(mine, other, *more)


def reduce_chip_rows(pieces, half, chips, moves, token):
    width = pieces[0][0].shape[1]
    middle = width // 2
    chains = [(piece, side) for piece in range(len(pieces)) for side in range(2)]
    received = [None] * len(chains)
    for distance in range(half, 0, -1):
        for i, (piece, side) in enumerate(chains):
            mine, other = pieces[piece]
            if distance == half:
                columns = slice(side * middle, (side + 1) * middle)
                total = add_call(mine, other, chips - 1, columns)
            else:
                received[i], token = lax.optimization_barrier((received[i], token))
                index = distance if side else half - 1 + distance
                place = side * middle if distance == half - 1 else 0
                total = add_call(mine, other, index, slice(0, width), received[i], place)
            received[i] = moves[side](total)
    return [(*pieces[p], *received[2 * p : 2 * p + 2]) for p in range(len(pieces))]


def per_device(chips, queries, keys, values, norm_gain, expert_ids, gates, w_gate, w_up, w_down):
    right, left, sibling = permutations(chips)
    half = chips // 2
    go_right = lambda x: lax.ppermute(x, "ctx", right)
    go_left = lambda x: lax.ppermute(x, "ctx", left)
    swap = lambda x: lax.ppermute(x, "ctx", sibling)

    me = lax.axis_index("ctx").astype(jnp.int32).reshape(1)
    tokens = queries.shape[0]
    hits = (expert_ids == 0).astype(jnp.float32)
    chosen = jnp.sum(hits, axis=1)
    position = jnp.arange(tokens, dtype=jnp.int32)
    before = (position[None, :] < position[:, None]).astype(jnp.float32)
    slot = jnp.sum(before * chosen[None, :], axis=1).astype(jnp.int32)
    table = jnp.logical_and(
        slot[None, :] == jnp.arange(CAP, dtype=jnp.int32)[:, None], chosen[None, :] > 0
    ).astype(jnp.float32)
    rest = jnp.sum(gates * hits, axis=1)
    weights = []
    for _ in range(PARTS):
        part = lax.reduce_precision(rest, 8, 7)
        weights.append(table * part[None, :])
        rest = rest - part
    weighted = jnp.concatenate(weights, axis=0).astype(jnp.bfloat16)
    table = table.astype(jnp.bfloat16)

    own, give, q_own, q_give = halves(me, (keys, values), (queries,))
    across_right, across_left = [
        lax.ppermute(give, "ctx", [(i, j ^ 1) for i, j in pairs]) for pairs in (right, left)
    ]
    chains = [(go_right(own), go_left(own)), (across_right, across_left)]
    sib, q_sib = swap(give), swap(q_give)
    sib_table = swap(table)
    attention = Attention(me, (q_own, q_sib), chips)
    state, shift, _ = attention.own(own, sib)
    sources = [own, sib]
    middle, late = HK // 4, None
    for step in range(1, half):
        *chains[0], state = lax.optimization_barrier((*chains[0], state))
        if late is not None:
            state, _ = attention.step(*late, (middle, HK // 2), shift, state)
        chains[1], _, state = lax.optimization_barrier((chains[1], chains[0], state))
        late = [chain[side] for side in range(2) for chain in chains], [step, step, -step, -step]
        sources += late[0]
        if step < half - 1:
            chains = [(go_right(chain[0]), go_left(chain[1])) for chain in chains]
        else:
            far_sib = go_right(chains[1][0][:tokens]), go_left(chains[1][1][tokens:])
            opposite = [go_right(chains[0][0]), *far_sib]
        state, _ = attention.step(*late, (0, middle), shift, state)
    state, _ = attention.step(*late, (middle, HK // 2), shift, state)
    opposite, state = lax.optimization_barrier((opposite, state))
    sources += opposite
    mine, theirs, *picked, gate, up = attention.last(
        opposite, shift, state, norm_gain[None, :], (table, sib_table), sources, (w_gate, w_up)
    )

    chains = [(0, 1), (1, 0), (0, 0), (1, 1)]
    moves = [(go_right, go_left)[side] for _, side in chains]
    received = [move(picked[core]) for move, (core, _) in zip(moves, chains)]
    rows = place(picked, [0, chips], (2 * chips * CAP, picked[0].shape[1]))
    theirs = swap(theirs)
    for step in range(1, half):
        spots = [core * chips + side * (half - 1) + step for core, side in chains]
        blocks = list(received)
        for i, move in enumerate(moves):
            if step < half - 1 or i < 2:
                blocks[i], rows = lax.optimization_barrier((received[i], rows))
                received[i] = move(blocks[i])
        if step < half - 1:
            rows = place(blocks, spots, rows)
    rows = place(blocks + received[:2], spots + [chips - 1, 2 * chips - 1], rows)
    hidden, downs = hidden_calls(me, rows, swap(rows), (gate, up), w_gate, w_up, w_down)

    partial = []
    for piece in range(PIECES):
        if piece == 0:
            own, sib, result = down_call(hidden, downs[piece], (me, mine, theirs))
        else:
            own, sib = down_call(hidden, downs[piece])
        partial.append((own, swap(sib)))
    mixed = None
    for piece, parts in enumerate(reduce_chip_rows(partial, half, chips, (go_right, go_left), weighted)):
        mixed = spread_call(parts, weighted, piece, PIECES, mixed)
    return (result, mixed)


def solution(mesh):
    placed = (
        P(("groups", "ctx"), None),
        P(("groups", "ctx"), None),
        P(("groups", "ctx"), None),
        P(),
        P(("groups", "ctx"), None),
        P(("groups", "ctx"), None),
        P(None, "ctx"),
        P(None, "ctx"),
        P("ctx", None),
    )
    return jax.shard_map(
        functools.partial(per_device, mesh.shape["ctx"] // 2),
        mesh=mesh,
        in_specs=placed,
        out_specs=(P(("groups", "ctx"), None), P(("groups", "ctx"), None)),
        check_vma=False,
    )
```

```python
import functools
import math

import jax
import jax.numpy as jnp
from jax import lax
from jax.experimental import pallas as pl
from jax.experimental.pallas import tpu as pltpu
from jax.sharding import PartitionSpec as P

HQ = 64
HK = 8
DH = 128
CAP = 16
GROUP = HQ // HK
WIDE = GROUP * DH
LOG_SCALE = math.log2(math.e) / math.sqrt(DH)
MASKED = -1e30
PIECES = 2
ATTEND_MIB = 11
SMALL = pl.CostEstimate(flops=1, bytes_accessed=1, transcendentals=0)
SUM_LIMIT = 2.0**100
PARTS = 3
STACK = 4
MIB = 1 << 20


def in_hbm(x):
    return pltpu.with_memory_space_constraint(x, pltpu.HBM)


def ring_order(chips):
    return list(range(0, chips, 2)) + list(range(1, chips, 2))[::-1]


def permutations(chips):
    order = ring_order(chips)
    right, left = [], []
    for place in range(chips):
        here, there = order[place], order[(place + 1) % chips]
        for core in range(2):
            right.append((2 * here + core, 2 * there + core))
            left.append((2 * there + core, 2 * here + core))
    sibling = [(i, i ^ 1) for i in range(2 * chips)]
    return right, left, sibling


def chip_at(me, step, chips):
    chip = me // 2
    place = jnp.where(chip % 2 == 0, chip // 2, chips - 1 - chip // 2)
    source = (place - step + 2 * chips) % chips
    return jnp.where(source < chips // 2, 2 * source, 2 * (chips - 1 - source) + 1)


def head_rows(own, sib, first):
    pieces = []
    for h in range(first, first + STACK):
        columns = slice(h * DH, (h + 1) * DH)
        pieces += [own[:, columns], sib[:, columns]]
    return jnp.concatenate(pieces, axis=0)


def with_ones(values):
    return jnp.concatenate([values, jnp.ones_like(values)], axis=1)


def scores_of(queries, keys):
    return LOG_SCALE * lax.dot_general(
        queries, keys, (((1,), (1,)), ((), ())), preferred_element_type=jnp.float32
    )


def weights_of(scores, shift):
    return jnp.exp2(scores - jnp.concatenate([shift] * (scores.shape[1] // DH), axis=1))


def row_top(scores):
    return jnp.broadcast_to(jnp.max(scores, axis=1, keepdims=True), (scores.shape[0], DH))


def allowed_here(core, tokens):
    rows, columns = STACK * 2 * tokens, 2 * tokens

    def position(axis):
        place = lax.broadcasted_iota(jnp.int32, (rows, columns), axis) % (2 * tokens)
        return jnp.where(place < tokens, core * tokens + place, (1 - core) * tokens + place - tokens)

    return position(1) <= position(0)


def group_queries(queries, group):
    columns = pl.ds(pl.multiple_of(group * WIDE, WIDE), WIDE)
    return [ref[:, columns] for ref in queries]


def for_groups(body, first=0, stop=HK // 2):
    def step(group, carry):
        body(group, pl.ds(pl.multiple_of(group * DH, DH), DH))
        return carry

    lax.fori_loop(first, stop, step, 0)


def fold(queries, first, keys, values, shift):
    scores = scores_of(head_rows(*queries, first), keys)
    return jnp.dot(
        weights_of(scores, shift).astype(jnp.bfloat16), values, preferred_element_type=jnp.float32
    )


def block_of(ref, columns):
    if isinstance(ref, tuple):
        return ref[0][:, columns], ref[1][:, columns]
    tokens = ref.shape[0] // 2
    return ref[:tokens, columns], ref[tokens:, columns]


def join_blocks(refs, factors, columns):
    pairs = [block_of(ref, columns) for ref in refs]
    keys = jnp.concatenate([key for key, _ in pairs], axis=0)
    values = [with_ones(value) * factor for (_, value), factor in zip(pairs, factors)]
    return keys, jnp.concatenate(values, axis=0)


def factors_of(me, places, chips):
    flags = [chip_at(me, place, chips) < me // 2 for place in places]
    return flags, [jnp.where(flag, 1.0, 0.0).astype(jnp.bfloat16) for flag in flags]


def chunks(tokens):
    size = STACK * 2 * tokens
    return [(first, slice(first // STACK * size, (first // STACK + 1) * size)) for first in range(0, GROUP, STACK)]


def own_kernel(loads, me_ref, q_ref, sib_q_ref, own_ref, sib_ref, *refs):
    acc_ref, total_ref, shift_ref = refs[loads : loads + 3]
    copies = start_loads(loads, refs[:loads], refs[loads + 3 :])
    tokens = q_ref.shape[0]
    allowed = allowed_here(me_ref[0] % 2, tokens)

    def one_group(group, columns):
        keys, values = join_blocks((own_ref, sib_ref), (1, 1), columns)
        queries = group_queries((q_ref, sib_q_ref), group)
        for first, rows in chunks(tokens):
            scores = jnp.where(allowed, scores_of(head_rows(*queries, first), keys), MASKED)
            shift = row_top(scores)
            weights = weights_of(scores, shift).astype(jnp.bfloat16)
            update = jnp.dot(weights, values, preferred_element_type=jnp.float32)
            acc_ref[group, rows, :] = update[:, :DH]
            total_ref[group, rows, :] = update[:, DH:]
            shift_ref[group, rows, :] = shift

    for_groups(one_group)
    for copy in copies:
        copy.wait()


def start_loads(loads, sources, rest):
    copies = [
        pltpu.make_async_copy(source, target, sem)
        for source, target, sem in zip(sources, rest[:loads], rest[loads : 2 * loads])
    ]
    for copy in copies:
        copy.start()
    return copies


def step_kernel(chips, places, groups, loads, me_ref, q_ref, sib_q_ref, *refs):
    count = len(places)
    blocks, shift_ref = refs[:count], refs[count]
    refs = refs[count + 3 :]
    acc_ref, total_ref = refs[loads : loads + 2]
    copies = start_loads(loads, refs[:loads], refs[loads + 2 :])
    tokens = q_ref.shape[0]
    flags, factors = factors_of(me_ref[0], places, chips)

    @pl.when(functools.reduce(jnp.logical_or, flags))
    def _():
        def one_group(group, columns):
            keys, values = join_blocks(blocks, factors, columns)
            queries = group_queries((q_ref, sib_q_ref), group)
            for first, rows in chunks(tokens):
                update = fold(queries, first, keys, values, shift_ref[group, rows, :])
                acc_ref[group, rows, :] += update[:, :DH]
                total_ref[group, rows, :] += update[:, DH:]

        for_groups(one_group, *groups)

    for copy in copies:
        copy.wait()


def divide(acc, total):
    inverse = pl.reciprocal(total, approx=True)
    inverse = inverse * (2.0 - total * inverse)
    return (acc * inverse).astype(jnp.bfloat16)


def put_heads(out_refs, rows_ref, tables, group, result):
    tokens = out_refs[0].shape[0]
    columns = pl.ds(pl.multiple_of(group * WIDE, WIDE), WIDE)
    for i, (out_ref, table) in enumerate(zip(out_refs, tables)):
        pieces = [
            result[(2 * h + i) * tokens : (2 * h + i + 1) * tokens] for h in range(GROUP)
        ]
        piece = jnp.concatenate(pieces, axis=1)
        out_ref[:, columns] = piece
        rows_ref[i * CAP : (i + 1) * CAP, columns] = jnp.dot(
            table[...], piece, preferred_element_type=jnp.float32
        )


def running_attention(chips, me, sources, q_refs, put, scratch, sem):
    keys_ref, values_ref, acc_ref, total_ref, top_ref = scratch
    tokens = q_refs[0].shape[0]

    def fetch(source, target):
        copy = pltpu.make_async_copy(source, target, sem)
        copy.start()
        copy.wait()

    def one_group(group, columns):
        queries = group_queries(q_refs, group)
        for i in range(chips - 1):
            for j, block in enumerate(sources[2 * i : 2 * i + 2]):
                rows = pl.ds(j * tokens, tokens)
                fetch(block.at[pl.ds(0, tokens), columns], keys_ref.at[i, rows])
                fetch(block.at[pl.ds(tokens, tokens), columns], values_ref.at[i, rows])
        whole, key, value = sources[2 * chips - 2 :]
        own, sib = pl.ds(0, tokens), pl.ds(tokens, tokens)
        fetch(whole.at[own, columns], keys_ref.at[chips - 1, own])
        fetch(whole.at[sib, columns], values_ref.at[chips - 1, own])
        fetch(key.at[:, columns], keys_ref.at[chips - 1, sib])
        fetch(value.at[:, columns], values_ref.at[chips - 1, sib])
        acc_ref[...] = jnp.zeros_like(acc_ref)
        total_ref[...] = jnp.zeros_like(total_ref)
        top_ref[...] = jnp.full_like(top_ref, 2 * MASKED)

        def one_chip(i, inner):
            place = jnp.where(i % 2 == 1, (i + 1) // 2, -(i // 2))
            chip = chip_at(me, place, chips)

            @pl.when(chip <= me // 2)
            def _():
                keys, values = keys_ref[i], with_ones(values_ref[i])
                barred = jnp.where(chip == me // 2, MASKED, 0.0)
                bias = jnp.where(allowed_here(me % 2, tokens), 0.0, barred)
                for first, rows in chunks(tokens):
                    scores = scores_of(head_rows(*queries, first), keys)
                    scores = jnp.where(bias < 0.0, MASKED, scores)
                    old = top_ref[rows, :]
                    top = jnp.maximum(old, row_top(scores))
                    factor = jnp.exp2(old - top)
                    weights = weights_of(scores, top).astype(jnp.bfloat16)
                    update = jnp.dot(weights, values, preferred_element_type=jnp.float32)
                    acc_ref[rows, :] = acc_ref[rows, :] * factor + update[:, :DH]
                    total_ref[rows, :] = total_ref[rows, :] * factor + update[:, DH:]
                    top_ref[rows, :] = top

            return inner

        lax.fori_loop(0, chips, one_chip, 0)
        put(group, divide(acc_ref[...], total_ref[...]))

    for_groups(one_group)


def last_kernel(chips, me_ref, q_ref, sib_q_ref, *refs):
    blocks, (shift_ref, acc_ref, total_ref, gain_ref) = (refs[0], refs[1:3]), refs[3:7]
    tables, sources = refs[7:9], refs[9 : 10 + 2 * chips]
    refs = refs[10 + 2 * chips :]
    weights, refs = refs[:2], refs[2:]
    out_refs, picked_refs, loaded = refs[:2], refs[2:4], refs[4:6]
    rows_ref, worst_ref, sem, load_sems, *scratch = refs[6:]
    loads = [
        pltpu.make_async_copy(half_rows(me_ref, weight, False), target, load_sems.at[i])
        for i, (weight, target) in enumerate(zip(weights, loaded))
    ]
    for load in loads:
        load.start()
    q_refs = (q_ref, sib_q_ref)
    tokens, half_width = q_ref.shape
    me = me_ref[0]
    _, factors = factors_of(me, [chips // 2] * 2, chips)
    worst_ref[...] = jnp.zeros_like(worst_ref)

    def put(group, result):
        put_heads(out_refs, rows_ref, tables, group, result)

    def one_group(group, columns):
        keys, values = join_blocks(blocks, factors, columns)
        queries = group_queries(q_refs, group)
        results = []
        for first, rows in chunks(tokens):
            update = fold(queries, first, keys, values, shift_ref[group, rows, :])
            total = total_ref[group, rows, :] + update[:, DH:]
            worst_ref[...] = jnp.maximum(worst_ref[...], jnp.where(total <= SUM_LIMIT, 0.0, 1.0))
            results.append(divide(acc_ref[group, rows, :] + update[:, :DH], total))
        put(group, jnp.concatenate(results, axis=0))

    for_groups(one_group)
    fits = jnp.max(worst_ref[...]) < 0.5

    @pl.when(jnp.logical_not(fits))
    def _():
        running_attention(chips, me, sources, q_refs, put, scratch, sem)

    columns = pl.ds(pl.multiple_of(me % 2 * half_width, half_width), half_width)
    rows = rows_ref[...]
    squares = jnp.broadcast_to(jnp.sum(rows * rows, axis=1, keepdims=True), (2 * CAP, DH))
    upper = squares.astype(jnp.bfloat16).astype(jnp.float32)
    lower = (squares - upper).astype(jnp.bfloat16).astype(jnp.float32)
    lane = lax.broadcasted_iota(jnp.int32, squares.shape, 1)
    rows = (rows * gain_ref[:, columns]).astype(jnp.bfloat16)
    squares = jnp.where(lane < DH // 2, upper, lower).astype(jnp.bfloat16)
    for i, ref in enumerate(picked_refs):
        ref[:, :half_width] = rows[i * CAP : (i + 1) * CAP]
        ref[:, half_width:] = squares[i * CAP : (i + 1) * CAP]
    for load in loads:
        load.wait()


class Attention:
    def __init__(self, me, queries, chips):
        self.me, self.queries, self.chips = me, queries, chips
        self.tokens, self.width = queries[0].shape
        self.rows = 2 * GROUP * self.tokens
        self.state_shape = pltpu.VMEM((HK // 2, self.rows, DH), jnp.float32)

    def call(self, kernel, name, args, others, out_shape, out_others, scratch, aliases=None):
        vmem, anywhere = pl.BlockSpec(memory_space=pltpu.VMEM), pl.BlockSpec(memory_space=pl.ANY)
        return pl.pallas_call(
            kernel,
            in_specs=[pl.BlockSpec(memory_space=pltpu.SMEM)]
            + [vmem] * (2 + len(args))
            + [anywhere] * len(others),
            out_specs=[vmem] * len(out_shape) + [anywhere] * len(out_others),
            out_shape=[*out_shape, *out_others],
            scratch_shapes=scratch,
            input_output_aliases=aliases or {},
            compiler_params=pltpu.CompilerParams(vmem_limit_bytes=ATTEND_MIB * MIB),
            cost_estimate=SMALL,
            name=name,
        )(self.me, *self.queries, *args, *others)

    def own(self, own, sib, weights=()):
        loads = len(weights)
        results = self.call(
            functools.partial(own_kernel, loads),
            "attend_own",
            (own, sib),
            [in_hbm(x) for x in weights],
            [self.state_shape] * 3,
            [pltpu.VMEM(x.shape, x.dtype) for x in weights],
            [pltpu.SemaphoreType.DMA] * loads,
        )
        return list(results[:2]), results[2], results[3:]

    def step(self, blocks, places, groups, shift, state, weights=()):
        count, loads = len(blocks), len(weights)
        results = self.call(
            functools.partial(step_kernel, self.chips, places, groups, loads),
            "attend_step",
            (*blocks, shift, *state),
            [in_hbm(x) for x in weights],
            [self.state_shape] * 2,
            [pltpu.VMEM(x.shape, x.dtype) for x in weights],
            [pltpu.SemaphoreType.DMA] * loads,
            {count + 4: 0, count + 5: 1},
        )
        return list(results[:2]), results[2:]

    def last(self, blocks, shift, state, gain, tables, sources, weights):
        out = pltpu.VMEM((self.tokens, self.width), jnp.bfloat16)
        picked = pltpu.VMEM((CAP, self.width + DH), jnp.bfloat16)
        loaded = [pltpu.VMEM((x.shape[0] // 2, x.shape[1]), x.dtype) for x in weights]
        kept = pltpu.VMEM((self.chips, 2 * self.tokens, DH), jnp.bfloat16)
        sums = pltpu.VMEM((self.rows, DH), jnp.float32)
        return self.call(
            functools.partial(last_kernel, self.chips),
            "attend_last",
            (*blocks, shift, *state, gain, *tables),
            (*sources, *(in_hbm(x) for x in weights)),
            [out, out, picked, picked],
            loaded,
            [
                pltpu.VMEM((2 * CAP, self.width), jnp.float32),
                pltpu.VMEM((STACK * 2 * self.tokens, DH), jnp.float32),
                pltpu.SemaphoreType.DMA,
                pltpu.SemaphoreType.DMA((len(weights),)),
                kept,
                kept,
                sums,
                sums,
                sums,
            ],
        )


def halves_kernel(stacks, me_ref, *refs):
    count = sum(stacks)
    sources, outs, sems = list(refs[:count]), refs[count:-1], refs[-1]
    core = me_ref[0] % 2
    copies = []
    for size, keep_ref, give_ref in zip(stacks, outs[::2], outs[1::2]):
        for i in range(size):
            source = sources.pop(0)
            rows, width = source.shape
            for side, target in ((core, keep_ref), (1 - core, give_ref)):
                columns = pl.ds(pl.multiple_of(side * (width // 2), width // 2), width // 2)
                copies.append((source.at[:, columns], target.at[pl.ds(i * rows, rows)]))
    copies = [pltpu.make_async_copy(*ends, sems.at[i]) for i, ends in enumerate(copies)]
    for copy in copies:
        copy.start()
    for copy in copies:
        copy.wait()


def halves(me, *stacks):
    anywhere = pl.BlockSpec(memory_space=pl.ANY)
    arrays = [x for stack in stacks for x in stack]
    outs = []
    for stack in stacks:
        rows, width = stack[0].shape
        outs += [pltpu.VMEM((len(stack) * rows, width // 2), stack[0].dtype)] * 2
    return pl.pallas_call(
        functools.partial(halves_kernel, [len(stack) for stack in stacks]),
        in_specs=[pl.BlockSpec(memory_space=pltpu.SMEM)] + [anywhere] * len(arrays),
        out_specs=[anywhere] * len(outs),
        out_shape=outs,
        scratch_shapes=[pltpu.SemaphoreType.DMA((2 * len(arrays),))],
        compiler_params=pltpu.CompilerParams(vmem_limit_bytes=MIB),
        cost_estimate=SMALL,
        name="halves",
    )(me, *(in_hbm(x) for x in arrays))


def half_rows(me_ref, ref, sibling):
    half = ref.shape[0] // 2
    side = 1 - me_ref[0] % 2 if sibling else me_ref[0] % 2
    return ref.at[pl.ds(pl.multiple_of(side * half, half), half), :]


def place_kernel(spots, *refs):
    blocks, out_ref = refs[: len(spots)], refs[-1]
    for index, ref in zip(spots, blocks):
        out_ref[index * CAP : (index + 1) * CAP] = ref[...]


def place(blocks, spots, rows):
    vmem = pl.BlockSpec(memory_space=pltpu.VMEM)
    earlier = [] if isinstance(rows, tuple) else [rows]
    shape = rows.shape if earlier else rows
    return pl.pallas_call(
        functools.partial(place_kernel, spots),
        in_specs=[vmem] * (len(blocks) + len(earlier)),
        out_specs=vmem,
        out_shape=pltpu.VMEM(shape, jnp.bfloat16),
        input_output_aliases={len(blocks): 0} if earlier else {},
        compiler_params=pltpu.CompilerParams(vmem_limit_bytes=4 * MIB),
        cost_estimate=SMALL,
        name="place",
    )(*blocks, *earlier)


def contract(rows_ref, gate_ref, up_ref, gate_sum, up_sum, order):
    half = gate_ref.shape[0]
    depth = min(1024, half)

    def one_part(step, carry):
        columns = pl.ds(pl.multiple_of(step * depth, depth), depth)
        part = order(rows_ref[:, columns])
        gate_sum[...] += jnp.dot(part, gate_ref[columns, :], preferred_element_type=jnp.float32)
        up_sum[...] += jnp.dot(part, up_ref[columns, :], preferred_element_type=jnp.float32)
        return carry

    lax.fori_loop(0, half // depth, one_part, 0)


def first_kernel(me_ref, rows_ref, gate_ref, up_ref, *refs):
    sources, (gate_sum, up_sum), targets, sems = refs[:2], refs[2:4], refs[4:6], refs[6]
    copies = [
        pltpu.make_async_copy(half_rows(me_ref, source, True), target, sems.at[i])
        for i, (source, target) in enumerate(zip(sources, targets))
    ]
    for copy in copies:
        copy.start()
    gate_sum[...] = jnp.zeros_like(gate_sum)
    up_sum[...] = jnp.zeros_like(up_sum)
    contract(rows_ref, gate_ref, up_ref, gate_sum, up_sum, lambda part: part)
    for copy in copies:
        copy.wait()


def second_kernel(rows_ref, gate_ref, up_ref, own_ref, gate_in, up_in, source_ref, out_ref, *refs):
    targets, (gate_sum, up_sum, sems) = refs[:PIECES], refs[PIECES:]
    piece = targets[0].shape[1]
    copies = [
        pltpu.make_async_copy(source_ref.at[:, pl.ds(i * piece, piece)], target, sems.at[i])
        for i, target in enumerate(targets)
    ]
    for copy in copies:
        copy.start()
    middle, half = rows_ref.shape[0] // 2, gate_ref.shape[0]

    def order(part):
        return jnp.concatenate([part[middle:], part[:middle]], axis=0)

    gate_sum[...] = gate_in[...]
    up_sum[...] = up_in[...]
    contract(rows_ref, gate_ref, up_ref, gate_sum, up_sum, order)
    squares = own_ref[:, half:].astype(jnp.float32) + order(rows_ref[:, half:].astype(jnp.float32))
    squares = squares[:, :1] + squares[:, DH // 2 : DH // 2 + 1]
    factor = lax.rsqrt(squares / (2 * half) + 1e-05)
    gate = gate_sum[...] * factor
    out_ref[...] = (gate / (1.0 + jnp.exp(-gate)) * (up_sum[...] * factor)).astype(jnp.bfloat16)
    for copy in copies:
        copy.wait()


def hidden_calls(me, rows, other_rows, loaded, w_gate, w_up, w_down):
    count, units, width = rows.shape[0], w_down.shape[0], w_down.shape[1]
    vmem, anywhere = pl.BlockSpec(memory_space=pltpu.VMEM), pl.BlockSpec(memory_space=pl.ANY)
    sums = [pltpu.VMEM((count, units), jnp.float32)] * 2
    params = pltpu.CompilerParams(vmem_limit_bytes=8 * MIB)
    cost = pl.CostEstimate(
        flops=2 * count * width * units, bytes_accessed=2 * width * units, transcendentals=count * units
    )
    *partial, gate, up = pl.pallas_call(
        first_kernel,
        in_specs=[pl.BlockSpec(memory_space=pltpu.SMEM)] + [vmem] * 3 + [anywhere] * 2,
        out_specs=[vmem] * 2 + [anywhere] * 2,
        out_shape=sums + [pltpu.VMEM((width // 2, units), w_gate.dtype)] * 2,
        scratch_shapes=[pltpu.SemaphoreType.DMA((2,))],
        compiler_params=params,
        cost_estimate=cost,
        name="hidden_first",
    )(me, rows, *loaded, in_hbm(w_gate), in_hbm(w_up))
    hidden, *downs = pl.pallas_call(
        second_kernel,
        in_specs=[vmem] * 6 + [anywhere],
        out_specs=[vmem] + [anywhere] * PIECES,
        out_shape=[pltpu.VMEM((count, units), jnp.bfloat16)]
        + [pltpu.VMEM((units, width // PIECES), w_down.dtype)] * PIECES,
        scratch_shapes=sums + [pltpu.SemaphoreType.DMA((PIECES,))],
        compiler_params=params,
        cost_estimate=cost,
        name="hidden_second",
    )(other_rows, gate, up, rows, *partial, in_hbm(w_down))
    return hidden, downs


def down_kernel(hidden_ref, down_ref, *refs):
    copies = []
    if len(refs) == 2:
        own_ref, sib_ref = refs
    else:
        me_ref, *parts, own_ref, sib_ref, result_ref, sems = refs
        width = parts[0].shape[1]
        core = me_ref[0] % 2
        for i, (side, source) in enumerate(zip((core, 1 - core), parts)):
            columns = pl.ds(pl.multiple_of(side * width, width), width)
            copies.append(pltpu.make_async_copy(source, result_ref.at[:, columns], sems.at[i]))
    for copy in copies:
        copy.start()
    middle, width = own_ref.shape
    cols = min(1024, width)

    def one_part(step, carry):
        columns = pl.ds(pl.multiple_of(step * cols, cols), cols)
        part = jnp.dot(hidden_ref[...], down_ref[:, columns], preferred_element_type=jnp.float32)
        part = part.astype(jnp.bfloat16)
        own_ref[:, columns] = part[:middle]
        sib_ref[:, columns] = part[middle:]
        return carry

    lax.fori_loop(0, width // cols, one_part, 0)
    for copy in copies:
        copy.wait()


def down_call(hidden, w_down, halves=()):
    rows, units = hidden.shape
    width = w_down.shape[1]
    vmem, anywhere = pl.BlockSpec(memory_space=pltpu.VMEM), pl.BlockSpec(memory_space=pl.ANY)
    more = [pl.BlockSpec(memory_space=pltpu.SMEM), anywhere, anywhere] if halves else []
    outs = [pltpu.VMEM((rows // 2, width), jnp.bfloat16)] * 2
    if halves:
        tokens, part = halves[1].shape
        outs.append(jax.ShapeDtypeStruct((tokens, 2 * part), jnp.bfloat16))
    return pl.pallas_call(
        down_kernel,
        in_specs=[vmem] * 2 + more,
        out_specs=[vmem] * 2 + [anywhere] * (len(outs) - 2),
        out_shape=outs,
        scratch_shapes=[pltpu.SemaphoreType.DMA((2,))] if halves else [],
        compiler_params=pltpu.CompilerParams(vmem_limit_bytes=8 * MIB),
        cost_estimate=pl.CostEstimate(
            flops=2 * rows * width * units,
            bytes_accessed=2 * width * units + 2 * rows * width,
            transcendentals=0,
        ),
        name="down",
    )(hidden, w_down, *halves)


def spread_kernel(start, *refs):
    parts, table_ref, out_ref, kept_ref, sems = refs[:4], refs[4], *refs[-3:]
    table = table_ref[...]
    width = kept_ref.shape[1]
    cols = min(1024, width)
    copies = []
    for i in range(width // cols):
        columns = slice(i * cols, (i + 1) * cols)
        total = sum(ref[:CAP, columns].astype(jnp.float32) for ref in parts).astype(jnp.bfloat16)
        kept_ref[:, columns] = lax.dot_general(
            table,
            jnp.concatenate([total] * PARTS, axis=0),
            (((0,), (0,)), ((), ())),
            preferred_element_type=jnp.float32,
        ).astype(jnp.bfloat16)
        target = out_ref.at[:, pl.ds(start + i * cols, cols)]
        copies.append(pltpu.make_async_copy(kept_ref.at[:, pl.ds(i * cols, cols)], target, sems.at[i]))
        copies[-1].start()
    for copy in copies:
        copy.wait()


def spread_call(parts, table, piece, pieces, previous):
    tokens = table.shape[1]
    width = parts[0].shape[1]
    earlier = [] if previous is None else [previous]
    vmem, anywhere = pl.BlockSpec(memory_space=pltpu.VMEM), pl.BlockSpec(memory_space=pl.ANY)
    return pl.pallas_call(
        functools.partial(spread_kernel, piece * width),
        in_specs=[vmem] * 5 + [anywhere] * len(earlier),
        out_specs=anywhere,
        out_shape=jax.ShapeDtypeStruct((tokens, width * pieces), jnp.bfloat16),
        input_output_aliases={5: 0} if earlier else {},
        scratch_shapes=[
            pltpu.VMEM((tokens, width), jnp.bfloat16),
            pltpu.SemaphoreType.DMA((max(1, width // 1024),)),
        ],
        compiler_params=pltpu.CompilerParams(vmem_limit_bytes=8 * MIB),
        cost_estimate=SMALL,
        name="spread",
    )(*parts, table, *earlier)


def add_kernel(row, columns, place, mine_ref, other_ref, *refs):
    received_ref, out_ref = (refs[0] if len(refs) > 1 else None), refs[-1]
    rows = slice(row, row + CAP)
    total = mine_ref[rows, columns].astype(jnp.float32) + other_ref[rows, columns].astype(jnp.float32)
    if received_ref is None:
        out_ref[...] = total.astype(jnp.bfloat16)
        return
    start, width = place, received_ref.shape[1]
    part = total[:, start : start + width] + received_ref[...].astype(jnp.float32)
    out_ref[:, start : start + width] = part.astype(jnp.bfloat16)
    if width < out_ref.shape[1]:
        rest = slice(width, None) if start == 0 else slice(0, start)
        out_ref[:, rest] = total[:, rest].astype(jnp.bfloat16)


def add_call(mine, other, index, columns, received=None, place=0):
    vmem = pl.BlockSpec(memory_space=pltpu.VMEM)
    more = () if received is None else (received,)
    return pl.pallas_call(
        functools.partial(add_kernel, index * CAP, columns, place),
        in_specs=[vmem] * (2 + len(more)),
        out_specs=vmem,
        out_shape=pltpu.VMEM((CAP, columns.stop - columns.start), jnp.bfloat16),
        compiler_params=pltpu.CompilerParams(vmem_limit_bytes=4 * MIB),
        cost_estimate=SMALL,
        name="add",
    )(mine, other, *more)


def reduce_chip_rows(pieces, half, chips, moves, token):
    width = pieces[0][0].shape[1]
    middle = width // 2
    chains = [(piece, side) for piece in range(len(pieces)) for side in range(2)]
    received = [None] * len(chains)
    for distance in range(half, 0, -1):
        for i, (piece, side) in enumerate(chains):
            mine, other = pieces[piece]
            if distance == half:
                columns = slice(side * middle, (side + 1) * middle)
                total = add_call(mine, other, chips - 1, columns)
            else:
                received[i], token = lax.optimization_barrier((received[i], token))
                index = distance if side else half - 1 + distance
                place = side * middle if distance == half - 1 else 0
                total = add_call(mine, other, index, slice(0, width), received[i], place)
            received[i] = moves[side](total)
    return [(*pieces[p], *received[2 * p : 2 * p + 2]) for p in range(len(pieces))]


def per_device(chips, queries, keys, values, norm_gain, expert_ids, gates, w_gate, w_up, w_down):
    right, left, sibling = permutations(chips)
    half = chips // 2
    go_right = lambda x: lax.ppermute(x, "ctx", right)
    go_left = lambda x: lax.ppermute(x, "ctx", left)
    swap = lambda x: lax.ppermute(x, "ctx", sibling)

    me = lax.axis_index("ctx").astype(jnp.int32).reshape(1)
    tokens = queries.shape[0]
    hits = (expert_ids == 0).astype(jnp.float32)
    chosen = jnp.sum(hits, axis=1)
    position = jnp.arange(tokens, dtype=jnp.int32)
    before = (position[None, :] < position[:, None]).astype(jnp.float32)
    slot = jnp.sum(before * chosen[None, :], axis=1).astype(jnp.int32)
    table = jnp.logical_and(
        slot[None, :] == jnp.arange(CAP, dtype=jnp.int32)[:, None], chosen[None, :] > 0
    ).astype(jnp.float32)
    rest = jnp.sum(gates * hits, axis=1)
    weights = []
    for _ in range(PARTS):
        part = lax.reduce_precision(rest, 8, 7)
        weights.append(table * part[None, :])
        rest = rest - part
    weighted = jnp.concatenate(weights, axis=0).astype(jnp.bfloat16)
    table = table.astype(jnp.bfloat16)

    own, give, q_own, q_give = halves(me, (keys, values), (queries,))
    across_right, across_left = [
        lax.ppermute(give, "ctx", [(i, j ^ 1) for i, j in pairs]) for pairs in (right, left)
    ]
    chains = [(go_right(own), go_left(own)), (across_right, across_left)]
    sib, q_sib = swap(give), swap(q_give)
    sib_table = swap(table)
    attention = Attention(me, (q_own, q_sib), chips)
    state, shift, _ = attention.own(own, sib)
    sources = [own, sib]
    middle, late = HK // 4, None
    for step in range(1, half):
        *chains[0], state = lax.optimization_barrier((*chains[0], state))
        if late is not None:
            state, _ = attention.step(*late, (middle, HK // 2), shift, state)
        chains[1], _, state = lax.optimization_barrier((chains[1], chains[0], state))
        late = [chain[side] for side in range(2) for chain in chains], [step, step, -step, -step]
        sources += late[0]
        if step < half - 1:
            chains = [(go_right(chain[0]), go_left(chain[1])) for chain in chains]
        else:
            far_sib = go_right(chains[1][0][:tokens]), go_left(chains[1][1][tokens:])
            opposite = [go_right(chains[0][0]), *far_sib]
        state, _ = attention.step(*late, (0, middle), shift, state)
    state, _ = attention.step(*late, (middle, HK // 2), shift, state)
    opposite, state = lax.optimization_barrier((opposite, state))
    sources += opposite
    mine, theirs, *picked, gate, up = attention.last(
        opposite, shift, state, norm_gain[None, :], (table, sib_table), sources, (w_gate, w_up)
    )

    chains = [(0, 1), (1, 0), (0, 0), (1, 1)]
    moves = [(go_right, go_left)[side] for _, side in chains]
    received = [move(picked[core]) for move, (core, _) in zip(moves, chains)]
    rows = place(picked, [0, chips], (2 * chips * CAP, picked[0].shape[1]))
    theirs = swap(theirs)
    for step in range(1, half):
        spots = [core * chips + side * (half - 1) + step for core, side in chains]
        blocks = list(received)
        for i, move in enumerate(moves):
            if step < half - 1 or i < 2:
                blocks[i], rows = lax.optimization_barrier((received[i], rows))
                received[i] = move(blocks[i])
        if step < half - 1:
            rows = place(blocks, spots, rows)
    rows = place(blocks + received[:2], spots + [chips - 1, 2 * chips - 1], rows)
    hidden, downs = hidden_calls(me, rows, swap(rows), (gate, up), w_gate, w_up, w_down)

    partial = []
    for piece in range(PIECES):
        if piece == 0:
            own, sib, result = down_call(hidden, downs[piece], (me, mine, theirs))
        else:
            own, sib = down_call(hidden, downs[piece])
        partial.append((own, swap(sib)))
    mixed = None
    for piece, parts in enumerate(reduce_chip_rows(partial, half, chips, (go_right, go_left), weighted)):
        mixed = spread_call(parts, weighted, piece, PIECES, mixed)
    return (result, mixed)


def solution(mesh):
    placed = (
        P(("groups", "ctx"), None),
        P(("groups", "ctx"), None),
        P(("groups", "ctx"), None),
        P(),
        P(("groups", "ctx"), None),
        P(("groups", "ctx"), None),
        P(None, "ctx"),
        P(None, "ctx"),
        P("ctx", None),
    )
    return jax.shard_map(
        functools.partial(per_device, mesh.shape["ctx"] // 2),
        mesh=mesh,
        in_specs=placed,
        out_specs=(P(("groups", "ctx"), None), P(("groups", "ctx"), None)),
        check_vma=False,
    )
```

```python
import functools
import math

import jax
import jax.numpy as jnp
from jax import lax
from jax.experimental import pallas as pl
from jax.experimental.pallas import tpu as pltpu
from jax.sharding import PartitionSpec as P

HQ = 64
HK = 8
DH = 128
CAP = 16
GROUP = HQ // HK
WIDE = GROUP * DH
LOG_SCALE = math.log2(math.e) / math.sqrt(DH)
MASKED = -1e30
PIECES = 2
ATTEND_MIB = 11
SMALL = pl.CostEstimate(flops=1, bytes_accessed=1, transcendentals=0)
SUM_LIMIT = 2.0**100
PARTS = 3
STACK = 8
MIB = 1 << 20


def in_hbm(x):
    return pltpu.with_memory_space_constraint(x, pltpu.HBM)


def ring_order(chips):
    return list(range(0, chips, 2)) + list(range(1, chips, 2))[::-1]


def permutations(chips):
    order = ring_order(chips)
    right, left = [], []
    for place in range(chips):
        here, there = order[place], order[(place + 1) % chips]
        for core in range(2):
            right.append((2 * here + core, 2 * there + core))
            left.append((2 * there + core, 2 * here + core))
    sibling = [(i, i ^ 1) for i in range(2 * chips)]
    return right, left, sibling


def chip_at(me, step, chips):
    chip = me // 2
    place = jnp.where(chip % 2 == 0, chip // 2, chips - 1 - chip // 2)
    source = (place - step + 2 * chips) % chips
    return jnp.where(source < chips // 2, 2 * source, 2 * (chips - 1 - source) + 1)


def head_rows(own, sib, first):
    pieces = []
    for h in range(first, first + STACK):
        columns = slice(h * DH, (h + 1) * DH)
        pieces += [own[:, columns], sib[:, columns]]
    return jnp.concatenate(pieces, axis=0)


def with_ones(values):
    return jnp.concatenate([values, jnp.ones_like(values)], axis=1)


def scores_of(queries, keys):
    return LOG_SCALE * lax.dot_general(
        queries, keys, (((1,), (1,)), ((), ())), preferred_element_type=jnp.float32
    )


def weights_of(scores, shift):
    return jnp.exp2(scores - jnp.concatenate([shift] * (scores.shape[1] // DH), axis=1))


def row_top(scores):
    return jnp.broadcast_to(jnp.max(scores, axis=1, keepdims=True), (scores.shape[0], DH))


def allowed_here(core, tokens):
    rows, columns = STACK * 2 * tokens, 2 * tokens

    def position(axis):
        place = lax.broadcasted_iota(jnp.int32, (rows, columns), axis) % (2 * tokens)
        return jnp.where(place < tokens, core * tokens + place, (1 - core) * tokens + place - tokens)

    return position(1) <= position(0)


def group_queries(queries, group):
    columns = pl.ds(pl.multiple_of(group * WIDE, WIDE), WIDE)
    return [ref[:, columns] for ref in queries]


def for_groups(body, first=0, stop=HK // 2):
    def step(group, carry):
        body(group, pl.ds(pl.multiple_of(group * DH, DH), DH))
        return carry

    lax.fori_loop(first, stop, step, 0)


def fold(queries, first, keys, values, shift):
    scores = scores_of(head_rows(*queries, first), keys)
    return jnp.dot(
        weights_of(scores, shift).astype(jnp.bfloat16), values, preferred_element_type=jnp.float32
    )


def block_of(ref, columns):
    if isinstance(ref, tuple):
        return ref[0][:, columns], ref[1][:, columns]
    tokens = ref.shape[0] // 2
    return ref[:tokens, columns], ref[tokens:, columns]


def join_blocks(refs, factors, columns):
    pairs = [block_of(ref, columns) for ref in refs]
    keys = jnp.concatenate([key for key, _ in pairs], axis=0)
    values = [with_ones(value) * factor for (_, value), factor in zip(pairs, factors)]
    return keys, jnp.concatenate(values, axis=0)


def factors_of(me, places, chips):
    flags = [chip_at(me, place, chips) < me // 2 for place in places]
    return flags, [jnp.where(flag, 1.0, 0.0).astype(jnp.bfloat16) for flag in flags]


def chunks(tokens):
    size = STACK * 2 * tokens
    return [(first, slice(first // STACK * size, (first // STACK + 1) * size)) for first in range(0, GROUP, STACK)]


def own_kernel(loads, me_ref, q_ref, sib_q_ref, own_ref, sib_ref, *refs):
    acc_ref, total_ref, shift_ref = refs[loads : loads + 3]
    copies = start_loads(loads, refs[:loads], refs[loads + 3 :])
    tokens = q_ref.shape[0]
    allowed = allowed_here(me_ref[0] % 2, tokens)

    def one_group(group, columns):
        keys, values = join_blocks((own_ref, sib_ref), (1, 1), columns)
        queries = group_queries((q_ref, sib_q_ref), group)
        for first, rows in chunks(tokens):
            scores = jnp.where(allowed, scores_of(head_rows(*queries, first), keys), MASKED)
            shift = row_top(scores)
            weights = weights_of(scores, shift).astype(jnp.bfloat16)
            update = jnp.dot(weights, values, preferred_element_type=jnp.float32)
            acc_ref[group, rows, :] = update[:, :DH]
            total_ref[group, rows, :] = update[:, DH:]
            shift_ref[group, rows, :] = shift

    for_groups(one_group)
    for copy in copies:
        copy.wait()


def start_loads(loads, sources, rest):
    copies = [
        pltpu.make_async_copy(source, target, sem)
        for source, target, sem in zip(sources, rest[:loads], rest[loads : 2 * loads])
    ]
    for copy in copies:
        copy.start()
    return copies


def step_kernel(chips, places, groups, loads, me_ref, q_ref, sib_q_ref, *refs):
    count = len(places)
    blocks, shift_ref = refs[:count], refs[count]
    refs = refs[count + 3 :]
    acc_ref, total_ref = refs[loads : loads + 2]
    copies = start_loads(loads, refs[:loads], refs[loads + 2 :])
    tokens = q_ref.shape[0]
    flags, factors = factors_of(me_ref[0], places, chips)

    @pl.when(functools.reduce(jnp.logical_or, flags))
    def _():
        def one_group(group, columns):
            keys, values = join_blocks(blocks, factors, columns)
            queries = group_queries((q_ref, sib_q_ref), group)
            for first, rows in chunks(tokens):
                update = fold(queries, first, keys, values, shift_ref[group, rows, :])
                acc_ref[group, rows, :] += update[:, :DH]
                total_ref[group, rows, :] += update[:, DH:]

        for_groups(one_group, *groups)

    for copy in copies:
        copy.wait()


def divide(acc, total):
    inverse = pl.reciprocal(total, approx=True)
    inverse = inverse * (2.0 - total * inverse)
    return (acc * inverse).astype(jnp.bfloat16)


def put_heads(out_refs, rows_ref, tables, group, result):
    tokens = out_refs[0].shape[0]
    columns = pl.ds(pl.multiple_of(group * WIDE, WIDE), WIDE)
    for i, (out_ref, table) in enumerate(zip(out_refs, tables)):
        pieces = [
            result[(2 * h + i) * tokens : (2 * h + i + 1) * tokens] for h in range(GROUP)
        ]
        piece = jnp.concatenate(pieces, axis=1)
        out_ref[:, columns] = piece
        rows_ref[i * CAP : (i + 1) * CAP, columns] = jnp.dot(
            table[...], piece, preferred_element_type=jnp.float32
        )


def running_attention(chips, me, sources, q_refs, put, scratch, sem):
    keys_ref, values_ref, acc_ref, total_ref, top_ref = scratch
    tokens = q_refs[0].shape[0]

    def fetch(source, target):
        copy = pltpu.make_async_copy(source, target, sem)
        copy.start()
        copy.wait()

    def one_group(group, columns):
        queries = group_queries(q_refs, group)
        for i in range(chips - 1):
            for j, block in enumerate(sources[2 * i : 2 * i + 2]):
                rows = pl.ds(j * tokens, tokens)
                fetch(block.at[pl.ds(0, tokens), columns], keys_ref.at[i, rows])
                fetch(block.at[pl.ds(tokens, tokens), columns], values_ref.at[i, rows])
        whole, key, value = sources[2 * chips - 2 :]
        own, sib = pl.ds(0, tokens), pl.ds(tokens, tokens)
        fetch(whole.at[own, columns], keys_ref.at[chips - 1, own])
        fetch(whole.at[sib, columns], values_ref.at[chips - 1, own])
        fetch(key.at[:, columns], keys_ref.at[chips - 1, sib])
        fetch(value.at[:, columns], values_ref.at[chips - 1, sib])
        acc_ref[...] = jnp.zeros_like(acc_ref)
        total_ref[...] = jnp.zeros_like(total_ref)
        top_ref[...] = jnp.full_like(top_ref, 2 * MASKED)

        def one_chip(i, inner):
            place = jnp.where(i % 2 == 1, (i + 1) // 2, -(i // 2))
            chip = chip_at(me, place, chips)

            @pl.when(chip <= me // 2)
            def _():
                keys, values = keys_ref[i], with_ones(values_ref[i])
                barred = jnp.where(chip == me // 2, MASKED, 0.0)
                bias = jnp.where(allowed_here(me % 2, tokens), 0.0, barred)
                for first, rows in chunks(tokens):
                    scores = scores_of(head_rows(*queries, first), keys)
                    scores = jnp.where(bias < 0.0, MASKED, scores)
                    old = top_ref[rows, :]
                    top = jnp.maximum(old, row_top(scores))
                    factor = jnp.exp2(old - top)
                    weights = weights_of(scores, top).astype(jnp.bfloat16)
                    update = jnp.dot(weights, values, preferred_element_type=jnp.float32)
                    acc_ref[rows, :] = acc_ref[rows, :] * factor + update[:, :DH]
                    total_ref[rows, :] = total_ref[rows, :] * factor + update[:, DH:]
                    top_ref[rows, :] = top

            return inner

        lax.fori_loop(0, chips, one_chip, 0)
        put(group, divide(acc_ref[...], total_ref[...]))

    for_groups(one_group)


def last_kernel(chips, me_ref, q_ref, sib_q_ref, *refs):
    blocks, (shift_ref, acc_ref, total_ref, gain_ref) = (refs[0], refs[1:3]), refs[3:7]
    tables, sources = refs[7:9], refs[9 : 10 + 2 * chips]
    refs = refs[10 + 2 * chips :]
    weights, refs = refs[:2], refs[2:]
    out_refs, picked_refs, loaded = refs[:2], refs[2:4], refs[4:6]
    rows_ref, worst_ref, sem, load_sems, *scratch = refs[6:]
    loads = [
        pltpu.make_async_copy(half_rows(me_ref, weight, False), target, load_sems.at[i])
        for i, (weight, target) in enumerate(zip(weights, loaded))
    ]
    for load in loads:
        load.start()
    q_refs = (q_ref, sib_q_ref)
    tokens, half_width = q_ref.shape
    me = me_ref[0]
    _, factors = factors_of(me, [chips // 2] * 2, chips)
    worst_ref[...] = jnp.zeros_like(worst_ref)

    def put(group, result):
        put_heads(out_refs, rows_ref, tables, group, result)

    def one_group(group, columns):
        keys, values = join_blocks(blocks, factors, columns)
        queries = group_queries(q_refs, group)
        results = []
        for first, rows in chunks(tokens):
            update = fold(queries, first, keys, values, shift_ref[group, rows, :])
            total = total_ref[group, rows, :] + update[:, DH:]
            worst_ref[...] = jnp.maximum(worst_ref[...], jnp.where(total <= SUM_LIMIT, 0.0, 1.0))
            results.append(divide(acc_ref[group, rows, :] + update[:, :DH], total))
        put(group, jnp.concatenate(results, axis=0))

    for_groups(one_group)
    fits = jnp.max(worst_ref[...]) < 0.5

    @pl.when(jnp.logical_not(fits))
    def _():
        running_attention(chips, me, sources, q_refs, put, scratch, sem)

    columns = pl.ds(pl.multiple_of(me % 2 * half_width, half_width), half_width)
    rows = rows_ref[...]
    squares = jnp.broadcast_to(jnp.sum(rows * rows, axis=1, keepdims=True), (2 * CAP, DH))
    upper = squares.astype(jnp.bfloat16).astype(jnp.float32)
    lower = (squares - upper).astype(jnp.bfloat16).astype(jnp.float32)
    lane = lax.broadcasted_iota(jnp.int32, squares.shape, 1)
    rows = (rows * gain_ref[:, columns]).astype(jnp.bfloat16)
    squares = jnp.where(lane < DH // 2, upper, lower).astype(jnp.bfloat16)
    for i, ref in enumerate(picked_refs):
        ref[:, :half_width] = rows[i * CAP : (i + 1) * CAP]
        ref[:, half_width:] = squares[i * CAP : (i + 1) * CAP]
    for load in loads:
        load.wait()


class Attention:
    def __init__(self, me, queries, chips):
        self.me, self.queries, self.chips = me, queries, chips
        self.tokens, self.width = queries[0].shape
        self.rows = 2 * GROUP * self.tokens
        self.state_shape = pltpu.VMEM((HK // 2, self.rows, DH), jnp.float32)

    def call(self, kernel, name, args, others, out_shape, out_others, scratch, aliases=None):
        vmem, anywhere = pl.BlockSpec(memory_space=pltpu.VMEM), pl.BlockSpec(memory_space=pl.ANY)
        return pl.pallas_call(
            kernel,
            in_specs=[pl.BlockSpec(memory_space=pltpu.SMEM)]
            + [vmem] * (2 + len(args))
            + [anywhere] * len(others),
            out_specs=[vmem] * len(out_shape) + [anywhere] * len(out_others),
            out_shape=[*out_shape, *out_others],
            scratch_shapes=scratch,
            input_output_aliases=aliases or {},
            compiler_params=pltpu.CompilerParams(vmem_limit_bytes=ATTEND_MIB * MIB),
            cost_estimate=SMALL,
            name=name,
        )(self.me, *self.queries, *args, *others)

    def own(self, own, sib, weights=()):
        loads = len(weights)
        results = self.call(
            functools.partial(own_kernel, loads),
            "attend_own",
            (own, sib),
            [in_hbm(x) for x in weights],
            [self.state_shape] * 3,
            [pltpu.VMEM(x.shape, x.dtype) for x in weights],
            [pltpu.SemaphoreType.DMA] * loads,
        )
        return list(results[:2]), results[2], results[3:]

    def step(self, blocks, places, groups, shift, state, weights=()):
        count, loads = len(blocks), len(weights)
        results = self.call(
            functools.partial(step_kernel, self.chips, places, groups, loads),
            "attend_step",
            (*blocks, shift, *state),
            [in_hbm(x) for x in weights],
            [self.state_shape] * 2,
            [pltpu.VMEM(x.shape, x.dtype) for x in weights],
            [pltpu.SemaphoreType.DMA] * loads,
            {count + 4: 0, count + 5: 1},
        )
        return list(results[:2]), results[2:]

    def last(self, blocks, shift, state, gain, tables, sources, weights):
        out = pltpu.VMEM((self.tokens, self.width), jnp.bfloat16)
        picked = pltpu.VMEM((CAP, self.width + DH), jnp.bfloat16)
        loaded = [pltpu.VMEM((x.shape[0] // 2, x.shape[1]), x.dtype) for x in weights]
        kept = pltpu.VMEM((self.chips, 2 * self.tokens, DH), jnp.bfloat16)
        sums = pltpu.VMEM((self.rows, DH), jnp.float32)
        return self.call(
            functools.partial(last_kernel, self.chips),
            "attend_last",
            (*blocks, shift, *state, gain, *tables),
            (*sources, *(in_hbm(x) for x in weights)),
            [out, out, picked, picked],
            loaded,
            [
                pltpu.VMEM((2 * CAP, self.width), jnp.float32),
                pltpu.VMEM((STACK * 2 * self.tokens, DH), jnp.float32),
                pltpu.SemaphoreType.DMA,
                pltpu.SemaphoreType.DMA((len(weights),)),
                kept,
                kept,
                sums,
                sums,
                sums,
            ],
        )


def halves_kernel(stacks, me_ref, *refs):
    count = sum(stacks)
    sources, outs, sems = list(refs[:count]), refs[count:-1], refs[-1]
    core = me_ref[0] % 2
    copies = []
    for size, keep_ref, give_ref in zip(stacks, outs[::2], outs[1::2]):
        for i in range(size):
            source = sources.pop(0)
            rows, width = source.shape
            for side, target in ((core, keep_ref), (1 - core, give_ref)):
                columns = pl.ds(pl.multiple_of(side * (width // 2), width // 2), width // 2)
                copies.append((source.at[:, columns], target.at[pl.ds(i * rows, rows)]))
    copies = [pltpu.make_async_copy(*ends, sems.at[i]) for i, ends in enumerate(copies)]
    for copy in copies:
        copy.start()
    for copy in copies:
        copy.wait()


def halves(me, *stacks):
    anywhere = pl.BlockSpec(memory_space=pl.ANY)
    arrays = [x for stack in stacks for x in stack]
    outs = []
    for stack in stacks:
        rows, width = stack[0].shape
        outs += [pltpu.VMEM((len(stack) * rows, width // 2), stack[0].dtype)] * 2
    return pl.pallas_call(
        functools.partial(halves_kernel, [len(stack) for stack in stacks]),
        in_specs=[pl.BlockSpec(memory_space=pltpu.SMEM)] + [anywhere] * len(arrays),
        out_specs=[anywhere] * len(outs),
        out_shape=outs,
        scratch_shapes=[pltpu.SemaphoreType.DMA((2 * len(arrays),))],
        compiler_params=pltpu.CompilerParams(vmem_limit_bytes=MIB),
        cost_estimate=SMALL,
        name="halves",
    )(me, *(in_hbm(x) for x in arrays))


def half_rows(me_ref, ref, sibling):
    half = ref.shape[0] // 2
    side = 1 - me_ref[0] % 2 if sibling else me_ref[0] % 2
    return ref.at[pl.ds(pl.multiple_of(side * half, half), half), :]


def place_kernel(spots, *refs):
    blocks, out_ref = refs[: len(spots)], refs[-1]
    for index, ref in zip(spots, blocks):
        out_ref[index * CAP : (index + 1) * CAP] = ref[...]


def place(blocks, spots, rows):
    vmem = pl.BlockSpec(memory_space=pltpu.VMEM)
    earlier = [] if isinstance(rows, tuple) else [rows]
    shape = rows.shape if earlier else rows
    return pl.pallas_call(
        functools.partial(place_kernel, spots),
        in_specs=[vmem] * (len(blocks) + len(earlier)),
        out_specs=vmem,
        out_shape=pltpu.VMEM(shape, jnp.bfloat16),
        input_output_aliases={len(blocks): 0} if earlier else {},
        compiler_params=pltpu.CompilerParams(vmem_limit_bytes=4 * MIB),
        cost_estimate=SMALL,
        name="place",
    )(*blocks, *earlier)


def contract(rows_ref, gate_ref, up_ref, gate_sum, up_sum, order):
    half = gate_ref.shape[0]
    depth = min(1024, half)

    def one_part(step, carry):
        columns = pl.ds(pl.multiple_of(step * depth, depth), depth)
        part = order(rows_ref[:, columns])
        gate_sum[...] += jnp.dot(part, gate_ref[columns, :], preferred_element_type=jnp.float32)
        up_sum[...] += jnp.dot(part, up_ref[columns, :], preferred_element_type=jnp.float32)
        return carry

    lax.fori_loop(0, half // depth, one_part, 0)


def first_kernel(me_ref, rows_ref, gate_ref, up_ref, *refs):
    sources, (gate_sum, up_sum), targets, sems = refs[:2], refs[2:4], refs[4:6], refs[6]
    copies = [
        pltpu.make_async_copy(half_rows(me_ref, source, True), target, sems.at[i])
        for i, (source, target) in enumerate(zip(sources, targets))
    ]
    for copy in copies:
        copy.start()
    gate_sum[...] = jnp.zeros_like(gate_sum)
    up_sum[...] = jnp.zeros_like(up_sum)
    contract(rows_ref, gate_ref, up_ref, gate_sum, up_sum, lambda part: part)
    for copy in copies:
        copy.wait()


def second_kernel(rows_ref, gate_ref, up_ref, own_ref, gate_in, up_in, source_ref, out_ref, *refs):
    targets, (gate_sum, up_sum, sems) = refs[:PIECES], refs[PIECES:]
    piece = targets[0].shape[1]
    copies = [
        pltpu.make_async_copy(source_ref.at[:, pl.ds(i * piece, piece)], target, sems.at[i])
        for i, target in enumerate(targets)
    ]
    for copy in copies:
        copy.start()
    middle, half = rows_ref.shape[0] // 2, gate_ref.shape[0]

    def order(part):
        return jnp.concatenate([part[middle:], part[:middle]], axis=0)

    gate_sum[...] = gate_in[...]
    up_sum[...] = up_in[...]
    contract(rows_ref, gate_ref, up_ref, gate_sum, up_sum, order)
    squares = own_ref[:, half:].astype(jnp.float32) + order(rows_ref[:, half:].astype(jnp.float32))
    squares = squares[:, :1] + squares[:, DH // 2 : DH // 2 + 1]
    factor = lax.rsqrt(squares / (2 * half) + 1e-05)
    gate = gate_sum[...] * factor
    out_ref[...] = (gate / (1.0 + jnp.exp(-gate)) * (up_sum[...] * factor)).astype(jnp.bfloat16)
    for copy in copies:
        copy.wait()


def hidden_calls(me, rows, other_rows, loaded, w_gate, w_up, w_down):
    count, units, width = rows.shape[0], w_down.shape[0], w_down.shape[1]
    vmem, anywhere = pl.BlockSpec(memory_space=pltpu.VMEM), pl.BlockSpec(memory_space=pl.ANY)
    sums = [pltpu.VMEM((count, units), jnp.float32)] * 2
    params = pltpu.CompilerParams(vmem_limit_bytes=8 * MIB)
    cost = pl.CostEstimate(
        flops=2 * count * width * units, bytes_accessed=2 * width * units, transcendentals=count * units
    )
    *partial, gate, up = pl.pallas_call(
        first_kernel,
        in_specs=[pl.BlockSpec(memory_space=pltpu.SMEM)] + [vmem] * 3 + [anywhere] * 2,
        out_specs=[vmem] * 2 + [anywhere] * 2,
        out_shape=sums + [pltpu.VMEM((width // 2, units), w_gate.dtype)] * 2,
        scratch_shapes=[pltpu.SemaphoreType.DMA((2,))],
        compiler_params=params,
        cost_estimate=cost,
        name="hidden_first",
    )(me, rows, *loaded, in_hbm(w_gate), in_hbm(w_up))
    hidden, *downs = pl.pallas_call(
        second_kernel,
        in_specs=[vmem] * 6 + [anywhere],
        out_specs=[vmem] + [anywhere] * PIECES,
        out_shape=[pltpu.VMEM((count, units), jnp.bfloat16)]
        + [pltpu.VMEM((units, width // PIECES), w_down.dtype)] * PIECES,
        scratch_shapes=sums + [pltpu.SemaphoreType.DMA((PIECES,))],
        compiler_params=params,
        cost_estimate=cost,
        name="hidden_second",
    )(other_rows, gate, up, rows, *partial, in_hbm(w_down))
    return hidden, downs


def down_kernel(hidden_ref, down_ref, *refs):
    copies = []
    if len(refs) == 2:
        own_ref, sib_ref = refs
    else:
        me_ref, *parts, own_ref, sib_ref, result_ref, sems = refs
        width = parts[0].shape[1]
        core = me_ref[0] % 2
        for i, (side, source) in enumerate(zip((core, 1 - core), parts)):
            columns = pl.ds(pl.multiple_of(side * width, width), width)
            copies.append(pltpu.make_async_copy(source, result_ref.at[:, columns], sems.at[i]))
    for copy in copies:
        copy.start()
    middle, width = own_ref.shape
    cols = min(1024, width)

    def one_part(step, carry):
        columns = pl.ds(pl.multiple_of(step * cols, cols), cols)
        part = jnp.dot(hidden_ref[...], down_ref[:, columns], preferred_element_type=jnp.float32)
        part = part.astype(jnp.bfloat16)
        own_ref[:, columns] = part[:middle]
        sib_ref[:, columns] = part[middle:]
        return carry

    lax.fori_loop(0, width // cols, one_part, 0)
    for copy in copies:
        copy.wait()


def down_call(hidden, w_down, halves=()):
    rows, units = hidden.shape
    width = w_down.shape[1]
    vmem, anywhere = pl.BlockSpec(memory_space=pltpu.VMEM), pl.BlockSpec(memory_space=pl.ANY)
    more = [pl.BlockSpec(memory_space=pltpu.SMEM), anywhere, anywhere] if halves else []
    outs = [pltpu.VMEM((rows // 2, width), jnp.bfloat16)] * 2
    if halves:
        tokens, part = halves[1].shape
        outs.append(jax.ShapeDtypeStruct((tokens, 2 * part), jnp.bfloat16))
    return pl.pallas_call(
        down_kernel,
        in_specs=[vmem] * 2 + more,
        out_specs=[vmem] * 2 + [anywhere] * (len(outs) - 2),
        out_shape=outs,
        scratch_shapes=[pltpu.SemaphoreType.DMA((2,))] if halves else [],
        compiler_params=pltpu.CompilerParams(vmem_limit_bytes=8 * MIB),
        cost_estimate=pl.CostEstimate(
            flops=2 * rows * width * units,
            bytes_accessed=2 * width * units + 2 * rows * width,
            transcendentals=0,
        ),
        name="down",
    )(hidden, w_down, *halves)


def spread_kernel(start, *refs):
    parts, table_ref, out_ref, kept_ref, sems = refs[:4], refs[4], *refs[-3:]
    table = table_ref[...]
    width = kept_ref.shape[1]
    cols = min(1024, width)
    copies = []
    for i in range(width // cols):
        columns = slice(i * cols, (i + 1) * cols)
        total = sum(ref[:CAP, columns].astype(jnp.float32) for ref in parts).astype(jnp.bfloat16)
        kept_ref[:, columns] = lax.dot_general(
            table,
            jnp.concatenate([total] * PARTS, axis=0),
            (((0,), (0,)), ((), ())),
            preferred_element_type=jnp.float32,
        ).astype(jnp.bfloat16)
        target = out_ref.at[:, pl.ds(start + i * cols, cols)]
        copies.append(pltpu.make_async_copy(kept_ref.at[:, pl.ds(i * cols, cols)], target, sems.at[i]))
        copies[-1].start()
    for copy in copies:
        copy.wait()


def spread_call(parts, table, piece, pieces, previous):
    tokens = table.shape[1]
    width = parts[0].shape[1]
    earlier = [] if previous is None else [previous]
    vmem, anywhere = pl.BlockSpec(memory_space=pltpu.VMEM), pl.BlockSpec(memory_space=pl.ANY)
    return pl.pallas_call(
        functools.partial(spread_kernel, piece * width),
        in_specs=[vmem] * 5 + [anywhere] * len(earlier),
        out_specs=anywhere,
        out_shape=jax.ShapeDtypeStruct((tokens, width * pieces), jnp.bfloat16),
        input_output_aliases={5: 0} if earlier else {},
        scratch_shapes=[
            pltpu.VMEM((tokens, width), jnp.bfloat16),
            pltpu.SemaphoreType.DMA((max(1, width // 1024),)),
        ],
        compiler_params=pltpu.CompilerParams(vmem_limit_bytes=8 * MIB),
        cost_estimate=SMALL,
        name="spread",
    )(*parts, table, *earlier)


def add_kernel(row, columns, place, mine_ref, other_ref, *refs):
    received_ref, out_ref = (refs[0] if len(refs) > 1 else None), refs[-1]
    rows = slice(row, row + CAP)
    total = mine_ref[rows, columns].astype(jnp.float32) + other_ref[rows, columns].astype(jnp.float32)
    if received_ref is None:
        out_ref[...] = total.astype(jnp.bfloat16)
        return
    start, width = place, received_ref.shape[1]
    part = total[:, start : start + width] + received_ref[...].astype(jnp.float32)
    out_ref[:, start : start + width] = part.astype(jnp.bfloat16)
    if width < out_ref.shape[1]:
        rest = slice(width, None) if start == 0 else slice(0, start)
        out_ref[:, rest] = total[:, rest].astype(jnp.bfloat16)


def add_call(mine, other, index, columns, received=None, place=0):
    vmem = pl.BlockSpec(memory_space=pltpu.VMEM)
    more = () if received is None else (received,)
    return pl.pallas_call(
        functools.partial(add_kernel, index * CAP, columns, place),
        in_specs=[vmem] * (2 + len(more)),
        out_specs=vmem,
        out_shape=pltpu.VMEM((CAP, columns.stop - columns.start), jnp.bfloat16),
        compiler_params=pltpu.CompilerParams(vmem_limit_bytes=4 * MIB),
        cost_estimate=SMALL,
        name="add",
    )(mine, other, *more)


def reduce_chip_rows(pieces, half, chips, moves, token):
    width = pieces[0][0].shape[1]
    middle = width // 2
    chains = [(piece, side) for piece in range(len(pieces)) for side in range(2)]
    received = [None] * len(chains)
    for distance in range(half, 0, -1):
        for i, (piece, side) in enumerate(chains):
            mine, other = pieces[piece]
            if distance == half:
                columns = slice(side * middle, (side + 1) * middle)
                total = add_call(mine, other, chips - 1, columns)
            else:
                received[i], token = lax.optimization_barrier((received[i], token))
                index = distance if side else half - 1 + distance
                place = side * middle if distance == half - 1 else 0
                total = add_call(mine, other, index, slice(0, width), received[i], place)
            received[i] = moves[side](total)
    return [(*pieces[p], *received[2 * p : 2 * p + 2]) for p in range(len(pieces))]


def per_device(chips, queries, keys, values, norm_gain, expert_ids, gates, w_gate, w_up, w_down):
    right, left, sibling = permutations(chips)
    half = chips // 2
    go_right = lambda x: lax.ppermute(x, "ctx", right)
    go_left = lambda x: lax.ppermute(x, "ctx", left)
    swap = lambda x: lax.ppermute(x, "ctx", sibling)

    me = lax.axis_index("ctx").astype(jnp.int32).reshape(1)
    tokens = queries.shape[0]
    hits = (expert_ids == 0).astype(jnp.float32)
    chosen = jnp.sum(hits, axis=1)
    position = jnp.arange(tokens, dtype=jnp.int32)
    before = (position[None, :] < position[:, None]).astype(jnp.float32)
    slot = jnp.sum(before * chosen[None, :], axis=1).astype(jnp.int32)
    table = jnp.logical_and(
        slot[None, :] == jnp.arange(CAP, dtype=jnp.int32)[:, None], chosen[None, :] > 0
    ).astype(jnp.float32)
    rest = jnp.sum(gates * hits, axis=1)
    weights = []
    for _ in range(PARTS):
        part = lax.reduce_precision(rest, 8, 7)
        weights.append(table * part[None, :])
        rest = rest - part
    weighted = jnp.concatenate(weights, axis=0).astype(jnp.bfloat16)
    table = table.astype(jnp.bfloat16)

    own, give, q_own, q_give = halves(me, (keys, values), (queries,))
    across_right, across_left = [
        lax.ppermute(give, "ctx", [(i, j ^ 1) for i, j in pairs]) for pairs in (right, left)
    ]
    chains = [(go_right(own), go_left(own)), (across_right, across_left)]
    sib, q_sib = swap(give), swap(q_give)
    sib_table = swap(table)
    attention = Attention(me, (q_own, q_sib), chips)
    state, shift, _ = attention.own(own, sib)
    sources = [own, sib]
    middle, late = HK // 4, None
    for step in range(1, half):
        *chains[0], state = lax.optimization_barrier((*chains[0], state))
        if late is not None:
            state, _ = attention.step(*late, (middle, HK // 2), shift, state)
        chains[1], _, state = lax.optimization_barrier((chains[1], chains[0], state))
        late = [chain[side] for side in range(2) for chain in chains], [step, step, -step, -step]
        sources += late[0]
        if step < half - 1:
            chains = [(go_right(chain[0]), go_left(chain[1])) for chain in chains]
        else:
            far_sib = go_right(chains[1][0][:tokens]), go_left(chains[1][1][tokens:])
            opposite = [go_right(chains[0][0]), *far_sib]
        state, _ = attention.step(*late, (0, middle), shift, state)
    state, _ = attention.step(*late, (middle, HK // 2), shift, state)
    opposite, state = lax.optimization_barrier((opposite, state))
    sources += opposite
    mine, theirs, *picked, gate, up = attention.last(
        opposite, shift, state, norm_gain[None, :], (table, sib_table), sources, (w_gate, w_up)
    )

    chains = [(0, 1), (1, 0), (0, 0), (1, 1)]
    moves = [(go_right, go_left)[side] for _, side in chains]
    received = [move(picked[core]) for move, (core, _) in zip(moves, chains)]
    rows = place(picked, [0, chips], (2 * chips * CAP, picked[0].shape[1]))
    theirs = swap(theirs)
    for step in range(1, half):
        spots = [core * chips + side * (half - 1) + step for core, side in chains]
        blocks = list(received)
        for i, move in enumerate(moves):
            if step < half - 1 or i < 2:
                blocks[i], rows = lax.optimization_barrier((received[i], rows))
                received[i] = move(blocks[i])
        if step < half - 1:
            rows = place(blocks, spots, rows)
    rows = place(blocks + received[:2], spots + [chips - 1, 2 * chips - 1], rows)
    hidden, downs = hidden_calls(me, rows, swap(rows), (gate, up), w_gate, w_up, w_down)

    partial = []
    for piece in range(PIECES):
        if piece == 0:
            own, sib, result = down_call(hidden, downs[piece], (me, mine, theirs))
        else:
            own, sib = down_call(hidden, downs[piece])
        partial.append((own, swap(sib)))
    mixed = None
    for piece, parts in enumerate(reduce_chip_rows(partial, half, chips, (go_right, go_left), weighted)):
        mixed = spread_call(parts, weighted, piece, PIECES, mixed)
    return (result, mixed)


def solution(mesh):
    placed = (
        P(("groups", "ctx"), None),
        P(("groups", "ctx"), None),
        P(("groups", "ctx"), None),
        P(),
        P(("groups", "ctx"), None),
        P(("groups", "ctx"), None),
        P(None, "ctx"),
        P(None, "ctx"),
        P("ctx", None),
    )
    return jax.shard_map(
        functools.partial(per_device, mesh.shape["ctx"] // 2),
        mesh=mesh,
        in_specs=placed,
        out_specs=(P(("groups", "ctx"), None), P(("groups", "ctx"), None)),
        check_vma=False,
    )
```
